32 devices in a mesh: dp: 8 (over y, x, core), ctx: 4 (over z).
Axes of the slice: x: 2, y: 2, z: 4, core: 2. Of those that a mesh axis runs over, the one named last changes fastest.
Arguments:
- block_in: bfloat16 [8, 2048, 768], P('dp', 'ctx'), may hold values from -6 to 6
- out_grad: bfloat16 [8, 2048, 768], P('dp', 'ctx'), may hold values from -6 to 6
- lengths: int32 [8], P('dp'), may hold values from 128 to 2048, as said below
- ln1_gain: bfloat16 [768], P(('dp', 'ctx')), may hold values from 0.099609375 to 1.8984375
- ln1_bias: bfloat16 [768], P(('dp', 'ctx')), may hold values from -3 to 3
- qkv_weight: bfloat16 [768, 2304], P(('dp', 'ctx')), may hold values from -0.25 to 0.25
- qkv_bias: bfloat16 [2304], P(('dp', 'ctx')), may hold values from -3 to 3
- out_weight: bfloat16 [768, 768], P(('dp', 'ctx')), may hold values from -1.75 to 1.75
- out_bias: bfloat16 [768], P(('dp', 'ctx')), may hold values from -3 to 3
- ln2_gain: bfloat16 [768], P(('dp', 'ctx')), may hold values from 0.099609375 to 1.8984375
- ln2_bias: bfloat16 [768], P(('dp', 'ctx')), may hold values from -3 to 3
- fc1_weight: bfloat16 [768, 3072], P(('dp', 'ctx')), may hold values from -0.21875 to 0.21875
- fc1_bias: bfloat16 [3072], P(('dp', 'ctx')), may hold values from -3 to 3
- fc2_weight: bfloat16 [3072, 768], P(('dp', 'ctx')), may hold values from -0.109375 to 0.109375
- fc2_bias: bfloat16 [768], P(('dp', 'ctx')), may hold values from -3 to 3
Outputs:
- block_out: bfloat16 [8, 2048, 768], P('dp', 'ctx')
- input_grad: bfloat16 [8, 2048, 768], P('dp', 'ctx')
- ln1_gain_grad: float32 [768], P(('dp', 'ctx'))
- ln1_bias_grad: float32 [768], P(('dp', 'ctx'))
- qkv_weight_grad: float32 [768, 2304], P(('dp', 'ctx'))
- qkv_bias_grad: float32 [2304], P(('dp', 'ctx'))
- out_weight_grad: float32 [768, 768], P(('dp', 'ctx'))
- out_bias_grad: float32 [768], P(('dp', 'ctx'))
- ln2_gain_grad: float32 [768], P(('dp', 'ctx'))
- ln2_bias_grad: float32 [768], P(('dp', 'ctx'))
- fc1_weight_grad: float32 [768, 3072], P(('dp', 'ctx'))
- fc1_bias_grad: float32 [3072], P(('dp', 'ctx'))
- fc2_weight_grad: float32 [3072, 768], P(('dp', 'ctx'))
- fc2_bias_grad: float32 [768], P(('dp', 'ctx'))
- example_norms: float32 [8], P('dp')
The draws below stay inside these ranges and needn't reach their ends.
Inputs may be any that keep to these rules, and one draw needn't show every extreme that they name: Example e holds real tokens at positions 0 to lengths[e] - 1 and padding after them; at least one example is 2048 long.
All inputs are finite; a program needn't handle non-finite values.
Results may differ from the reference program's by a relative error of at most 0.012.
The reference program's roundings to bfloat16 on the way count: a program that leaves them out, or rounds other values in their place, can miss the bound.
Values may be sent and summed in bfloat16 or wider, within the bound.
A program may use at most 96 MiB of HBM per device.

```python
import math
import jax
import jax.numpy as jnp
from jax import lax

D = 768
HEADS = 12
HEAD_DIM = 64
ROT = 16
FF = 3072
LEN = 2048
MIN_LEN = 128
EXAMPLES = 8


shared_rank = 8


def draw_lengths(key, part):
    level_key, other_key, extra_key, place_key = jax.random.split(key, 4)
    levels = int(math.log2(LEN // MIN_LEN))
    levels_drawn = jnp.maximum(jax.random.randint(level_key, (EXAMPLES,), 0, levels + 1), jax.random.randint(other_key, (EXAMPLES,), 0, levels + 1))
    base_len = MIN_LEN * jnp.power(2, levels_drawn)
    extra_len = jax.random.randint(extra_key, (EXAMPLES,), 0, base_len)
    length = jnp.minimum(base_len + extra_len, LEN)
    chosen = jax.random.randint(place_key, (), 0, EXAMPLES)
    return jnp.where(jnp.arange(EXAMPLES) == chosen, LEN, length).astype(jnp.int32)


def shared_signs(key):
    return jax.random.rademacher(key, (EXAMPLES, LEN, shared_rank), jnp.float32)


def shared_part(signs, directions, amplitude):
    summed = jnp.zeros((EXAMPLES, LEN, D), jnp.float32)
    for place in range(shared_rank):
        summed = summed + signs[:, :, place:place + 1] * directions[:, place:place + 1, :]
    return summed * (amplitude / math.sqrt(shared_rank))


def draw_block_in(key, part):
    signs = shared_signs(key)
    key = jax.random.fold_in(key, 11)
    noise_key, direction_key = jax.random.split(key, 2)
    directions = jax.random.normal(direction_key, (EXAMPLES, shared_rank, D), jnp.float32)
    noise = jnp.clip(jax.random.normal(noise_key, (EXAMPLES, LEN, D), jnp.float32), -4.0, 4.0)
    summed = 0.7 * noise + shared_part(signs, directions, 0.7)
    return jnp.clip(summed, -6.0, 6.0).astype(jnp.bfloat16)


def draw_out_grad(key, part):
    signs = shared_signs(key)
    key = jax.random.fold_in(key, 7)
    noise_key, direction_key, flip_key = jax.random.split(key, 3)
    directions = jax.random.normal(direction_key, (EXAMPLES, shared_rank, D), jnp.float32)
    flips = jax.random.rademacher(flip_key, (EXAMPLES, LEN, 1), jnp.float32)
    noise = 0.6 * jnp.clip(jax.random.normal(noise_key, (EXAMPLES, LEN, D), jnp.float32), -3.0, 3.0)
    ramp = 0.7 * (1.0 + 2.0 * jnp.arange(LEN, dtype=jnp.float32) / LEN)
    summed = noise + ramp[None, :, None] * flips * shared_part(signs, directions, 0.8)
    return jnp.clip(summed, -6.0, 6.0).astype(jnp.bfloat16)


def shard_levels(rng, shape, pieces, low, largest):
    loudness = 1.0
    for position, blocks in pieces:
        draws = jax.random.uniform(jax.random.fold_in(jax.random.fold_in(rng, 6), position), (blocks,), jnp.float32, low / len(pieces), largest / len(pieces))
        loudness = loudness * jnp.repeat(jnp.exp(draws), shape[position] // blocks).reshape((-1,) + (1,) * (len(shape) - 1 - position))
    return loudness


def gaussian(stream_key, shape, deviation, limit, cuts=(), held_as=jnp.bfloat16):
    array = jax.random.normal(stream_key, shape, jnp.float32) * deviation
    if len(cuts) > 0:
        array = shard_levels(stream_key, shape, cuts, -0.22, 0.18) * array
    return jnp.clip(array, min=-limit, max=limit).astype(held_as)


def setup_inputs(seed: int = 0) -> dict:
    keys = jax.random.split(jax.random.key(seed), 16)
    block_in = draw_block_in(jax.random.fold_in(keys[15], 71), 0)
    out_grad = draw_out_grad(jax.random.fold_in(keys[15], 71), 0)
    lengths = draw_lengths(jax.random.fold_in(keys[15], 71), 0)
    ln1_gain = jnp.clip(1.0 + 0.18 * jax.random.normal(keys[3], (D,), jnp.float32), 0.099609375, 1.8984375).astype(jnp.bfloat16)
    ln1_bias = gaussian(keys[4], (D,), 0.5, 3.0, ((0, 32),))
    qkv_weight = gaussian(keys[5], (D, 3 * D), (2 * D // 3) ** -0.5, 0.25, ((0, 32),))
    qkv_bias = gaussian(keys[6], (3 * D,), 0.5, 3.0, ((0, 32),))
    out_weight = gaussian(keys[7], (D, D), (D // 64) ** -0.5, 1.75, ((0, 32),))
    out_bias = gaussian(keys[8], (D,), 0.5, 3.0, ((0, 32),))
    ln2_gain = jnp.clip(1.0 + 0.18 * jax.random.normal(keys[9], (D,), jnp.float32), 0.099609375, 1.8984375).astype(jnp.bfloat16)
    ln2_bias = gaussian(keys[10], (D,), 0.5, 3.0, ((0, 32),))
    fc1_weight = gaussian(keys[11], (D, FF), D ** -0.5, 0.21875, ((0, 32),))
    fc1_bias = gaussian(keys[12], (FF,), 0.5, 3.0, ((0, 32),))
    fc2_weight = gaussian(keys[13], (FF, D), FF ** -0.5, 0.109375, ((0, 32),))
    fc2_bias = gaussian(keys[14], (D,), 0.5, 3.0, ((0, 32),))
    return dict(block_in=block_in, out_grad=out_grad, lengths=lengths, ln1_gain=ln1_gain, ln1_bias=ln1_bias, qkv_weight=qkv_weight, qkv_bias=qkv_bias, out_weight=out_weight, out_bias=out_bias, ln2_gain=ln2_gain, ln2_bias=ln2_bias, fc1_weight=fc1_weight, fc1_bias=fc1_bias, fc2_weight=fc2_weight, fc2_bias=fc2_bias)


@jax.custom_vjp
def low(v):
    return lax.optimization_barrier(v.astype(jnp.bfloat16)).astype(jnp.float32)

@jax.custom_vjp
def low_back(v):
    return v

def low_keep(v):
    return (low(v), None)

def low_pass(kept, grad):
    return (grad,)

def back_keep(v):
    return (v, None)

def back_low(kept, grad):
    return (low(grad),)
low.defvjp(low_keep, low_pass)
low_back.defvjp(back_keep, back_low)
highest = lax.Precision.HIGHEST
eps_norm = 1e-05
neg_big = -1e+30
query_block = 512

def layer_norm(values, norm_gain, norm_shift):
    row_mean = lax.optimization_barrier(jnp.mean(values, axis=-1, keepdims=True))
    centered = values - row_mean
    row_var = lax.optimization_barrier(jnp.mean(centered * centered, axis=-1, keepdims=True))
    return centered * lax.rsqrt(row_var + eps_norm) * norm_gain + norm_shift

def rotary_tables(positions):
    freq_index = jnp.arange(ROT // 2, dtype=jnp.float32)
    inv_freqs = jnp.exp(freq_index * (-2.0 * math.log(10000.0) / ROT))
    angles = positions.astype(jnp.float32)[:, None] * inv_freqs[None, :]
    return (jnp.cos(angles)[:, None, :], jnp.sin(angles)[:, None, :])

def turn(values, cosine, sine_table):
    half_width = cosine.shape[-1]
    first_half = values[..., :half_width]
    second_half = values[..., half_width:2 * half_width]
    return jnp.concatenate([first_half * cosine - second_half * sine_table, second_half * cosine + first_half * sine_table, values[..., 2 * half_width:]], axis=-1)

def gelu_exact(pre_act):
    return 0.5 * pre_act * (1.0 + lax.erf(pre_act / math.sqrt(2.0)))

def attend_rows(queries, row_start, key_rows, value_rows, length):
    block_rows = queries.shape[0]
    scores = low_back(jnp.einsum('bhd,khd->hbk', queries, key_rows, precision=highest) * HEAD_DIM ** (-0.5))
    row_pos = row_start + jnp.arange(block_rows, dtype=jnp.int32)
    key_pos = jnp.arange(key_rows.shape[0], dtype=jnp.int32)
    valid = (key_pos[None, :] <= row_pos[:, None]) & (key_pos[None, :] < length)
    scores = jnp.where(valid[None], scores, neg_big)
    exponent = jnp.exp(scores - lax.optimization_barrier(jnp.max(scores, axis=-1, keepdims=True)))
    weights = exponent / lax.optimization_barrier(jnp.sum(exponent, axis=-1, keepdims=True))
    return jnp.einsum('hbk,khd->bhd', low(weights), value_rows, precision=highest)

def forward_one(block_rows, params, length):
    ln1_gain, ln1_bias, qkv_weight, qkv_bias, out_weight, out_bias, ln2_gain, ln2_bias, fc1_weight, fc1_bias, fc2_weight, fc2_bias = params
    positions = jnp.arange(LEN, dtype=jnp.int32)
    cosine, sine_table = rotary_tables(positions)
    attn_in = low(layer_norm(block_rows, ln1_gain, ln1_bias))
    qkv_all = low_back(jnp.dot(attn_in, qkv_weight, precision=highest) + qkv_bias)
    heads_shape = (LEN, HEADS, HEAD_DIM)
    queries = low(turn(qkv_all[:, :D].reshape(heads_shape), cosine, sine_table))
    key_rows = low(turn(qkv_all[:, D:2 * D].reshape(heads_shape), cosine, sine_table))
    value_rows = low(qkv_all[:, 2 * D:].reshape(heads_shape))
    block_width = min(query_block, LEN)
    block_count = LEN // block_width
    query_blocks = queries.reshape(block_count, block_width, HEADS, HEAD_DIM)
    starts = jnp.arange(block_count, dtype=jnp.int32) * block_width
    row_step = jax.checkpoint(lambda block_pair: attend_rows(block_pair[0], block_pair[1], key_rows, value_rows, length))
    attended = lax.map(row_step, (query_blocks, starts)).reshape(LEN, D)
    context = low(low_back(attended))
    attn_out = jnp.dot(context, out_weight, precision=highest) + out_bias
    mlp_in = low(layer_norm(block_rows, ln2_gain, ln2_bias))
    pre_act = low_back(jnp.dot(mlp_in, fc1_weight, precision=highest) + fc1_bias)
    hidden = low(gelu_exact(pre_act))
    mlp_out = jnp.dot(hidden, fc2_weight, precision=highest) + fc2_bias
    return block_rows + attn_out + mlp_out

def reference(block_in, out_grad, lengths, ln1_gain, ln1_bias, qkv_weight, qkv_bias, out_weight, out_bias, ln2_gain, ln2_bias, fc1_weight, fc1_bias, fc2_weight, fc2_bias):
    params = tuple((single.astype(jnp.float32) for single in (ln1_gain, ln1_bias, qkv_weight, qkv_bias, out_weight, out_bias, ln2_gain, ln2_bias, fc1_weight, fc1_bias, fc2_weight, fc2_bias)))
    positions = jnp.arange(LEN, dtype=jnp.int32)

    def one_example(running, inputs):
        block_rows, grad_rows, length = inputs
        rows_float = block_rows.astype(jnp.float32)
        live_rows = (positions < length).astype(jnp.float32)[:, None]
        cotangent = grad_rows.astype(jnp.float32) * live_rows
        result, pull_back = jax.vjp(lambda values, weights: forward_one(values, weights, length), rows_float, params)
        grad_input, grad_params = pull_back(cotangent)
        squares = sum((jnp.sum(gradient * gradient) for gradient in grad_params))
        return (running, (result.astype(jnp.bfloat16), grad_input.astype(jnp.bfloat16), grad_params, jnp.sqrt(squares)))
    unused, (block_out, input_grad, grad_params, example_norms) = lax.scan(one_example, jnp.zeros((), jnp.float32), (block_in, out_grad, lengths))
    mean_norm = jnp.mean(example_norms)
    factors = mean_norm / jnp.maximum(example_norms, mean_norm)
    clipped = [lax.optimization_barrier(jnp.sum(factors.reshape((-1,) + (1,) * (gradient.ndim - 1)) * gradient, axis=0)) for gradient in grad_params]
    return (block_out, input_grad, clipped[0], clipped[1], clipped[2], clipped[3], clipped[4], clipped[5], clipped[6], clipped[7], clipped[8], clipped[9], clipped[10], clipped[11], example_norms)
```

```python
import functools
import math

import jax
import jax.numpy as jnp
import numpy as np
from jax import lax
from jax.experimental import pallas as pl
from jax.experimental.pallas import tpu as pltpu
from jax.sharding import PartitionSpec as P

D = 768
HEADS = 12
HEAD_DIM = 64
ROT = 16
PAD = 128
eps_norm = 1e-05
neg_big = -1e30
root_half = math.sqrt(0.5)
inv_root_two_pi = 1.0 / math.sqrt(2.0 * math.pi)
f32 = jnp.float32
bf16 = jnp.bfloat16
VMEM_BYTES = 60 * 2**20


def dot(a, b, dims=((1,), (0,))):
    return lax.dot_general(a, b, (dims, ((), ())), preferred_element_type=f32)


def norm_parts(values):
    centered = values - jnp.mean(values, axis=-1, keepdims=True)
    row_var = jnp.mean(centered * centered, axis=-1, keepdims=True)
    inverse = lax.rsqrt(row_var + eps_norm)
    return centered * inverse, inverse


def turn(u, cosine, sine, first):
    partner = jnp.where(first, pltpu.roll(u, PAD - ROT // 2, 1), pltpu.roll(u, ROT // 2, 1))
    return u * cosine + partner * sine


def split3(v):
    hi = v.astype(bf16).astype(f32)
    mid = (v - hi).astype(bf16).astype(f32)
    low = (v - hi - mid).astype(bf16).astype(f32)
    return hi, mid, low


def fold(op, s):
    out = s[:, :PAD]
    for t in range(1, s.shape[1] // PAD):
        out = op(out, s[:, t * PAD : (t + 1) * PAD])
    return out


def attn_fwd_kernel(
    len_ref, x_ref, g_ref, b_ref, w_ref, wb_ref, cos_ref, sin_ref,
    q_ref, k_ref, v_ref, cf_ref, s_scr, q_scr, m_scr, l_scr, acc_scr,
):
    i = pl.program_id(0)
    nh = k_ref.shape[0]
    rows = x_ref.shape[0]
    length = len_ref[0]
    xhat, unused = norm_parts(x_ref[...].astype(f32))
    a1 = (xhat * g_ref[...] + b_ref[...]).astype(bf16)
    cosine, sine = cos_ref[...], sin_ref[...]
    lane = lax.broadcasted_iota(jnp.int32, (rows, PAD), 1)
    first = lane < ROT // 2
    key_pos = i * rows + lax.broadcasted_iota(jnp.int32, (rows, PAD), 0)
    key_bias = jnp.where(key_pos < length, 0.0, neg_big)
    here = pl.ds(pl.multiple_of(i * rows, rows), rows)
    qkv = dot(a1, w_ref[...]) + wb_ref[...]
    for h in range(nh):
        q = turn(qkv[:, h * PAD : (h + 1) * PAD], cosine, sine, first) * HEAD_DIM**-0.5
        q_scr[h] = q.astype(bf16)
        k = turn(qkv[:, (nh + h) * PAD : (nh + h + 1) * PAD], cosine, sine, first)
        k_ref[h, here] = jnp.where(lane == HEAD_DIM, key_bias, k).astype(bf16)
        v_ref[h, here] = qkv[:, (2 * nh + h) * PAD : (2 * nh + h + 1) * PAD].astype(bf16)

    causal = lax.broadcasted_iota(jnp.int32, (rows, rows), 0) >= lax.broadcasted_iota(
        jnp.int32, (rows, rows), 1
    )
    for h in range(nh):
        s = dot(q_scr[h], k_ref[h, here], ((1,), (1,)))
        s = jnp.where(causal, s, neg_big)
        s_scr[h, i] = s
        m_scr[h] = fold(jnp.maximum, s)

    def scores(j, carry):
        there = pl.ds(pl.multiple_of(j * rows, rows), rows)
        for h in range(nh):
            s = dot(q_scr[h], k_ref[h, there], ((1,), (1,)))
            s_scr[h, j] = s
            m_scr[h] = jnp.maximum(m_scr[h], fold(jnp.maximum, s))
        return carry

    lax.fori_loop(0, i, scores, 0)
    for h in range(nh):
        m_scr[h] = jnp.broadcast_to(jnp.max(m_scr[h], axis=-1, keepdims=True), (rows, PAD))
        l_scr[h] = jnp.zeros((rows, PAD), f32)
        acc_scr[h] = jnp.zeros((rows, PAD), f32)

    def weigh(j, carry):
        there = pl.ds(pl.multiple_of(j * rows, rows), rows)
        for h in range(nh):
            p = jnp.exp(s_scr[h, j] - m_scr[h][:, :1])
            l_scr[h] += fold(jnp.add, p)
            acc_scr[h] += dot(p.astype(bf16), v_ref[h, there])
        return carry

    lax.fori_loop(0, i + 1, weigh, 0)
    for h in range(nh):
        total = jnp.sum(l_scr[h], axis=-1, keepdims=True)
        cf_ref[:, h * PAD : (h + 1) * PAD] = acc_scr[h] / total
        hi, mid, low = split3(-(m_scr[h][:, :1] + jnp.log(total)))
        q = q_scr[h].astype(f32)
        q = jnp.where(lane == HEAD_DIM + 1, hi, q)
        q = jnp.where(lane == HEAD_DIM + 2, mid, q)
        q = jnp.where(lane == HEAD_DIM + 3, low, q)
        q_ref[h] = q.astype(bf16)


def mlp_kernel(
    x_ref, dy_ref, cf_ref, g_ref, b_ref, wo_ref, w1_ref, b1_ref, w2_ref,
    part_ref, u_ref, dw1_ref, dw2_ref, vec_ref,
):
    i = pl.program_id(0)
    xhat, unused = norm_parts(x_ref[...].astype(f32))
    gain = g_ref[...]
    a2 = (xhat * gain + b_ref[...]).astype(bf16)
    z = dot(a2, w1_ref[...]) + b1_ref[...]
    cdf = 0.5 * (1.0 + lax.erf(z * root_half))
    hidden = (z * cdf).astype(bf16)
    part = dot(hidden, w2_ref[...]) + dot(cf_ref[...].astype(bf16), wo_ref[...])
    part_ref[...] = part.astype(part_ref.dtype)
    dy = dy_ref[...]
    slope = cdf + z * jnp.exp(-0.5 * z * z) * inv_root_two_pi
    dz = (dot(dy, w2_ref[...], ((1,), (1,))) * slope).astype(bf16)
    da2 = dot(dz, w1_ref[...], ((1,), (1,)))
    u_ref[...] = (da2 * gain).astype(u_ref.dtype)
    dw1 = dot(a2, dz, ((0,), (0,)))
    dw2 = dot(hidden, dy, ((0,), (0,)))
    sums = [
        jnp.sum(dz.astype(f32), axis=0, keepdims=True),
        jnp.sum(da2 * xhat, axis=0, keepdims=True),
        jnp.sum(da2, axis=0, keepdims=True),
        jnp.sum(dy.astype(f32), axis=0, keepdims=True),
    ]

    @pl.when(i == 0)
    def _():
        dw1_ref[...] = dw1
        dw2_ref[...] = dw2
        for t in range(4):
            vec_ref[t : t + 1] = sums[t]

    @pl.when(i > 0)
    def _():
        dw1_ref[...] += dw1
        dw2_ref[...] += dw2
        for t in range(4):
            vec_ref[t : t + 1] += sums[t]


def attn_bwd_kernel(
    x_ref, dy_ref, cf_ref, u_in_ref, q_ref, k_ref, v_ref, g_ref, b_ref, w_ref, wo_ref,
    cos_ref, sin_ref,
    u_ref, dw_ref, dwo_ref, vec_ref, dwb_ref, dk_scr, dv_scr, dq_scr, dc_scr, dqkv_scr,
):
    step = pl.program_id(0)
    blocks = pl.num_programs(0)
    i = blocks - 1 - step
    nh = k_ref.shape[0]
    rows = x_ref.shape[0]
    lane = lax.broadcasted_iota(jnp.int32, (rows, PAD), 1)
    first = lane < ROT // 2
    here = pl.ds(pl.multiple_of(i * rows, rows), rows)
    dy = dy_ref[...]
    dc_all = dot(dy, wo_ref[...], ((1,), (1,))).astype(bf16)
    for h in range(nh):
        dc = dc_all[:, h * PAD : (h + 1) * PAD].astype(f32)
        delta = jnp.sum(dc * cf_ref[:, h * PAD : (h + 1) * PAD], axis=-1, keepdims=True)
        hi, mid, low = split3(-delta)
        dc = jnp.where(lane == HEAD_DIM, hi, dc)
        dc = jnp.where(lane == HEAD_DIM + 1, mid, dc)
        dc = jnp.where(lane == HEAD_DIM + 2, low, dc)
        dc_scr[h] = dc.astype(bf16)

    @pl.when(step == 0)
    def _():
        dk_scr[...] = jnp.zeros_like(dk_scr)
        dv_scr[...] = jnp.zeros_like(dv_scr)

    causal = lax.broadcasted_iota(jnp.int32, (rows, rows), 0) <= lax.broadcasted_iota(
        jnp.int32, (rows, rows), 1
    )

    def block(j, diagonal):
        there = pl.ds(pl.multiple_of(j * rows, rows), rows)
        for h in range(nh):
            k = k_ref[h, there]
            q = q_ref[h]
            dc = dc_scr[h]
            st = dot(k, q, ((1,), (1,)))
            pt = jnp.exp(st)
            if diagonal:
                pt = jnp.where(causal, pt, 0.0)
            dpt = dot(v_ref[h, there], dc, ((1,), (1,)))
            dst = (pt * dpt).astype(bf16)
            dv_scr[h, there] += dot(pt.astype(bf16), dc)
            dk_scr[h, there] += dot(dst, q)
            dq = dot(dst, k, ((0,), (0,)))
            if diagonal:
                dq_scr[h] = dq
            else:
                dq_scr[h] += dq

    block(i, True)

    def off(j, carry):
        block(j, False)
        return carry

    lax.fori_loop(0, i, off, 0)
    cosine, sine = cos_ref[...], -sin_ref[...]
    real = lane < HEAD_DIM
    for h in range(nh):
        dq = turn(dq_scr[h], cosine, sine, first) * HEAD_DIM**-0.5
        dk = turn(dk_scr[h, here], cosine, sine, first)
        for place, part in ((h, dq), (nh + h, dk), (2 * nh + h, dv_scr[h, here])):
            dqkv_scr[:, place * PAD : (place + 1) * PAD] = jnp.where(real, part, 0.0).astype(bf16)
    dqkv = dqkv_scr[...]
    xhat, unused = norm_parts(x_ref[...].astype(f32))
    gain = g_ref[...]
    a1 = (xhat * gain + b_ref[...]).astype(bf16)
    da1 = dot(dqkv, w_ref[...], ((1,), (1,)))
    u_ref[...] = (u_in_ref[...].astype(f32) + da1 * gain).astype(u_ref.dtype)
    dw = dot(a1, dqkv, ((0,), (0,)))
    dwo = dot(cf_ref[...].astype(bf16), dy, ((0,), (0,)))
    sums = [jnp.sum(da1 * xhat, axis=0, keepdims=True), jnp.sum(da1, axis=0, keepdims=True)]
    dwb = jnp.sum(dqkv.astype(f32), axis=0, keepdims=True)

    @pl.when(step == 0)
    def _():
        dw_ref[...] = dw
        dwo_ref[...] = dwo
        dwb_ref[...] = dwb
        for t in range(2):
            vec_ref[t : t + 1] = sums[t]

    @pl.when(step > 0)
    def _():
        dw_ref[...] += dw
        dwo_ref[...] += dwo
        dwb_ref[...] += dwb
        for t in range(2):
            vec_ref[t : t + 1] += sums[t]


def whole(shape):
    return pl.BlockSpec(shape, lambda i: (0,) * len(shape), pipeline_mode=pl.Buffered(1))


def sds(shape, dtype):
    return jax.ShapeDtypeStruct(shape, dtype)


def params():
    return pltpu.CompilerParams(
        dimension_semantics=("arbitrary",), vmem_limit_bytes=VMEM_BYTES
    )


def attn_fwd(length, x, g1, b1, w, wb, cosine, sine, nh, rows):
    t = x.shape[0]
    return pl.pallas_call(
        attn_fwd_kernel,
        grid=(t // rows,),
        out_shape=(
            sds((nh, t, PAD), bf16), sds((nh, t, PAD), bf16), sds((nh, t, PAD), bf16),
            sds((t, nh * PAD), f32),
        ),
        in_specs=[
            pl.BlockSpec(memory_space=pltpu.SMEM),
            pl.BlockSpec((rows, D), lambda i: (i, 0)),
            whole((1, D)), whole((1, D)), whole(w.shape), whole(wb.shape),
            pl.BlockSpec((rows, PAD), lambda i: (i, 0)),
            pl.BlockSpec((rows, PAD), lambda i: (i, 0)),
        ],
        out_specs=(
            pl.BlockSpec((nh, rows, PAD), lambda i: (0, i, 0)),
            whole((nh, t, PAD)), whole((nh, t, PAD)),
            pl.BlockSpec((rows, nh * PAD), lambda i: (i, 0)),
        ),
        scratch_shapes=[
            pltpu.VMEM((nh, t // rows, rows, rows), f32),
            pltpu.VMEM((nh, rows, PAD), bf16),
            pltpu.VMEM((nh, rows, PAD), f32),
            pltpu.VMEM((nh, rows, PAD), f32),
            pltpu.VMEM((nh, rows, PAD), f32),
        ],
        compiler_params=params(),
        name="attn_fwd",
    )(length, x, g1, b1, w, wb, cosine, sine)


def mlp(x, dy, cf, g2, b2, wo, w1, bias1, w2, rows):
    t = x.shape[0]
    ff = w1.shape[1]
    row = pl.BlockSpec((rows, D), lambda i: (i, 0))
    return pl.pallas_call(
        mlp_kernel,
        grid=(t // rows,),
        out_shape=(
            sds((t, D), bf16), sds((t, D), f32), sds((D, ff), f32), sds((ff, D), f32),
            sds((8, D), f32),
        ),
        in_specs=[
            row, row, pl.BlockSpec((rows, cf.shape[1]), lambda i: (i, 0)),
            whole((1, D)), whole((1, D)), whole(wo.shape), whole(w1.shape), whole((1, ff)),
            whole(w2.shape),
        ],
        out_specs=(row, row, whole((D, ff)), whole((ff, D)), whole((8, D))),
        compiler_params=params(),
        name="mlp",
    )(x, dy, cf, g2, b2, wo, w1, bias1, w2)


def attn_bwd(x, dy, cf, u_in, q, k, v, g1, b1, w, wo, cosine, sine, rows):
    t = x.shape[0]
    nh = q.shape[0]
    n = t // rows
    wide = w.shape[1]
    row = pl.BlockSpec((rows, D), lambda i: (n - 1 - i, 0))
    lanes = pl.BlockSpec((rows, PAD), lambda i: (n - 1 - i, 0))
    return pl.pallas_call(
        attn_bwd_kernel,
        grid=(n,),
        out_shape=(
            sds((t, D), bf16), sds((D, wide), f32), sds((nh * PAD, D), f32), sds((8, D), f32),
            sds((1, wide), f32),
        ),
        in_specs=[
            row, row, pl.BlockSpec((rows, nh * PAD), lambda i: (n - 1 - i, 0)), row,
            pl.BlockSpec((nh, rows, PAD), lambda i: (0, n - 1 - i, 0)),
            whole(k.shape), whole(v.shape), whole((1, D)), whole((1, D)), whole(w.shape),
            whole(wo.shape), lanes, lanes,
        ],
        out_specs=(
            row, whole((D, wide)), whole((nh * PAD, D)), whole((8, D)), whole((1, wide)),
        ),
        scratch_shapes=[
            pltpu.VMEM((nh, t, PAD), f32),
            pltpu.VMEM((nh, t, PAD), f32),
            pltpu.VMEM((nh, rows, PAD), f32),
            pltpu.VMEM((nh, rows, PAD), bf16),
            pltpu.VMEM((rows, wide), bf16),
        ],
        compiler_params=params(),
        name="attn_bwd",
    )(x, dy, cf, u_in, q, k, v, g1, b1, w, wo, cosine, sine)


def tables(t):
    inv_freqs = np.exp(np.arange(ROT // 2, dtype=np.float32) * np.float32(-2.0 * math.log(10000.0) / ROT))
    angles = np.arange(t, dtype=np.float32)[:, None] * inv_freqs.astype(np.float32)[None, :]
    cosine = np.ones((t, PAD), np.float32)
    sine = np.zeros((t, PAD), np.float32)
    half = ROT // 2
    cosine[:, :half] = cosine[:, half:ROT] = np.cos(angles)
    sine[:, :half] = -np.sin(angles)
    sine[:, half:ROT] = np.sin(angles)
    return jnp.asarray(cosine), jnp.asarray(sine)


def local(
    block_in, out_grad, lengths, ln1_gain, ln1_bias, qkv_weight, qkv_bias, out_weight, out_bias,
    ln2_gain, ln2_bias, fc1_weight, fc1_bias, fc2_weight, fc2_bias,
):
    tp = lax.axis_size("ctx")
    dp = lax.axis_size("dp")
    world = dp * tp
    z = lax.axis_index("ctx")
    d = lax.axis_index("dp")
    nh = HEADS // tp
    local_rows = block_in.shape[1]
    t = local_rows * tp
    rows = min(512, local_rows)
    part = D // tp
    r_in = D // world
    r_ff = fc2_weight.shape[0]
    ff = r_ff * dp

    x_own = block_in[0]
    pos = z * local_rows + jnp.arange(local_rows, dtype=jnp.int32)
    dy_own = jnp.where((pos < lengths[0])[:, None], out_grad[0], jnp.zeros((), bf16))
    x = lax.all_gather(x_own, "ctx", axis=0, tiled=True)
    dy = lax.all_gather(dy_own, "ctx", axis=0, tiled=True)

    w_qkv = jnp.moveaxis(qkv_weight.reshape(r_in, 3, tp, part), 2, 0).reshape(tp, r_in, 3 * part)
    w_qkv = lax.all_to_all(w_qkv, "ctx", 0, 0)
    w_qkv = lax.all_gather(w_qkv, "dp", axis=0, tiled=True).reshape(D, 3 * part)
    w1 = jnp.moveaxis(fc1_weight.reshape(r_in, dp, tp, r_ff), 2, 0).reshape(tp, r_in, ff)
    w1 = lax.all_to_all(w1, "ctx", 0, 0)
    w1 = lax.all_gather(w1, "dp", axis=0, tiled=True).reshape(D, ff)
    w2 = lax.all_gather(fc2_weight, "dp", axis=0, tiled=True)
    wo = lax.all_gather(out_weight, ("dp", "ctx"), axis=0, tiled=True)
    wo = lax.dynamic_slice_in_dim(wo, z * part, part, axis=0)
    vectors = jnp.concatenate(
        [ln1_gain, ln1_bias, out_bias, ln2_gain, ln2_bias, fc2_bias, qkv_bias, fc1_bias]
    )
    vectors = lax.all_gather(vectors, ("dp", "ctx"), axis=0).astype(f32)
    g1, b1, b_out, g2, b2, b_down = [
        vectors[:, s * r_in : (s + 1) * r_in].reshape(1, D) for s in range(6)
    ]
    b_qkv = vectors[:, 6 * r_in : 9 * r_in].reshape(3, tp, part)
    b_qkv = lax.dynamic_slice_in_dim(b_qkv, z, 1, axis=1).reshape(3 * nh, HEAD_DIM)
    b_up = vectors[:, 9 * r_in :].reshape(dp, tp, r_ff)
    b_up = lax.dynamic_slice_in_dim(b_up, z, 1, axis=1).reshape(1, ff)

    w_pad = jnp.pad(w_qkv.reshape(D, 3 * nh, HEAD_DIM), ((0, 0), (0, 0), (0, PAD - HEAD_DIM)))
    w_pad = w_pad.reshape(D, 3 * nh * PAD)
    extra = np.zeros((3 * nh, PAD - HEAD_DIM), np.float32)
    extra[:nh, 0] = HEAD_DIM**0.5
    extra[nh : 2 * nh, 1:4] = 1.0
    extra[2 * nh :, 0:3] = 1.0
    b_pad = jnp.concatenate([b_qkv, jnp.asarray(extra)], axis=1).reshape(1, 3 * nh * PAD)
    wo_pad = jnp.pad(wo.reshape(nh, HEAD_DIM, D), ((0, 0), (0, PAD - HEAD_DIM), (0, 0)))
    wo_pad = wo_pad.reshape(nh * PAD, D)
    cosine, sine = tables(t)

    q, k, v, cf = attn_fwd(lengths, x, g1, b1, w_pad, b_pad, cosine, sine, nh, rows)
    out_part, u_mlp, dw1, dw2, vec2 = mlp(x, dy, cf, g2, b2, wo_pad, w1, b_up, w2, rows // 2)
    out_sum = lax.psum_scatter(out_part, "ctx", scatter_dimension=0, tiled=True)
    block_out = (x_own.astype(f32) + b_out + b_down + out_sum.astype(f32)).astype(bf16)
    u_part, dw_pad, dwo_pad, vec1, dwb_pad = attn_bwd(
        x, dy, cf, u_mlp, q, k, v, g1, b1, w_pad, wo_pad, cosine, sine, rows
    )
    u = lax.psum_scatter(u_part, "ctx", scatter_dimension=0, tiled=True).astype(f32)
    xhat, inverse = norm_parts(x_own.astype(f32))
    back = inverse * (
        u
        - jnp.mean(u, axis=-1, keepdims=True)
        - xhat * jnp.mean(u * xhat, axis=-1, keepdims=True)
    )
    input_grad = (dy_own.astype(f32) + back).astype(bf16)

    dw = dw_pad.reshape(D, 3 * nh, PAD)[:, :, :HEAD_DIM].reshape(D, 3 * part)
    dwo = dwo_pad.reshape(nh, PAD, D)[:, :HEAD_DIM].reshape(part, D)
    dwb = dwb_pad.reshape(3 * nh, PAD)[:, :HEAD_DIM].reshape(3, part)
    squares = sum(jnp.sum(m * m) for m in (dw, dwo, dwb, dw1, dw2, vec2[0]))
    norm_vecs, squares = lax.psum(
        (jnp.stack([vec1[0], vec1[1], vec2[1], vec2[2]]), squares), "ctx"
    )
    squares = squares + jnp.sum(norm_vecs * norm_vecs) + 2.0 * jnp.sum(vec2[3] * vec2[3])
    example_norm = jnp.sqrt(squares)
    mean_norm = lax.psum(example_norm, "dp") / dp
    factor = mean_norm / jnp.maximum(example_norm, mean_norm)

    def over_dp(m):
        return lax.psum_scatter(
            (m * factor).astype(bf16), "dp", scatter_dimension=0, tiled=True
        )

    def back_rows(m):
        m = lax.all_to_all(m.reshape(tp, r_in, m.shape[1]), "ctx", 0, 0)
        return m.astype(f32)

    g_qkv = back_rows(over_dp(dw)).reshape(tp, r_in, 3, part)
    g_qkv = jnp.moveaxis(g_qkv, 0, 2).reshape(r_in, 3 * D)
    g_fc1 = back_rows(over_dp(dw1)).reshape(tp, r_in, dp, r_ff)
    g_fc1 = jnp.moveaxis(g_fc1, 0, 2).reshape(r_in, ff * tp)
    g_fc2 = over_dp(dw2).astype(f32)
    moves = []
    for zz in range(tp):
        for dd in range(dp):
            moves.append((dd * tp + zz, zz * dp + dd))
    g_out = lax.ppermute(over_dp(dwo), ("dp", "ctx"), moves).astype(f32)

    share = jnp.where(z == 0, factor, 0.0)
    full_qkv = lax.dynamic_update_slice_in_dim(
        jnp.zeros((3, tp, part), f32), dwb[:, None] * factor, z, axis=1
    )
    full_up = lax.dynamic_update_slice_in_dim(
        jnp.zeros((dp, tp, r_ff), f32), vec2[0].reshape(dp, 1, r_ff) * factor, z, axis=1
    )
    small = jnp.concatenate(
        [
            (norm_vecs * share).reshape(4, world, r_in).swapaxes(0, 1).reshape(world, 4 * r_in),
            (vec2[3] * share).reshape(world, r_in),
            full_qkv.reshape(world, 3 * r_in),
            full_up.reshape(world, r_ff),
        ],
        axis=1,
    )
    small = lax.psum(small, ("dp", "ctx"))
    mine = lax.dynamic_slice_in_dim(small, d * tp + z, 1, axis=0)[0]
    cut = [mine[s * r_in : (s + 1) * r_in] for s in range(5)]
    return (
        block_out[None], input_grad[None],
        cut[0], cut[1], g_qkv, mine[5 * r_in : 8 * r_in], g_out, cut[4],
        cut[2], cut[3], g_fc1, mine[8 * r_in :], g_fc2, cut[4],
        example_norm[None],
    )


def solution(mesh):
    both = ("dp", "ctx")
    vec, mat, act = P(both), P(both, None), P("dp", "ctx", None)
    weights = (vec, vec, mat, vec, mat, vec, vec, vec, mat, vec, mat, vec)
    return jax.shard_map(
        local,
        mesh=mesh,
        in_specs=(act, act, P("dp")) + weights,
        out_specs=(act, act) + weights + (P("dp"),),
        check_vma=False,
    )
```

```python
import functools
import math

import jax
import jax.numpy as jnp
import numpy as np
from jax import lax
from jax.experimental import pallas as pl
from jax.experimental.pallas import tpu as pltpu
from jax.sharding import PartitionSpec as P

D = 768
HEADS = 12
HEAD_DIM = 64
ROT = 16
PAD = 128
eps_norm = 1e-05
neg_big = -1e30
root_half = math.sqrt(0.5)
inv_root_two_pi = 1.0 / math.sqrt(2.0 * math.pi)
f32 = jnp.float32
bf16 = jnp.bfloat16
VMEM_BYTES = 60 * 2**20


def dot(a, b, dims=((1,), (0,))):
    return lax.dot_general(a, b, (dims, ((), ())), preferred_element_type=f32)


def norm_parts(values):
    centered = values - jnp.mean(values, axis=-1, keepdims=True)
    row_var = jnp.mean(centered * centered, axis=-1, keepdims=True)
    inverse = lax.rsqrt(row_var + eps_norm)
    return centered * inverse, inverse


def turn(u, cosine, sine, first):
    partner = jnp.where(first, pltpu.roll(u, PAD - ROT // 2, 1), pltpu.roll(u, ROT // 2, 1))
    return u * cosine + partner * sine


def split3(v):
    hi = v.astype(bf16).astype(f32)
    mid = (v - hi).astype(bf16).astype(f32)
    low = (v - hi - mid).astype(bf16).astype(f32)
    return hi, mid, low


def fold(op, s):
    out = s[:, :PAD]
    for t in range(1, s.shape[1] // PAD):
        out = op(out, s[:, t * PAD : (t + 1) * PAD])
    return out


def attn_fwd_kernel(
    len_ref, x_ref, g_ref, b_ref, w_ref, wb_ref, cos_ref, sin_ref,
    q_ref, k_ref, v_ref, cf_ref, c_ref, w_scr, s_scr, q_scr, m_scr, l_scr, acc_scr,
):
    i = pl.program_id(0)
    nh = k_ref.shape[0]
    rows = x_ref.shape[0]
    length = len_ref[0]

    @pl.when(i == 0)
    def _():
        for h in range(3 * nh):
            w_scr[:, h * PAD : h * PAD + HEAD_DIM] = w_ref[:, h * HEAD_DIM : (h + 1) * HEAD_DIM]
            w_scr[:, h * PAD + HEAD_DIM : (h + 1) * PAD] = jnp.zeros((D, PAD - HEAD_DIM), bf16)

    xhat, unused = norm_parts(x_ref[...].astype(f32))
    a1 = (xhat * g_ref[...] + b_ref[...]).astype(bf16)
    cosine, sine = cos_ref[...], sin_ref[...]
    lane = lax.broadcasted_iota(jnp.int32, (rows, PAD), 1)
    first = lane < ROT // 2
    key_pos = i * rows + lax.broadcasted_iota(jnp.int32, (rows, PAD), 0)
    key_bias = jnp.where(key_pos < length, 0.0, neg_big)
    here = pl.ds(pl.multiple_of(i * rows, rows), rows)
    qkv = dot(a1, w_scr[...]) + wb_ref[...]
    for h in range(nh):
        q = turn(qkv[:, h * PAD : (h + 1) * PAD], cosine, sine, first) * HEAD_DIM**-0.5
        q_scr[h] = q.astype(bf16)
        k = turn(qkv[:, (nh + h) * PAD : (nh + h + 1) * PAD], cosine, sine, first)
        k_ref[h, here] = jnp.where(lane == HEAD_DIM, key_bias, k).astype(bf16)
        v_ref[h, here] = qkv[:, (2 * nh + h) * PAD : (2 * nh + h + 1) * PAD].astype(bf16)

    causal = lax.broadcasted_iota(jnp.int32, (rows, rows), 0) >= lax.broadcasted_iota(
        jnp.int32, (rows, rows), 1
    )
    for h in range(nh):
        s = dot(q_scr[h], k_ref[h, here], ((1,), (1,)))
        s = jnp.where(causal, s, neg_big)
        s_scr[h, i] = s
        m_scr[h] = fold(jnp.maximum, s)

    def scores(j, carry):
        there = pl.ds(pl.multiple_of(j * rows, rows), rows)
        for h in range(nh):
            s = dot(q_scr[h], k_ref[h, there], ((1,), (1,)))
            s_scr[h, j] = s
            m_scr[h] = jnp.maximum(m_scr[h], fold(jnp.maximum, s))
        return carry

    lax.fori_loop(0, i, scores, 0)
    for h in range(nh):
        m_scr[h] = jnp.broadcast_to(jnp.max(m_scr[h], axis=-1, keepdims=True), (rows, PAD))
        l_scr[h] = jnp.zeros((rows, PAD), f32)
        acc_scr[h] = jnp.zeros((rows, PAD), f32)

    def weigh(j, carry):
        there = pl.ds(pl.multiple_of(j * rows, rows), rows)
        for h in range(nh):
            p = jnp.exp(s_scr[h, j] - m_scr[h][:, :1])
            l_scr[h] += fold(jnp.add, p)
            acc_scr[h] += dot(p.astype(bf16), v_ref[h, there])
        return carry

    lax.fori_loop(0, i + 1, weigh, 0)
    for h in range(nh):
        total = jnp.sum(l_scr[h], axis=-1, keepdims=True)
        context = acc_scr[h] / total
        cf_ref[:, h * PAD : (h + 1) * PAD] = context
        c_ref[:, h * HEAD_DIM : (h + 1) * HEAD_DIM] = context[:, :HEAD_DIM].astype(bf16)
        hi, mid, low = split3(-(m_scr[h][:, :1] + jnp.log(total)))
        q = q_scr[h].astype(f32)
        q = jnp.where(lane == HEAD_DIM + 1, hi, q)
        q = jnp.where(lane == HEAD_DIM + 2, mid, q)
        q = jnp.where(lane == HEAD_DIM + 3, low, q)
        q_ref[h] = q.astype(bf16)


def squares_of(m):
    return jnp.sum(jnp.sum(m * m, axis=0, keepdims=True), axis=1, keepdims=True)


def mlp_kernel(
    x_ref, dy_ref, c_ref, g_ref, b_ref, wo_ref, w1_ref, b1_ref, w2_ref,
    part_ref, u_ref, dw1_ref, dw2_ref, vec_ref, dw1_scr, dw2_scr,
):
    i = pl.program_id(0)
    xhat, unused = norm_parts(x_ref[...].astype(f32))
    gain = g_ref[...]
    a2 = (xhat * gain + b_ref[...]).astype(bf16)
    z = dot(a2, w1_ref[...]) + b1_ref[...]
    cdf = 0.5 * (1.0 + lax.erf(z * root_half))
    hidden = (z * cdf).astype(bf16)
    part = dot(hidden, w2_ref[...]) + dot(c_ref[...], wo_ref[...])
    part_ref[...] = part.astype(part_ref.dtype)
    dy = dy_ref[...]
    slope = cdf + z * jnp.exp(-0.5 * z * z) * inv_root_two_pi
    dz = (dot(dy, w2_ref[...], ((1,), (1,))) * slope).astype(bf16)
    da2 = dot(dz, w1_ref[...], ((1,), (1,)))
    u_ref[...] = (da2 * gain).astype(u_ref.dtype)

    @pl.when(i == 0)
    def _():
        dw1_scr[...] = jnp.zeros_like(dw1_scr)
        dw2_scr[...] = jnp.zeros_like(dw2_scr)
        vec_ref[...] = jnp.zeros_like(vec_ref)

    dw1_scr[...] += dot(a2, dz, ((0,), (0,)))
    dw2_scr[...] += dot(hidden, dy, ((0,), (0,)))
    vec_ref[2:3] += jnp.sum(da2 * xhat, axis=0, keepdims=True)
    vec_ref[3:4] += jnp.sum(da2, axis=0, keepdims=True)
    vec_ref[4:5] += jnp.sum(dz.astype(f32), axis=0, keepdims=True)
    vec_ref[6:7] += jnp.sum(dy.astype(f32), axis=0, keepdims=True)

    @pl.when(i == pl.num_programs(0) - 1)
    def _():
        dw1_ref[...] = dw1_scr[...].astype(bf16)
        dw2_ref[...] = dw2_scr[...].astype(bf16)
        vec_ref[7:8, 0:1] = squares_of(dw1_scr[...]) + squares_of(dw2_scr[...])


def attn_bwd_kernel(
    x_ref, dy_ref, cf_ref, c_ref, u_in_ref, q_ref, k_ref, v_ref, g_ref, b_ref, w_ref, wo_ref,
    cos_ref, sin_ref, vec_in_ref,
    u_ref, dw_ref, dwo_ref, vec_ref,
    wo_scr, dk_scr, dv_scr, dq_scr, dc_scr, dqkv_scr, dw_scr, dwo_scr,
):
    step = pl.program_id(0)
    blocks = pl.num_programs(0)
    i = blocks - 1 - step
    nh = k_ref.shape[0]
    rows = x_ref.shape[0]
    wide = 3 * nh * HEAD_DIM
    lane = lax.broadcasted_iota(jnp.int32, (rows, PAD), 1)
    first = lane < ROT // 2
    here = pl.ds(pl.multiple_of(i * rows, rows), rows)

    @pl.when(step == 0)
    def _():
        dk_scr[...] = jnp.zeros_like(dk_scr)
        dv_scr[...] = jnp.zeros_like(dv_scr)
        dw_scr[...] = jnp.zeros_like(dw_scr)
        dwo_scr[...] = jnp.zeros_like(dwo_scr)
        vec_ref[...] = vec_in_ref[...]
        for h in range(nh):
            wo_scr[h * PAD : h * PAD + HEAD_DIM] = wo_ref[h * HEAD_DIM : (h + 1) * HEAD_DIM]
            wo_scr[h * PAD + HEAD_DIM : (h + 1) * PAD] = jnp.zeros((PAD - HEAD_DIM, D), bf16)

    dy = dy_ref[...]
    dc_all = dot(dy, wo_scr[...], ((1,), (1,))).astype(bf16)
    for h in range(nh):
        dc = dc_all[:, h * PAD : (h + 1) * PAD].astype(f32)
        delta = jnp.sum(dc * cf_ref[:, h * PAD : (h + 1) * PAD], axis=-1, keepdims=True)
        hi, mid, low = split3(-delta)
        dc = jnp.where(lane == HEAD_DIM, hi, dc)
        dc = jnp.where(lane == HEAD_DIM + 1, mid, dc)
        dc = jnp.where(lane == HEAD_DIM + 2, low, dc)
        dc_scr[h] = dc.astype(bf16)

    causal = lax.broadcasted_iota(jnp.int32, (rows, rows), 0) <= lax.broadcasted_iota(
        jnp.int32, (rows, rows), 1
    )

    def block(j, diagonal):
        there = pl.ds(pl.multiple_of(j * rows, rows), rows)
        for h in range(nh):
            k = k_ref[h, there]
            q = q_ref[h]
            dc = dc_scr[h]
            pt = jnp.exp(dot(k, q, ((1,), (1,))))
            if diagonal:
                pt = jnp.where(causal, pt, 0.0)
            dpt = dot(v_ref[h, there], dc, ((1,), (1,)))
            dst = (pt * dpt).astype(bf16)
            dv_scr[h, there] += dot(pt.astype(bf16), dc)
            dk_scr[h, there] += dot(dst, q)
            dq = dot(dst, k, ((0,), (0,)))
            if diagonal:
                dq_scr[h] = dq
            else:
                dq_scr[h] += dq

    block(i, True)

    def off(j, carry):
        block(j, False)
        return carry

    lax.fori_loop(0, i, off, 0)
    cosine, sine = cos_ref[...], -sin_ref[...]
    for h in range(nh):
        dq = turn(dq_scr[h], cosine, sine, first) * HEAD_DIM**-0.5
        dk = turn(dk_scr[h, here], cosine, sine, first)
        for at, part in ((h, dq), (nh + h, dk), (2 * nh + h, dv_scr[h, here])):
            dqkv_scr[:, at * HEAD_DIM : (at + 1) * HEAD_DIM] = part[:, :HEAD_DIM].astype(bf16)
    dqkv = dqkv_scr[...]
    xhat, unused = norm_parts(x_ref[...].astype(f32))
    gain = g_ref[...]
    a1 = (xhat * gain + b_ref[...]).astype(bf16)
    da1 = dot(dqkv, w_ref[...], ((1,), (1,)))
    u_ref[...] = (u_in_ref[...].astype(f32) + da1 * gain).astype(u_ref.dtype)
    dw_scr[...] += dot(a1, dqkv, ((0,), (0,)))
    dwo_scr[...] += dot(c_ref[...], dy, ((0,), (0,)))
    vec_ref[0:1] += jnp.sum(da1 * xhat, axis=0, keepdims=True)
    vec_ref[1:2] += jnp.sum(da1, axis=0, keepdims=True)
    vec_ref[5:6, :wide] += jnp.sum(dqkv.astype(f32), axis=0, keepdims=True)

    @pl.when(step == blocks - 1)
    def _():
        dw_ref[...] = dw_scr[...].astype(bf16)
        dwo_ref[...] = dwo_scr[...].astype(bf16)
        vec_ref[7:8, 0:1] += squares_of(dw_scr[...]) + squares_of(dwo_scr[...])


def whole(shape):
    return pl.BlockSpec(shape, lambda i: (0,) * len(shape), pipeline_mode=pl.Buffered(1))


def sds(shape, dtype):
    return jax.ShapeDtypeStruct(shape, dtype)


def params():
    return pltpu.CompilerParams(
        dimension_semantics=("arbitrary",), vmem_limit_bytes=VMEM_BYTES
    )


def attn_fwd(length, x, g1, b1, w, wb, cosine, sine, nh, rows):
    t = x.shape[0]
    lanes = pl.BlockSpec((rows, PAD), lambda i: (i, 0))
    return pl.pallas_call(
        attn_fwd_kernel,
        grid=(t // rows,),
        out_shape=(
            sds((nh, t, PAD), bf16), sds((nh, t, PAD), bf16), sds((nh, t, PAD), bf16),
            sds((t, nh * PAD), f32), sds((t, nh * HEAD_DIM), bf16),
        ),
        in_specs=[
            pl.BlockSpec(memory_space=pltpu.SMEM),
            pl.BlockSpec((rows, D), lambda i: (i, 0)),
            whole((1, D)), whole((1, D)), whole(w.shape), whole(wb.shape), lanes, lanes,
        ],
        out_specs=(
            pl.BlockSpec((nh, rows, PAD), lambda i: (0, i, 0)),
            whole((nh, t, PAD)), whole((nh, t, PAD)),
            pl.BlockSpec((rows, nh * PAD), lambda i: (i, 0)),
            pl.BlockSpec((rows, nh * HEAD_DIM), lambda i: (i, 0)),
        ),
        scratch_shapes=[
            pltpu.VMEM((D, 3 * nh * PAD), bf16),
            pltpu.VMEM((nh, t // rows, rows, rows), f32),
            pltpu.VMEM((nh, rows, PAD), bf16),
            pltpu.VMEM((nh, rows, PAD), f32),
            pltpu.VMEM((nh, rows, PAD), f32),
            pltpu.VMEM((nh, rows, PAD), f32),
        ],
        compiler_params=params(),
        name="attn_fwd",
    )(length, x, g1, b1, w, wb, cosine, sine)


def mlp(x, dy, c, g2, b2, wo, w1, bias1, w2, rows):
    t = x.shape[0]
    ff = w1.shape[1]
    row = pl.BlockSpec((rows, D), lambda i: (i, 0))
    return pl.pallas_call(
        mlp_kernel,
        grid=(t // rows,),
        out_shape=(
            sds((t, D), bf16), sds((t, D), f32), sds((D, ff), bf16), sds((ff, D), bf16),
            sds((8, D), f32),
        ),
        in_specs=[
            row, row, pl.BlockSpec((rows, c.shape[1]), lambda i: (i, 0)),
            whole((1, D)), whole((1, D)), whole(wo.shape), whole(w1.shape), whole((1, ff)),
            whole(w2.shape),
        ],
        out_specs=(row, row, whole((D, ff)), whole((ff, D)), whole((8, D))),
        scratch_shapes=[pltpu.VMEM((D, ff), f32), pltpu.VMEM((ff, D), f32)],
        compiler_params=params(),
        name="mlp",
    )(x, dy, c, g2, b2, wo, w1, bias1, w2)


def attn_bwd(x, dy, cf, c, u_in, q, k, v, g1, b1, w, wo, cosine, sine, vec, rows):
    t = x.shape[0]
    nh = q.shape[0]
    n = t // rows
    wide = w.shape[1]
    row = pl.BlockSpec((rows, D), lambda i: (n - 1 - i, 0))
    lanes = pl.BlockSpec((rows, PAD), lambda i: (n - 1 - i, 0))
    return pl.pallas_call(
        attn_bwd_kernel,
        grid=(n,),
        out_shape=(
            sds((t, D), bf16), sds((D, wide), bf16), sds((nh * HEAD_DIM, D), bf16),
            sds((8, D), f32),
        ),
        in_specs=[
            row, row, pl.BlockSpec((rows, nh * PAD), lambda i: (n - 1 - i, 0)),
            pl.BlockSpec((rows, nh * HEAD_DIM), lambda i: (n - 1 - i, 0)), row,
            pl.BlockSpec((nh, rows, PAD), lambda i: (0, n - 1 - i, 0)),
            whole(k.shape), whole(v.shape), whole((1, D)), whole((1, D)), whole(w.shape),
            whole(wo.shape), lanes, lanes, whole((8, D)),
        ],
        out_specs=(row, whole((D, wide)), whole((nh * HEAD_DIM, D)), whole((8, D))),
        scratch_shapes=[
            pltpu.VMEM((nh * PAD, D), bf16),
            pltpu.VMEM((nh, t, PAD), f32),
            pltpu.VMEM((nh, t, PAD), f32),
            pltpu.VMEM((nh, rows, PAD), f32),
            pltpu.VMEM((nh, rows, PAD), bf16),
            pltpu.VMEM((rows, wide), bf16),
            pltpu.VMEM((D, wide), f32),
            pltpu.VMEM((nh * HEAD_DIM, D), f32),
        ],
        compiler_params=params(),
        name="attn_bwd",
    )(x, dy, cf, c, u_in, q, k, v, g1, b1, w, wo, cosine, sine, vec)


def tables(t):
    inv_freqs = np.exp(np.arange(ROT // 2, dtype=np.float32) * np.float32(-2.0 * math.log(10000.0) / ROT))
    angles = np.arange(t, dtype=np.float32)[:, None] * inv_freqs.astype(np.float32)[None, :]
    cosine = np.ones((t, PAD), np.float32)
    sine = np.zeros((t, PAD), np.float32)
    half = ROT // 2
    cosine[:, :half] = cosine[:, half:ROT] = np.cos(angles)
    sine[:, :half] = -np.sin(angles)
    sine[:, half:ROT] = np.sin(angles)
    return jnp.asarray(cosine), jnp.asarray(sine)


MESH = pl.DeviceIdType.MESH
AX = ("dp", "ctx")
CHUNKS = 2


def place():
    d, z = lax.axis_index("dp"), lax.axis_index("ctx")
    c, pair, g = lax.rem(d, 2), lax.div(d, 2), lax.div(z, 2)
    y = lax.rem(g + lax.rem(z, 2), 2)
    return d, z, c, pair, g, y


def mirror(m, g):
    return jnp.where(g == 0, m, 3 - m)


def rcopy(src, dst, ss, rs, device):
    return pltpu.make_async_remote_copy(
        src_ref=src, dst_ref=dst, send_sem=ss, recv_sem=rs, device_id=device, device_id_type=MESH
    )


def column_peer(pair, c, z, o):
    m = lax.rem(c * 4 + z + o, 8)
    return lax.div(m, 4), lax.rem(m, 4)


def barrier_all(np_, d, z, c, pair):
    bar = pltpu.get_barrier_semaphore()
    for o in range(1, 8):
        c2, z2 = column_peer(pair, c, z, o)
        pl.semaphore_signal(bar, inc=1, device_id=(2 * pair + c2, z2), device_id_type=MESH)
    for o in range(1, np_):
        pl.semaphore_signal(
            bar, inc=1, device_id=(2 * lax.rem(pair + o, np_) + c, z), device_id_type=MESH
        )
    pl.semaphore_wait(bar, 7 + np_ - 1)


class Spread:
    def __init__(self, own, out, ls, ss, rs):
        self.own, self.out, self.ls, self.ss, self.rs = own, out, ls, ss, rs
        self.rows = out.shape[1] // CHUNKS
        d, z, c, pair, g, y = place()
        self.d, self.z, self.c, self.g, self.y = d, z, c, g, y
        self.prim = c == g
        self.sib = (d + 1 - 2 * c, z)
        self.partner = (d, z + 1 - 2 * lax.rem(z, 2))
        self.far = (d, 1 + c)

    def cut(self, ref, j):
        return ref.at[pl.ds(j * self.rows, self.rows)]

    def send(self, q, j, way, device, src=None):
        src = self.cut(self.out.at[q], j) if src is None else src
        return rcopy(
            src, self.cut(self.out.at[q], j), self.ss.at[way, q, j], self.rs.at[q, j], device
        )

    def start(self):
        own = [self.cut(self.own, j) for j in range(CHUNKS)]

        @pl.when(self.prim)
        def _():
            pltpu.make_async_copy(self.own, self.out.at[self.z], self.ls).start()
            for j in range(CHUNKS):
                self.send(self.z, j, 0, self.partner, own[j]).start()
            for j in range(CHUNKS):
                self.send(self.z, j, 1, self.sib, own[j]).start()

        @pl.when(jnp.logical_not(self.prim))
        def _():
            for j in range(CHUNKS):
                self.send(self.z, j, 0, self.far, own[j]).start()

    def wait_recv(self, q, j):
        self.send(q, j, 0, self.sib).wait_recv()

    def finish(self):
        far = (mirror(2, self.g), mirror(3, self.g))
        end, mid = mirror(0, self.g), mirror(1, self.g)

        @pl.when(jnp.logical_and(self.prim, self.y == 1))
        def _():
            for j in range(CHUNKS):
                for q in far:
                    self.wait_recv(q, j)
                    self.send(q, j, 0, self.partner).start()
                    self.send(q, j, 1, self.sib).start()
            for j in range(CHUNKS):
                self.wait_recv(end, j)
                self.send(end, j, 1, self.sib).start()
            for j in range(CHUNKS):
                for q in far + (mid,):
                    self.send(q, j, 0, self.partner).wait_send()

        @pl.when(jnp.logical_and(self.prim, self.y == 0))
        def _():
            for q, j in [(mid, j) for j in range(CHUNKS)] + [
                (q, j) for j in range(CHUNKS) for q in far
            ]:
                self.wait_recv(q, j)
                self.send(q, j, 1, self.sib).start()
            for j in range(CHUNKS):
                self.send(end, j, 0, self.partner).wait_send()

        @pl.when(self.prim)
        def _():
            pltpu.make_async_copy(self.own, self.out.at[self.z], self.ls).wait()
            for q in range(4):
                for j in range(CHUNKS):
                    self.send(q, j, 1, self.sib).wait_send()

        @pl.when(jnp.logical_not(self.prim))
        def _():
            for q in range(4):
                for j in range(CHUNKS):
                    self.wait_recv(q, j)
            for j in range(CHUNKS):
                self.send(self.z, j, 0, self.far).wait_send()


class Weights:
    def __init__(self, np_, sliced, w2, wo, ls, ss, rs):
        self.np_, self.sliced, self.w2, self.wo = np_, sliced, w2, wo
        self.ls, self.ss, self.rs = ls, ss, rs
        self.here = place()

    def first(self, s, o):
        d, z, c, pair, g, y = self.here
        src, out, by_slice = self.sliced[s]
        if o == 0:
            return pltpu.make_async_copy(
                src.at[2 * y + c] if by_slice else src, out.at[pair, c, z], self.ls.at[s]
            )
        c2, z2 = column_peer(pair, c, z, o)
        y2 = lax.rem(lax.div(z2, 2) + lax.rem(z2, 2), 2)
        return rcopy(
            src.at[2 * y2 + c2] if by_slice else src, out.at[pair, c, z],
            self.ss.at[s, o - 1], self.rs.at[s, o - 1], (2 * pair + c2, z2),
        )

    def second(self, s, o):
        d, z, c, pair, g, y = self.here
        out = self.sliced[s][1] if s < len(self.sliced) else self.w2[1]
        return rcopy(
            out.at[pair], out.at[pair], self.ss.at[s, 7 + o - 1], self.rs.at[s, 7 + o - 1],
            (2 * lax.rem(pair + o, self.np_) + c, z),
        )

    def start(self):
        d, z, c, pair, g, y = self.here
        n = len(self.sliced)
        for s in range(n):
            for o in range(8):
                self.first(s, o).start()
        if self.w2 is not None:
            for o in range(2):
                self.w2_first(o).start()
        if self.wo is not None:
            self.wo_first(lambda cp: cp.start())

    def w2_first(self, o):
        d, z, c, pair, g, y = self.here
        src, out = self.w2
        n = len(self.sliced)
        if o == 0:
            return pltpu.make_async_copy(src, out.at[pair, g], self.ls.at[n])
        return rcopy(src, out.at[pair, g], self.ss.at[n, 0], self.rs.at[n, 0], (d, 3 - z))

    def wo_parts(self):
        d, z, c, pair, g, y = self.here
        per = self.np_ // 4
        owner = lax.div(pair, per)
        return per, owner, lax.rem(owner, 2), lax.div(owner, 2)

    def wo_first(self, do, sending=True):
        d, z, c, pair, g, y = self.here
        src, out = self.wo
        n = len(self.sliced) + 1
        per, owner, c_to, y_to = self.wo_parts()
        slot = out.at[lax.rem(pair, per), c, z]
        for t in range(2):
            z_to = jnp.where(t == 0, y_to, 3 - y_to)
            mine = jnp.logical_and(c == c_to, z == z_to)

            @pl.when(mine)
            def _():
                do(pltpu.make_async_copy(src, slot, self.ls.at[n]))

            @pl.when(jnp.logical_not(mine))
            def _():
                cp = rcopy(
                    src, slot, self.ss.at[n, t], self.rs.at[n, c * 4 + z], (2 * pair + c_to, z_to)
                )
                do(cp)

    def wo_second(self, o):
        d, z, c, pair, g, y = self.here
        per = self.np_ // 4
        out = self.wo[1]
        n = len(self.sliced) + 1
        slot = out.at[lax.rem(pair, per)]
        return rcopy(
            slot, slot, self.ss.at[n, 8 + o - 1], self.rs.at[n, 8 + o - 1],
            (2 * lax.rem(pair + o, self.np_) + c, z),
        )

    def between(self, s):
        self.first(s, 0).wait()
        for o in range(1, 8):
            self.first(s, o).wait_recv()
        for o in range(1, self.np_):
            self.second(s, o).start()

    def between_w2(self):
        n = len(self.sliced)
        self.w2_first(0).wait()
        self.w2_first(1).wait_recv()
        for o in range(1, self.np_):
            self.second(n, o).start()

    def between_wo(self):
        d, z, c, pair, g, y = self.here
        n = len(self.sliced) + 1
        per, owner, c_to, y_to = self.wo_parts()

        @pl.when(owner == 2 * y + c)
        def _():
            for c2 in range(2):
                for z2 in range(4):
                    own = jnp.logical_and(c == c2, z == z2)

                    @pl.when(jnp.logical_not(own))
                    def _():
                        slot = self.wo[1].at[0, c2, z2]
                        rcopy(
                            slot, slot, self.ss.at[n, 0], self.rs.at[n, c2 * 4 + z2], (d + 1 - 2 * c, z)
                        ).wait_recv()
            pltpu.make_async_copy(
                self.wo[0], self.wo[1].at[0, c, z], self.ls.at[n]
            ).wait()
            for o in range(1, self.np_):
                self.wo_second(o).start()

    def finish(self, s):
        for o in range(1, 8):
            self.first(s, o).wait_send()
        for o in range(1, self.np_):
            self.second(s, o).wait()

    def finish_w2(self):
        n = len(self.sliced)
        self.w2_first(1).wait_send()
        for o in range(1, self.np_):
            self.second(n, o).wait()

    def finish_wo(self):
        d, z, c, pair, g, y = self.here
        n = len(self.sliced) + 1
        per, owner, c_to, y_to = self.wo_parts()
        for t in range(2):
            z_to = jnp.where(t == 0, y_to, 3 - y_to)

            @pl.when(jnp.logical_not(jnp.logical_and(c == c_to, z == z_to)))
            def _():
                rcopy(
                    self.wo[0], self.wo[1].at[0, c, z], self.ss.at[n, t], self.rs.at[n, 0], (d + 1 - 2 * c, z)
                ).wait_send()

        @pl.when(owner == 2 * y + c)
        def _():
            for o in range(1, self.np_):
                self.wo_second(o).wait_send()

        for o in range(1, self.np_):
            source = lax.div(lax.rem(pair + self.np_ - o, self.np_), per)

            @pl.when(source == 2 * y + c)
            def _():
                self.wo_second(o).wait_recv()


def gather_kernel(
    np_, x, dy, wq, w1, w2, wo, vec, xg, dyg, wqg, w1g, w2g, wog, vecg,
    ls_x, ss_x, rs_x, ls_dy, ss_dy, rs_dy, ls_w, ss_w, rs_w,
):
    d, z, c, pair, g, y = place()
    barrier_all(np_, d, z, c, pair)
    sx = Spread(x, xg, ls_x, ss_x, rs_x)
    sdy = Spread(dy, dyg, ls_dy, ss_dy, rs_dy)
    w = Weights(
        np_, [(vec, vecg, False), (wq, wqg, True), (w1, w1g, True)], (w2, w2g), (wo, wog),
        ls_w, ss_w, rs_w,
    )
    w.start()
    sx.start()
    for s in range(3):
        w.between(s)
    w.between_wo()
    w.between_w2()
    sx.finish()
    sdy.start()
    sdy.finish()
    for s in range(3):
        w.finish(s)
    w.finish_wo()
    w.finish_w2()


def spread_sems():
    return [
        pltpu.SemaphoreType.DMA,
        pltpu.SemaphoreType.DMA((2, 4, CHUNKS)),
        pltpu.SemaphoreType.DMA((4, CHUNKS)),
    ]


def gather(np_, x, dy, wq, w1, w2, wo, vec, collective_id=1):
    rows = x.shape[0]
    any_ = pl.BlockSpec(memory_space=pl.ANY)
    outs = (
        sds((4, rows, D), bf16), sds((4, rows, D), bf16),
        sds((np_, 2, 4) + wq.shape[1:], bf16), sds((np_, 2, 4) + w1.shape[1:], bf16),
        sds((np_, 2) + w2.shape, bf16), sds((np_ // 4, 2, 4) + wo.shape, bf16),
        sds((np_, 2, 4) + vec.shape, bf16),
    )
    return pl.pallas_call(
        functools.partial(gather_kernel, np_),
        out_shape=outs,
        in_specs=[any_] * 7,
        out_specs=(any_,) * 7,
        scratch_shapes=spread_sems() + spread_sems() + [
            pltpu.SemaphoreType.DMA((5,)),
            pltpu.SemaphoreType.DMA((5, 8 + np_)),
            pltpu.SemaphoreType.DMA((5, 8 + np_)),
        ],
        compiler_params=pltpu.CompilerParams(
            collective_id=collective_id, has_side_effects=True, vmem_limit_bytes=VMEM_BYTES
        ),
        name="gather",
    )(x, dy, wq, w1, w2, wo, vec)


PIECES = 4


class Reduce:
    def __init__(self, part, out, extra, bufs, ls, ss, rs):
        self.part, self.out, self.extra = part, out, extra
        self.from_sib, self.from_far, self.to_far, self.mine, self.done = bufs
        self.ls, self.ss, self.rs = ls, ss, rs
        d, z, c, pair, g, y = place()
        self.role = jnp.where(c == g, 0, 1)
        self.y = y
        self.sib = (d + 1 - 2 * c, z)
        self.partner = (d, z + 1 - 2 * lax.rem(z, 2))
        self.q_here = mirror(2 * y + self.role, g)
        self.q_there = mirror(2 * (1 - y) + self.role, g)
        self.sib_here = mirror(2 * y + 1 - self.role, g)
        self.sib_there = mirror(2 * (1 - y) + 1 - self.role, g)
        self.owner = (2 * pair + g, self.q_here)
        self.self_owner = jnp.logical_and(self.role == 0, y == 0)
        self.self_source = jnp.where(c == 0, z, 3 - z) == 0
        self.rows = self.out.shape[0] // PIECES

    def rows_of(self, j):
        return pl.ds(j * self.rows, self.rows)

    def to_sib(self, t, j):
        q = self.sib_there if t == 0 else self.sib_here
        r = self.rows_of(j)
        return rcopy(
            self.part.at[q, r], self.from_sib.at[t, r], self.ss.at[t, j], self.rs.at[t, j], self.sib
        )

    def load(self, t):
        q = self.q_there if t == 0 else self.q_here
        return pltpu.make_async_copy(self.part.at[q], self.mine.at[t], self.ls.at[t])

    def load_extra(self, e):
        src, dst = self.extra[e]
        return pltpu.make_async_copy(src.at[self.q_here], dst, self.ls.at[2 + e])

    def across(self, j):
        r = self.rows_of(j)
        return rcopy(
            self.to_far.at[r], self.from_far.at[r], self.ss.at[2, j], self.rs.at[2, j], self.partner
        )

    def home(self, j):
        r = self.rows_of(j)
        return rcopy(
            self.done.at[r], self.out.at[r], self.ss.at[3, j], self.rs.at[3, j], self.owner
        )

    def keep(self):
        return pltpu.make_async_copy(self.done, self.out, self.ls.at[4])

    def start(self):
        for t in range(2):
            for j in range(PIECES):
                self.to_sib(t, j).start()
        for t in range(2):
            self.load(t).start()
        for e in range(len(self.extra)):
            self.load_extra(e).start()

    def add_near(self):
        self.load(0).wait()
        for j in range(PIECES):
            r = self.rows_of(j)
            self.to_sib(0, j).wait_recv()
            total = self.mine[0, r].astype(f32) + self.from_sib[0, r].astype(f32)
            self.to_far[r] = total.astype(bf16)
            self.across(j).start()
        self.load(1).wait()
        for e in range(len(self.extra)):
            self.load_extra(e).wait()

    def add_far(self, finish):
        for j in range(PIECES):
            r = self.rows_of(j)
            self.to_sib(1, j).wait_recv()
            self.across(j).wait_recv()
            total = self.mine[1, r].astype(f32) + self.from_sib[1, r].astype(f32)
            total = total + self.from_far[r].astype(f32)
            self.done[r] = finish(total, r).astype(bf16)

            @pl.when(jnp.logical_not(self.self_owner))
            def _():
                self.home(j).start()

    def finish(self):
        @pl.when(self.self_owner)
        def _():
            self.keep().start()
            self.keep().wait()

        for j in range(PIECES):
            @pl.when(jnp.logical_not(self.self_source))
            def _():
                self.home(j).wait_recv()

        for j in range(PIECES):
            self.to_sib(0, j).wait_send()
            self.to_sib(1, j).wait_send()
            self.across(j).wait_send()

            @pl.when(jnp.logical_not(self.self_owner))
            def _():
                self.home(j).wait_send()


def reduce_scratch(rows, extras):
    return [
        pltpu.VMEM((2, rows, D), bf16), pltpu.VMEM((rows, D), bf16), pltpu.VMEM((rows, D), bf16),
        pltpu.VMEM((2, rows, D), bf16), pltpu.VMEM((rows, D), bf16),
    ] + [pltpu.VMEM((rows, D), bf16)] * extras + [
        pltpu.SemaphoreType.DMA((5,)),
        pltpu.SemaphoreType.DMA((4, PIECES)),
        pltpu.SemaphoreType.DMA((4, PIECES)),
    ]


def reduce_out_kernel(
    np_, part, xg, bias, out, from_sib, from_far, to_far, mine, done, xq, ls, ss, rs,
):
    d, z, c, pair, g, y = place()
    barrier_all(np_, d, z, c, pair)
    red = Reduce(
        part, out, [(xg, xq)], (from_sib, from_far, to_far, mine, done), ls, ss, rs
    )
    red.start()
    red.add_near()
    red.add_far(lambda total, r: xq[r].astype(f32) + bias[...] + total)
    red.finish()


def reduce_out(np_, part, xg, bias, collective_id=2):
    rows = part.shape[1]
    any_ = pl.BlockSpec(memory_space=pl.ANY)
    return pl.pallas_call(
        functools.partial(reduce_out_kernel, np_),
        out_shape=sds((rows, D), bf16),
        in_specs=[any_, any_, pl.BlockSpec(memory_space=pltpu.VMEM)],
        out_specs=any_,
        scratch_shapes=reduce_scratch(rows, 1),
        compiler_params=pltpu.CompilerParams(
            collective_id=collective_id, has_side_effects=True, vmem_limit_bytes=VMEM_BYTES
        ),
        name="reduce_out",
    )(part, xg, bias)


class Swap:
    def __init__(self, np_, arrays, wo, ls, ss, rs):
        self.np_, self.arrays, self.wo, self.ls, self.ss, self.rs = np_, arrays, wo, ls, ss, rs
        self.here = place()

    def copy(self, s, o):
        d, z, c, pair, g, y = self.here
        src, dst = self.arrays[s]
        to = lax.rem(pair + o, self.np_)
        if o == 0:
            return pltpu.make_async_copy(src.at[pair], dst.at[pair], self.ls.at[s])
        return rcopy(
            src.at[to], dst.at[pair], self.ss.at[s, o], self.rs.at[s, o], (2 * to + c, z)
        )

    def copy_wo(self, o):
        d, z, c, pair, g, y = self.here
        src, dst = self.wo
        n = len(self.arrays)
        per = self.np_ // 4
        to = lax.rem(pair + o, self.np_)
        if o == 0:
            return pltpu.make_async_copy(src.at[lax.rem(pair, per)], dst.at[pair], self.ls.at[n])
        return rcopy(
            src.at[lax.rem(to, per)], dst.at[pair], self.ss.at[n, o], self.rs.at[n, o],
            (2 * to + c, z),
        )

    def collects(self, pair2):
        d, z, c, pair, g, y = self.here
        return lax.div(pair2, self.np_ // 4) == 2 * y + c

    def start(self):
        d, z, c, pair, g, y = self.here
        for s in range(len(self.arrays)):
            for o in range(1, self.np_):
                self.copy(s, o).start()
            self.copy(s, 0).start()
        if self.wo is not None:
            for o in range(self.np_):
                @pl.when(self.collects(lax.rem(pair + o, self.np_)))
                def _():
                    self.copy_wo(o).start()

    def finish(self):
        d, z, c, pair, g, y = self.here
        for s in range(len(self.arrays)):
            for o in range(self.np_):
                self.copy(s, o).wait()
        if self.wo is not None:
            for o in range(self.np_):
                @pl.when(self.collects(lax.rem(pair + o, self.np_)))
                def _():
                    if o == 0:
                        self.copy_wo(o).wait()
                    else:
                        self.copy_wo(o).wait_send()

                if o > 0:
                    @pl.when(self.collects(pair))
                    def _():
                        self.copy_wo(o).wait_recv()


def group_peer(o):
    d, z, c, pair, g, y = place()
    c2 = 1 - c if o % 2 else c
    z2 = z + 1 - 2 * lax.rem(z, 2) if o // 2 else z
    return 2 * pair + c2, z2


class Group:
    def __init__(self, own, all_, ls, ss, rs):
        self.own, self.all_, self.ls, self.ss, self.rs = own, all_, ls, ss, rs
        d, z, c, pair, g, y = place()
        self.k = 2 * y + c

    def copy(self, o):
        if o == 0:
            return pltpu.make_async_copy(self.own, self.all_.at[self.k], self.ls)
        return rcopy(
            self.own, self.all_.at[self.k], self.ss.at[o - 1], self.rs.at[o - 1], group_peer(o)
        )

    def start(self):
        for o in range(4):
            self.copy(o).start()

    def finish(self):
        for o in range(4):
            self.copy(o).wait()


def norm_back(total, x, dy):
    xhat, inverse = norm_parts(x.astype(f32))
    back = inverse * (
        total
        - jnp.mean(total, axis=-1, keepdims=True)
        - xhat * jnp.mean(total * xhat, axis=-1, keepdims=True)
    )
    return dy.astype(f32) + back


def tail_kernel(
    np_, part, xg, dyg, sums, dw1, dw2, dw, dwo,
    out, sums_all, r1, r2, rq, ro,
    from_sib, from_far, to_far, mine, done, xq, dyq, ls, ss, rs,
    ls_s, ss_s, rs_s, ls_g, ss_g, rs_g,
):
    d, z, c, pair, g, y = place()
    barrier_all(np_, d, z, c, pair)
    red = Reduce(
        part, out, [(xg, xq), (dyg, dyq)], (from_sib, from_far, to_far, mine, done), ls, ss, rs
    )
    grp = Group(sums, sums_all, ls_g, ss_g, rs_g)
    swap = Swap(np_, [(dw, rq), (dw1, r1), (dw2, r2)], (dwo, ro), ls_s, ss_s, rs_s)
    red.start()
    grp.start()
    swap.start()
    red.add_near()
    red.add_far(lambda total, r: norm_back(total, xq[r], dyq[r]))
    grp.finish()
    red.finish()
    swap.finish()


def tail(np_, part, xg, dyg, sums, dw1, dw2, dw, dwo, collective_id=3):
    rows = part.shape[1]
    any_ = pl.BlockSpec(memory_space=pl.ANY)
    wo_rows = dwo.shape[1]
    return pl.pallas_call(
        functools.partial(tail_kernel, np_),
        out_shape=(
            sds((rows, D), bf16), sds((4,) + sums.shape, f32),
            sds(dw1.shape, bf16), sds(dw2.shape, bf16), sds(dw.shape, bf16),
            sds((np_, wo_rows, D), bf16),
        ),
        in_specs=[any_] * 8,
        out_specs=(any_,) * 6,
        scratch_shapes=reduce_scratch(rows, 2) + [
            pltpu.SemaphoreType.DMA((4,)),
            pltpu.SemaphoreType.DMA((4, np_)),
            pltpu.SemaphoreType.DMA((4, np_)),
            pltpu.SemaphoreType.DMA,
            pltpu.SemaphoreType.DMA((3,)),
            pltpu.SemaphoreType.DMA((3,)),
        ],
        compiler_params=pltpu.CompilerParams(
            collective_id=collective_id, has_side_effects=True, vmem_limit_bytes=VMEM_BYTES
        ),
        name="tail",
    )(part, xg, dyg, sums, dw1, dw2, dw, dwo)


def same_slice_peer(np_, e):
    d, z, c, pair, g, y = place()
    to = lax.rem(pair * 2 + g + e, 2 * np_)
    pair2, g2 = lax.div(to, 2), lax.rem(to, 2)
    return to, (2 * pair2 + c, jnp.where(g2 == g, z, 3 - z))


def clip_kernel(
    np_, msg, r1, r2, rq, ro,
    t1, tq, t2, to, pieces,
    b1, bq, b2, bo, s1, sq, s2, so, m_all, p_out, ls, ss_m, rs_m, ss, rs,
):
    d, z, c, pair, g, y = place()
    bar = pltpu.get_barrier_semaphore()
    for o in range(1, 8):
        c2, z2 = column_peer(pair, c, z, o)
        pl.semaphore_signal(bar, inc=1, device_id=(2 * pair + c2, z2), device_id_type=MESH)
    for e in range(1, 2 * np_):
        unused, peer = same_slice_peer(np_, e)
        pl.semaphore_signal(bar, inc=1, device_id=peer, device_id_type=MESH)
    loads = [
        pltpu.make_async_copy(src, dst, ls.at[n])
        for n, (src, dst) in enumerate(((rq, bq), (r1, b1), (r2, b2), (ro, bo)))
    ]
    per = np_ // 4
    collects = lax.div(pair, per) == 2 * y + c
    for cp in loads[:3]:
        cp.start()

    @pl.when(collects)
    def _():
        loads[3].start()

    me = pair * 2 + g
    pl.semaphore_wait(bar, 7 + 2 * np_ - 1)

    def tell(e):
        to_, peer = same_slice_peer(np_, e)
        return rcopy(msg.at[to_], m_all.at[me], ss_m.at[e], rs_m.at[e], peer)

    own = pltpu.make_async_copy(msg.at[me], m_all.at[me], ls.at[4])
    own.start()
    for e in range(1, 2 * np_):
        tell(e).start()
    own.wait()
    for e in range(1, 2 * np_):
        tell(e).wait()
    norms = [jnp.sqrt(m_all[e, 3:4, 0:1]) for e in range(2 * np_)]
    mean_norm = sum(norms) / (2 * np_)
    factors = [mean_norm / jnp.maximum(n, mean_norm) for n in norms]
    p_out[...] = sum(f * m_all[e] for e, f in enumerate(factors))
    p_out[4:5, 0:1] = sum(jnp.where(d == e, n, 0.0) for e, n in enumerate(norms))
    group_factors = [
        jnp.where(g == 0, factors[2 * n], factors[2 * n + 1]) for n in range(np_)
    ]
    for cp in loads[:3]:
        cp.wait()

    def rows_to(s, src, dst, o, slot):
        c2, z2 = column_peer(pair, c, z, o)
        if o == 0:
            return pltpu.make_async_copy(src.at[c2, z2], dst.at[slot], ls.at[5 + s])
        return rcopy(
            src.at[c2, z2], dst.at[slot], ss.at[s, o], rs.at[s, o], (2 * pair + c2, z2)
        )

    for n, (buf, acc, dst) in enumerate(((bq, sq, tq), (b1, s1, t1))):
        for c2 in range(2):
            for z2 in range(4):
                total = sum(f * buf[m, c2, z2].astype(f32) for m, f in enumerate(group_factors))
                acc[c2, z2] = total.astype(acc.dtype)
        for o in range(8):
            rows_to(n, acc, dst, o, c * 4 + z).start()

    for t in range(2):
        total = sum(f * b2[m, t].astype(f32) for m, f in enumerate(group_factors))
        s2[t] = total.astype(s2.dtype)
    mirror_copy = rcopy(s2.at[1 - g], t2.at[1], ss.at[2, 0], rs.at[2, 0], (d, 3 - z))
    mirror_copy.start()
    kept = pltpu.make_async_copy(s2.at[g], t2.at[0], ls.at[7])
    kept.start()

    def wo_to(o):
        c2, z2 = column_peer(pair, c, z, o)
        if o == 0:
            return pltpu.make_async_copy(so.at[c2, z2], to.at[g], ls.at[8])
        return rcopy(
            so.at[c2, z2], to.at[g], ss.at[3, o], rs.at[3, g], (2 * pair + c2, z2)
        )

    @pl.when(collects)
    def _():
        loads[3].wait()
        for c2 in range(2):
            for z2 in range(4):
                total = sum(f * bo[m, c2, z2].astype(f32) for m, f in enumerate(group_factors))
                so[c2, z2] = total.astype(so.dtype)
        for o in range(8):
            wo_to(o).start()

    final = pltpu.make_async_copy(p_out, pieces, ls.at[9])
    final.start()
    for n, (acc, dst) in enumerate(((sq, tq), (s1, t1))):
        for o in range(8):
            rows_to(n, acc, dst, o, c * 4 + z).wait()
    mirror_copy.wait()
    kept.wait()

    @pl.when(collects)
    def _():
        wo_to(0).wait()
        for o in range(1, 8):
            wo_to(o).wait_send()

    for t in range(2):
        @pl.when(jnp.logical_or(jnp.logical_not(collects), g != t))
        def _():
            rcopy(so.at[0, 0], to.at[t], ss.at[3, 0], rs.at[3, t], (d, 3 - z)).wait_recv()

    final.wait()


def clip(np_, msg, r1, r2, rq, ro, collective_id=4):
    any_ = pl.BlockSpec(memory_space=pl.ANY)
    dma = pltpu.SemaphoreType.DMA
    return pl.pallas_call(
        functools.partial(clip_kernel, np_),
        out_shape=(
            sds((8,) + r1.shape[3:], bf16), sds((8,) + rq.shape[3:], bf16),
            sds((2,) + r2.shape[2:], bf16), sds((2,) + ro.shape[3:], bf16), sds(msg.shape[1:], f32),
        ),
        in_specs=[any_] * 5,
        out_specs=(any_,) * 5,
        scratch_shapes=[
            pltpu.VMEM(r1.shape, bf16), pltpu.VMEM(rq.shape, bf16), pltpu.VMEM(r2.shape, bf16),
            pltpu.VMEM(ro.shape, bf16),
            pltpu.VMEM(r1.shape[1:], bf16), pltpu.VMEM(rq.shape[1:], bf16),
            pltpu.VMEM(r2.shape[1:], bf16), pltpu.VMEM(ro.shape[1:], bf16),
            pltpu.VMEM(msg.shape, f32), pltpu.VMEM(msg.shape[1:], f32),
            dma((10,)), dma((2 * np_,)), dma((2 * np_,)), dma((4, 8)), dma((4, 8)),
        ],
        compiler_params=pltpu.CompilerParams(
            collective_id=collective_id, has_side_effects=True, vmem_limit_bytes=VMEM_BYTES
        ),
        name="clip",
    )(msg, r1, r2, rq, ro)


def local(
    block_in, out_grad, lengths, ln1_gain, ln1_bias, qkv_weight, qkv_bias, out_weight, out_bias,
    ln2_gain, ln2_bias, fc1_weight, fc1_bias, fc2_weight, fc2_bias,
):
    tp = lax.axis_size("ctx")
    dp = lax.axis_size("dp")
    np_ = dp // 2
    world = dp * tp
    d, z, c, pair, g, y = place()
    slice_at = 2 * y + c
    nh = HEADS // tp
    local_rows = block_in.shape[1]
    t = local_rows * tp
    rows = min(512, local_rows)
    part = D // tp
    r_in = D // world
    r_ff = fc2_weight.shape[0]
    ff = r_ff * dp

    x_own = block_in[0]
    pos = z * local_rows + jnp.arange(local_rows, dtype=jnp.int32)
    dy_own = jnp.where((pos < lengths[0])[:, None], out_grad[0], jnp.zeros((), bf16))

    w_qkv = jnp.moveaxis(qkv_weight.reshape(r_in, 3, tp, part), 2, 0).reshape(tp, r_in, 3 * part)
    w1 = fc1_weight.reshape(r_in, np_, 2, tp, r_ff)
    w1 = jnp.stack([w1[:, :, :, s] for s in (0, 3, 1, 2)], axis=3)
    w1 = w1.reshape(r_in, np_, 2, 2, 2, r_ff).transpose(3, 2, 0, 1, 4, 5).reshape(tp, r_in, ff)
    length_parts = jnp.stack([lengths[0] // 256, lengths[0] % 256]).astype(bf16)
    vectors = jnp.concatenate(
        [
            ln1_gain, ln1_bias, out_bias, ln2_gain, ln2_bias, fc2_bias, qkv_bias, fc1_bias,
            length_parts,
        ]
    )
    n_vec = 9 * r_in + r_ff
    vectors = jnp.pad(vectors, (0, 16 * PAD - n_vec - 2)).reshape(16, PAD)

    x, dy, w_qkv, w1, w2, wo, vectors = gather(
        np_, x_own, dy_own, w_qkv, w1, fc2_weight, out_weight, vectors
    )
    xq, dyq = x, dy
    x, dy = x.reshape(t, D), dy.reshape(t, D)
    w_qkv = w_qkv.reshape(D, 3 * part)
    w1, w2, wo = w1.reshape(D, ff), w2.reshape(ff, D), wo.reshape(part, D)
    vectors = vectors.reshape(np_, 2, tp, 16 * PAD).astype(f32)
    lengths_here = lax.dynamic_slice(vectors, (pair, g, 0, n_vec), (1, 1, 1, 2)).reshape(2)
    length = (lengths_here[0] * 256.0 + lengths_here[1]).astype(jnp.int32).reshape(1)
    b_up = lax.dynamic_slice_in_dim(vectors, c, 1, axis=1)[:, 0, :, 9 * r_in : n_vec]
    b_up = jnp.where(
        y == 0,
        jnp.stack([b_up[:, 0], b_up[:, 3]], axis=1),
        jnp.stack([b_up[:, 1], b_up[:, 2]], axis=1),
    ).reshape(1, ff)
    vectors = vectors.reshape(world, 16 * PAD)
    g1, b1, b_out, g2, b2, b_down = [
        vectors[:, s * r_in : (s + 1) * r_in].reshape(1, D) for s in range(6)
    ]
    b_qkv = vectors[:, 6 * r_in : 9 * r_in].reshape(3, tp, part)
    b_qkv = lax.dynamic_slice_in_dim(b_qkv, slice_at, 1, axis=1).reshape(3 * nh, HEAD_DIM)
    extra = np.zeros((3 * nh, PAD - HEAD_DIM), np.float32)
    extra[:nh, 0] = HEAD_DIM**0.5
    extra[nh : 2 * nh, 1:4] = 1.0
    extra[2 * nh :, 0:3] = 1.0
    b_pad = jnp.concatenate([b_qkv, jnp.asarray(extra)], axis=1).reshape(1, 3 * nh * PAD)
    cosine, sine = tables(t)

    q, k, v, cf, ctx = attn_fwd(length, x, g1, b1, w_qkv, b_pad, cosine, sine, nh, rows)
    out_part, u_mlp, dw1, dw2, vec = mlp(x, dy, ctx, g2, b2, wo, w1, b_up, w2, rows // 2)
    block_out = reduce_out(np_, out_part.reshape(4, local_rows, D), xq, b_out + b_down)
    u_part, dw, dwo, vec = attn_bwd(
        x, dy, cf, ctx, u_mlp, q, k, v, g1, b1, w_qkv, wo, cosine, sine, vec, rows
    )
    per = np_ // 4
    input_grad, sums, r1, r2, rq, ro = tail(
        np_, u_part.reshape(4, local_rows, D), xq, dyq, vec,
        dw1.reshape(np_, D // np_, ff), dw2.reshape(np_, 2 * r_ff, D),
        dw.reshape(np_, D // np_, 3 * part), dwo.reshape(per, part // per, D),
    )
    d_vecs = jnp.concatenate([jnp.sum(sums[:, :4], axis=0), sums[:1, 6]], axis=0)
    squares = (
        jnp.sum(d_vecs * d_vecs) + jnp.sum(sums[0, 6] * sums[0, 6])
        + jnp.sum(sums[:, 4] * sums[:, 4]) + jnp.sum(sums[:, 5] * sums[:, 5])
        + jnp.sum(sums[:, 7, 0])
    )

    def for_owners(m):
        m = lax.dynamic_index_in_dim(m, c, axis=m.ndim - 3, keepdims=False)
        m = jnp.where(
            y == 0,
            jnp.stack([m[..., 0, :], m[..., 3, :]], axis=-2),
            jnp.stack([m[..., 1, :], m[..., 2, :]], axis=-2),
        )
        return m

    p_vecs = jnp.moveaxis(for_owners(d_vecs.reshape(5, np_, 2, tp, r_in)), 0, 2)
    p_vecs = p_vecs.reshape(np_, 2, 5 * r_in)
    p_qkv = sums[:, 5, : 3 * part].reshape(tp, 3, part).swapaxes(0, 1)
    p_qkv = for_owners(p_qkv.reshape(np_, 2, tp, 3 * r_in))
    p_up = vec[4].reshape(np_, 2, r_ff)
    msg = jnp.stack(
        [jnp.pad(m, ((0, 0), (0, 0), (0, PAD - m.shape[2]))) for m in (p_vecs, p_qkv, p_up)]
        + [jnp.broadcast_to(squares, (np_, 2, PAD))] + [jnp.zeros((np_, 2, PAD), f32)] * 4,
        axis=2,
    ).reshape(2 * np_, 8, PAD)
    t1, tq, t2, to, mine = clip(
        np_, msg, r1.reshape(np_, 2, tp, r_in, ff), r2.reshape(np_, 2, r_ff, D),
        rq.reshape(np_, 2, tp, r_in, 3 * part), ro.reshape(np_, 2, tp, r_in, D),
    )
    t1 = t1.reshape(2, tp, r_in, ff).astype(f32)
    t1 = jnp.stack([t1[:, 0] + t1[:, 3], t1[:, 1] + t1[:, 2]], axis=1)
    t1 = t1.reshape(2, 2, r_in, np_, 2, r_ff)
    t1 = jnp.stack([t1[:, s, :, :, e] for s, e in ((0, 0), (1, 0), (1, 1), (0, 1))], axis=0)
    g_fc1 = t1.transpose(2, 3, 1, 0, 4).reshape(r_in, ff * tp)
    tq = tq.reshape(2, tp, r_in, 3, part).astype(f32)
    tq = jnp.stack([tq[:, 0] + tq[:, 3], tq[:, 1] + tq[:, 2]], axis=0)
    g_qkv = tq.reshape(tp, r_in, 3, part).transpose(1, 2, 0, 3).reshape(r_in, 3 * D)
    g_fc2 = jnp.sum(t2.astype(f32), axis=0)
    g_out = jnp.sum(to.astype(f32), axis=0)
    cut = [mine[0, s * r_in : (s + 1) * r_in] for s in range(5)]
    return (
        block_out[None], input_grad[None],
        cut[0], cut[1], g_qkv, mine[1, : 3 * r_in], g_out, cut[4],
        cut[2], cut[3], g_fc1, mine[2, :r_ff], g_fc2, cut[4],
        mine[4, :1],
    )


def solution(mesh):
    both = ("dp", "ctx")
    vec, mat, act = P(both), P(both, None), P("dp", "ctx", None)
    weights = (vec, vec, mat, vec, mat, vec, vec, vec, mat, vec, mat, vec)
    return jax.shard_map(
        local,
        mesh=mesh,
        in_specs=(act, act, P("dp")) + weights,
        out_specs=(act, act) + weights + (P("dp"),),
        check_vma=False,
    )
```

```python
import functools
import math

import jax
import jax.numpy as jnp
import numpy as np
from jax import lax
from jax.experimental import pallas as pl
from jax.experimental.pallas import tpu as pltpu
from jax.sharding import PartitionSpec as P

D = 768
HEADS = 12
HEAD_DIM = 64
ROT = 16
PAD = 128
eps_norm = 1e-05
neg_big = -1e30
root_half = math.sqrt(0.5)
inv_root_two_pi = 1.0 / math.sqrt(2.0 * math.pi)
f32 = jnp.float32
bf16 = jnp.bfloat16
VMEM_BYTES = 60 * 2**20


def dot(a, b, dims=((1,), (0,))):
    return lax.dot_general(a, b, (dims, ((), ())), preferred_element_type=f32)


def norm_parts(values):
    centered = values - jnp.mean(values, axis=-1, keepdims=True)
    row_var = jnp.mean(centered * centered, axis=-1, keepdims=True)
    inverse = lax.rsqrt(row_var + eps_norm)
    return centered * inverse, inverse


def turn(u, cosine, sine, first):
    partner = jnp.where(first, pltpu.roll(u, PAD - ROT // 2, 1), pltpu.roll(u, ROT // 2, 1))
    return u * cosine + partner * sine


def split3(v):
    hi = v.astype(bf16).astype(f32)
    mid = (v - hi).astype(bf16).astype(f32)
    low = (v - hi - mid).astype(bf16).astype(f32)
    return hi, mid, low


def fold(op, s):
    out = s[:, :PAD]
    for t in range(1, s.shape[1] // PAD):
        out = op(out, s[:, t * PAD : (t + 1) * PAD])
    return out


def attn_fwd_kernel(
    np_, len_ref, x_ref, tab_ref, w_ref, wb_ref, cos_ref, sin_ref, dy, w2, wo,
    q_ref, k_ref, v_ref, cf_ref, c_ref, dyg, w2g, wog,
    w_scr, s_scr, q_scr, m_scr, l_scr, acc_scr, ls_dy, ss_dy, rs_dy, ls_w, ss_w, rs_w,
):
    i = pl.program_id(0)
    nh = k_ref.shape[0]
    rows = x_ref.shape[0]
    spread = Spread(dy, dyg, ls_dy, ss_dy, rs_dy)
    weights = Weights(np_, [], (w2, w2g), (wo, wog), ls_w, ss_w, rs_w)

    @pl.when(i == 0)
    def _():
        d, z, c, pair, g, y = place()
        barrier_all(np_, d, z, c, pair)
        weights.start()
        spread.start()

    @pl.when(i == 1)
    def _():
        weights.between_wo()
        weights.between_w2()

    @pl.when(i == 2)
    def _():
        spread.forward(0)

    @pl.when(i == 3)
    def _():
        spread.forward(1)

    @pl.when(i == 0)
    def _():
        for h in range(3 * nh):
            w_scr[:, h * PAD : h * PAD + HEAD_DIM] = w_ref[:, h * HEAD_DIM : (h + 1) * HEAD_DIM]
            w_scr[:, h * PAD + HEAD_DIM : (h + 1) * PAD] = jnp.zeros((D, PAD - HEAD_DIM), bf16)

    xhat, unused = norm_parts(x_ref[...].astype(f32))
    a1 = (xhat * tab_ref[0:1] + tab_ref[1:2]).astype(bf16)
    cosine, sine = cos_ref[...], sin_ref[...]
    lane = lax.broadcasted_iota(jnp.int32, (rows, PAD), 1)
    first = lane < ROT // 2
    key_pos = i * rows + lax.broadcasted_iota(jnp.int32, (rows, PAD), 0)
    key_bias = jnp.where(key_pos.astype(f32) < len_ref[...], 0.0, neg_big)
    here = pl.ds(pl.multiple_of(i * rows, rows), rows)
    qkv = dot(a1, w_scr[...]) + wb_ref[...]
    for h in range(nh):
        q = turn(qkv[:, h * PAD : (h + 1) * PAD], cosine, sine, first) * HEAD_DIM**-0.5
        q_scr[h] = q.astype(bf16)
        k = turn(qkv[:, (nh + h) * PAD : (nh + h + 1) * PAD], cosine, sine, first)
        k_ref[h, here] = jnp.where(lane == HEAD_DIM, key_bias, k).astype(bf16)
        v_ref[h, here] = qkv[:, (2 * nh + h) * PAD : (2 * nh + h + 1) * PAD].astype(bf16)

    causal = lax.broadcasted_iota(jnp.int32, (rows, rows), 0) >= lax.broadcasted_iota(
        jnp.int32, (rows, rows), 1
    )
    for h in range(nh):
        s = dot(q_scr[h], k_ref[h, here], ((1,), (1,)))
        s = jnp.where(causal, s, neg_big)
        s_scr[h, i] = s
        m_scr[h] = fold(jnp.maximum, s)

    def scores(j, carry):
        there = pl.ds(pl.multiple_of(j * rows, rows), rows)
        for h in range(nh):
            s = dot(q_scr[h], k_ref[h, there], ((1,), (1,)))
            s_scr[h, j] = s
            m_scr[h] = jnp.maximum(m_scr[h], fold(jnp.maximum, s))
        return carry

    lax.fori_loop(0, i, scores, 0)
    for h in range(nh):
        m_scr[h] = jnp.broadcast_to(jnp.max(m_scr[h], axis=-1, keepdims=True), (rows, PAD))
        l_scr[h] = jnp.zeros((rows, PAD), f32)
        acc_scr[h] = jnp.zeros((rows, PAD), f32)

    def weigh(j, carry):
        there = pl.ds(pl.multiple_of(j * rows, rows), rows)
        for h in range(nh):
            p = jnp.exp(s_scr[h, j] - m_scr[h][:, :1])
            l_scr[h] += fold(jnp.add, p)
            acc_scr[h] += dot(p.astype(bf16), v_ref[h, there])
        return carry

    lax.fori_loop(0, i + 1, weigh, 0)
    for h in range(nh):
        total = jnp.sum(l_scr[h], axis=-1, keepdims=True)
        context = acc_scr[h] / total
        cf_ref[:, h * PAD : (h + 1) * PAD] = context
        c_ref[:, h * HEAD_DIM : (h + 1) * HEAD_DIM] = context[:, :HEAD_DIM].astype(bf16)
        hi, mid, low = split3(-(m_scr[h][:, :1] + jnp.log(total)))
        q = q_scr[h].astype(f32)
        q = jnp.where(lane == HEAD_DIM + 1, hi, q)
        q = jnp.where(lane == HEAD_DIM + 2, mid, q)
        q = jnp.where(lane == HEAD_DIM + 3, low, q)
        q_ref[h] = q.astype(bf16)

    @pl.when(i == pl.num_programs(0) - 1)
    def _():
        spread.finish()
        weights.finish_wo()
        weights.finish_w2()


def squares_of(m):
    return jnp.sum(jnp.sum(m * m, axis=0, keepdims=True), axis=1, keepdims=True)


def mlp_kernel(
    x_ref, dy_ref, c_ref, tab_ref, wo_ref, w1_ref, w2_ref,
    part_ref, u_ref, dw1_ref, dw2_ref, vec_ref, dw1_scr, dw2_scr,
):
    i = pl.program_id(0)
    xhat, unused = norm_parts(x_ref[...].astype(f32))
    gain = tab_ref[3:4]
    a2 = (xhat * gain + tab_ref[4:5]).astype(bf16)
    z = dot(a2, w1_ref[...]) + tab_ref[5:6]
    cdf = 0.5 * (1.0 + lax.erf(z * root_half))
    hidden = (z * cdf).astype(bf16)
    part = dot(hidden, w2_ref[...]) + dot(c_ref[...], wo_ref[...])
    part_ref[...] = part.astype(part_ref.dtype)
    dy = dy_ref[...]
    slope = cdf + z * jnp.exp(-0.5 * z * z) * inv_root_two_pi
    dz = (dot(dy, w2_ref[...], ((1,), (1,))) * slope).astype(bf16)
    da2 = dot(dz, w1_ref[...], ((1,), (1,)))
    u_ref[...] = (da2 * gain).astype(u_ref.dtype)

    @pl.when(i == 0)
    def _():
        dw1_scr[...] = jnp.zeros_like(dw1_scr)
        dw2_scr[...] = jnp.zeros_like(dw2_scr)
        vec_ref[...] = jnp.zeros_like(vec_ref)

    dw1_scr[...] += dot(a2, dz, ((0,), (0,)))
    dw2_scr[...] += dot(hidden, dy, ((0,), (0,)))
    vec_ref[2:3] += jnp.sum(da2 * xhat, axis=0, keepdims=True)
    vec_ref[3:4] += jnp.sum(da2, axis=0, keepdims=True)
    vec_ref[4:5] += jnp.sum(dz.astype(f32), axis=0, keepdims=True)
    vec_ref[6:7] += jnp.sum(dy.astype(f32), axis=0, keepdims=True)

    @pl.when(i == pl.num_programs(0) - 1)
    def _():
        dw1_ref[...] = dw1_scr[...].astype(bf16)
        dw2_ref[...] = dw2_scr[...].astype(bf16)
        vec_ref[7:8, 0:1] = squares_of(dw1_scr[...]) + squares_of(dw2_scr[...])


def attn_bwd_kernel(
    np_, r_in, r_ff, x_ref, dy_ref, cf_ref, c_ref, u_in_ref, q_ref, k_ref, v_ref, tab_ref, w_ref,
    wo_ref, cos_ref, sin_ref, vec_in_ref, hot_ref, qkv_at, part, xg, dyg, dw1, dw2,
    block_out, input_grad, t1, tq, t2, to, pieces,
    wo_scr, dk_scr, dv_scr, dq_scr, dc_scr, dqkv_scr, dw_scr, dwo_scr, vec_ref, u_scr, dw, dwo,
    from_sib, from_far, to_far, mine, done, xq, ls_o, ss_o, rs_o,
    from_sib2, from_far2, to_far2, done2, dyq, ls_u, ss_u, rs_u,
    ls_s, ss_s, rs_s, ls_w, ss_w, rs_w, sums_all, ls_g, ss_g, rs_g,
    b1, bq, b2, bo, s1, sq, s2, so, msg, m_all, p_out, ls, ss_m, rs_m, ss, rs,
):
    step = pl.program_id(0)
    blocks = pl.num_programs(0)
    i = blocks - 1 - step
    nh = k_ref.shape[0]
    rows = x_ref.shape[0]
    wide = 3 * nh * HEAD_DIM
    lane = lax.broadcasted_iota(jnp.int32, (rows, PAD), 1)
    first = lane < ROT // 2
    here = pl.ds(pl.multiple_of(i * rows, rows), rows)
    red = Reduce(
        part, block_out, [(xg, xq)], (from_sib, from_far, to_far, mine, done), ls_o, ss_o, rs_o
    )
    red_u = ReduceQuarters(
        u_scr, input_grad, (from_sib2, from_far2, to_far2, done2), ls_u, ss_u, rs_u
    )
    swap = Swap(np_, [(dw1, b1), (dw2, b2)], None, ls_s, ss_s, rs_s)
    load_dy = pltpu.make_async_copy(dyg.at[red.q_here], dyq, ls.at[4])

    def back(total, r):
        return norm_back(total, xq[r], dyq[r])

    @pl.when(step == 0)
    def _():
        meet(np_)
        red.start()
        load_dy.start()
        swap.start()

    @pl.when(step == 2)
    def _():
        red.add_far(lambda total, r: xq[r].astype(f32) + tab_ref[2:3] + total)

    @pl.when(step == 0)
    def _():
        dk_scr[...] = jnp.zeros_like(dk_scr)
        dv_scr[...] = jnp.zeros_like(dv_scr)
        dw_scr[...] = jnp.zeros_like(dw_scr)
        dwo_scr[...] = jnp.zeros_like(dwo_scr)
        vec_ref[...] = vec_in_ref[...]
        for h in range(nh):
            wo_scr[h * PAD : h * PAD + HEAD_DIM] = wo_ref[h * HEAD_DIM : (h + 1) * HEAD_DIM]
            wo_scr[h * PAD + HEAD_DIM : (h + 1) * PAD] = jnp.zeros((PAD - HEAD_DIM, D), bf16)

    dy = dy_ref[...]
    dc_all = dot(dy, wo_scr[...], ((1,), (1,))).astype(bf16)
    for h in range(nh):
        dc = dc_all[:, h * PAD : (h + 1) * PAD].astype(f32)
        delta = jnp.sum(dc * cf_ref[:, h * PAD : (h + 1) * PAD], axis=-1, keepdims=True)
        hi, mid, low = split3(-delta)
        dc = jnp.where(lane == HEAD_DIM, hi, dc)
        dc = jnp.where(lane == HEAD_DIM + 1, mid, dc)
        dc = jnp.where(lane == HEAD_DIM + 2, low, dc)
        dc_scr[h] = dc.astype(bf16)

    @pl.when(step == 0)
    def _():
        red.add_near()

    causal = lax.broadcasted_iota(jnp.int32, (rows, rows), 0) <= lax.broadcasted_iota(
        jnp.int32, (rows, rows), 1
    )

    def block(j, diagonal):
        there = pl.ds(pl.multiple_of(j * rows, rows), rows)
        for h in range(nh):
            k = k_ref[h, there]
            q = q_ref[h]
            dc = dc_scr[h]
            pt = jnp.exp(dot(k, q, ((1,), (1,))))
            if diagonal:
                pt = jnp.where(causal, pt, 0.0)
            dpt = dot(v_ref[h, there], dc, ((1,), (1,)))
            dst = (pt * dpt).astype(bf16)
            dv_scr[h, there] += dot(pt.astype(bf16), dc)
            dk_scr[h, there] += dot(dst, q)
            dq = dot(dst, k, ((0,), (0,)))
            if diagonal:
                dq_scr[h] = dq
            else:
                dq_scr[h] += dq

    block(i, True)

    def off(j, carry):
        block(j, False)
        return carry

    lax.fori_loop(0, i, off, 0)
    cosine, sine = cos_ref[...], -sin_ref[...]
    for h in range(nh):
        dq = turn(dq_scr[h], cosine, sine, first) * HEAD_DIM**-0.5
        dk = turn(dk_scr[h, here], cosine, sine, first)
        for at, piece in ((h, dq), (nh + h, dk), (2 * nh + h, dv_scr[h, here])):
            dqkv_scr[:, at * HEAD_DIM : (at + 1) * HEAD_DIM] = piece[:, :HEAD_DIM].astype(bf16)
    dqkv = dqkv_scr[...]
    xhat, unused = norm_parts(x_ref[...].astype(f32))
    gain = tab_ref[0:1]
    a1 = (xhat * gain + tab_ref[1:2]).astype(bf16)
    da1 = dot(dqkv, w_ref[...], ((1,), (1,)))
    u_scr[i] = (u_in_ref[...] + da1 * gain).astype(bf16)
    red_u.ready(i)
    dw_scr[...] += dot(a1, dqkv, ((0,), (0,)))
    dwo_scr[...] += dot(c_ref[...], dy, ((0,), (0,)))
    vec_ref[0:1] += jnp.sum(da1 * xhat, axis=0, keepdims=True)
    vec_ref[1:2] += jnp.sum(da1, axis=0, keepdims=True)
    vec_ref[5:6, :wide] += jnp.sum(dqkv.astype(f32), axis=0, keepdims=True)
    red_u.push(i)

    @pl.when(step == blocks - 1)
    def _():
        vec_ref[7:8, 0:1] += squares_of(dw_scr[...]) + squares_of(dwo_scr[...])
        share = D // np_
        for n in range(np_):
            dw[n] = dw_scr[n * share : (n + 1) * share].astype(bf16)
        per = np_ // 4
        share_o = dwo_scr.shape[0] // per
        for n in range(per):
            dwo[n] = dwo_scr[n * share_o : (n + 1) * share_o].astype(bf16)
        load_dy.wait()
        finish_all(
            np_, r_in, r_ff, wide // 3, red, red_u, swap, back,
            dw, dwo, vec_ref, hot_ref, qkv_at, t1, tq, t2, to, pieces,
            ls_w, ss_w, rs_w, sums_all, ls_g, ss_g, rs_g,
            b1, bq, b2, bo, s1, sq, s2, so, msg, m_all, p_out, ls, ss_m, rs_m, ss, rs,
        )


def whole(shape):
    return pl.BlockSpec(shape, lambda i: (0,) * len(shape), pipeline_mode=pl.Buffered(1))


def sds(shape, dtype):
    return jax.ShapeDtypeStruct(shape, dtype)


def params(collective_id=None):
    return pltpu.CompilerParams(
        dimension_semantics=("arbitrary",), vmem_limit_bytes=VMEM_BYTES,
        collective_id=collective_id, has_side_effects=collective_id is not None,
    )


def weight_sems(np_, n):
    return [
        pltpu.SemaphoreType.DMA((n,)),
        pltpu.SemaphoreType.DMA((n, 8 + np_)),
        pltpu.SemaphoreType.DMA((n, 8 + np_)),
    ]


def attn_fwd(np_, length, x, tab, w, wb, cosine, sine, dy, w2, wo, nh, rows):
    t = x.shape[0]
    lanes = pl.BlockSpec((rows, PAD), lambda i: (i, 0))
    any_ = pl.BlockSpec(memory_space=pl.ANY)
    return pl.pallas_call(
        functools.partial(attn_fwd_kernel, np_),
        grid=(t // rows,),
        out_shape=(
            sds((nh, t, PAD), bf16), sds((nh, t, PAD), bf16), sds((nh, t, PAD), bf16),
            sds((t, nh * PAD), f32), sds((t, nh * HEAD_DIM), bf16),
            sds((4,) + dy.shape, bf16),
            sds((np_, 2) + w2.shape, bf16), sds((np_ // 4, 2, 4) + wo.shape, bf16),
        ),
        in_specs=[
            whole((1, PAD)), pl.BlockSpec((rows, D), lambda i: (i, 0)),
            whole((8, D)), whole(w.shape), whole(wb.shape), lanes, lanes,
            any_, any_, any_,
        ],
        out_specs=(
            pl.BlockSpec((nh, rows, PAD), lambda i: (0, i, 0)),
            whole((nh, t, PAD)), whole((nh, t, PAD)),
            pl.BlockSpec((rows, nh * PAD), lambda i: (i, 0)),
            pl.BlockSpec((rows, nh * HEAD_DIM), lambda i: (i, 0)),
            any_, any_, any_,
        ),
        scratch_shapes=[
            pltpu.VMEM((D, 3 * nh * PAD), bf16),
            pltpu.VMEM((nh, t // rows, rows, rows), f32),
            pltpu.VMEM((nh, rows, PAD), bf16),
            pltpu.VMEM((nh, rows, PAD), f32),
            pltpu.VMEM((nh, rows, PAD), f32),
            pltpu.VMEM((nh, rows, PAD), f32),
        ] + spread_sems() + weight_sems(np_, 2),
        compiler_params=params(2),
        name="attn_fwd",
    )(length, x, tab, w, wb, cosine, sine, dy, w2, wo)


def mlp(x, dy, c, tab, wo, w1, w2, rows):
    t = x.shape[0]
    ff = w1.shape[1]
    row = pl.BlockSpec((rows, D), lambda i: (i, 0))
    return pl.pallas_call(
        mlp_kernel,
        grid=(t // rows,),
        out_shape=(
            sds((t, D), bf16), sds((t, D), f32), sds((D, ff), bf16), sds((ff, D), bf16),
            sds((8, D), f32),
        ),
        in_specs=[
            row, row, pl.BlockSpec((rows, c.shape[1]), lambda i: (i, 0)),
            whole((8, D)), whole(wo.shape), whole(w1.shape), whole(w2.shape),
        ],
        out_specs=(row, row, whole((D, ff)), whole((ff, D)), whole((8, D))),
        scratch_shapes=[pltpu.VMEM((D, ff), f32), pltpu.VMEM((ff, D), f32)],
        compiler_params=params(),
        name="mlp",
    )(x, dy, c, tab, wo, w1, w2)


def attn_bwd(
    np_, r_in, r_ff, x, dy, cf, c, u_in, q, k, v, tab, w, wo, cosine, sine, vec,
    part, xg, dyg, dw1, dw2, rows,
):
    t = x.shape[0]
    nh = q.shape[0]
    n = t // rows
    wide = w.shape[1]
    part_w = wide // 3
    quarter = part.shape[1]
    ff = dw1.shape[2]
    per = np_ // 4
    row = pl.BlockSpec((rows, D), lambda i: (n - 1 - i, 0))
    lanes = pl.BlockSpec((rows, PAD), lambda i: (n - 1 - i, 0))
    any_ = pl.BlockSpec(memory_space=pl.ANY)
    dma = pltpu.SemaphoreType.DMA
    vm = pltpu.VMEM
    hot, qkv_at = one_hot_tables(np_, r_in, r_ff, part_w)
    per_owner = lambda cols: vm((2, 4, r_in, cols), bf16)
    block = vm((quarter, D), bf16)
    return pl.pallas_call(
        functools.partial(attn_bwd_kernel, np_, r_in, r_ff),
        grid=(n,),
        out_shape=(
            sds((quarter, D), bf16), sds((quarter, D), bf16), sds((8, r_in, ff), bf16),
            sds((8, r_in, wide), bf16), sds((2, r_ff, D), bf16), sds((2, r_in, D), bf16),
            sds((8, PAD), f32),
        ),
        in_specs=[
            row, row, pl.BlockSpec((rows, nh * PAD), lambda i: (n - 1 - i, 0)),
            pl.BlockSpec((rows, nh * HEAD_DIM), lambda i: (n - 1 - i, 0)), row,
            pl.BlockSpec((nh, rows, PAD), lambda i: (0, n - 1 - i, 0)),
            whole(k.shape), whole(v.shape), whole((8, D)), whole(w.shape),
            whole(wo.shape), lanes, lanes, whole((8, D)), whole(hot.shape), whole(qkv_at.shape),
            any_, any_, any_, any_, any_,
        ],
        out_specs=(any_,) * 7,
        scratch_shapes=[
            vm((nh * PAD, D), bf16), vm((nh, t, PAD), f32), vm((nh, t, PAD), f32),
            vm((nh, rows, PAD), f32), vm((nh, rows, PAD), bf16), vm((rows, wide), bf16),
            vm((D, wide), f32), vm((nh * HEAD_DIM, D), f32), vm((8, D), f32),
            vm((4, quarter, D), bf16), vm((np_, D // np_, wide), bf16),
            vm((per, part_w // per, D), bf16),
        ] + reduce_scratch(quarter, 1) + [
            vm((2, quarter, D), bf16), block, block, block, block,
            dma((5,)), dma((4, PIECES)), dma((4, PIECES)),
        ] + swap_sems(np_, 2) + swap_sems(np_, 2) + [
            vm((4, 8, D), f32), dma, dma((3,)), dma((3,)),
            vm(dw1.shape, bf16), vm((np_, D // np_, wide), bf16), vm(dw2.shape, bf16),
            vm((np_, part_w // per, D), bf16),
            per_owner(ff), per_owner(wide), vm((2, r_ff, D), bf16), per_owner(D),
            vm((2 * np_, 8, PAD), f32), vm((2 * np_, 8, PAD), f32), vm((8, PAD), f32),
            dma((10,)), dma((2 * np_,)), dma((2 * np_,)), dma((4, 8)), dma((4, 8)),
        ],
        compiler_params=params(3),
        name="attn_bwd",
    )(x, dy, cf, c, u_in, q, k, v, tab, w, wo, cosine, sine, vec, hot, qkv_at, part, xg, dyg, dw1, dw2)


def swap_sems(np_, n):
    return [
        pltpu.SemaphoreType.DMA((n,)),
        pltpu.SemaphoreType.DMA((n, np_)),
        pltpu.SemaphoreType.DMA((n, np_)),
    ]


def tables(t):
    inv_freqs = np.exp(np.arange(ROT // 2, dtype=np.float32) * np.float32(-2.0 * math.log(10000.0) / ROT))
    angles = np.arange(t, dtype=np.float32)[:, None] * inv_freqs.astype(np.float32)[None, :]
    cosine = np.ones((t, PAD), np.float32)
    sine = np.zeros((t, PAD), np.float32)
    half = ROT // 2
    cosine[:, :half] = cosine[:, half:ROT] = np.cos(angles)
    sine[:, :half] = -np.sin(angles)
    sine[:, half:ROT] = np.sin(angles)
    return jnp.asarray(cosine), jnp.asarray(sine)


MESH = pl.DeviceIdType.MESH
AX = ("dp", "ctx")
CHUNKS = 2


def place():
    d, z = lax.axis_index("dp"), lax.axis_index("ctx")
    c, pair, g = lax.rem(d, 2), lax.div(d, 2), lax.div(z, 2)
    y = lax.rem(g + lax.rem(z, 2), 2)
    return d, z, c, pair, g, y


def mirror(m, g):
    return jnp.where(g == 0, m, 3 - m)


def rcopy(src, dst, ss, rs, device):
    return pltpu.make_async_remote_copy(
        src_ref=src, dst_ref=dst, send_sem=ss, recv_sem=rs, device_id=device, device_id_type=MESH
    )


def column_peer(pair, c, z, o):
    m = lax.rem(c * 4 + z + o, 8)
    return lax.div(m, 4), lax.rem(m, 4)


def barrier_all(np_, d, z, c, pair):
    bar = pltpu.get_barrier_semaphore()
    for o in range(1, 8):
        c2, z2 = column_peer(pair, c, z, o)
        pl.semaphore_signal(bar, inc=1, device_id=(2 * pair + c2, z2), device_id_type=MESH)
    for o in range(1, np_):
        pl.semaphore_signal(
            bar, inc=1, device_id=(2 * lax.rem(pair + o, np_) + c, z), device_id_type=MESH
        )
    pl.semaphore_wait(bar, 7 + np_ - 1)


class Spread:
    def __init__(self, own, out, ls, ss, rs):
        self.own, self.out, self.ls, self.ss, self.rs = own, out, ls, ss, rs
        self.rows = out.shape[1] // CHUNKS
        d, z, c, pair, g, y = place()
        self.d, self.z, self.c, self.g, self.y = d, z, c, g, y
        self.prim = c == g
        self.sib = (d + 1 - 2 * c, z)
        self.partner = (d, z + 1 - 2 * lax.rem(z, 2))
        self.far = (d, 1 + c)

    def cut(self, ref, j):
        return ref.at[pl.ds(j * self.rows, self.rows)]

    def send(self, q, j, way, device, src=None):
        src = self.cut(self.out.at[q], j) if src is None else src
        return rcopy(
            src, self.cut(self.out.at[q], j), self.ss.at[way, q, j], self.rs.at[q, j], device
        )

    def start(self):
        own = [self.cut(self.own, j) for j in range(CHUNKS)]

        @pl.when(self.prim)
        def _():
            pltpu.make_async_copy(self.own, self.out.at[self.z], self.ls).start()
            for j in range(CHUNKS):
                self.send(self.z, j, 0, self.partner, own[j]).start()
            for j in range(CHUNKS):
                self.send(self.z, j, 1, self.sib, own[j]).start()

        @pl.when(jnp.logical_not(self.prim))
        def _():
            for j in range(CHUNKS):
                self.send(self.z, j, 0, self.far, own[j]).start()

    def wait_recv(self, q, j):
        self.send(q, j, 0, self.sib).wait_recv()

    def forward(self, j):
        far = (mirror(2, self.g), mirror(3, self.g))
        end, mid = mirror(0, self.g), mirror(1, self.g)

        @pl.when(jnp.logical_and(self.prim, self.y == 1))
        def _():
            for q in far:
                self.wait_recv(q, j)
                self.send(q, j, 0, self.partner).start()
                self.send(q, j, 1, self.sib).start()
            self.wait_recv(end, j)
            self.send(end, j, 1, self.sib).start()

        @pl.when(jnp.logical_and(self.prim, self.y == 0))
        def _():
            self.wait_recv(mid, j)
            self.send(mid, j, 1, self.sib).start()
            if j > 0:
                for q in far:
                    self.wait_recv(q, j - 1)
                    self.send(q, j - 1, 1, self.sib).start()

    def finish(self):
        far = (mirror(2, self.g), mirror(3, self.g))
        end, mid = mirror(0, self.g), mirror(1, self.g)

        @pl.when(jnp.logical_and(self.prim, self.y == 0))
        def _():
            for q in far:
                self.wait_recv(q, CHUNKS - 1)
                self.send(q, CHUNKS - 1, 1, self.sib).start()
            for j in range(CHUNKS):
                self.send(end, j, 0, self.partner).wait_send()

        @pl.when(jnp.logical_and(self.prim, self.y == 1))
        def _():
            for j in range(CHUNKS):
                for q in far + (mid,):
                    self.send(q, j, 0, self.partner).wait_send()

        @pl.when(self.prim)
        def _():
            pltpu.make_async_copy(self.own, self.out.at[self.z], self.ls).wait()
            for q in range(4):
                for j in range(CHUNKS):
                    self.send(q, j, 1, self.sib).wait_send()

        @pl.when(jnp.logical_not(self.prim))
        def _():
            for q in range(4):
                for j in range(CHUNKS):
                    self.wait_recv(q, j)
            for j in range(CHUNKS):
                self.send(self.z, j, 0, self.far).wait_send()


class Weights:
    def __init__(self, np_, sliced, w2, wo, ls, ss, rs):
        self.np_, self.sliced, self.w2, self.wo = np_, sliced, w2, wo
        self.ls, self.ss, self.rs = ls, ss, rs
        self.here = place()

    def first(self, s, o):
        d, z, c, pair, g, y = self.here
        src, out, by_slice = self.sliced[s]
        if o == 0:
            return pltpu.make_async_copy(
                src.at[2 * y + c] if by_slice else src, out.at[pair, c, z], self.ls.at[s]
            )
        c2, z2 = column_peer(pair, c, z, o)
        y2 = lax.rem(lax.div(z2, 2) + lax.rem(z2, 2), 2)
        return rcopy(
            src.at[2 * y2 + c2] if by_slice else src, out.at[pair, c, z],
            self.ss.at[s, o - 1], self.rs.at[s, o - 1], (2 * pair + c2, z2),
        )

    def second(self, s, o):
        d, z, c, pair, g, y = self.here
        out = self.sliced[s][1] if s < len(self.sliced) else self.w2[1]
        return rcopy(
            out.at[pair], out.at[pair], self.ss.at[s, 7 + o - 1], self.rs.at[s, 7 + o - 1],
            (2 * lax.rem(pair + o, self.np_) + c, z),
        )

    def start(self):
        d, z, c, pair, g, y = self.here
        n = len(self.sliced)
        for s in range(n):
            for o in range(8):
                self.first(s, o).start()
        if self.w2 is not None:
            for o in range(2):
                self.w2_first(o).start()
        if self.wo is not None:
            self.wo_first(lambda cp: cp.start())

    def w2_first(self, o):
        d, z, c, pair, g, y = self.here
        src, out = self.w2
        n = len(self.sliced)
        if o == 0:
            return pltpu.make_async_copy(src, out.at[pair, g], self.ls.at[n])
        return rcopy(src, out.at[pair, g], self.ss.at[n, 0], self.rs.at[n, 0], (d, 3 - z))

    def wo_parts(self):
        d, z, c, pair, g, y = self.here
        per = self.np_ // 4
        owner = lax.div(pair, per)
        return per, owner, lax.rem(owner, 2), lax.div(owner, 2)

    def wo_first(self, do, sending=True):
        d, z, c, pair, g, y = self.here
        src, out = self.wo
        n = len(self.sliced) + 1
        per, owner, c_to, y_to = self.wo_parts()
        slot = out.at[lax.rem(pair, per), c, z]
        for t in range(2):
            z_to = jnp.where(t == 0, y_to, 3 - y_to)
            mine = jnp.logical_and(c == c_to, z == z_to)

            @pl.when(mine)
            def _():
                do(pltpu.make_async_copy(src, slot, self.ls.at[n]))

            @pl.when(jnp.logical_not(mine))
            def _():
                cp = rcopy(
                    src, slot, self.ss.at[n, t], self.rs.at[n, c * 4 + z], (2 * pair + c_to, z_to)
                )
                do(cp)

    def wo_second(self, o):
        d, z, c, pair, g, y = self.here
        per = self.np_ // 4
        out = self.wo[1]
        n = len(self.sliced) + 1
        slot = out.at[lax.rem(pair, per)]
        return rcopy(
            slot, slot, self.ss.at[n, 8 + o - 1], self.rs.at[n, 8 + o - 1],
            (2 * lax.rem(pair + o, self.np_) + c, z),
        )

    def between(self, s):
        self.first(s, 0).wait()
        for o in range(1, 8):
            self.first(s, o).wait_recv()
        for o in range(1, self.np_):
            self.second(s, o).start()

    def between_w2(self):
        n = len(self.sliced)
        self.w2_first(0).wait()
        self.w2_first(1).wait_recv()
        for o in range(1, self.np_):
            self.second(n, o).start()

    def between_wo(self):
        d, z, c, pair, g, y = self.here
        n = len(self.sliced) + 1
        per, owner, c_to, y_to = self.wo_parts()

        @pl.when(owner == 2 * y + c)
        def _():
            for c2 in range(2):
                for z2 in range(4):
                    own = jnp.logical_and(c == c2, z == z2)

                    @pl.when(jnp.logical_not(own))
                    def _():
                        slot = self.wo[1].at[0, c2, z2]
                        rcopy(
                            slot, slot, self.ss.at[n, 0], self.rs.at[n, c2 * 4 + z2], (d + 1 - 2 * c, z)
                        ).wait_recv()
            pltpu.make_async_copy(
                self.wo[0], self.wo[1].at[0, c, z], self.ls.at[n]
            ).wait()
            for o in range(1, self.np_):
                self.wo_second(o).start()

    def finish(self, s):
        for o in range(1, 8):
            self.first(s, o).wait_send()
        for o in range(1, self.np_):
            self.second(s, o).wait()

    def finish_w2(self):
        n = len(self.sliced)
        self.w2_first(1).wait_send()
        for o in range(1, self.np_):
            self.second(n, o).wait()

    def finish_wo(self):
        d, z, c, pair, g, y = self.here
        n = len(self.sliced) + 1
        per, owner, c_to, y_to = self.wo_parts()
        for t in range(2):
            z_to = jnp.where(t == 0, y_to, 3 - y_to)

            @pl.when(jnp.logical_not(jnp.logical_and(c == c_to, z == z_to)))
            def _():
                rcopy(
                    self.wo[0], self.wo[1].at[0, c, z], self.ss.at[n, t], self.rs.at[n, 0], (d + 1 - 2 * c, z)
                ).wait_send()

        @pl.when(owner == 2 * y + c)
        def _():
            for o in range(1, self.np_):
                self.wo_second(o).wait_send()

        for o in range(1, self.np_):
            source = lax.div(lax.rem(pair + self.np_ - o, self.np_), per)

            @pl.when(source == 2 * y + c)
            def _():
                self.wo_second(o).wait_recv()


def decode_tables(np_, r_in, r_ff, part, nh):
    wide = 3 * nh * PAD
    f = np.arange(D)
    by_d = np.zeros((8, D), np.int32)
    by_d[0], by_d[1] = f // r_in, f % r_in
    by_d[2], by_d[3], by_d[4] = f // (2 * r_ff), (f // r_ff) % 2, f % r_ff
    p = np.arange(wide)
    head, lane = p // PAD, p % PAD
    by_q = np.full((8, wide), -1, np.int32)
    for k in range(4):
        at = (head // nh) * D + k * part + (head % nh) * HEAD_DIM + lane
        real = lane < HEAD_DIM
        by_q[k, real] = (at // (3 * r_in))[real]
        by_q[4 + k, real] = (r_in + at % (3 * r_in))[real]
    extra = np.zeros((1, wide), np.float32)
    extra[0, (head < nh) & (lane == HEAD_DIM)] = HEAD_DIM**0.5
    keys = (head >= nh) & (head < 2 * nh)
    extra[0, keys & (lane > HEAD_DIM) & (lane < HEAD_DIM + 4)] = 1.0
    extra[0, (head >= 2 * nh) & (lane >= HEAD_DIM) & (lane < HEAD_DIM + 3)] = 1.0
    return jnp.asarray(by_d), jnp.asarray(by_q), jnp.asarray(extra)


def decode(np_, r_in, r_ff, vec, by_d, by_q, extra, tab, b_pad, length):
    d, z, c, pair, g, y = place()
    world = 8 * np_
    packed = vec[...].reshape(world * 16, PAD)
    m = lax.broadcasted_iota(jnp.int32, (world, world * 16), 1)
    n = lax.broadcasted_iota(jnp.int32, (world, world * 16), 0)
    row = [
        dot(jnp.where(m == 16 * n + r, 1.0, 0.0).astype(bf16), packed).astype(bf16)
        for r in range(3)
    ]

    def pick(x, lanes, owner):
        w = lanes.shape[1]
        hot = lax.broadcasted_iota(jnp.int32, (PAD, w), 0) == lanes
        got = dot(x, jnp.where(hot, 1.0, 0.0).astype(bf16))
        mine = lax.broadcasted_iota(jnp.int32, (world, w), 0) == owner
        return jnp.sum(jnp.where(mine, got, 0.0), axis=0, keepdims=True)

    owner, lanes = by_d[0:1], by_d[1:2]
    tab[0:1] = pick(row[0], lanes, owner)
    tab[1:2] = pick(row[0], lanes + r_in, owner)
    tab[2:3] = pick(row[0], lanes + 2 * r_in, owner) + pick(row[1], lanes, owner)
    tab[3:4] = pick(row[0], lanes + 3 * r_in, owner)
    tab[4:5] = pick(row[0], lanes + 4 * r_in, owner)
    owner = by_d[2:3] * 8 + c * 4 + jnp.where(by_d[3:4] == 0, y, 3 - y)
    tab[5:6] = pick(row[2], by_d[4:5], owner)
    tab[6:8] = jnp.zeros((2, D), f32)
    k = 2 * y + c
    b_pad[...] = pick(row[1], by_q[pl.ds(4 + k, 1)], by_q[pl.ds(k, 1)]) + extra[...]
    mine = lax.broadcasted_iota(jnp.int32, (world, PAD), 0) == (2 * pair + g) * 4
    parts = jnp.sum(jnp.where(mine, row[2].astype(f32), 0.0), axis=0, keepdims=True)
    lane = lax.broadcasted_iota(jnp.int32, (1, PAD), 1)
    parts = jnp.where(lane == r_ff, parts * 256.0, jnp.where(lane == r_ff + 1, parts, 0.0))
    length[...] = jnp.broadcast_to(jnp.sum(parts, axis=1, keepdims=True), (1, PAD))


def gather_kernel(
    np_, r_in, r_ff, x, wq, w1, vec_own, by_d, by_q, extra,
    xg, wqg, w1g, tab, b_pad, length, vec, ls_x, ss_x, rs_x, ls_w, ss_w, rs_w,
):
    d, z, c, pair, g, y = place()
    barrier_all(np_, d, z, c, pair)
    spread = Spread(x, xg, ls_x, ss_x, rs_x)
    weights = Weights(
        np_, [(vec_own, vec, False), (wq, wqg, True), (w1, w1g, True)], None, None,
        ls_w, ss_w, rs_w,
    )
    weights.start()
    spread.start()
    for s in range(3):
        weights.between(s)
    spread.forward(0)
    weights.finish(0)
    decode(np_, r_in, r_ff, vec, by_d, by_q, extra, tab, b_pad, length)
    spread.forward(1)
    spread.finish()
    for s in range(1, 3):
        weights.finish(s)


def spread_sems():
    return [
        pltpu.SemaphoreType.DMA,
        pltpu.SemaphoreType.DMA((2, 4, CHUNKS)),
        pltpu.SemaphoreType.DMA((4, CHUNKS)),
    ]


def gather(np_, r_in, r_ff, nh, x, wq, w1, vec, collective_id=1):
    any_ = pl.BlockSpec(memory_space=pl.ANY)
    vmem = pl.BlockSpec(memory_space=pltpu.VMEM)
    wide = 3 * nh * PAD
    return pl.pallas_call(
        functools.partial(gather_kernel, np_, r_in, r_ff),
        out_shape=(
            sds((4,) + x.shape, bf16), sds((np_, 2, 4) + wq.shape[1:], bf16),
            sds((np_, 2, 4) + w1.shape[1:], bf16),
            sds((8, D), f32), sds((1, wide), f32), sds((1, PAD), f32),
        ),
        in_specs=[any_] * 4 + [vmem] * 3,
        out_specs=(any_,) * 3 + (vmem,) * 3,
        scratch_shapes=[pltpu.VMEM((np_, 2, 4, 16, PAD), bf16)] + spread_sems()
        + weight_sems(np_, 3),
        compiler_params=pltpu.CompilerParams(
            collective_id=collective_id, has_side_effects=True, vmem_limit_bytes=VMEM_BYTES
        ),
        name="gather",
    )(x, wq, w1, vec, *decode_tables(np_, r_in, r_ff, wq.shape[2] // 3, nh))


PIECES = 4


class Reduce:
    def __init__(self, part, out, extra, bufs, ls, ss, rs):
        self.part, self.out, self.extra = part, out, extra
        self.from_sib, self.from_far, self.to_far, self.mine, self.done = bufs
        self.ls, self.ss, self.rs = ls, ss, rs
        d, z, c, pair, g, y = place()
        self.role = jnp.where(c == g, 0, 1)
        self.y = y
        self.sib = (d + 1 - 2 * c, z)
        self.partner = (d, z + 1 - 2 * lax.rem(z, 2))
        self.q_here = mirror(2 * y + self.role, g)
        self.q_there = mirror(2 * (1 - y) + self.role, g)
        self.sib_here = mirror(2 * y + 1 - self.role, g)
        self.sib_there = mirror(2 * (1 - y) + 1 - self.role, g)
        self.owner = (2 * pair + g, self.q_here)
        self.self_owner = jnp.logical_and(self.role == 0, y == 0)
        self.self_source = jnp.where(c == 0, z, 3 - z) == 0
        self.rows = self.out.shape[0] // PIECES

    def rows_of(self, j):
        return pl.ds(j * self.rows, self.rows)

    def to_sib(self, t, j):
        q = self.sib_there if t == 0 else self.sib_here
        r = self.rows_of(j)
        return rcopy(
            self.part.at[q, r], self.from_sib.at[t, r], self.ss.at[t, j], self.rs.at[t, j], self.sib
        )

    def load(self, t):
        q = self.q_there if t == 0 else self.q_here
        return pltpu.make_async_copy(self.part.at[q], self.mine.at[t], self.ls.at[t])

    def load_extra(self, e):
        src, dst = self.extra[e]
        return pltpu.make_async_copy(src.at[self.q_here], dst, self.ls.at[2 + e])

    def across(self, j):
        r = self.rows_of(j)
        return rcopy(
            self.to_far.at[r], self.from_far.at[r], self.ss.at[2, j], self.rs.at[2, j], self.partner
        )

    def home(self, j):
        r = self.rows_of(j)
        return rcopy(
            self.done.at[r], self.out.at[r], self.ss.at[3, j], self.rs.at[3, j], self.owner
        )

    def keep(self):
        return pltpu.make_async_copy(self.done, self.out, self.ls.at[4])

    def start(self):
        for t in range(2):
            for j in range(PIECES):
                self.to_sib(t, j).start()
        for t in range(2):
            self.load(t).start()
        for e in range(len(self.extra)):
            self.load_extra(e).start()

    def add_near(self):
        self.load(0).wait()
        for j in range(PIECES):
            r = self.rows_of(j)
            self.to_sib(0, j).wait_recv()
            total = self.mine[0, r].astype(f32) + self.from_sib[0, r].astype(f32)
            self.to_far[r] = total.astype(bf16)
            self.across(j).start()
        self.load(1).wait()
        for e in range(len(self.extra)):
            self.load_extra(e).wait()

    def add_far(self, finish):
        for j in range(PIECES):
            r = self.rows_of(j)
            self.to_sib(1, j).wait_recv()
            self.across(j).wait_recv()
            total = self.mine[1, r].astype(f32) + self.from_sib[1, r].astype(f32)
            total = total + self.from_far[r].astype(f32)
            self.done[r] = finish(total, r).astype(bf16)

            @pl.when(jnp.logical_not(self.self_owner))
            def _():
                self.home(j).start()

    def finish(self):
        @pl.when(self.self_owner)
        def _():
            self.keep().start()
            self.keep().wait()

        for j in range(PIECES):
            @pl.when(jnp.logical_not(self.self_source))
            def _():
                self.home(j).wait_recv()

        for j in range(PIECES):
            self.to_sib(0, j).wait_send()
            self.to_sib(1, j).wait_send()
            self.across(j).wait_send()

            @pl.when(jnp.logical_not(self.self_owner))
            def _():
                self.home(j).wait_send()


def reduce_scratch(rows, extras):
    return [
        pltpu.VMEM((2, rows, D), bf16), pltpu.VMEM((rows, D), bf16), pltpu.VMEM((rows, D), bf16),
        pltpu.VMEM((2, rows, D), bf16), pltpu.VMEM((rows, D), bf16),
    ] + [pltpu.VMEM((rows, D), bf16)] * extras + [
        pltpu.SemaphoreType.DMA((5,)),
        pltpu.SemaphoreType.DMA((4, PIECES)),
        pltpu.SemaphoreType.DMA((4, PIECES)),
    ]


class ReduceQuarters(Reduce):
    def __init__(self, part, out, bufs, ls, ss, rs):
        from_sib, from_far, to_far, done = bufs
        super().__init__(part, out, [], (from_sib, from_far, to_far, None, done), ls, ss, rs)

    def ready(self, q):
        for t, mine in ((0, self.sib_there), (1, self.sib_here)):
            @pl.when(mine == q)
            def _():
                for j in range(PIECES):
                    self.to_sib(t, j).start()

    def push(self, q):
        @pl.when(self.q_there == q)
        def _():
            for j in range(PIECES):
                r = self.rows_of(j)
                self.to_sib(0, j).wait_recv()
                total = self.part[q, r].astype(f32) + self.from_sib[0, r].astype(f32)
                self.to_far[r] = total.astype(bf16)
                self.across(j).start()

    def pull(self, q, finish):
        @pl.when(self.q_here == q)
        def _():
            for j in range(PIECES):
                r = self.rows_of(j)
                self.to_sib(1, j).wait_recv()
                self.across(j).wait_recv()
                total = self.part[q, r].astype(f32) + self.from_sib[1, r].astype(f32)
                total = total + self.from_far[r].astype(f32)
                self.done[r] = finish(total, r).astype(bf16)

                @pl.when(jnp.logical_not(self.self_owner))
                def _():
                    self.home(j).start()


class Swap:
    def __init__(self, np_, arrays, wo, ls, ss, rs):
        self.np_, self.arrays, self.wo, self.ls, self.ss, self.rs = np_, arrays, wo, ls, ss, rs
        self.here = place()

    def copy(self, s, o):
        d, z, c, pair, g, y = self.here
        src, dst = self.arrays[s]
        to = lax.rem(pair + o, self.np_)
        if o == 0:
            return pltpu.make_async_copy(src.at[pair], dst.at[pair], self.ls.at[s])
        return rcopy(
            src.at[to], dst.at[pair], self.ss.at[s, o], self.rs.at[s, o], (2 * to + c, z)
        )

    def copy_wo(self, o):
        d, z, c, pair, g, y = self.here
        src, dst = self.wo
        n = len(self.arrays)
        per = self.np_ // 4
        to = lax.rem(pair + o, self.np_)
        if o == 0:
            return pltpu.make_async_copy(src.at[lax.rem(pair, per)], dst.at[pair], self.ls.at[n])
        return rcopy(
            src.at[lax.rem(to, per)], dst.at[pair], self.ss.at[n, o], self.rs.at[n, o],
            (2 * to + c, z),
        )

    def collects(self, pair2):
        d, z, c, pair, g, y = self.here
        return lax.div(pair2, self.np_ // 4) == 2 * y + c

    def start(self):
        d, z, c, pair, g, y = self.here
        for s in range(len(self.arrays)):
            for o in range(1, self.np_):
                self.copy(s, o).start()
            self.copy(s, 0).start()
        if self.wo is not None:
            for o in range(self.np_):
                @pl.when(self.collects(lax.rem(pair + o, self.np_)))
                def _():
                    self.copy_wo(o).start()

    def finish(self):
        d, z, c, pair, g, y = self.here
        for s in range(len(self.arrays)):
            for o in range(self.np_):
                self.copy(s, o).wait()
        if self.wo is not None:
            for o in range(self.np_):
                @pl.when(self.collects(lax.rem(pair + o, self.np_)))
                def _():
                    if o == 0:
                        self.copy_wo(o).wait()
                    else:
                        self.copy_wo(o).wait_send()

                if o > 0:
                    @pl.when(self.collects(pair))
                    def _():
                        self.copy_wo(o).wait_recv()


def group_peer(o):
    d, z, c, pair, g, y = place()
    c2 = 1 - c if o % 2 else c
    z2 = z + 1 - 2 * lax.rem(z, 2) if o // 2 else z
    return 2 * pair + c2, z2


class Group:
    def __init__(self, own, all_, ls, ss, rs):
        self.own, self.all_, self.ls, self.ss, self.rs = own, all_, ls, ss, rs
        d, z, c, pair, g, y = place()
        self.k = 2 * y + c

    def copy(self, o):
        if o == 0:
            return pltpu.make_async_copy(self.own, self.all_.at[self.k], self.ls)
        return rcopy(
            self.own, self.all_.at[self.k], self.ss.at[o - 1], self.rs.at[o - 1], group_peer(o)
        )

    def start(self):
        for o in range(4):
            self.copy(o).start()

    def finish(self):
        for o in range(4):
            self.copy(o).wait()


def norm_back(total, x, dy):
    xhat, inverse = norm_parts(x.astype(f32))
    back = inverse * (
        total
        - jnp.mean(total, axis=-1, keepdims=True)
        - xhat * jnp.mean(total * xhat, axis=-1, keepdims=True)
    )
    return dy.astype(f32) + back


def same_slice_peer(np_, e):
    d, z, c, pair, g, y = place()
    to = lax.rem(pair * 2 + g + e, 2 * np_)
    pair2, g2 = lax.div(to, 2), lax.rem(to, 2)
    return to, (2 * pair2 + c, jnp.where(g2 == g, z, 3 - z))


def one_hot_tables(np_, r_in, r_ff, part):
    f = np.arange(D)
    lane = np.arange(PAD)
    place_qkv = (f // part) * D + f % part
    tables_ = [f % r_in, f % r_ff] + [(place_qkv + k * part) % (3 * r_in) for k in range(4)]
    hot = np.stack([(t[:, None] == lane[None, :]) for t in tables_]).astype(np.float32)
    hot[2:, 3 * part :] = 0.0
    return jnp.asarray(hot, bf16), jnp.asarray(place_qkv[None], jnp.int32)


def pieces_of(np_, sums_all, sums, hot_ref, qkv_at, r_in, r_ff, part, msg):
    d, z, c, pair, g, y = place()
    n = 2 * np_
    e = lax.broadcasted_iota(jnp.int32, (n, D), 0)
    f = lax.broadcasted_iota(jnp.int32, (n, D), 1)
    group = lax.rem(e, 2)
    index = (lax.div(e, 2) * 2 + c) * 4 + jnp.where(group == 0, y, 3 - y)

    def select(rows_, inside, hot):
        picked = []
        for row in rows_:
            for v in split3(row):
                picked.append(jnp.where(inside, v, 0.0))
        got = dot(jnp.concatenate(picked, axis=0).astype(bf16), hot)
        return [
            got[3 * s * n : (3 * s + 1) * n] + got[(3 * s + 1) * n : (3 * s + 2) * n]
            + got[(3 * s + 2) * n : (3 * s + 3) * n]
            for s in range(len(rows_))
        ]

    d_vecs = sums_all[0, 0:4] + sums_all[1, 0:4] + sums_all[2, 0:4] + sums_all[3, 0:4]
    rows_ = [d_vecs[s : s + 1] for s in range(4)] + [sums[6:7]]
    inside = jnp.logical_and(f >= index * r_in, f < (index + 1) * r_in)
    got = select(rows_, inside, hot_ref[0])
    first = got[0]
    for s in range(1, 5):
        first = first + pltpu.roll(got[s], s * r_in, 1)
    second = jnp.zeros((n, PAD), f32)
    for k in range(4):
        at = qkv_at[...] + k * part
        inside = jnp.logical_and(at >= index * (3 * r_in), at < (index + 1) * (3 * r_in))
        second = second + select([sums_all[k, 5:6]], inside, hot_ref[2 + k])[0]
    inside = jnp.logical_and(f >= e * r_ff, f < (e + 1) * r_ff)
    third = select([sums[4:5]], inside, hot_ref[1])[0]
    squares = squares_of(d_vecs) + 2.0 * squares_of(sums[6:7])
    for k in range(4):
        squares = squares + squares_of(sums_all[k, 4:6]) + sums_all[k, 7:8, 0:1]
    for s in range(n):
        msg[s, 0:1] = first[s : s + 1]
        msg[s, 1:2] = second[s : s + 1]
        msg[s, 2:3] = third[s : s + 1]
        msg[s, 3:4] = jnp.broadcast_to(squares, (1, PAD))
        msg[s, 4:8] = jnp.zeros((4, PAD), f32)


def meet(np_):
    d, z, c, pair, g, y = place()
    bar = pltpu.get_barrier_semaphore()
    for o in range(1, 8):
        c2, z2 = column_peer(pair, c, z, o)
        pl.semaphore_signal(bar, inc=1, device_id=(2 * pair + c2, z2), device_id_type=MESH)
    for e in range(1, 2 * np_):
        unused, peer = same_slice_peer(np_, e)
        pl.semaphore_signal(bar, inc=1, device_id=peer, device_id_type=MESH)
    pl.semaphore_wait(bar, 7 + 2 * np_ - 1)


def finish_all(
    np_, r_in, r_ff, part_w, red_out, red, swap1, back,
    dw, dwo, sums, hot_ref, qkv_at, t1, tq, t2, to, pieces,
    ls_w, ss_w, rs_w, sums_all, ls_g, ss_g, rs_g,
    b1, bq, b2, bo, s1, sq, s2, so, msg, m_all, p_out, ls, ss_m, rs_m, ss, rs,
):
    d, z, c, pair, g, y = place()
    grp = Group(sums, sums_all, ls_g, ss_g, rs_g)
    swap = Swap(np_, [(dw, bq)], (dwo, bo), ls_w, ss_w, rs_w)
    grp.start()
    swap.start()
    red.pull(3, back)
    grp.finish()
    pieces_of(np_, sums_all, sums, hot_ref, qkv_at, r_in, r_ff, part_w, msg)
    me = pair * 2 + g

    def tell(e):
        to_, peer = same_slice_peer(np_, e)
        return rcopy(msg.at[to_], m_all.at[me], ss_m.at[e], rs_m.at[e], peer)

    own = pltpu.make_async_copy(msg.at[me], m_all.at[me], ls.at[0])
    own.start()
    for e in range(1, 2 * np_):
        tell(e).start()
    red.pull(2, back)
    red.pull(1, back)
    own.wait()
    for e in range(1, 2 * np_):
        tell(e).wait()
    norms = [jnp.sqrt(m_all[e, 3:4, 0:1]) for e in range(2 * np_)]
    mean_norm = sum(norms) / (2 * np_)
    factors = [mean_norm / jnp.maximum(n, mean_norm) for n in norms]
    p_out[...] = sum(f * m_all[e] for e, f in enumerate(factors))
    p_out[4:5, 0:1] = sum(jnp.where(d == e, n, 0.0) for e, n in enumerate(norms))
    group_factors = [
        jnp.where(g == 0, factors[2 * n], factors[2 * n + 1]) for n in range(np_)
    ]
    final = pltpu.make_async_copy(p_out, pieces, ls.at[9])
    final.start()
    collects = swap.collects(pair)
    swap1.finish()

    def rows_to(s, src, dst, o, slot):
        c2, z2 = column_peer(pair, c, z, o)
        if o == 0:
            return pltpu.make_async_copy(src.at[c2, z2], dst.at[slot], ls.at[5 + s])
        return rcopy(
            src.at[c2, z2], dst.at[slot], ss.at[s, o], rs.at[s, o], (2 * pair + c2, z2)
        )

    def scaled(n, buf, acc, dst):
        for c2 in range(2):
            for z2 in range(4):
                at = pl.ds((c2 * 4 + z2) * r_in, r_in)
                total = sum(f * buf[m, at].astype(f32) for m, f in enumerate(group_factors))
                acc[c2, z2] = total.astype(acc.dtype)
        for o in range(8):
            rows_to(n, acc, dst, o, c * 4 + z).start()

    for t in range(2):
        at = pl.ds(t * r_ff, r_ff)
        total = sum(f * b2[m, at].astype(f32) for m, f in enumerate(group_factors))
        s2[t] = total.astype(s2.dtype)
    mirror_copy = rcopy(s2.at[1 - g], t2.at[1], ss.at[2, 0], rs.at[2, 0], (d, 3 - z))
    mirror_copy.start()
    kept = pltpu.make_async_copy(s2.at[g], t2.at[0], ls.at[7])
    kept.start()
    scaled(1, b1, s1, t1)
    swap.finish()
    scaled(0, bq, sq, tq)

    def wo_to(o):
        c2, z2 = column_peer(pair, c, z, o)
        if o == 0:
            return pltpu.make_async_copy(so.at[c2, z2], to.at[g], ls.at[8])
        return rcopy(
            so.at[c2, z2], to.at[g], ss.at[3, o], rs.at[3, g], (2 * pair + c2, z2)
        )

    @pl.when(collects)
    def _():
        for c2 in range(2):
            for z2 in range(4):
                at = pl.ds((c2 * 4 + z2) * r_in, r_in)
                total = sum(f * bo[m, at].astype(f32) for m, f in enumerate(group_factors))
                so[c2, z2] = total.astype(so.dtype)
        for o in range(8):
            wo_to(o).start()

    red.pull(0, back)
    for n, (acc, dst) in enumerate(((sq, tq), (s1, t1))):
        for o in range(8):
            rows_to(n, acc, dst, o, c * 4 + z).wait()
    mirror_copy.wait()
    kept.wait()

    @pl.when(collects)
    def _():
        wo_to(0).wait()
        for o in range(1, 8):
            wo_to(o).wait_send()

    for t in range(2):
        @pl.when(jnp.logical_or(jnp.logical_not(collects), g != t))
        def _():
            rcopy(so.at[0, 0], to.at[t], ss.at[3, 0], rs.at[3, t], (d, 3 - z)).wait_recv()

    final.wait()
    red_out.finish()
    red.finish()


def local(
    block_in, out_grad, lengths, ln1_gain, ln1_bias, qkv_weight, qkv_bias, out_weight, out_bias,
    ln2_gain, ln2_bias, fc1_weight, fc1_bias, fc2_weight, fc2_bias,
):
    tp = lax.axis_size("ctx")
    dp = lax.axis_size("dp")
    np_ = dp // 2
    world = dp * tp
    d, z, c, pair, g, y = place()
    nh = HEADS // tp
    local_rows = block_in.shape[1]
    t = local_rows * tp
    rows = min(512, local_rows)
    part = D // tp
    r_in = D // world
    r_ff = fc2_weight.shape[0]
    ff = r_ff * dp

    x_own = block_in[0]
    pos = z * local_rows + jnp.arange(local_rows, dtype=jnp.int32)
    dy_own = jnp.where((pos < lengths[0])[:, None], out_grad[0], jnp.zeros((), bf16))

    w_qkv = jnp.moveaxis(qkv_weight.reshape(r_in, 3, tp, part), 2, 0).reshape(tp, r_in, 3 * part)
    w1 = fc1_weight.reshape(r_in, np_, 2, tp, r_ff)
    w1 = jnp.stack([w1[:, :, :, s] for s in (0, 3, 1, 2)], axis=3)
    w1 = w1.reshape(r_in, np_, 2, 2, 2, r_ff).transpose(3, 2, 0, 1, 4, 5).reshape(tp, r_in, ff)
    length_parts = jnp.stack([lengths[0] // 256, lengths[0] % 256]).astype(bf16)
    packed, at = jnp.zeros((16 * PAD,), bf16), 0
    for row_of in (
        (ln1_gain, ln1_bias, out_bias, ln2_gain, ln2_bias), (fc2_bias, qkv_bias),
        (fc1_bias, length_parts),
    ):
        start = at
        for one in row_of:
            packed = packed + jnp.pad(one, (start, 16 * PAD - start - one.shape[0]))
            start += one.shape[0]
        at += PAD
    xq, w_qkv, w1, tab, b_pad, length = gather(
        np_, r_in, r_ff, nh, x_own, w_qkv, w1, packed.reshape(16, PAD)
    )
    x = xq.reshape(t, D)
    w_qkv, w1 = w_qkv.reshape(D, 3 * part), w1.reshape(D, ff)
    cosine, sine = tables(t)
    q, k, v, cf, ctx, dyq, w2, wo = attn_fwd(
        np_, length, x, tab, w_qkv, b_pad, cosine, sine, dy_own, fc2_weight, out_weight, nh, rows
    )
    dy = dyq.reshape(t, D)
    w2, wo = w2.reshape(ff, D), wo.reshape(part, D)
    out_part, u_mlp, dw1, dw2, vec = mlp(x, dy, ctx, tab, wo, w1, w2, rows // 2)
    block_out, input_grad, t1, tq, t2, to, mine = attn_bwd(
        np_, r_in, r_ff, x, dy, cf, ctx, u_mlp, q, k, v, tab, w_qkv, wo, cosine, sine, vec,
        out_part.reshape(4, local_rows, D), xq, dyq, dw1.reshape(np_, D // np_, ff),
        dw2.reshape(np_, 2 * r_ff, D), rows,
    )
    t1 = t1.reshape(2, tp, r_in, ff).astype(f32)
    t1 = jnp.stack([t1[:, 0] + t1[:, 3], t1[:, 1] + t1[:, 2]], axis=1)
    t1 = t1.reshape(2, 2, r_in, np_, 2, r_ff)
    t1 = jnp.stack([t1[:, s, :, :, e] for s, e in ((0, 0), (1, 0), (1, 1), (0, 1))], axis=0)
    g_fc1 = t1.transpose(2, 3, 1, 0, 4).reshape(r_in, ff * tp)
    tq = tq.reshape(2, tp, r_in, 3, part).astype(f32)
    tq = jnp.stack([tq[:, 0] + tq[:, 3], tq[:, 1] + tq[:, 2]], axis=0)
    g_qkv = tq.reshape(tp, r_in, 3, part).transpose(1, 2, 0, 3).reshape(r_in, 3 * D)
    g_fc2 = jnp.sum(t2.astype(f32), axis=0)
    g_out = jnp.sum(to.astype(f32), axis=0)
    cut = [mine[0, s * r_in : (s + 1) * r_in] for s in range(5)]
    return (
        block_out[None], input_grad[None],
        cut[0], cut[1], g_qkv, mine[1, : 3 * r_in], g_out, cut[4],
        cut[2], cut[3], g_fc1, mine[2, :r_ff], g_fc2, cut[4],
        mine[4, :1],
    )


def solution(mesh):
    both = ("dp", "ctx")
    vec, mat, act = P(both), P(both, None), P("dp", "ctx", None)
    weights = (vec, vec, mat, vec, mat, vec, vec, vec, mat, vec, mat, vec)
    return jax.shard_map(
        local,
        mesh=mesh,
        in_specs=(act, act, P("dp")) + weights,
        out_specs=(act, act) + weights + (P("dp"),),
        check_vma=False,
    )
```

```python
import functools
import math

import jax
import jax.numpy as jnp
import numpy as np
from jax import lax
from jax.experimental import pallas as pl
from jax.experimental.pallas import tpu as pltpu
from jax.sharding import PartitionSpec as P

D = 768
HEADS = 12
HEAD_DIM = 64
ROT = 16
PAD = 128
eps_norm = 1e-05
neg_big = -1e30
root_half = math.sqrt(0.5)
inv_root_two_pi = 1.0 / math.sqrt(2.0 * math.pi)
f32 = jnp.float32
bf16 = jnp.bfloat16
VMEM_BYTES = 60 * 2**20


def dot(a, b, dims=((1,), (0,))):
    return lax.dot_general(a, b, (dims, ((), ())), preferred_element_type=f32)


def norm_parts(values):
    centered = values - jnp.mean(values, axis=-1, keepdims=True)
    row_var = jnp.mean(centered * centered, axis=-1, keepdims=True)
    inverse = lax.rsqrt(row_var + eps_norm)
    return centered * inverse, inverse


def turn(u, cosine, sine, first):
    partner = jnp.where(first, pltpu.roll(u, PAD - ROT // 2, 1), pltpu.roll(u, ROT // 2, 1))
    return u * cosine + partner * sine


def split3(v):
    hi = v.astype(bf16).astype(f32)
    mid = (v - hi).astype(bf16).astype(f32)
    low = (v - hi - mid).astype(bf16).astype(f32)
    return hi, mid, low


def fold(op, s):
    out = s[:, :PAD]
    for t in range(1, s.shape[1] // PAD):
        out = op(out, s[:, t * PAD : (t + 1) * PAD])
    return out


def attn_fwd_kernel(
    np_, len_ref, x_ref, tab_ref, w_ref, wb_ref, cos_ref, sin_ref, dy, w2, wo,
    q_ref, k_ref, v_ref, cf_ref, c_ref, dyg, w2g, wog,
    w_scr, s_scr, q_scr, m_scr, l_scr, acc_scr, ls_dy, ss_dy, rs_dy, ls_w, ss_w, rs_w,
):
    i = pl.program_id(0)
    nh = k_ref.shape[0]
    rows = x_ref.shape[0]
    spread = Spread(dy, dyg, ls_dy, ss_dy, rs_dy)
    weights = Rows(np_, (w2, w2g), (wo, wog), ls_w, ss_w, rs_w)

    @pl.when(i == 0)
    def _():
        d, z, c, pair, g, y = place()
        barrier_all(np_, d, z, c, pair)
        weights.start()
        spread.start()

    @pl.when(i == 2)
    def _():
        spread.forward(1)

    @pl.when(i == 3)
    def _():
        spread.forward(3)

    @pl.when(i == 0)
    def _():
        for h in range(3 * nh):
            w_scr[:, h * PAD : h * PAD + HEAD_DIM] = w_ref[:, h * HEAD_DIM : (h + 1) * HEAD_DIM]
            w_scr[:, h * PAD + HEAD_DIM : (h + 1) * PAD] = jnp.zeros((D, PAD - HEAD_DIM), bf16)

    xhat, unused = norm_parts(x_ref[...].astype(f32))
    a1 = (xhat * tab_ref[0:1] + tab_ref[1:2]).astype(bf16)
    cosine, sine = cos_ref[...], sin_ref[...]
    lane = lax.broadcasted_iota(jnp.int32, (rows, PAD), 1)
    first = lane < ROT // 2
    key_pos = i * rows + lax.broadcasted_iota(jnp.int32, (rows, PAD), 0)
    key_bias = jnp.where(key_pos.astype(f32) < len_ref[...], 0.0, neg_big)
    here = pl.ds(pl.multiple_of(i * rows, rows), rows)
    qkv = dot(a1, w_scr[...]) + wb_ref[...]
    for h in range(nh):
        q = turn(qkv[:, h * PAD : (h + 1) * PAD], cosine, sine, first) * HEAD_DIM**-0.5
        q_scr[h] = q.astype(bf16)
        k = turn(qkv[:, (nh + h) * PAD : (nh + h + 1) * PAD], cosine, sine, first)
        k_ref[h, here] = jnp.where(lane == HEAD_DIM, key_bias, k).astype(bf16)
        v_ref[h, here] = qkv[:, (2 * nh + h) * PAD : (2 * nh + h + 1) * PAD].astype(bf16)

    causal = lax.broadcasted_iota(jnp.int32, (rows, rows), 0) >= lax.broadcasted_iota(
        jnp.int32, (rows, rows), 1
    )
    for h in range(nh):
        s = dot(q_scr[h], k_ref[h, here], ((1,), (1,)))
        s = jnp.where(causal, s, neg_big)
        s_scr[h, i] = s
        m_scr[h] = fold(jnp.maximum, s)

    def scores(j, carry):
        there = pl.ds(pl.multiple_of(j * rows, rows), rows)
        for h in range(nh):
            s = dot(q_scr[h], k_ref[h, there], ((1,), (1,)))
            s_scr[h, j] = s
            m_scr[h] = jnp.maximum(m_scr[h], fold(jnp.maximum, s))
        return carry

    lax.fori_loop(0, i, scores, 0)

    @pl.when(i == 1)
    def _():
        spread.forward(0)

    @pl.when(i == 2)
    def _():
        spread.forward(2)

    for h in range(nh):
        m_scr[h] = jnp.broadcast_to(jnp.max(m_scr[h], axis=-1, keepdims=True), (rows, PAD))
        l_scr[h] = jnp.zeros((rows, PAD), f32)
        acc_scr[h] = jnp.zeros((rows, PAD), f32)

    def weigh(j, carry):
        there = pl.ds(pl.multiple_of(j * rows, rows), rows)
        for h in range(nh):
            p = jnp.exp(s_scr[h, j] - m_scr[h][:, :1])
            l_scr[h] += fold(jnp.add, p)
            acc_scr[h] += dot(p.astype(bf16), v_ref[h, there])
        return carry

    lax.fori_loop(0, i + 1, weigh, 0)
    for h in range(nh):
        total = jnp.sum(l_scr[h], axis=-1, keepdims=True)
        context = acc_scr[h] / total
        cf_ref[:, h * PAD : (h + 1) * PAD] = context
        c_ref[:, h * HEAD_DIM : (h + 1) * HEAD_DIM] = context[:, :HEAD_DIM].astype(bf16)
        hi, mid, low = split3(-(m_scr[h][:, :1] + jnp.log(total)))
        q = q_scr[h].astype(f32)
        q = jnp.where(lane == HEAD_DIM + 1, hi, q)
        q = jnp.where(lane == HEAD_DIM + 2, mid, q)
        q = jnp.where(lane == HEAD_DIM + 3, low, q)
        q_ref[h] = q.astype(bf16)

    @pl.when(i == pl.num_programs(0) - 1)
    def _():
        spread.finish()
        weights.finish()


def squares_of(m):
    return jnp.sum(jnp.sum(m * m, axis=0, keepdims=True), axis=1, keepdims=True)


def mlp_kernel(
    x_ref, dy_ref, c_ref, cf_ref, tab_ref, wo_ref, w1_ref, w2_ref,
    part_ref, u_ref, dc_ref, dw1_ref, dw2_ref, dwo_ref, vec_ref,
    dw1_scr, dw2_scr, dwo_scr, wo_scr,
):
    i = pl.program_id(0)
    nh = wo_ref.shape[0] // HEAD_DIM
    rows = x_ref.shape[0]

    @pl.when(i == 0)
    def _():
        dw1_scr[...] = jnp.zeros_like(dw1_scr)
        dw2_scr[...] = jnp.zeros_like(dw2_scr)
        dwo_scr[...] = jnp.zeros_like(dwo_scr)
        vec_ref[...] = jnp.zeros_like(vec_ref)
        for h in range(nh):
            wo_scr[h * PAD : h * PAD + HEAD_DIM] = wo_ref[h * HEAD_DIM : (h + 1) * HEAD_DIM]
            wo_scr[h * PAD + HEAD_DIM : (h + 1) * PAD] = jnp.zeros((PAD - HEAD_DIM, D), bf16)

    xhat, unused = norm_parts(x_ref[...].astype(f32))
    gain = tab_ref[3:4]
    a2 = (xhat * gain + tab_ref[4:5]).astype(bf16)
    z = dot(a2, w1_ref[...]) + tab_ref[5:6]
    cdf = 0.5 * (1.0 + lax.erf(z * root_half))
    hidden = (z * cdf).astype(bf16)
    context = c_ref[...]
    part = dot(hidden, w2_ref[...]) + dot(context, wo_ref[...])
    part_ref[...] = part.astype(part_ref.dtype)
    dy = dy_ref[...]
    slope = cdf + z * jnp.exp(-0.5 * z * z) * inv_root_two_pi
    dz = (dot(dy, w2_ref[...], ((1,), (1,))) * slope).astype(bf16)

    da2 = dot(dz, w1_ref[...], ((1,), (1,)))
    u_ref[...] = (da2 * gain).astype(u_ref.dtype)
    lane = lax.broadcasted_iota(jnp.int32, (rows, PAD), 1)
    dc_all = dot(dy, wo_scr[...], ((1,), (1,))).astype(bf16)
    for h in range(nh):
        dc = dc_all[:, h * PAD : (h + 1) * PAD].astype(f32)
        delta = jnp.sum(dc * cf_ref[:, h * PAD : (h + 1) * PAD], axis=-1, keepdims=True)
        hi, mid, low = split3(-delta)
        dc = jnp.where(lane == HEAD_DIM, hi, dc)
        dc = jnp.where(lane == HEAD_DIM + 1, mid, dc)
        dc = jnp.where(lane == HEAD_DIM + 2, low, dc)
        dc_ref[h] = dc.astype(bf16)
    dw1_scr[...] += dot(a2, dz, ((0,), (0,)))
    dw2_scr[...] += dot(hidden, dy, ((0,), (0,)))
    dwo_scr[...] += dot(context, dy, ((0,), (0,)))
    vec_ref[2:3] += jnp.sum(da2 * xhat, axis=0, keepdims=True)
    vec_ref[3:4] += jnp.sum(da2, axis=0, keepdims=True)
    vec_ref[4:5] += jnp.sum(dz.astype(f32), axis=0, keepdims=True)
    vec_ref[6:7] += jnp.sum(dy.astype(f32), axis=0, keepdims=True)

    @pl.when(i == pl.num_programs(0) - 1)
    def _():
        dw1_ref[...] = dw1_scr[...].astype(bf16)
        dw2_ref[...] = dw2_scr[...].astype(bf16)
        dwo_ref[...] = dwo_scr[...].astype(bf16)
        vec_ref[7:8, 0:1] = (
            squares_of(dw1_scr[...]) + squares_of(dw2_scr[...]) + squares_of(dwo_scr[...])
        )


def attn_bwd_kernel(
    np_, r_in, r_ff, x_ref, u_in_ref, q_ref, k_ref, v_ref, dc_ref, tab_ref, w_ref,
    cos_ref, sin_ref, vec_in_ref, hot_ref, qkv_at, part, xg, dyg, dw1, dw2, dwo,
    block_out, input_grad, t1, tq, t2, to, pieces,
    dk_scr, dv_scr, dq_scr, dqkv_scr, dw_scr, vec_ref, u_scr, dw,
    from_sib, from_far, to_far, mine, done, xq, ls_o, ss_o, rs_o,
    from_sib2, from_far2, to_far2, done2, dyq, ls_u, ss_u, rs_u,
    ls_s, ss_s, rs_s, ls_w, ss_w, rs_w, sums_all, ls_g, ss_g, rs_g,
    b1, bq, b2, bo, s1, sq, s2, so, msg, m_all, p_out, ls, ss_m, rs_m, ss, rs,
):
    step = pl.program_id(0)
    blocks = pl.num_programs(0)
    g, y = place()[4:6]
    b = far_first(step)
    nh = k_ref.shape[0]
    rows = x_ref.shape[0]
    wide = 3 * nh * HEAD_DIM
    lane = lax.broadcasted_iota(jnp.int32, (rows, PAD), 1)
    first = lane < ROT // 2

    def block_rows(n):
        return pl.ds(pl.multiple_of(n * rows, rows), rows)

    here = block_rows(b)
    red = Reduce(
        part, block_out, [(xg, xq)], (from_sib, from_far, to_far, mine, done), ls_o, ss_o, rs_o
    )
    red_u = ReduceQuarters(
        u_scr, input_grad, (from_sib2, from_far2, to_far2, done2), ls_u, ss_u, rs_u
    )
    swap = Swap(np_, [(dw1, b1), (dw2, b2)], (dwo, bo), ls_s, ss_s, rs_s)

    load_dy = pltpu.make_async_copy(dyg.at[red.q_here], dyq, ls.at[4])

    def back(total, r):
        return norm_back(total, xq[r], dyq[r])

    @pl.when(step == 0)
    def _():
        meet(np_)
        red.start()
        load_dy.start()
        swap.start()
        dk_scr[...] = jnp.zeros_like(dk_scr)
        dv_scr[...] = jnp.zeros_like(dv_scr)
        dq_scr[...] = jnp.zeros_like(dq_scr)
        dw_scr[...] = jnp.zeros_like(dw_scr)
        vec_ref[...] = vec_in_ref[...]

    causal = lax.broadcasted_iota(jnp.int32, (rows, rows), 0) <= lax.broadcasted_iota(
        jnp.int32, (rows, rows), 1
    )

    def block(n, m, diagonal):
        asks, keys = block_rows(n), block_rows(m)
        for h in range(nh):
            k = k_ref[h, keys]
            q = q_ref[h, asks]
            dc = dc_ref[h, asks]
            pt = jnp.exp(dot(k, q, ((1,), (1,))))
            if diagonal:
                pt = jnp.where(causal, pt, 0.0)
            dpt = dot(v_ref[h, keys], dc, ((1,), (1,)))
            dst = (pt * dpt).astype(bf16)
            dv_scr[h, keys] += dot(pt.astype(bf16), dc)
            dk_scr[h, keys] += dot(dst, q)
            dq_scr[h, asks] += dot(dst, k, ((0,), (0,)))

    block(b, b, True)

    @pl.when(step == 0)
    def _():
        red.add_near()

    def off(n, carry):
        block(jnp.where(g == 0, b, b + 1 + n), jnp.where(g == 0, n, b), False)
        return carry

    lax.fori_loop(0, blocks - 1 - step, off, 0)

    @pl.when(step == 1)
    def _():
        red.add_far(lambda total, r: xq[r].astype(f32) + tab_ref[2:3] + total)
        load_dy.wait()

    @pl.when(step == 3)
    def _():
        red_u.pull(mirror(2, g), back)

    cosine, sine = cos_ref[...], -sin_ref[...]
    for h in range(nh):
        dq = turn(dq_scr[h, here], cosine, sine, first) * HEAD_DIM**-0.5
        dk = turn(dk_scr[h, here], cosine, sine, first)
        for at, piece in ((h, dq), (nh + h, dk), (2 * nh + h, dv_scr[h, here])):
            dqkv_scr[:, at * HEAD_DIM : (at + 1) * HEAD_DIM] = piece[:, :HEAD_DIM].astype(bf16)
    dqkv = dqkv_scr[...]
    xhat, unused = norm_parts(x_ref[...].astype(f32))
    gain = tab_ref[0:1]
    a1 = (xhat * gain + tab_ref[1:2]).astype(bf16)
    da1 = dot(dqkv, w_ref[...], ((1,), (1,)))
    u_scr[b] = (u_in_ref[...] + da1 * gain).astype(bf16)

    @pl.when(step < blocks - 1)
    def _():
        red_u.ready(b)

    dw_scr[...] += dot(a1, dqkv, ((0,), (0,)))
    vec_ref[0:1] += jnp.sum(da1 * xhat, axis=0, keepdims=True)
    vec_ref[1:2] += jnp.sum(da1, axis=0, keepdims=True)
    vec_ref[5:6, :wide] += jnp.sum(dqkv.astype(f32), axis=0, keepdims=True)

    @pl.when(step < blocks - 1)
    def _():
        red_u.push(b)

    @pl.when(step == 2)
    def _():
        red_u.pull(mirror(3, g), back)

    @pl.when(step == blocks - 1)
    def _():
        vec_ref[7:8, 0:1] += squares_of(dw_scr[...])
        share = D // np_
        for n in range(np_):
            dw[n] = dw_scr[n * share : (n + 1) * share].astype(bf16)
        finish_all(
            np_, r_in, r_ff, wide // 3, red, red_u, swap, back,
            dw, vec_ref, hot_ref, qkv_at, t1, tq, t2, to, pieces,
            ls_w, ss_w, rs_w, sums_all, ls_g, ss_g, rs_g,
            b1, bq, b2, bo, s1, sq, s2, so, msg, m_all, p_out, ls, ss_m, rs_m, ss, rs,
        )


def whole(shape):
    return pl.BlockSpec(shape, lambda i: (0,) * len(shape), pipeline_mode=pl.Buffered(1))


def sds(shape, dtype):
    return jax.ShapeDtypeStruct(shape, dtype)


def params(collective_id=None):
    return pltpu.CompilerParams(
        dimension_semantics=("arbitrary",), vmem_limit_bytes=VMEM_BYTES,
        collective_id=collective_id, has_side_effects=collective_id is not None,
    )


def weight_sems(np_, n):
    return [
        pltpu.SemaphoreType.DMA((n,)),
        pltpu.SemaphoreType.DMA((n, 8 + np_)),
        pltpu.SemaphoreType.DMA((n, 8 + np_)),
    ]


def attn_fwd(np_, length, x, tab, w, wb, cosine, sine, dy, w2, wo, nh, rows):
    t = x.shape[0]
    lanes = pl.BlockSpec((rows, PAD), lambda i: (i, 0))
    any_ = pl.BlockSpec(memory_space=pl.ANY)
    return pl.pallas_call(
        functools.partial(attn_fwd_kernel, np_),
        grid=(t // rows,),
        out_shape=(
            sds((nh, t, PAD), bf16), sds((nh, t, PAD), bf16), sds((nh, t, PAD), bf16),
            sds((t, nh * PAD), f32), sds((t, nh * HEAD_DIM), bf16),
            sds((4,) + dy.shape, bf16),
            sds((np_,) + w2.shape, bf16), sds(wo.shape, bf16),
        ),
        in_specs=[
            whole((1, PAD)), pl.BlockSpec((rows, D), lambda i: (i, 0)),
            whole((8, D)), whole(w.shape), whole(wb.shape), lanes, lanes,
            pl.BlockSpec(memory_space=pltpu.VMEM), any_, any_,
        ],
        out_specs=(
            pl.BlockSpec((nh, rows, PAD), lambda i: (0, i, 0)),
            whole((nh, t, PAD)), whole((nh, t, PAD)),
            pl.BlockSpec((rows, nh * PAD), lambda i: (i, 0)),
            pl.BlockSpec((rows, nh * HEAD_DIM), lambda i: (i, 0)),
            any_, any_, any_,
        ),
        scratch_shapes=[
            pltpu.VMEM((D, 3 * nh * PAD), bf16),
            pltpu.VMEM((nh, t // rows, rows, rows), f32),
            pltpu.VMEM((nh, rows, PAD), bf16),
            pltpu.VMEM((nh, rows, PAD), f32),
            pltpu.VMEM((nh, rows, PAD), f32),
            pltpu.VMEM((nh, rows, PAD), f32),
        ] + spread_sems() + swap_sems(np_, 2),
        compiler_params=params(2),
        name="attn_fwd",
    )(length, x, tab, w, wb, cosine, sine, dy, w2, wo)


def far_first(i):
    return mirror(3 - i, place()[4])


def mlp(x, dy, c, cf, tab, wo, w1, w2, rows):
    t = x.shape[0]
    ff = w1.shape[1]
    nh = wo.shape[0] // HEAD_DIM
    at = lambda cols: pl.BlockSpec((rows, cols), lambda i: (i, 0))
    vm = pltpu.VMEM
    return pl.pallas_call(
        mlp_kernel,
        grid=(t // rows,),
        out_shape=(
            sds((t, D), bf16), sds((t, D), f32), sds((nh, t, PAD), bf16), sds((D, ff), bf16),
            sds((ff, D), bf16), sds(wo.shape, bf16), sds((8, D), f32),
        ),
        in_specs=[
            at(D), at(D), at(c.shape[1]), at(cf.shape[1]),
            whole((8, D)), whole(wo.shape), whole(w1.shape), whole(w2.shape),
        ],
        out_specs=(
            at(D), at(D), pl.BlockSpec((nh, rows, PAD), lambda i: (0, i, 0)),
            whole((D, ff)), whole((ff, D)), whole(wo.shape), whole((8, D)),
        ),
        scratch_shapes=[
            vm((D, ff), f32), vm((ff, D), f32), vm(wo.shape, f32), vm((nh * PAD, D), bf16),
        ],
        compiler_params=params(),
        name="mlp",
    )(x, dy, c, cf, tab, wo, w1, w2)


def attn_bwd(
    np_, r_in, r_ff, x, u_in, q, k, v, dc, tab, w, cosine, sine, vec,
    part, xg, dyg, dw1, dw2, dwo,
):
    t = x.shape[0]
    nh = q.shape[0]
    wide = w.shape[1]
    quarter = part.shape[1]
    ff = dw1.shape[2]
    at = lambda cols: pl.BlockSpec((quarter, cols), lambda i: (far_first(i), 0))
    any_ = pl.BlockSpec(memory_space=pl.ANY)
    dma = pltpu.SemaphoreType.DMA
    vm = pltpu.VMEM
    hot, qkv_at = one_hot_tables(np_, r_in, r_ff, wide // 3)
    per_owner = lambda cols: vm((2, 4, r_in, cols), bf16)
    block = vm((quarter, D), bf16)
    return pl.pallas_call(
        functools.partial(attn_bwd_kernel, np_, r_in, r_ff),
        grid=(4,),
        out_shape=(
            sds((quarter, D), bf16), sds((quarter, D), bf16), sds((8, r_in, ff), bf16),
            sds((8, r_in, wide), bf16), sds((2, r_ff, D), bf16), sds((2, r_in, D), bf16),
            sds((8, PAD), f32),
        ),
        in_specs=[
            at(D), at(D), whole(q.shape), whole(k.shape), whole(v.shape), whole(dc.shape),
            whole((8, D)), whole(w.shape), at(PAD), at(PAD), whole((8, D)), whole(hot.shape),
            whole(qkv_at.shape),
        ] + [any_] * 6,
        out_specs=(any_,) * 7,
        scratch_shapes=[
            vm((nh, t, PAD), f32), vm((nh, t, PAD), f32), vm((nh, t, PAD), f32),
            vm((quarter, wide), bf16), vm((D, wide), f32), vm((8, D), f32),
            vm((4, quarter, D), bf16), vm((np_, D // np_, wide), bf16),
        ] + reduce_scratch(quarter, 1) + [
            vm((2, quarter, D), bf16), block, block, block, block,
            dma((5,)), dma((4, PIECES)), dma((4, PIECES)),
        ] + swap_sems(np_, 3) + swap_sems(np_, 1) + [
            vm((4, 8, D), f32), dma, dma((3,)), dma((3,)),
            vm(dw1.shape, bf16), vm((np_, D // np_, wide), bf16), vm(dw2.shape, bf16),
            vm((np_,) + dwo.shape[1:], bf16),
            per_owner(ff), per_owner(wide), vm((2, r_ff, D), bf16), per_owner(D),
            vm((2 * np_, 8, PAD), f32), vm((2 * np_, 8, PAD), f32), vm((8, PAD), f32),
            dma((10,)), dma((2 * np_,)), dma((2 * np_,)), dma((4, 8)), dma((4, 8)),
        ],
        compiler_params=params(3),
        name="attn_bwd",
    )(
        x, u_in, q, k, v, dc, tab, w, cosine, sine, vec, hot, qkv_at,
        part, xg, dyg, dw1, dw2, dwo,
    )


def assemble_kernel(np_, t1, tq, t2, to, fc1, qkv, fc2, out):
    r_ff = t2.shape[1]
    part_w = tq.shape[2] // 3
    for c in range(2):
        for y in range(2):
            a, b = (0, 3) if y == 0 else (1, 2)
            up = t1[4 * c + a].astype(f32) + t1[4 * c + b].astype(f32)
            for pair in range(np_):
                for e, z in enumerate((a, b)):
                    to_at = r_ff * (4 * (2 * pair + c) + z)
                    at = r_ff * (2 * pair + e)
                    fc1[:, to_at : to_at + r_ff] = up[:, at : at + r_ff]
            into = tq[4 * c + a].astype(f32) + tq[4 * c + b].astype(f32)
            for s in range(3):
                to_at = s * D + (2 * y + c) * part_w
                qkv[:, to_at : to_at + part_w] = into[:, s * part_w : (s + 1) * part_w]
    fc2[...] = t2[0].astype(f32) + t2[1].astype(f32)
    out[...] = to[0].astype(f32) + to[1].astype(f32)


def assemble(np_, t1, tq, t2, to):
    r_in = t1.shape[1]
    vmem = pl.BlockSpec(memory_space=pltpu.VMEM)
    return pl.pallas_call(
        functools.partial(assemble_kernel, np_),
        out_shape=(
            sds((r_in, t1.shape[2] * 4), f32), sds((r_in, tq.shape[2] * 4), f32),
            sds(t2.shape[1:], f32), sds(to.shape[1:], f32),
        ),
        in_specs=[vmem] * 4,
        out_specs=(vmem,) * 4,
        name="assemble",
    )(t1, tq, t2, to)


def swap_sems(np_, n):
    return [
        pltpu.SemaphoreType.DMA((n,)),
        pltpu.SemaphoreType.DMA((n, np_)),
        pltpu.SemaphoreType.DMA((n, np_)),
    ]


def tables(t):
    inv_freqs = np.exp(np.arange(ROT // 2, dtype=np.float32) * np.float32(-2.0 * math.log(10000.0) / ROT))
    angles = np.arange(t, dtype=np.float32)[:, None] * inv_freqs.astype(np.float32)[None, :]
    cosine = np.ones((t, PAD), np.float32)
    sine = np.zeros((t, PAD), np.float32)
    half = ROT // 2
    cosine[:, :half] = cosine[:, half:ROT] = np.cos(angles)
    sine[:, :half] = -np.sin(angles)
    sine[:, half:ROT] = np.sin(angles)
    return jnp.asarray(cosine), jnp.asarray(sine)


MESH = pl.DeviceIdType.MESH
AX = ("dp", "ctx")
CHUNKS = 4


def place():
    d, z = lax.axis_index("dp"), lax.axis_index("ctx")
    c, pair, g = lax.rem(d, 2), lax.div(d, 2), lax.div(z, 2)
    y = lax.rem(g + lax.rem(z, 2), 2)
    return d, z, c, pair, g, y


def mirror(m, g):
    return jnp.where(g == 0, m, 3 - m)


def rcopy(src, dst, ss, rs, device):
    return pltpu.make_async_remote_copy(
        src_ref=src, dst_ref=dst, send_sem=ss, recv_sem=rs, device_id=device, device_id_type=MESH
    )


def column_peer(pair, c, z, o):
    m = lax.rem(c * 4 + z + o, 8)
    return lax.div(m, 4), lax.rem(m, 4)


def barrier_all(np_, d, z, c, pair):
    bar = pltpu.get_barrier_semaphore()
    for o in range(1, 8):
        c2, z2 = column_peer(pair, c, z, o)
        pl.semaphore_signal(bar, inc=1, device_id=(2 * pair + c2, z2), device_id_type=MESH)
    for o in range(1, np_):
        pl.semaphore_signal(
            bar, inc=1, device_id=(2 * lax.rem(pair + o, np_) + c, z), device_id_type=MESH
        )
    pl.semaphore_wait(bar, 7 + np_ - 1)


class Spread:
    def __init__(self, own, out, ls, ss, rs):
        self.own, self.out, self.ls, self.ss, self.rs = own, out, ls, ss, rs
        self.rows = out.shape[1] // CHUNKS
        d, z, c, pair, g, y = place()
        self.d, self.z, self.c, self.g, self.y = d, z, c, g, y
        self.prim = c == g
        self.sib = (d + 1 - 2 * c, z)
        self.partner = (d, z + 1 - 2 * lax.rem(z, 2))
        self.far = (d, 1 + c)

    def cut(self, ref, j):
        return ref.at[pl.ds(j * self.rows, self.rows)]

    def send(self, q, j, way, device, src=None):
        src = self.cut(self.out.at[q], j) if src is None else src
        return rcopy(
            src, self.cut(self.out.at[q], j), self.ss.at[way, q, j], self.rs.at[q, j], device
        )

    def start(self):
        own = [self.cut(self.own, j) for j in range(CHUNKS)]

        @pl.when(self.prim)
        def _():
            pltpu.make_async_copy(self.own, self.out.at[self.z], self.ls).start()
            for j in range(CHUNKS):
                self.send(self.z, j, 0, self.partner, own[j]).start()
            for j in range(CHUNKS):
                self.send(self.z, j, 1, self.sib, own[j]).start()

        @pl.when(jnp.logical_not(self.prim))
        def _():
            for j in range(CHUNKS):
                self.send(self.z, j, 0, self.far, own[j]).start()

    def wait_recv(self, q, j):
        self.send(q, j, 0, self.sib).wait_recv()

    def forward(self, j):
        far = (mirror(2, self.g), mirror(3, self.g))
        end, mid = mirror(0, self.g), mirror(1, self.g)

        @pl.when(jnp.logical_and(self.prim, self.y == 1))
        def _():
            for q in far:
                self.wait_recv(q, j)
                self.send(q, j, 0, self.partner).start()
                self.send(q, j, 1, self.sib).start()
            self.wait_recv(end, j)
            self.send(end, j, 1, self.sib).start()

        @pl.when(jnp.logical_and(self.prim, self.y == 0))
        def _():
            self.wait_recv(mid, j)
            self.send(mid, j, 1, self.sib).start()
            if j > 0:
                for q in far:
                    self.wait_recv(q, j - 1)
                    self.send(q, j - 1, 1, self.sib).start()

    def finish(self):
        far = (mirror(2, self.g), mirror(3, self.g))
        end, mid = mirror(0, self.g), mirror(1, self.g)

        @pl.when(jnp.logical_and(self.prim, self.y == 0))
        def _():
            for q in far:
                self.wait_recv(q, CHUNKS - 1)
                self.send(q, CHUNKS - 1, 1, self.sib).start()
            for j in range(CHUNKS):
                self.send(end, j, 0, self.partner).wait_send()

        @pl.when(jnp.logical_and(self.prim, self.y == 1))
        def _():
            for j in range(CHUNKS):
                for q in far + (mid,):
                    self.send(q, j, 0, self.partner).wait_send()

        @pl.when(self.prim)
        def _():
            pltpu.make_async_copy(self.own, self.out.at[self.z], self.ls).wait()
            for q in range(4):
                for j in range(CHUNKS):
                    self.send(q, j, 1, self.sib).wait_send()

        @pl.when(jnp.logical_not(self.prim))
        def _():
            for q in range(4):
                for j in range(CHUNKS):
                    self.wait_recv(q, j)
            for j in range(CHUNKS):
                self.send(self.z, j, 0, self.far).wait_send()


class Weights:
    def __init__(self, np_, sliced, w2, wo, ls, ss, rs):
        self.np_, self.sliced, self.w2, self.wo = np_, sliced, w2, wo
        self.ls, self.ss, self.rs = ls, ss, rs
        self.here = place()

    def first(self, s, o):
        d, z, c, pair, g, y = self.here
        src, out, by_slice = self.sliced[s]
        if o == 0:
            return pltpu.make_async_copy(
                src.at[2 * y + c] if by_slice else src, out.at[pair, c, z], self.ls.at[s]
            )
        c2, z2 = column_peer(pair, c, z, o)
        y2 = lax.rem(lax.div(z2, 2) + lax.rem(z2, 2), 2)
        return rcopy(
            src.at[2 * y2 + c2] if by_slice else src, out.at[pair, c, z],
            self.ss.at[s, o - 1], self.rs.at[s, o - 1], (2 * pair + c2, z2),
        )

    def second(self, s, o):
        d, z, c, pair, g, y = self.here
        out = self.sliced[s][1]
        return rcopy(
            out.at[pair], out.at[pair], self.ss.at[s, 7 + o - 1], self.rs.at[s, 7 + o - 1],
            (2 * lax.rem(pair + o, self.np_) + c, z),
        )

    def start(self):
        d, z, c, pair, g, y = self.here
        n = len(self.sliced)
        for s in range(n):
            for o in range(8):
                self.first(s, o).start()

    def start_rows(self):
        for o in range(2):
            self.w2_first(o).start()
        self.wo_first(lambda cp: cp.start())

    def w2_first(self, o):
        d, z, c, pair, g, y = self.here
        src, out = self.w2
        n = len(self.sliced)
        if o == 0:
            return pltpu.make_async_copy(src, out.at[g], self.ls.at[n])
        return rcopy(src, out.at[g], self.ss.at[n, 0], self.rs.at[n, 0], (d, 3 - z))

    def wo_parts(self):
        d, z, c, pair, g, y = self.here
        per = self.np_ // 4
        owner = lax.div(pair, per)
        return per, owner, lax.rem(owner, 2), lax.div(owner, 2)

    def wo_first(self, do, sending=True):
        d, z, c, pair, g, y = self.here
        src, out = self.wo
        n = len(self.sliced) + 1
        per, owner, c_to, y_to = self.wo_parts()
        slot = out.at[lax.rem(pair, per), c, z]
        for t in range(2):
            z_to = jnp.where(t == 0, y_to, 3 - y_to)
            mine = jnp.logical_and(c == c_to, z == z_to)

            @pl.when(mine)
            def _():
                do(pltpu.make_async_copy(src, slot, self.ls.at[n]))

            @pl.when(jnp.logical_not(mine))
            def _():
                cp = rcopy(
                    src, slot, self.ss.at[n, t], self.rs.at[n, c * 4 + z], (2 * pair + c_to, z_to)
                )
                do(cp)

    def between(self, s):
        self.first(s, 0).wait()
        for o in range(1, 8):
            self.first(s, o).wait_recv()
        for o in range(1, self.np_):
            self.second(s, o).start()

    def finish_rows(self):
        d, z, c, pair, g, y = self.here
        n = len(self.sliced) + 1
        per, owner, c_to, y_to = self.wo_parts()
        for o in range(2):
            self.w2_first(o).wait()

        @pl.when(owner == 2 * y + c)
        def _():
            for c2 in range(2):
                for z2 in range(4):
                    own = jnp.logical_and(c == c2, z == z2)

                    @pl.when(jnp.logical_not(own))
                    def _():
                        slot = self.wo[1].at[0, c2, z2]
                        rcopy(
                            slot, slot, self.ss.at[n, 0], self.rs.at[n, c2 * 4 + z2],
                            (d + 1 - 2 * c, z),
                        ).wait_recv()
            pltpu.make_async_copy(
                self.wo[0], self.wo[1].at[0, c, z], self.ls.at[n]
            ).wait()

        for t in range(2):
            z_to = jnp.where(t == 0, y_to, 3 - y_to)

            @pl.when(jnp.logical_not(jnp.logical_and(c == c_to, z == z_to)))
            def _():
                rcopy(
                    self.wo[0], self.wo[1].at[0, c, z], self.ss.at[n, t], self.rs.at[n, 0],
                    (d + 1 - 2 * c, z),
                ).wait_send()

    def finish(self, s):
        for o in range(1, 8):
            self.first(s, o).wait_send()
        for o in range(1, self.np_):
            self.second(s, o).wait()


class Rows:
    def __init__(self, np_, w2, wo, ls, ss, rs):
        self.np_, self.w2, self.wo, self.ls, self.ss, self.rs = np_, w2, wo, ls, ss, rs
        self.here = place()

    def copy_w2(self, o):
        d, z, c, pair, g, y = self.here
        src, out = self.w2
        if o == 0:
            return pltpu.make_async_copy(src, out.at[pair], self.ls.at[0])
        to = (2 * lax.rem(pair + o, self.np_) + c, z)
        return rcopy(src, out.at[pair], self.ss.at[0, o], self.rs.at[0, o], to)

    def copy_wo(self, o):
        d, z, c, pair, g, y = self.here
        src, out = self.wo
        slot = lax.rem(pair, self.np_ // 4)
        if o == 0:
            return pltpu.make_async_copy(src.at[slot], out.at[slot], self.ls.at[1])
        to = (2 * lax.rem(pair + o, self.np_) + c, z)
        return rcopy(src.at[slot], out.at[slot], self.ss.at[1, o], self.rs.at[1, o], to)

    def holds(self, pair):
        d, z, c, unused, g, y = self.here
        return lax.div(pair, self.np_ // 4) == 2 * y + c

    def start(self):
        @pl.when(self.holds(self.here[3]))
        def _():
            for o in range(1, self.np_):
                self.copy_wo(o).start()
            self.copy_wo(0).start()

        for o in range(1, self.np_):
            self.copy_w2(o).start()
        self.copy_w2(0).start()

    def finish(self):
        pair = self.here[3]
        for o in range(self.np_):
            self.copy_w2(o).wait()

        @pl.when(self.holds(pair))
        def _():
            self.copy_wo(0).wait()
            for o in range(1, self.np_):
                self.copy_wo(o).wait_send()

        for o in range(1, self.np_):
            @pl.when(self.holds(lax.rem(pair + self.np_ - o, self.np_)))
            def _():
                self.copy_wo(o).wait_recv()


def decode_tables(np_, r_in, r_ff, part, nh):
    wide = 3 * nh * PAD
    f = np.arange(D)
    by_d = np.zeros((8, D), np.int32)
    by_d[0], by_d[1] = f // r_in, f % r_in
    by_d[2], by_d[3], by_d[4] = f // (2 * r_ff), (f // r_ff) % 2, f % r_ff
    p = np.arange(wide)
    head, lane = p // PAD, p % PAD
    by_q = np.full((8, wide), -1, np.int32)
    for k in range(4):
        at = (head // nh) * D + k * part + (head % nh) * HEAD_DIM + lane
        real = lane < HEAD_DIM
        by_q[k, real] = (at // (3 * r_in))[real]
        by_q[4 + k, real] = (r_in + at % (3 * r_in))[real]
    extra = np.zeros((1, wide), np.float32)
    extra[0, (head < nh) & (lane == HEAD_DIM)] = HEAD_DIM**0.5
    keys = (head >= nh) & (head < 2 * nh)
    extra[0, keys & (lane > HEAD_DIM) & (lane < HEAD_DIM + 4)] = 1.0
    extra[0, (head >= 2 * nh) & (lane >= HEAD_DIM) & (lane < HEAD_DIM + 3)] = 1.0
    return jnp.asarray(by_d), jnp.asarray(by_q), jnp.asarray(extra)


def decode(np_, r_in, r_ff, vec, by_d, by_q, extra, tab, b_pad, length):
    d, z, c, pair, g, y = place()
    world = 8 * np_
    packed = vec[...].reshape(world * 16, PAD)
    m = lax.broadcasted_iota(jnp.int32, (world, world * 16), 1)
    n = lax.broadcasted_iota(jnp.int32, (world, world * 16), 0)
    row = [
        dot(jnp.where(m == 16 * n + r, 1.0, 0.0).astype(bf16), packed).astype(bf16)
        for r in range(3)
    ]

    def pick(x, lanes, owner):
        w = lanes.shape[1]
        hot = lax.broadcasted_iota(jnp.int32, (PAD, w), 0) == lanes
        got = dot(x, jnp.where(hot, 1.0, 0.0).astype(bf16))
        mine = lax.broadcasted_iota(jnp.int32, (world, w), 0) == owner
        return jnp.sum(jnp.where(mine, got, 0.0), axis=0, keepdims=True)

    owner, lanes = by_d[0:1], by_d[1:2]
    tab[0:1] = pick(row[0], lanes, owner)
    tab[1:2] = pick(row[0], lanes + r_in, owner)
    tab[2:3] = pick(row[0], lanes + 2 * r_in, owner) + pick(row[1], lanes, owner)
    tab[3:4] = pick(row[0], lanes + 3 * r_in, owner)
    tab[4:5] = pick(row[0], lanes + 4 * r_in, owner)
    owner = by_d[2:3] * 8 + c * 4 + jnp.where(by_d[3:4] == 0, y, 3 - y)
    tab[5:6] = pick(row[2], by_d[4:5], owner)
    tab[6:8] = jnp.zeros((2, D), f32)
    k = 2 * y + c
    b_pad[...] = pick(row[1], by_q[pl.ds(4 + k, 1)], by_q[pl.ds(k, 1)]) + extra[...]
    mine = lax.broadcasted_iota(jnp.int32, (world, PAD), 0) == (2 * pair + g) * 4
    parts = jnp.sum(jnp.where(mine, row[2].astype(f32), 0.0), axis=0, keepdims=True)
    lane = lax.broadcasted_iota(jnp.int32, (1, PAD), 1)
    parts = jnp.where(lane == r_ff, parts * 256.0, jnp.where(lane == r_ff + 1, parts, 0.0))
    length[...] = jnp.broadcast_to(jnp.sum(parts, axis=1, keepdims=True), (1, PAD))


def gather_kernel(
    np_, r_in, r_ff, x, wq, w1, w2, wo, vec_own, by_d, by_q, extra,
    xg, wqg, w1g, w2p, wop, tab, b_pad, length, vec, ls_x, ss_x, rs_x, ls_w, ss_w, rs_w,
):
    d, z, c, pair, g, y = place()
    barrier_all(np_, d, z, c, pair)
    spread = Spread(x, xg, ls_x, ss_x, rs_x)
    weights = Weights(
        np_, [(vec_own, vec, False), (wq, wqg, True), (w1, w1g, True)], (w2, w2p), (wo, wop),
        ls_w, ss_w, rs_w,
    )
    weights.start()
    spread.start()
    weights.start_rows()
    for s in range(3):
        weights.between(s)
    spread.forward(0)
    weights.finish(0)
    decode(np_, r_in, r_ff, vec, by_d, by_q, extra, tab, b_pad, length)
    for j in range(1, CHUNKS):
        spread.forward(j)
    spread.finish()
    for s in range(1, 3):
        weights.finish(s)
    weights.finish_rows()


def spread_sems():
    return [
        pltpu.SemaphoreType.DMA,
        pltpu.SemaphoreType.DMA((2, 4, CHUNKS)),
        pltpu.SemaphoreType.DMA((4, CHUNKS)),
    ]


def gather(np_, r_in, r_ff, nh, x, wq, w1, w2, wo, vec, collective_id=1):
    any_ = pl.BlockSpec(memory_space=pl.ANY)
    vmem = pl.BlockSpec(memory_space=pltpu.VMEM)
    wide = 3 * nh * PAD
    return pl.pallas_call(
        functools.partial(gather_kernel, np_, r_in, r_ff),
        out_shape=(
            sds((4,) + x.shape, bf16), sds((np_, 2, 4) + wq.shape[1:], bf16),
            sds((np_, 2, 4) + w1.shape[1:], bf16), sds((2,) + w2.shape, bf16),
            sds((np_ // 4, 2, 4) + wo.shape, bf16),
            sds((8, D), f32), sds((1, wide), f32), sds((1, PAD), f32),
        ),
        in_specs=[any_] * 6 + [vmem] * 3,
        out_specs=(any_,) * 5 + (vmem,) * 3,
        scratch_shapes=[pltpu.VMEM((np_, 2, 4, 16, PAD), bf16)] + spread_sems()
        + weight_sems(np_, 5),
        compiler_params=pltpu.CompilerParams(
            collective_id=collective_id, has_side_effects=True, vmem_limit_bytes=VMEM_BYTES
        ),
        name="gather",
    )(x, wq, w1, w2, wo, vec, *decode_tables(np_, r_in, r_ff, wq.shape[2] // 3, nh))


PIECES = 4


class Reduce:
    def __init__(self, part, out, extra, bufs, ls, ss, rs):
        self.part, self.out, self.extra = part, out, extra
        self.from_sib, self.from_far, self.to_far, self.mine, self.done = bufs
        self.ls, self.ss, self.rs = ls, ss, rs
        d, z, c, pair, g, y = place()
        self.role = jnp.where(c == g, 0, 1)
        self.y = y
        self.sib = (d + 1 - 2 * c, z)
        self.partner = (d, z + 1 - 2 * lax.rem(z, 2))
        self.q_here = mirror(2 * y + self.role, g)
        self.q_there = mirror(2 * (1 - y) + self.role, g)
        self.sib_here = mirror(2 * y + 1 - self.role, g)
        self.sib_there = mirror(2 * (1 - y) + 1 - self.role, g)
        self.owner = (2 * pair + g, self.q_here)
        self.self_owner = jnp.logical_and(self.role == 0, y == 0)
        self.self_source = jnp.where(c == 0, z, 3 - z) == 0
        self.rows = self.out.shape[0] // PIECES

    def rows_of(self, j):
        return pl.ds(j * self.rows, self.rows)

    def to_sib(self, t, j):
        q = self.sib_there if t == 0 else self.sib_here
        r = self.rows_of(j)
        return rcopy(
            self.part.at[q, r], self.from_sib.at[t, r], self.ss.at[t, j], self.rs.at[t, j], self.sib
        )

    def load(self, t):
        q = self.q_there if t == 0 else self.q_here
        return pltpu.make_async_copy(self.part.at[q], self.mine.at[t], self.ls.at[t])

    def load_extra(self, e):
        src, dst = self.extra[e]
        return pltpu.make_async_copy(src.at[self.q_here], dst, self.ls.at[2 + e])

    def across(self, j):
        r = self.rows_of(j)
        return rcopy(
            self.to_far.at[r], self.from_far.at[r], self.ss.at[2, j], self.rs.at[2, j], self.partner
        )

    def home(self, j):
        r = self.rows_of(j)
        return rcopy(
            self.done.at[r], self.out.at[r], self.ss.at[3, j], self.rs.at[3, j], self.owner
        )

    def keep(self):
        return pltpu.make_async_copy(self.done, self.out, self.ls.at[4])

    def start(self):
        for t in range(2):
            for j in range(PIECES):
                self.to_sib(t, j).start()
        for t in range(2):
            self.load(t).start()
        for e in range(len(self.extra)):
            self.load_extra(e).start()

    def add_near(self):
        self.load(0).wait()
        for j in range(PIECES):
            r = self.rows_of(j)
            self.to_sib(0, j).wait_recv()
            total = self.mine[0, r].astype(f32) + self.from_sib[0, r].astype(f32)
            self.to_far[r] = total.astype(bf16)
            self.across(j).start()
        self.load(1).wait()
        for e in range(len(self.extra)):
            self.load_extra(e).wait()

    def add_far(self, finish):
        for j in range(PIECES):
            r = self.rows_of(j)
            self.to_sib(1, j).wait_recv()
            self.across(j).wait_recv()
            total = self.mine[1, r].astype(f32) + self.from_sib[1, r].astype(f32)
            total = total + self.from_far[r].astype(f32)
            self.done[r] = finish(total, r).astype(bf16)

            @pl.when(jnp.logical_not(self.self_owner))
            def _():
                self.home(j).start()

    def finish(self):
        @pl.when(self.self_owner)
        def _():
            self.keep().start()
            self.keep().wait()

        for j in range(PIECES):
            @pl.when(jnp.logical_not(self.self_source))
            def _():
                self.home(j).wait_recv()

        for j in range(PIECES):
            self.to_sib(0, j).wait_send()
            self.to_sib(1, j).wait_send()
            self.across(j).wait_send()

            @pl.when(jnp.logical_not(self.self_owner))
            def _():
                self.home(j).wait_send()


def reduce_scratch(rows, extras):
    return [
        pltpu.VMEM((2, rows, D), bf16), pltpu.VMEM((rows, D), bf16), pltpu.VMEM((rows, D), bf16),
        pltpu.VMEM((2, rows, D), bf16), pltpu.VMEM((rows, D), bf16),
    ] + [pltpu.VMEM((rows, D), bf16)] * extras + [
        pltpu.SemaphoreType.DMA((5,)),
        pltpu.SemaphoreType.DMA((4, PIECES)),
        pltpu.SemaphoreType.DMA((4, PIECES)),
    ]


class ReduceQuarters(Reduce):
    def __init__(self, part, out, bufs, ls, ss, rs):
        from_sib, from_far, to_far, done = bufs
        super().__init__(part, out, [], (from_sib, from_far, to_far, None, done), ls, ss, rs)

    def ready(self, q):
        for t, mine in ((0, self.sib_there), (1, self.sib_here)):
            @pl.when(mine == q)
            def _():
                for j in range(PIECES):
                    self.to_sib(t, j).start()

    def push(self, q):
        @pl.when(self.q_there == q)
        def _():
            for j in range(PIECES):
                r = self.rows_of(j)
                self.to_sib(0, j).wait_recv()
                total = self.part[q, r].astype(f32) + self.from_sib[0, r].astype(f32)
                self.to_far[r] = total.astype(bf16)
                self.across(j).start()

    def pull(self, q, finish):
        @pl.when(self.q_here == q)
        def _():
            for j in range(PIECES):
                r = self.rows_of(j)
                self.to_sib(1, j).wait_recv()
                self.across(j).wait_recv()
                total = self.part[q, r].astype(f32) + self.from_sib[1, r].astype(f32)
                total = total + self.from_far[r].astype(f32)
                self.done[r] = finish(total, r).astype(bf16)

                @pl.when(jnp.logical_not(self.self_owner))
                def _():
                    self.home(j).start()


class Swap:
    def __init__(self, np_, arrays, wo, ls, ss, rs):
        self.np_, self.arrays, self.wo, self.ls, self.ss, self.rs = np_, arrays, wo, ls, ss, rs
        self.here = place()

    def copy(self, s, o):
        d, z, c, pair, g, y = self.here
        src, dst = self.arrays[s]
        to = lax.rem(pair + o, self.np_)
        if o == 0:
            return pltpu.make_async_copy(src.at[pair], dst.at[pair], self.ls.at[s])
        return rcopy(
            src.at[to], dst.at[pair], self.ss.at[s, o], self.rs.at[s, o], (2 * to + c, z)
        )

    def copy_wo(self, o):
        d, z, c, pair, g, y = self.here
        src, dst = self.wo
        n = len(self.arrays)
        per = self.np_ // 4
        to = lax.rem(pair + o, self.np_)
        if o == 0:
            return pltpu.make_async_copy(src.at[lax.rem(pair, per)], dst.at[pair], self.ls.at[n])
        return rcopy(
            src.at[lax.rem(to, per)], dst.at[pair], self.ss.at[n, o], self.rs.at[n, o],
            (2 * to + c, z),
        )

    def collects(self, pair2):
        d, z, c, pair, g, y = self.here
        return lax.div(pair2, self.np_ // 4) == 2 * y + c

    def start(self):
        d, z, c, pair, g, y = self.here
        for s in range(len(self.arrays)):
            for o in range(1, self.np_):
                self.copy(s, o).start()
            self.copy(s, 0).start()
        if self.wo is not None:
            for o in range(self.np_):
                @pl.when(self.collects(lax.rem(pair + o, self.np_)))
                def _():
                    self.copy_wo(o).start()

    def finish(self):
        d, z, c, pair, g, y = self.here
        for s in range(len(self.arrays)):
            for o in range(self.np_):
                self.copy(s, o).wait()
        if self.wo is not None:
            for o in range(self.np_):
                @pl.when(self.collects(lax.rem(pair + o, self.np_)))
                def _():
                    if o == 0:
                        self.copy_wo(o).wait()
                    else:
                        self.copy_wo(o).wait_send()

                if o > 0:
                    @pl.when(self.collects(pair))
                    def _():
                        self.copy_wo(o).wait_recv()


def group_peer(o):
    d, z, c, pair, g, y = place()
    c2 = 1 - c if o % 2 else c
    z2 = z + 1 - 2 * lax.rem(z, 2) if o // 2 else z
    return 2 * pair + c2, z2


class Group:
    def __init__(self, own, all_, ls, ss, rs):
        self.own, self.all_, self.ls, self.ss, self.rs = own, all_, ls, ss, rs
        d, z, c, pair, g, y = place()
        self.k = 2 * y + c

    def copy(self, o):
        if o == 0:
            return pltpu.make_async_copy(self.own, self.all_.at[self.k], self.ls)
        return rcopy(
            self.own, self.all_.at[self.k], self.ss.at[o - 1], self.rs.at[o - 1], group_peer(o)
        )

    def start(self):
        for o in range(4):
            self.copy(o).start()

    def finish(self):
        for o in range(4):
            self.copy(o).wait()


def norm_back(total, x, dy):
    xhat, inverse = norm_parts(x.astype(f32))
    back = inverse * (
        total
        - jnp.mean(total, axis=-1, keepdims=True)
        - xhat * jnp.mean(total * xhat, axis=-1, keepdims=True)
    )
    return dy.astype(f32) + back


def same_slice_peer(np_, e):
    d, z, c, pair, g, y = place()
    to = lax.rem(pair * 2 + g + e, 2 * np_)
    pair2, g2 = lax.div(to, 2), lax.rem(to, 2)
    return to, (2 * pair2 + c, jnp.where(g2 == g, z, 3 - z))


def one_hot_tables(np_, r_in, r_ff, part):
    f = np.arange(D)
    lane = np.arange(PAD)
    place_qkv = (f // part) * D + f % part
    tables_ = [f % r_in, f % r_ff] + [(place_qkv + k * part) % (3 * r_in) for k in range(4)]
    hot = np.stack([(t[:, None] == lane[None, :]) for t in tables_]).astype(np.float32)
    hot[2:, 3 * part :] = 0.0
    return jnp.asarray(hot, bf16), jnp.asarray(place_qkv[None], jnp.int32)


def pieces_of(np_, sums_all, sums, hot_ref, qkv_at, r_in, r_ff, part, msg):
    d, z, c, pair, g, y = place()
    n = 2 * np_
    e = lax.broadcasted_iota(jnp.int32, (n, D), 0)
    f = lax.broadcasted_iota(jnp.int32, (n, D), 1)
    group = lax.rem(e, 2)
    index = (lax.div(e, 2) * 2 + c) * 4 + jnp.where(group == 0, y, 3 - y)

    def select(rows_, inside, hot):
        picked = []
        for row in rows_:
            for v in split3(row):
                picked.append(jnp.where(inside, v, 0.0))
        got = dot(jnp.concatenate(picked, axis=0).astype(bf16), hot)
        return [
            got[3 * s * n : (3 * s + 1) * n] + got[(3 * s + 1) * n : (3 * s + 2) * n]
            + got[(3 * s + 2) * n : (3 * s + 3) * n]
            for s in range(len(rows_))
        ]

    d_vecs = sums_all[0, 0:4] + sums_all[1, 0:4] + sums_all[2, 0:4] + sums_all[3, 0:4]
    rows_ = [d_vecs[s : s + 1] for s in range(4)] + [sums[6:7]]
    inside = jnp.logical_and(f >= index * r_in, f < (index + 1) * r_in)
    got = select(rows_, inside, hot_ref[0])
    first = got[0]
    for s in range(1, 5):
        first = first + pltpu.roll(got[s], s * r_in, 1)
    second = jnp.zeros((n, PAD), f32)
    for k in range(4):
        at = qkv_at[...] + k * part
        inside = jnp.logical_and(at >= index * (3 * r_in), at < (index + 1) * (3 * r_in))
        second = second + select([sums_all[k, 5:6]], inside, hot_ref[2 + k])[0]
    inside = jnp.logical_and(f >= e * r_ff, f < (e + 1) * r_ff)
    third = select([sums[4:5]], inside, hot_ref[1])[0]
    squares = squares_of(d_vecs) + 2.0 * squares_of(sums[6:7])
    for k in range(4):
        squares = squares + squares_of(sums_all[k, 4:6]) + sums_all[k, 7:8, 0:1]
    for s in range(n):
        msg[s, 0:1] = first[s : s + 1]
        msg[s, 1:2] = second[s : s + 1]
        msg[s, 2:3] = third[s : s + 1]
        msg[s, 3:4] = jnp.broadcast_to(squares, (1, PAD))
        msg[s, 4:8] = jnp.zeros((4, PAD), f32)


def meet(np_):
    d, z, c, pair, g, y = place()
    bar = pltpu.get_barrier_semaphore()
    for o in range(1, 8):
        c2, z2 = column_peer(pair, c, z, o)
        pl.semaphore_signal(bar, inc=1, device_id=(2 * pair + c2, z2), device_id_type=MESH)
    for e in range(1, 2 * np_):
        unused, peer = same_slice_peer(np_, e)
        pl.semaphore_signal(bar, inc=1, device_id=peer, device_id_type=MESH)
    pl.semaphore_wait(bar, 7 + 2 * np_ - 1)


def finish_all(
    np_, r_in, r_ff, part_w, red_out, red, swap1, back,
    dw, sums, hot_ref, qkv_at, t1, tq, t2, to, pieces,
    ls_w, ss_w, rs_w, sums_all, ls_g, ss_g, rs_g,
    b1, bq, b2, bo, s1, sq, s2, so, msg, m_all, p_out, ls, ss_m, rs_m, ss, rs,
):
    d, z, c, pair, g, y = place()
    grp = Group(sums, sums_all, ls_g, ss_g, rs_g)
    swap = Swap(np_, [(dw, bq)], None, ls_w, ss_w, rs_w)
    grp.start()
    swap.start()
    red.ready(mirror(0, g))
    grp.finish()
    pieces_of(np_, sums_all, sums, hot_ref, qkv_at, r_in, r_ff, part_w, msg)
    me = pair * 2 + g

    def tell(e):
        to_, peer = same_slice_peer(np_, e)
        return rcopy(msg.at[to_], m_all.at[me], ss_m.at[e], rs_m.at[e], peer)

    own = pltpu.make_async_copy(msg.at[me], m_all.at[me], ls.at[0])
    own.start()
    for e in range(1, 2 * np_):
        tell(e).start()
    red.push(mirror(0, g))
    red.pull(mirror(1, g), back)
    own.wait()
    for e in range(1, 2 * np_):
        tell(e).wait()
    norms = [jnp.sqrt(m_all[e, 3:4, 0:1]) for e in range(2 * np_)]
    mean_norm = sum(norms) / (2 * np_)
    factors = [mean_norm / jnp.maximum(n, mean_norm) for n in norms]
    p_out[...] = sum(f * m_all[e] for e, f in enumerate(factors))
    p_out[4:5, 0:1] = sum(jnp.where(d == e, n, 0.0) for e, n in enumerate(norms))
    group_factors = [
        jnp.where(g == 0, factors[2 * n], factors[2 * n + 1]) for n in range(np_)
    ]
    final = pltpu.make_async_copy(p_out, pieces, ls.at[9])
    final.start()
    collects = swap1.collects(pair)
    swap1.finish()

    def rows_to(s, src, dst, o, slot):
        c2, z2 = column_peer(pair, c, z, o)
        if o == 0:
            return pltpu.make_async_copy(src.at[c2, z2], dst.at[slot], ls.at[5 + s])
        return rcopy(
            src.at[c2, z2], dst.at[slot], ss.at[s, o], rs.at[s, o], (2 * pair + c2, z2)
        )

    def scaled(n, buf, acc, dst):
        for c2 in range(2):
            for z2 in range(4):
                at = pl.ds((c2 * 4 + z2) * r_in, r_in)
                total = sum(f * buf[m, at].astype(f32) for m, f in enumerate(group_factors))
                acc[c2, z2] = total.astype(acc.dtype)
        for o in range(8):
            rows_to(n, acc, dst, o, c * 4 + z).start()

    for t in range(2):
        at = pl.ds(t * r_ff, r_ff)
        total = sum(f * b2[m, at].astype(f32) for m, f in enumerate(group_factors))
        s2[t] = total.astype(s2.dtype)
    mirror_copy = rcopy(s2.at[1 - g], t2.at[1], ss.at[2, 0], rs.at[2, 0], (d, 3 - z))
    mirror_copy.start()
    kept = pltpu.make_async_copy(s2.at[g], t2.at[0], ls.at[7])
    kept.start()
    scaled(1, b1, s1, t1)
    swap.finish()
    scaled(0, bq, sq, tq)

    def wo_to(o):
        c2, z2 = column_peer(pair, c, z, o)
        if o == 0:
            return pltpu.make_async_copy(so.at[c2, z2], to.at[g], ls.at[8])
        return rcopy(
            so.at[c2, z2], to.at[g], ss.at[3, o], rs.at[3, g], (2 * pair + c2, z2)
        )

    @pl.when(collects)
    def _():
        for c2 in range(2):
            for z2 in range(4):
                at = pl.ds((c2 * 4 + z2) * r_in, r_in)
                total = sum(f * bo[m, at].astype(f32) for m, f in enumerate(group_factors))
                so[c2, z2] = total.astype(so.dtype)
        for o in range(8):
            wo_to(o).start()

    red.pull(mirror(0, g), back)
    for n, (acc, dst) in enumerate(((sq, tq), (s1, t1))):
        for o in range(8):
            rows_to(n, acc, dst, o, c * 4 + z).wait()
    mirror_copy.wait()
    kept.wait()

    @pl.when(collects)
    def _():
        wo_to(0).wait()
        for o in range(1, 8):
            wo_to(o).wait_send()

    for t in range(2):
        @pl.when(jnp.logical_or(jnp.logical_not(collects), g != t))
        def _():
            rcopy(so.at[0, 0], to.at[t], ss.at[3, 0], rs.at[3, t], (d, 3 - z)).wait_recv()

    final.wait()
    red_out.finish()
    red.finish()


def local(
    block_in, out_grad, lengths, ln1_gain, ln1_bias, qkv_weight, qkv_bias, out_weight, out_bias,
    ln2_gain, ln2_bias, fc1_weight, fc1_bias, fc2_weight, fc2_bias,
):
    tp = lax.axis_size("ctx")
    dp = lax.axis_size("dp")
    np_ = dp // 2
    world = dp * tp
    d, z, c, pair, g, y = place()
    nh = HEADS // tp
    local_rows = block_in.shape[1]
    t = local_rows * tp
    rows = min(512, local_rows)
    part = D // tp
    r_in = D // world
    r_ff = fc2_weight.shape[0]
    ff = r_ff * dp

    x_own = block_in[0]
    pos = z * local_rows + jnp.arange(local_rows, dtype=jnp.int32)
    dy_own = jnp.where((pos < lengths[0])[:, None], out_grad[0], jnp.zeros((), bf16))

    w_qkv = jnp.moveaxis(qkv_weight.reshape(r_in, 3, tp, part), 2, 0).reshape(tp, r_in, 3 * part)
    w1 = fc1_weight.reshape(r_in, np_, 2, tp, r_ff)
    w1 = jnp.stack([w1[:, :, :, s] for s in (0, 3, 1, 2)], axis=3)
    w1 = w1.reshape(r_in, np_, 2, 2, 2, r_ff).transpose(3, 2, 0, 1, 4, 5).reshape(tp, r_in, ff)
    length_parts = jnp.stack([lengths[0] // 256, lengths[0] % 256]).astype(bf16)
    packed, at = jnp.zeros((16 * PAD,), bf16), 0
    for row_of in (
        (ln1_gain, ln1_bias, out_bias, ln2_gain, ln2_bias), (fc2_bias, qkv_bias),
        (fc1_bias, length_parts),
    ):
        start = at
        for one in row_of:
            packed = packed + jnp.pad(one, (start, 16 * PAD - start - one.shape[0]))
            start += one.shape[0]
        at += PAD
    xq, w_qkv, w1, w2, wo, tab, b_pad, length = gather(
        np_, r_in, r_ff, nh, x_own, w_qkv, w1, fc2_weight, out_weight, packed.reshape(16, PAD)
    )
    x = xq.reshape(t, D)
    w_qkv, w1 = w_qkv.reshape(D, 3 * part), w1.reshape(D, ff)
    cosine, sine = tables(t)
    q, k, v, cf, ctx, dyq, w2, wo = attn_fwd(
        np_, length, x, tab, w_qkv, b_pad, cosine, sine, dy_own, w2, wo, nh, rows
    )
    w2, wo = w2.reshape(ff, D), wo.reshape(part, D)
    out_part, u_mlp, dc, dw1, dw2, dwo, vec = mlp(
        x, dyq.reshape(t, D), ctx, cf, tab, wo, w1, w2, rows
    )
    per = np_ // 4
    block_out, input_grad, t1, tq, t2, to, mine = attn_bwd(
        np_, r_in, r_ff, x, u_mlp, q, k, v, dc, tab, w_qkv, cosine, sine, vec,
        out_part.reshape(4, local_rows, D), xq, dyq, dw1.reshape(np_, D // np_, ff),
        dw2.reshape(np_, 2 * r_ff, D), dwo.reshape(per, part // per, D),
    )
    g_fc1, g_qkv, g_fc2, g_out = assemble(np_, t1, tq, t2, to)
    cut = [mine[0, s * r_in : (s + 1) * r_in] for s in range(5)]
    return (
        block_out[None], input_grad[None],
        cut[0], cut[1], g_qkv, mine[1, : 3 * r_in], g_out, cut[4],
        cut[2], cut[3], g_fc1, mine[2, :r_ff], g_fc2, cut[4],
        mine[4, :1],
    )


def solution(mesh):
    both = ("dp", "ctx")
    vec, mat, act = P(both), P(both, None), P("dp", "ctx", None)
    weights = (vec, vec, mat, vec, mat, vec, vec, vec, mat, vec, mat, vec)
    return jax.shard_map(
        local,
        mesh=mesh,
        in_specs=(act, act, P("dp")) + weights,
        out_specs=(act, act) + weights + (P("dp"),),
        check_vma=False,
    )
```

```python
import functools
import math

import jax
import jax.numpy as jnp
import numpy as np
from jax import lax
from jax.experimental import pallas as pl
from jax.experimental.pallas import tpu as pltpu
from jax.sharding import PartitionSpec as P

D = 768
HEADS = 12
HEAD_DIM = 64
ROT = 16
PAD = 128
eps_norm = 1e-05
neg_big = -1e30
root_half = math.sqrt(0.5)
inv_root_two_pi = 1.0 / math.sqrt(2.0 * math.pi)
f32 = jnp.float32
bf16 = jnp.bfloat16
VMEM_BYTES = 60 * 2**20


def dot(a, b, dims=((1,), (0,))):
    return lax.dot_general(a, b, (dims, ((), ())), preferred_element_type=f32)


def norm_parts(values):
    centered = values - jnp.mean(values, axis=-1, keepdims=True)
    row_var = jnp.mean(centered * centered, axis=-1, keepdims=True)
    inverse = lax.rsqrt(row_var + eps_norm)
    return centered * inverse, inverse


def turn(u, cosine, sine, first):
    partner = jnp.where(first, pltpu.roll(u, PAD - ROT // 2, 1), pltpu.roll(u, ROT // 2, 1))
    return u * cosine + partner * sine


def split3(v):
    hi = v.astype(bf16).astype(f32)
    mid = (v - hi).astype(bf16).astype(f32)
    low = (v - hi - mid).astype(bf16).astype(f32)
    return hi, mid, low


def fold(op, s):
    out = s[:, :PAD]
    for t in range(1, s.shape[1] // PAD):
        out = op(out, s[:, t * PAD : (t + 1) * PAD])
    return out


def attn_fwd_kernel(
    np_, len_ref, x_ref, tab_ref, w_ref, wb_ref, cos_ref, sin_ref, dy, w2, wo,
    q_ref, k_ref, v_ref, cf_ref, c_ref, dyg, w2g, wog,
    w_scr, s_scr, q_scr, m_scr, l_scr, acc_scr, ls_dy, ss_dy, rs_dy, ls_w, ss_w, rs_w,
):
    i = pl.program_id(0)
    nh = k_ref.shape[0]
    rows = x_ref.shape[0]
    spread = Spread(dy, dyg, ls_dy, ss_dy, rs_dy)
    weights = Rows(np_, (w2, w2g), (wo, wog), ls_w, ss_w, rs_w)

    @pl.when(i == 0)
    def _():
        d, z, c, pair, g, y = place()
        barrier_all(np_, d, z, c, pair)
        weights.start()
        spread.start()

    @pl.when(i == 2)
    def _():
        spread.forward(1)

    @pl.when(i == 3)
    def _():
        spread.forward(3)

    @pl.when(i == 0)
    def _():
        for h in range(3 * nh):
            w_scr[:, h * PAD : h * PAD + HEAD_DIM] = w_ref[:, h * HEAD_DIM : (h + 1) * HEAD_DIM]
            w_scr[:, h * PAD + HEAD_DIM : (h + 1) * PAD] = jnp.zeros((D, PAD - HEAD_DIM), bf16)

    xhat, unused = norm_parts(x_ref[...].astype(f32))
    a1 = (xhat * tab_ref[0:1] + tab_ref[1:2]).astype(bf16)
    cosine, sine = cos_ref[...], sin_ref[...]
    lane = lax.broadcasted_iota(jnp.int32, (rows, PAD), 1)
    first = lane < ROT // 2
    key_pos = i * rows + lax.broadcasted_iota(jnp.int32, (rows, PAD), 0)
    key_bias = jnp.where(key_pos.astype(f32) < len_ref[...], 0.0, neg_big)
    here = pl.ds(pl.multiple_of(i * rows, rows), rows)
    qkv = dot(a1, w_scr[...]) + wb_ref[...]
    for h in range(nh):
        q = turn(qkv[:, h * PAD : (h + 1) * PAD], cosine, sine, first) * HEAD_DIM**-0.5
        q_scr[h] = q.astype(bf16)
        k = turn(qkv[:, (nh + h) * PAD : (nh + h + 1) * PAD], cosine, sine, first)
        k_ref[h, here] = jnp.where(lane == HEAD_DIM, key_bias, k).astype(bf16)
        v_ref[h, here] = qkv[:, (2 * nh + h) * PAD : (2 * nh + h + 1) * PAD].astype(bf16)

    causal = lax.broadcasted_iota(jnp.int32, (rows, rows), 0) >= lax.broadcasted_iota(
        jnp.int32, (rows, rows), 1
    )
    for h in range(nh):
        s = dot(q_scr[h], k_ref[h, here], ((1,), (1,)))
        s = jnp.where(causal, s, neg_big)
        s_scr[h, i] = s
        m_scr[h] = fold(jnp.maximum, s)

    def scores(j, carry):
        there = pl.ds(pl.multiple_of(j * rows, rows), rows)
        for h in range(nh):
            s = dot(q_scr[h], k_ref[h, there], ((1,), (1,)))
            s_scr[h, j] = s
            m_scr[h] = jnp.maximum(m_scr[h], fold(jnp.maximum, s))
        return carry

    lax.fori_loop(0, i, scores, 0)

    @pl.when(i == 1)
    def _():
        spread.forward(0)

    @pl.when(i == 2)
    def _():
        spread.forward(2)

    for h in range(nh):
        m_scr[h] = jnp.broadcast_to(jnp.max(m_scr[h], axis=-1, keepdims=True), (rows, PAD))
        l_scr[h] = jnp.zeros((rows, PAD), f32)
        acc_scr[h] = jnp.zeros((rows, PAD), f32)

    def weigh(j, carry):
        there = pl.ds(pl.multiple_of(j * rows, rows), rows)
        for h in range(nh):
            p = jnp.exp(s_scr[h, j] - m_scr[h][:, :1])
            l_scr[h] += fold(jnp.add, p)
            acc_scr[h] += dot(p.astype(bf16), v_ref[h, there])
        return carry

    lax.fori_loop(0, i + 1, weigh, 0)
    for h in range(nh):
        total = jnp.sum(l_scr[h], axis=-1, keepdims=True)
        context = acc_scr[h] / total
        cf_ref[:, h * PAD : (h + 1) * PAD] = context
        c_ref[:, h * HEAD_DIM : (h + 1) * HEAD_DIM] = context[:, :HEAD_DIM].astype(bf16)
        hi, mid, low = split3(-(m_scr[h][:, :1] + jnp.log(total)))
        q = q_scr[h].astype(f32)
        q = jnp.where(lane == HEAD_DIM + 1, hi, q)
        q = jnp.where(lane == HEAD_DIM + 2, mid, q)
        q = jnp.where(lane == HEAD_DIM + 3, low, q)
        q_ref[h] = q.astype(bf16)

    @pl.when(i == pl.num_programs(0) - 1)
    def _():
        spread.finish()
        weights.finish()


def squares_of(m):
    return jnp.sum(jnp.sum(m * m, axis=0, keepdims=True), axis=1, keepdims=True)


def mlp_kernel(
    x_ref, dy_ref, c_ref, cf_ref, tab_ref, wo_ref, w1_ref, w2_ref,
    part_ref, u_ref, dc_ref, dw1_ref, dw2_ref, dwo_ref, vec_ref,
    dw1_scr, dw2_scr, dwo_scr, wo_scr,
):
    i = pl.program_id(0)
    nh = wo_ref.shape[0] // HEAD_DIM
    rows = x_ref.shape[0]

    @pl.when(i == 0)
    def _():
        dw1_scr[...] = jnp.zeros_like(dw1_scr)
        dw2_scr[...] = jnp.zeros_like(dw2_scr)
        dwo_scr[...] = jnp.zeros_like(dwo_scr)
        vec_ref[...] = jnp.zeros_like(vec_ref)
        for h in range(nh):
            wo_scr[h * PAD : h * PAD + HEAD_DIM] = wo_ref[h * HEAD_DIM : (h + 1) * HEAD_DIM]
            wo_scr[h * PAD + HEAD_DIM : (h + 1) * PAD] = jnp.zeros((PAD - HEAD_DIM, D), bf16)

    xhat, unused = norm_parts(x_ref[...].astype(f32))
    gain = tab_ref[3:4]
    a2 = (xhat * gain + tab_ref[4:5]).astype(bf16)
    z = dot(a2, w1_ref[...]) + tab_ref[5:6]
    cdf = 0.5 * (1.0 + lax.erf(z * root_half))
    hidden = (z * cdf).astype(bf16)
    context = c_ref[...]
    part = dot(hidden, w2_ref[...]) + dot(context, wo_ref[...])
    part_ref[...] = part.astype(part_ref.dtype)
    dy = dy_ref[...]
    slope = cdf + z * jnp.exp(-0.5 * z * z) * inv_root_two_pi
    dz = (dot(dy, w2_ref[...], ((1,), (1,))) * slope).astype(bf16)

    da2 = dot(dz, w1_ref[...], ((1,), (1,)))
    u_ref[...] = (da2 * gain).astype(u_ref.dtype)
    lane = lax.broadcasted_iota(jnp.int32, (rows, PAD), 1)
    dc_all = dot(dy, wo_scr[...], ((1,), (1,))).astype(bf16)
    for h in range(nh):
        dc = dc_all[:, h * PAD : (h + 1) * PAD].astype(f32)
        delta = jnp.sum(dc * cf_ref[:, h * PAD : (h + 1) * PAD], axis=-1, keepdims=True)
        hi, mid, low = split3(-delta)
        dc = jnp.where(lane == HEAD_DIM, hi, dc)
        dc = jnp.where(lane == HEAD_DIM + 1, mid, dc)
        dc = jnp.where(lane == HEAD_DIM + 2, low, dc)
        dc_ref[h] = dc.astype(bf16)
    dw1_scr[...] += dot(a2, dz, ((0,), (0,)))
    dw2_scr[...] += dot(hidden, dy, ((0,), (0,)))
    dwo_scr[...] += dot(context, dy, ((0,), (0,)))
    vec_ref[2:3] += jnp.sum(da2 * xhat, axis=0, keepdims=True)
    vec_ref[3:4] += jnp.sum(da2, axis=0, keepdims=True)
    vec_ref[4:5] += jnp.sum(dz.astype(f32), axis=0, keepdims=True)
    vec_ref[6:7] += jnp.sum(dy.astype(f32), axis=0, keepdims=True)

    @pl.when(i == pl.num_programs(0) - 1)
    def _():
        dw1_ref[...] = dw1_scr[...].astype(bf16)
        dw2_ref[...] = dw2_scr[...].astype(bf16)
        dwo_ref[...] = dwo_scr[...].astype(bf16)
        vec_ref[7:8, 0:1] = (
            squares_of(dw1_scr[...]) + squares_of(dw2_scr[...]) + squares_of(dwo_scr[...])
        )


def attn_bwd_kernel(
    np_, r_in, r_ff, x_ref, u_in_ref, q_ref, k_ref, v_ref, dc_ref, tab_ref, w_ref,
    cos_ref, sin_ref, vec_in_ref, hot_ref, qkv_at, part, xg, dyg, dw1, dw2, dwo,
    block_out, input_grad, t1, tq, t2, to, pieces,
    dk_scr, dv_scr, dq_scr, dqkv_scr, dw_scr, vec_ref, u_scr, dw,
    from_sib, from_far, to_far, mine, done, xq, ls_o, ss_o, rs_o,
    from_sib2, from_far2, to_far2, done2, dyq, ls_u, ss_u, rs_u,
    ls_s, ss_s, rs_s, ls_w, ss_w, rs_w, sums_all, ls_g, ss_g, rs_g,
    b1, bq, b2, bo, s1, sq, s2, so, msg, m_all, p_out, ls, ss_m, rs_m, ss, rs,
):
    step = pl.program_id(0)
    blocks = pl.num_programs(0)
    g, y = place()[4:6]
    b = far_first(step)
    nh = k_ref.shape[0]
    rows = x_ref.shape[0]
    wide = 3 * nh * HEAD_DIM
    lane = lax.broadcasted_iota(jnp.int32, (rows, PAD), 1)
    first = lane < ROT // 2

    def block_rows(n):
        return pl.ds(pl.multiple_of(n * rows, rows), rows)

    here = block_rows(b)
    red = Reduce(
        part, block_out, [(xg, xq)], (from_sib, from_far, to_far, mine, done), ls_o, ss_o, rs_o
    )
    red_u = ReduceQuarters(
        u_scr, input_grad, (from_sib2, from_far2, to_far2, done2), ls_u, ss_u, rs_u
    )
    swap = Swap(np_, [(dw1, b1), (dw2, b2)], (dwo, bo), ls_s, ss_s, rs_s)

    load_dy = pltpu.make_async_copy(dyg.at[red.q_here], dyq, ls.at[4])

    def back(total, r):
        return norm_back(total, xq[r], dyq[r])

    @pl.when(step == 0)
    def _():
        meet(np_)
        red.start()
        load_dy.start()
        swap.start()
        dk_scr[...] = jnp.zeros_like(dk_scr)
        dv_scr[...] = jnp.zeros_like(dv_scr)
        dq_scr[...] = jnp.zeros_like(dq_scr)
        dw_scr[...] = jnp.zeros_like(dw_scr)
        vec_ref[...] = vec_in_ref[...]

    causal = lax.broadcasted_iota(jnp.int32, (rows, rows), 0) <= lax.broadcasted_iota(
        jnp.int32, (rows, rows), 1
    )

    def block(n, m, diagonal):
        asks, keys = block_rows(n), block_rows(m)
        for h in range(nh):
            k = k_ref[h, keys]
            q = q_ref[h, asks]
            dc = dc_ref[h, asks]
            pt = jnp.exp(dot(k, q, ((1,), (1,))))
            if diagonal:
                pt = jnp.where(causal, pt, 0.0)
            dpt = dot(v_ref[h, keys], dc, ((1,), (1,)))
            dst = (pt * dpt).astype(bf16)
            dv_scr[h, keys] += dot(pt.astype(bf16), dc)
            dk_scr[h, keys] += dot(dst, q)
            dq_scr[h, asks] += dot(dst, k, ((0,), (0,)))

    block(b, b, True)

    @pl.when(step == 0)
    def _():
        red.add_near()

    def off(n, carry):
        block(jnp.where(g == 0, b, b + 1 + n), jnp.where(g == 0, n, b), False)
        return carry

    lax.fori_loop(0, blocks - 1 - step, off, 0)

    @pl.when(step == 1)
    def _():
        red.add_far(lambda total, r: xq[r].astype(f32) + tab_ref[2:3] + total)
        load_dy.wait()

    @pl.when(step == 3)
    def _():
        red_u.pull(mirror(2, g), back)

    cosine, sine = cos_ref[...], -sin_ref[...]
    for h in range(nh):
        dq = turn(dq_scr[h, here], cosine, sine, first) * HEAD_DIM**-0.5
        dk = turn(dk_scr[h, here], cosine, sine, first)
        for at, piece in ((h, dq), (nh + h, dk), (2 * nh + h, dv_scr[h, here])):
            dqkv_scr[:, at * HEAD_DIM : (at + 1) * HEAD_DIM] = piece[:, :HEAD_DIM].astype(bf16)
    dqkv = dqkv_scr[...]
    xhat, unused = norm_parts(x_ref[...].astype(f32))
    gain = tab_ref[0:1]
    a1 = (xhat * gain + tab_ref[1:2]).astype(bf16)
    da1 = dot(dqkv, w_ref[...], ((1,), (1,)))
    u_scr[b] = (u_in_ref[...] + da1 * gain).astype(bf16)

    @pl.when(step < blocks - 1)
    def _():
        red_u.ready(b)

    dw_scr[...] += dot(a1, dqkv, ((0,), (0,)))
    vec_ref[0:1] += jnp.sum(da1 * xhat, axis=0, keepdims=True)
    vec_ref[1:2] += jnp.sum(da1, axis=0, keepdims=True)
    vec_ref[5:6, :wide] += jnp.sum(dqkv.astype(f32), axis=0, keepdims=True)

    @pl.when(step < blocks - 1)
    def _():
        red_u.push(b)

    @pl.when(step == 2)
    def _():
        red_u.pull(mirror(3, g), back)

    @pl.when(step == blocks - 1)
    def _():
        vec_ref[7:8, 0:1] += squares_of(dw_scr[...])
        share = D // np_
        for n in range(np_):
            dw[n] = dw_scr[n * share : (n + 1) * share].astype(bf16)
        finish_all(
            np_, r_in, r_ff, wide // 3, red, red_u, swap, back,
            dw, vec_ref, hot_ref, qkv_at, t1, tq, t2, to, pieces,
            ls_w, ss_w, rs_w, sums_all, ls_g, ss_g, rs_g,
            b1, bq, b2, bo, s1, sq, s2, so, msg, m_all, p_out, ls, ss_m, rs_m, ss, rs,
        )


def whole(shape):
    return pl.BlockSpec(shape, lambda i: (0,) * len(shape), pipeline_mode=pl.Buffered(1))


def sds(shape, dtype):
    return jax.ShapeDtypeStruct(shape, dtype)


def params(collective_id=None):
    return pltpu.CompilerParams(
        dimension_semantics=("arbitrary",), vmem_limit_bytes=VMEM_BYTES,
        collective_id=collective_id, has_side_effects=collective_id is not None,
    )


def weight_sems(np_, n):
    return [
        pltpu.SemaphoreType.DMA((n,)),
        pltpu.SemaphoreType.DMA((n, 8 + np_)),
        pltpu.SemaphoreType.DMA((n, 8 + np_)),
    ]


def attn_fwd(np_, length, x, tab, w, wb, cosine, sine, dy, w2, wo, nh, rows):
    t = x.shape[0]
    lanes = pl.BlockSpec((rows, PAD), lambda i: (i, 0))
    any_ = pl.BlockSpec(memory_space=pl.ANY)
    return pl.pallas_call(
        functools.partial(attn_fwd_kernel, np_),
        grid=(t // rows,),
        out_shape=(
            sds((nh, t, PAD), bf16), sds((nh, t, PAD), bf16), sds((nh, t, PAD), bf16),
            sds((t, nh * PAD), f32), sds((t, nh * HEAD_DIM), bf16),
            sds((4,) + dy.shape, bf16),
            sds((np_,) + w2.shape, bf16), sds(wo.shape, bf16),
        ),
        in_specs=[
            whole((1, PAD)), pl.BlockSpec((rows, D), lambda i: (i, 0)),
            whole((8, D)), whole(w.shape), whole(wb.shape), lanes, lanes,
            pl.BlockSpec(memory_space=pltpu.VMEM), any_, any_,
        ],
        out_specs=(
            pl.BlockSpec((nh, rows, PAD), lambda i: (0, i, 0)),
            whole((nh, t, PAD)), whole((nh, t, PAD)),
            pl.BlockSpec((rows, nh * PAD), lambda i: (i, 0)),
            pl.BlockSpec((rows, nh * HEAD_DIM), lambda i: (i, 0)),
            any_, any_, any_,
        ),
        scratch_shapes=[
            pltpu.VMEM((D, 3 * nh * PAD), bf16),
            pltpu.VMEM((nh, t // rows, rows, rows), f32),
            pltpu.VMEM((nh, rows, PAD), bf16),
            pltpu.VMEM((nh, rows, PAD), f32),
            pltpu.VMEM((nh, rows, PAD), f32),
            pltpu.VMEM((nh, rows, PAD), f32),
        ] + spread_sems() + swap_sems(np_, 2),
        compiler_params=params(2),
        name="attn_fwd",
    )(length, x, tab, w, wb, cosine, sine, dy, w2, wo)


def far_first(i):
    return mirror(3 - i, place()[4])


def mlp(x, dy, c, cf, tab, wo, w1, w2, rows):
    t = x.shape[0]
    ff = w1.shape[1]
    nh = wo.shape[0] // HEAD_DIM
    at = lambda cols: pl.BlockSpec((rows, cols), lambda i: (i, 0))
    vm = pltpu.VMEM
    return pl.pallas_call(
        mlp_kernel,
        grid=(t // rows,),
        out_shape=(
            sds((t, D), bf16), sds((t, D), f32), sds((nh, t, PAD), bf16), sds((D, ff), bf16),
            sds((ff, D), bf16), sds(wo.shape, bf16), sds((8, D), f32),
        ),
        in_specs=[
            at(D), at(D), at(c.shape[1]), at(cf.shape[1]),
            whole((8, D)), whole(wo.shape), whole(w1.shape), whole(w2.shape),
        ],
        out_specs=(
            at(D), at(D), pl.BlockSpec((nh, rows, PAD), lambda i: (0, i, 0)),
            whole((D, ff)), whole((ff, D)), whole(wo.shape), whole((8, D)),
        ),
        scratch_shapes=[
            vm((D, ff), f32), vm((ff, D), f32), vm(wo.shape, f32), vm((nh * PAD, D), bf16),
        ],
        compiler_params=params(),
        name="mlp",
    )(x, dy, c, cf, tab, wo, w1, w2)


def attn_bwd(
    np_, r_in, r_ff, x, u_in, q, k, v, dc, tab, w, cosine, sine, vec,
    part, xg, dyg, dw1, dw2, dwo,
):
    t = x.shape[0]
    nh = q.shape[0]
    wide = w.shape[1]
    quarter = part.shape[1]
    ff = dw1.shape[2]
    at = lambda cols: pl.BlockSpec((quarter, cols), lambda i: (far_first(i), 0))
    any_ = pl.BlockSpec(memory_space=pl.ANY)
    dma = pltpu.SemaphoreType.DMA
    vm = pltpu.VMEM
    hot, qkv_at = one_hot_tables(np_, r_in, r_ff, wide // 3)
    per_owner = lambda cols: vm((2, 4, r_in, cols), bf16)
    block = vm((quarter, D), bf16)
    return pl.pallas_call(
        functools.partial(attn_bwd_kernel, np_, r_in, r_ff),
        grid=(4,),
        out_shape=(
            sds((quarter, D), bf16), sds((quarter, D), bf16), sds((8, r_in, ff), bf16),
            sds((8, r_in, wide), bf16), sds((2, r_ff, D), bf16), sds((2, r_in, D), bf16),
            sds((8, PAD), f32),
        ),
        in_specs=[
            at(D), at(D), whole(q.shape), whole(k.shape), whole(v.shape), whole(dc.shape),
            whole((8, D)), whole(w.shape), at(PAD), at(PAD), whole((8, D)), whole(hot.shape),
            whole(qkv_at.shape),
        ] + [any_] * 6,
        out_specs=(any_,) * 7,
        scratch_shapes=[
            vm((nh, t, PAD), f32), vm((nh, t, PAD), f32), vm((nh, t, PAD), f32),
            vm((quarter, wide), bf16), vm((D, wide), f32), vm((8, D), f32),
            vm((4, quarter, D), bf16), vm((np_, D // np_, wide), bf16),
        ] + reduce_scratch(quarter, 1) + [
            vm((2, quarter, D), bf16), block, block, block, block,
            dma((5,)), dma((4, PIECES)), dma((4, PIECES)),
        ] + swap_sems(np_, 3) + swap_sems(np_, 1) + [
            vm((4, 8, D), f32), dma, dma((3,)), dma((3,)),
            vm(dw1.shape, bf16), vm((np_, D // np_, wide), bf16), vm(dw2.shape, bf16),
            vm((np_,) + dwo.shape[1:], bf16),
            per_owner(ff), per_owner(wide), vm((2, r_ff, D), bf16), per_owner(D),
            vm((2 * np_, 8, PAD), f32), vm((2 * np_, 8, PAD), f32), vm((8, PAD), f32),
            dma((10,)), dma((2 * np_,)), dma((2 * np_,)), dma((4, 8)), dma((4, 8)),
        ],
        compiler_params=params(3),
        name="attn_bwd",
    )(
        x, u_in, q, k, v, dc, tab, w, cosine, sine, vec, hot, qkv_at,
        part, xg, dyg, dw1, dw2, dwo,
    )


def assemble_kernel(
    np_, out_in, grad_in, t1, tq, t2, to, pieces,
    out_o, grad_o, g1, b1, qkv, qkv_b, out, out_b, g2, b2, fc1, fc1_b, fc2, fc2_b, norm,
):
    r_ff, r_in = t2.shape[1], t1.shape[1]
    part_w = tq.shape[2] // 3
    out_o[...] = out_in[...]
    grad_o[...] = grad_in[...]
    for s, ref in enumerate((g1, b1, g2, b2, out_b)):
        ref[...] = pieces[0, s * r_in : (s + 1) * r_in]
    fc2_b[...] = pieces[0, 4 * r_in : 5 * r_in]
    qkv_b[...] = pieces[1, : 3 * r_in]
    fc1_b[...] = pieces[2, :r_ff]
    norm[...] = pieces[4, :1]
    for c in range(2):
        for y in range(2):
            a, b = (0, 3) if y == 0 else (1, 2)
            up = t1[4 * c + a].astype(f32) + t1[4 * c + b].astype(f32)
            for pair in range(np_):
                for e, z in enumerate((a, b)):
                    to_at = r_ff * (4 * (2 * pair + c) + z)
                    at = r_ff * (2 * pair + e)
                    fc1[:, to_at : to_at + r_ff] = up[:, at : at + r_ff]
            into = tq[4 * c + a].astype(f32) + tq[4 * c + b].astype(f32)
            for s in range(3):
                to_at = s * D + (2 * y + c) * part_w
                qkv[:, to_at : to_at + part_w] = into[:, s * part_w : (s + 1) * part_w]
    fc2[...] = t2[0].astype(f32) + t2[1].astype(f32)
    out[...] = to[0].astype(f32) + to[1].astype(f32)


def assemble(np_, out, grad, t1, tq, t2, to, pieces):
    r_in, r_ff = t1.shape[1], t2.shape[1]
    vmem = pl.BlockSpec(memory_space=pltpu.VMEM)
    vec = sds((r_in,), f32)
    outs = (
        sds(out.shape, bf16), sds(grad.shape, bf16), vec, vec,
        sds((r_in, tq.shape[2] * 4), f32), sds((3 * r_in,), f32), sds(to.shape[1:], f32), vec,
        vec, vec, sds((r_in, t1.shape[2] * 4), f32), sds((r_ff,), f32), sds(t2.shape[1:], f32),
        vec, sds((1,), f32),
    )
    return pl.pallas_call(
        functools.partial(assemble_kernel, np_),
        out_shape=outs,
        in_specs=[vmem] * 7,
        out_specs=(vmem,) * len(outs),
        name="assemble",
    )(out, grad, t1, tq, t2, to, pieces)


def swap_sems(np_, n):
    return [
        pltpu.SemaphoreType.DMA((n,)),
        pltpu.SemaphoreType.DMA((n, np_)),
        pltpu.SemaphoreType.DMA((n, np_)),
    ]


def tables(t):
    inv_freqs = np.exp(np.arange(ROT // 2, dtype=np.float32) * np.float32(-2.0 * math.log(10000.0) / ROT))
    angles = np.arange(t, dtype=np.float32)[:, None] * inv_freqs.astype(np.float32)[None, :]
    cosine = np.ones((t, PAD), np.float32)
    sine = np.zeros((t, PAD), np.float32)
    half = ROT // 2
    cosine[:, :half] = cosine[:, half:ROT] = np.cos(angles)
    sine[:, :half] = -np.sin(angles)
    sine[:, half:ROT] = np.sin(angles)
    return jnp.asarray(cosine), jnp.asarray(sine)


MESH = pl.DeviceIdType.MESH
AX = ("dp", "ctx")
CHUNKS = 4


def place():
    d, z = lax.axis_index("dp"), lax.axis_index("ctx")
    c, pair, g = lax.rem(d, 2), lax.div(d, 2), lax.div(z, 2)
    y = lax.rem(g + lax.rem(z, 2), 2)
    return d, z, c, pair, g, y


def mirror(m, g):
    return jnp.where(g == 0, m, 3 - m)


def rcopy(src, dst, ss, rs, device):
    return pltpu.make_async_remote_copy(
        src_ref=src, dst_ref=dst, send_sem=ss, recv_sem=rs, device_id=device, device_id_type=MESH
    )


def column_peer(pair, c, z, o):
    m = lax.rem(c * 4 + z + o, 8)
    return lax.div(m, 4), lax.rem(m, 4)


def barrier_all(np_, d, z, c, pair):
    bar = pltpu.get_barrier_semaphore()
    for o in range(1, 8):
        c2, z2 = column_peer(pair, c, z, o)
        pl.semaphore_signal(bar, inc=1, device_id=(2 * pair + c2, z2), device_id_type=MESH)
    for o in range(1, np_):
        pl.semaphore_signal(
            bar, inc=1, device_id=(2 * lax.rem(pair + o, np_) + c, z), device_id_type=MESH
        )
    pl.semaphore_wait(bar, 7 + np_ - 1)


class Spread:
    def __init__(self, own, out, ls, ss, rs):
        self.own, self.out, self.ls, self.ss, self.rs = own, out, ls, ss, rs
        self.rows = out.shape[1] // CHUNKS
        d, z, c, pair, g, y = place()
        self.d, self.z, self.c, self.g, self.y = d, z, c, g, y
        self.prim = c == g
        self.sib = (d + 1 - 2 * c, z)
        self.partner = (d, z + 1 - 2 * lax.rem(z, 2))
        self.far = (d, 1 + c)

    def cut(self, ref, j):
        return ref.at[pl.ds(j * self.rows, self.rows)]

    def send(self, q, j, way, device, src=None):
        src = self.cut(self.out.at[q], j) if src is None else src
        return rcopy(
            src, self.cut(self.out.at[q], j), self.ss.at[way, q, j], self.rs.at[q, j], device
        )

    def start(self):
        own = [self.cut(self.own, j) for j in range(CHUNKS)]

        @pl.when(self.prim)
        def _():
            pltpu.make_async_copy(self.own, self.out.at[self.z], self.ls).start()
            for j in range(CHUNKS):
                self.send(self.z, j, 0, self.partner, own[j]).start()
            for j in range(CHUNKS):
                self.send(self.z, j, 1, self.sib, own[j]).start()

        @pl.when(jnp.logical_not(self.prim))
        def _():
            for j in range(CHUNKS):
                self.send(self.z, j, 0, self.far, own[j]).start()

    def wait_recv(self, q, j):
        self.send(q, j, 0, self.sib).wait_recv()

    def forward(self, j):
        far = (mirror(2, self.g), mirror(3, self.g))
        end, mid = mirror(0, self.g), mirror(1, self.g)

        @pl.when(jnp.logical_and(self.prim, self.y == 1))
        def _():
            for q in far:
                self.wait_recv(q, j)
                self.send(q, j, 0, self.partner).start()
                self.send(q, j, 1, self.sib).start()
            self.wait_recv(end, j)
            self.send(end, j, 1, self.sib).start()

        @pl.when(jnp.logical_and(self.prim, self.y == 0))
        def _():
            self.wait_recv(mid, j)
            self.send(mid, j, 1, self.sib).start()
            if j > 0:
                for q in far:
                    self.wait_recv(q, j - 1)
                    self.send(q, j - 1, 1, self.sib).start()

    def finish(self):
        far = (mirror(2, self.g), mirror(3, self.g))
        end, mid = mirror(0, self.g), mirror(1, self.g)

        @pl.when(jnp.logical_and(self.prim, self.y == 0))
        def _():
            for q in far:
                self.wait_recv(q, CHUNKS - 1)
                self.send(q, CHUNKS - 1, 1, self.sib).start()
            for j in range(CHUNKS):
                self.send(end, j, 0, self.partner).wait_send()

        @pl.when(jnp.logical_and(self.prim, self.y == 1))
        def _():
            for j in range(CHUNKS):
                for q in far + (mid,):
                    self.send(q, j, 0, self.partner).wait_send()

        @pl.when(self.prim)
        def _():
            pltpu.make_async_copy(self.own, self.out.at[self.z], self.ls).wait()
            for q in range(4):
                for j in range(CHUNKS):
                    self.send(q, j, 1, self.sib).wait_send()

        @pl.when(jnp.logical_not(self.prim))
        def _():
            for q in range(4):
                for j in range(CHUNKS):
                    self.wait_recv(q, j)
            for j in range(CHUNKS):
                self.send(self.z, j, 0, self.far).wait_send()


class Weights:
    def __init__(self, np_, sliced, w2, wo, ls, ss, rs):
        self.np_, self.sliced, self.w2, self.wo = np_, sliced, w2, wo
        self.ls, self.ss, self.rs = ls, ss, rs
        self.here = place()

    def first(self, s, o):
        d, z, c, pair, g, y = self.here
        src, out, by_slice = self.sliced[s]
        if o == 0:
            return pltpu.make_async_copy(
                src.at[2 * y + c] if by_slice else src, out.at[pair, c, z], self.ls.at[s]
            )
        c2, z2 = column_peer(pair, c, z, o)
        y2 = lax.rem(lax.div(z2, 2) + lax.rem(z2, 2), 2)
        return rcopy(
            src.at[2 * y2 + c2] if by_slice else src, out.at[pair, c, z],
            self.ss.at[s, o - 1], self.rs.at[s, o - 1], (2 * pair + c2, z2),
        )

    def second(self, s, o):
        d, z, c, pair, g, y = self.here
        out = self.sliced[s][1]
        return rcopy(
            out.at[pair], out.at[pair], self.ss.at[s, 7 + o - 1], self.rs.at[s, 7 + o - 1],
            (2 * lax.rem(pair + o, self.np_) + c, z),
        )

    def start(self):
        d, z, c, pair, g, y = self.here
        n = len(self.sliced)
        for s in range(n):
            for o in range(8):
                self.first(s, o).start()

    def start_rows(self):
        for o in range(2):
            self.w2_first(o).start()
        self.wo_first(lambda cp: cp.start())

    def w2_first(self, o):
        d, z, c, pair, g, y = self.here
        src, out = self.w2
        n = len(self.sliced)
        if o == 0:
            return pltpu.make_async_copy(src, out.at[g], self.ls.at[n])
        return rcopy(src, out.at[g], self.ss.at[n, 0], self.rs.at[n, 0], (d, 3 - z))

    def wo_parts(self):
        d, z, c, pair, g, y = self.here
        per = self.np_ // 4
        owner = lax.div(pair, per)
        return per, owner, lax.rem(owner, 2), lax.div(owner, 2)

    def wo_first(self, do, sending=True):
        d, z, c, pair, g, y = self.here
        src, out = self.wo
        n = len(self.sliced) + 1
        per, owner, c_to, y_to = self.wo_parts()
        slot = out.at[lax.rem(pair, per), c, z]
        for t in range(2):
            z_to = jnp.where(t == 0, y_to, 3 - y_to)
            mine = jnp.logical_and(c == c_to, z == z_to)

            @pl.when(mine)
            def _():
                do(pltpu.make_async_copy(src, slot, self.ls.at[n]))

            @pl.when(jnp.logical_not(mine))
            def _():
                cp = rcopy(
                    src, slot, self.ss.at[n, t], self.rs.at[n, c * 4 + z], (2 * pair + c_to, z_to)
                )
                do(cp)

    def between(self, s):
        self.first(s, 0).wait()
        for o in range(1, 8):
            self.first(s, o).wait_recv()
        for o in range(1, self.np_):
            self.second(s, o).start()

    def finish_rows(self):
        d, z, c, pair, g, y = self.here
        n = len(self.sliced) + 1
        per, owner, c_to, y_to = self.wo_parts()
        for o in range(2):
            self.w2_first(o).wait()

        @pl.when(owner == 2 * y + c)
        def _():
            for c2 in range(2):
                for z2 in range(4):
                    own = jnp.logical_and(c == c2, z == z2)

                    @pl.when(jnp.logical_not(own))
                    def _():
                        slot = self.wo[1].at[0, c2, z2]
                        rcopy(
                            slot, slot, self.ss.at[n, 0], self.rs.at[n, c2 * 4 + z2],
                            (d + 1 - 2 * c, z),
                        ).wait_recv()
            pltpu.make_async_copy(
                self.wo[0], self.wo[1].at[0, c, z], self.ls.at[n]
            ).wait()

        for t in range(2):
            z_to = jnp.where(t == 0, y_to, 3 - y_to)

            @pl.when(jnp.logical_not(jnp.logical_and(c == c_to, z == z_to)))
            def _():
                rcopy(
                    self.wo[0], self.wo[1].at[0, c, z], self.ss.at[n, t], self.rs.at[n, 0],
                    (d + 1 - 2 * c, z),
                ).wait_send()

    def finish(self, s):
        for o in range(1, 8):
            self.first(s, o).wait_send()
        for o in range(1, self.np_):
            self.second(s, o).wait()


class Rows:
    def __init__(self, np_, w2, wo, ls, ss, rs):
        self.np_, self.w2, self.wo, self.ls, self.ss, self.rs = np_, w2, wo, ls, ss, rs
        self.here = place()

    def copy_w2(self, o):
        d, z, c, pair, g, y = self.here
        src, out = self.w2
        if o == 0:
            return pltpu.make_async_copy(src, out.at[pair], self.ls.at[0])
        to = (2 * lax.rem(pair + o, self.np_) + c, z)
        return rcopy(src, out.at[pair], self.ss.at[0, o], self.rs.at[0, o], to)

    def copy_wo(self, o):
        d, z, c, pair, g, y = self.here
        src, out = self.wo
        slot = lax.rem(pair, self.np_ // 4)
        if o == 0:
            return pltpu.make_async_copy(src.at[slot], out.at[slot], self.ls.at[1])
        to = (2 * lax.rem(pair + o, self.np_) + c, z)
        return rcopy(src.at[slot], out.at[slot], self.ss.at[1, o], self.rs.at[1, o], to)

    def holds(self, pair):
        d, z, c, unused, g, y = self.here
        return lax.div(pair, self.np_ // 4) == 2 * y + c

    def start(self):
        @pl.when(self.holds(self.here[3]))
        def _():
            for o in range(1, self.np_):
                self.copy_wo(o).start()
            self.copy_wo(0).start()

        for o in range(1, self.np_):
            self.copy_w2(o).start()
        self.copy_w2(0).start()

    def finish(self):
        pair = self.here[3]
        for o in range(self.np_):
            self.copy_w2(o).wait()

        @pl.when(self.holds(pair))
        def _():
            self.copy_wo(0).wait()
            for o in range(1, self.np_):
                self.copy_wo(o).wait_send()

        for o in range(1, self.np_):
            @pl.when(self.holds(lax.rem(pair + self.np_ - o, self.np_)))
            def _():
                self.copy_wo(o).wait_recv()


def decode_tables(np_, r_in, r_ff, part, nh):
    wide = 3 * nh * PAD
    f = np.arange(D)
    by_d = np.zeros((8, D), np.int32)
    by_d[0], by_d[1] = f // r_in, f % r_in
    by_d[2], by_d[3], by_d[4] = f // (2 * r_ff), (f // r_ff) % 2, f % r_ff
    p = np.arange(wide)
    head, lane = p // PAD, p % PAD
    by_q = np.full((8, wide), -1, np.int32)
    for k in range(4):
        at = (head // nh) * D + k * part + (head % nh) * HEAD_DIM + lane
        real = lane < HEAD_DIM
        by_q[k, real] = (at // (3 * r_in))[real]
        by_q[4 + k, real] = (r_in + at % (3 * r_in))[real]
    extra = np.zeros((1, wide), np.float32)
    extra[0, (head < nh) & (lane == HEAD_DIM)] = HEAD_DIM**0.5
    keys = (head >= nh) & (head < 2 * nh)
    extra[0, keys & (lane > HEAD_DIM) & (lane < HEAD_DIM + 4)] = 1.0
    extra[0, (head >= 2 * nh) & (lane >= HEAD_DIM) & (lane < HEAD_DIM + 3)] = 1.0
    return jnp.asarray(by_d), jnp.asarray(by_q), jnp.asarray(extra)


def decode(np_, r_in, r_ff, vec, by_d, by_q, extra, tab, b_pad, length):
    d, z, c, pair, g, y = place()
    world = 8 * np_
    packed = vec[...].reshape(world * 16, PAD)
    m = lax.broadcasted_iota(jnp.int32, (world, world * 16), 1)
    n = lax.broadcasted_iota(jnp.int32, (world, world * 16), 0)
    row = [
        dot(jnp.where(m == 16 * n + r, 1.0, 0.0).astype(bf16), packed).astype(bf16)
        for r in range(3)
    ]

    def pick(x, lanes, owner):
        w = lanes.shape[1]
        hot = lax.broadcasted_iota(jnp.int32, (PAD, w), 0) == lanes
        got = dot(x, jnp.where(hot, 1.0, 0.0).astype(bf16))
        mine = lax.broadcasted_iota(jnp.int32, (world, w), 0) == owner
        return jnp.sum(jnp.where(mine, got, 0.0), axis=0, keepdims=True)

    owner, lanes = by_d[0:1], by_d[1:2]
    tab[0:1] = pick(row[0], lanes, owner)
    tab[1:2] = pick(row[0], lanes + r_in, owner)
    tab[2:3] = pick(row[0], lanes + 2 * r_in, owner) + pick(row[1], lanes, owner)
    tab[3:4] = pick(row[0], lanes + 3 * r_in, owner)
    tab[4:5] = pick(row[0], lanes + 4 * r_in, owner)
    owner = by_d[2:3] * 8 + c * 4 + jnp.where(by_d[3:4] == 0, y, 3 - y)
    tab[5:6] = pick(row[2], by_d[4:5], owner)
    tab[6:8] = jnp.zeros((2, D), f32)
    k = 2 * y + c
    b_pad[...] = pick(row[1], by_q[pl.ds(4 + k, 1)], by_q[pl.ds(k, 1)]) + extra[...]
    mine = lax.broadcasted_iota(jnp.int32, (world, PAD), 0) == (2 * pair + g) * 4
    parts = jnp.sum(jnp.where(mine, row[2].astype(f32), 0.0), axis=0, keepdims=True)
    lane = lax.broadcasted_iota(jnp.int32, (1, PAD), 1)
    parts = jnp.where(lane == r_ff, parts * 256.0, jnp.where(lane == r_ff + 1, parts, 0.0))
    length[...] = jnp.broadcast_to(jnp.sum(parts, axis=1, keepdims=True), (1, PAD))


def gather_kernel(
    np_, r_in, r_ff, len_ref, x, grad, qkv_w, fc1_w, w2, wo, vec_own, by_d, by_q, extra,
    xg, dy_own, wqg, w1g, w2p, wop, tab, b_pad, length, wq, w1, dy, ls_m, vec, ls_x, ss_x, rs_x, ls_w, ss_w, rs_w,
):
    d, z, c, pair, g, y = place()
    load = pltpu.make_async_copy(grad, dy, ls_m.at[0])
    load.start()
    part_w = wq.shape[2] // 3
    for k in range(4):
        y2, c2 = k // 2, k % 2
        for s in range(3):
            at = s * D + k * part_w
            wq[k, :, s * part_w : (s + 1) * part_w] = qkv_w[:, at : at + part_w]
        for n in range(np_):
            for e, z2 in enumerate((0, 3) if y2 == 0 else (1, 2)):
                at = r_ff * (4 * (2 * n + c2) + z2)
                to = r_ff * (2 * n + e)
                w1[k, :, to : to + r_ff] = fc1_w[:, at : at + r_ff]
    barrier_all(np_, d, z, c, pair)
    spread = Spread(x, xg, ls_x, ss_x, rs_x)
    weights = Weights(
        np_, [(vec_own, vec, False), (wq, wqg, True), (w1, w1g, True)], (w2, w2p), (wo, wop),
        ls_w, ss_w, rs_w,
    )
    weights.start()
    spread.start()
    weights.start_rows()
    load.wait()
    pos = z * dy.shape[0] + lax.broadcasted_iota(jnp.int32, (dy.shape[0], 1), 0)
    dy[...] = jnp.where(pos < len_ref[0], dy[...].astype(f32), 0.0).astype(bf16)
    store = pltpu.make_async_copy(dy, dy_own, ls_m.at[1])
    store.start()
    for s in range(3):
        weights.between(s)
    spread.forward(0)
    weights.finish(0)
    decode(np_, r_in, r_ff, vec, by_d, by_q, extra, tab, b_pad, length)
    for j in range(1, CHUNKS):
        spread.forward(j)
    spread.finish()
    for s in range(1, 3):
        weights.finish(s)
    weights.finish_rows()
    store.wait()


def spread_sems():
    return [
        pltpu.SemaphoreType.DMA,
        pltpu.SemaphoreType.DMA((2, 4, CHUNKS)),
        pltpu.SemaphoreType.DMA((4, CHUNKS)),
    ]


def gather(
    np_, r_in, r_ff, nh, length, x, grad, qkv_w, fc1_w, w2, wo, vec, collective_id=1
):
    any_ = pl.BlockSpec(memory_space=pl.ANY)
    vmem = pl.BlockSpec(memory_space=pltpu.VMEM)
    wide = 3 * nh * PAD
    thin, ff = qkv_w.shape[1] // 4, fc1_w.shape[1] // 4
    return pl.pallas_call(
        functools.partial(gather_kernel, np_, r_in, r_ff),
        out_shape=(
            sds((4,) + x.shape, bf16), sds(x.shape, bf16), sds((np_, 2, 4, r_in, thin), bf16),
            sds((np_, 2, 4, r_in, ff), bf16), sds((2,) + w2.shape, bf16),
            sds((np_ // 4, 2, 4) + wo.shape, bf16),
            sds((8, D), f32), sds((1, wide), f32), sds((1, PAD), f32),
        ),
        in_specs=[pl.BlockSpec(memory_space=pltpu.SMEM), any_, any_, vmem, vmem, any_, any_, any_]
        + [vmem] * 3,
        out_specs=(any_,) * 6 + (vmem,) * 3,
        scratch_shapes=[
            pltpu.VMEM((4, r_in, thin), bf16), pltpu.VMEM((4, r_in, ff), bf16),
            pltpu.VMEM(x.shape, bf16), pltpu.SemaphoreType.DMA((2,)),
            pltpu.VMEM((np_, 2, 4, 16, PAD), bf16),
        ] + spread_sems() + weight_sems(np_, 5),
        compiler_params=pltpu.CompilerParams(
            collective_id=collective_id, has_side_effects=True, vmem_limit_bytes=VMEM_BYTES
        ),
        name="gather",
    )(length, x, grad, qkv_w, fc1_w, w2, wo, vec, *decode_tables(np_, r_in, r_ff, thin // 3, nh))


PIECES = 4


class Reduce:
    def __init__(self, part, out, extra, bufs, ls, ss, rs):
        self.part, self.out, self.extra = part, out, extra
        self.from_sib, self.from_far, self.to_far, self.mine, self.done = bufs
        self.ls, self.ss, self.rs = ls, ss, rs
        d, z, c, pair, g, y = place()
        self.role = jnp.where(c == g, 0, 1)
        self.y = y
        self.sib = (d + 1 - 2 * c, z)
        self.partner = (d, z + 1 - 2 * lax.rem(z, 2))
        self.q_here = mirror(2 * y + self.role, g)
        self.q_there = mirror(2 * (1 - y) + self.role, g)
        self.sib_here = mirror(2 * y + 1 - self.role, g)
        self.sib_there = mirror(2 * (1 - y) + 1 - self.role, g)
        self.owner = (2 * pair + g, self.q_here)
        self.self_owner = jnp.logical_and(self.role == 0, y == 0)
        self.self_source = jnp.where(c == 0, z, 3 - z) == 0
        self.rows = self.out.shape[0] // PIECES

    def rows_of(self, j):
        return pl.ds(j * self.rows, self.rows)

    def to_sib(self, t, j):
        q = self.sib_there if t == 0 else self.sib_here
        r = self.rows_of(j)
        return rcopy(
            self.part.at[q, r], self.from_sib.at[t, r], self.ss.at[t, j], self.rs.at[t, j], self.sib
        )

    def load(self, t):
        q = self.q_there if t == 0 else self.q_here
        return pltpu.make_async_copy(self.part.at[q], self.mine.at[t], self.ls.at[t])

    def load_extra(self, e):
        src, dst = self.extra[e]
        return pltpu.make_async_copy(src.at[self.q_here], dst, self.ls.at[2 + e])

    def across(self, j):
        r = self.rows_of(j)
        return rcopy(
            self.to_far.at[r], self.from_far.at[r], self.ss.at[2, j], self.rs.at[2, j], self.partner
        )

    def home(self, j):
        r = self.rows_of(j)
        return rcopy(
            self.done.at[r], self.out.at[r], self.ss.at[3, j], self.rs.at[3, j], self.owner
        )

    def keep(self):
        return pltpu.make_async_copy(self.done, self.out, self.ls.at[4])

    def start(self):
        for t in range(2):
            for j in range(PIECES):
                self.to_sib(t, j).start()
        for t in range(2):
            self.load(t).start()
        for e in range(len(self.extra)):
            self.load_extra(e).start()

    def add_near(self):
        self.load(0).wait()
        for j in range(PIECES):
            r = self.rows_of(j)
            self.to_sib(0, j).wait_recv()
            total = self.mine[0, r].astype(f32) + self.from_sib[0, r].astype(f32)
            self.to_far[r] = total.astype(bf16)
            self.across(j).start()
        self.load(1).wait()
        for e in range(len(self.extra)):
            self.load_extra(e).wait()

    def add_far(self, finish):
        for j in range(PIECES):
            r = self.rows_of(j)
            self.to_sib(1, j).wait_recv()
            self.across(j).wait_recv()
            total = self.mine[1, r].astype(f32) + self.from_sib[1, r].astype(f32)
            total = total + self.from_far[r].astype(f32)
            self.done[r] = finish(total, r).astype(bf16)

            @pl.when(jnp.logical_not(self.self_owner))
            def _():
                self.home(j).start()

    def finish(self):
        @pl.when(self.self_owner)
        def _():
            self.keep().start()
            self.keep().wait()

        for j in range(PIECES):
            @pl.when(jnp.logical_not(self.self_source))
            def _():
                self.home(j).wait_recv()

        for j in range(PIECES):
            self.to_sib(0, j).wait_send()
            self.to_sib(1, j).wait_send()
            self.across(j).wait_send()

            @pl.when(jnp.logical_not(self.self_owner))
            def _():
                self.home(j).wait_send()


def reduce_scratch(rows, extras):
    return [
        pltpu.VMEM((2, rows, D), bf16), pltpu.VMEM((rows, D), bf16), pltpu.VMEM((rows, D), bf16),
        pltpu.VMEM((2, rows, D), bf16), pltpu.VMEM((rows, D), bf16),
    ] + [pltpu.VMEM((rows, D), bf16)] * extras + [
        pltpu.SemaphoreType.DMA((5,)),
        pltpu.SemaphoreType.DMA((4, PIECES)),
        pltpu.SemaphoreType.DMA((4, PIECES)),
    ]


class ReduceQuarters(Reduce):
    def __init__(self, part, out, bufs, ls, ss, rs):
        from_sib, from_far, to_far, done = bufs
        super().__init__(part, out, [], (from_sib, from_far, to_far, None, done), ls, ss, rs)

    def ready(self, q):
        for t, mine in ((0, self.sib_there), (1, self.sib_here)):
            @pl.when(mine == q)
            def _():
                for j in range(PIECES):
                    self.to_sib(t, j).start()

    def push(self, q):
        @pl.when(self.q_there == q)
        def _():
            for j in range(PIECES):
                r = self.rows_of(j)
                self.to_sib(0, j).wait_recv()
                total = self.part[q, r].astype(f32) + self.from_sib[0, r].astype(f32)
                self.to_far[r] = total.astype(bf16)
                self.across(j).start()

    def pull(self, q, finish):
        @pl.when(self.q_here == q)
        def _():
            for j in range(PIECES):
                r = self.rows_of(j)
                self.to_sib(1, j).wait_recv()
                self.across(j).wait_recv()
                total = self.part[q, r].astype(f32) + self.from_sib[1, r].astype(f32)
                total = total + self.from_far[r].astype(f32)
                self.done[r] = finish(total, r).astype(bf16)

                @pl.when(jnp.logical_not(self.self_owner))
                def _():
                    self.home(j).start()


class Swap:
    def __init__(self, np_, arrays, wo, ls, ss, rs):
        self.np_, self.arrays, self.wo, self.ls, self.ss, self.rs = np_, arrays, wo, ls, ss, rs
        self.here = place()

    def copy(self, s, o):
        d, z, c, pair, g, y = self.here
        src, dst = self.arrays[s]
        to = lax.rem(pair + o, self.np_)
        if o == 0:
            return pltpu.make_async_copy(src.at[pair], dst.at[pair], self.ls.at[s])
        return rcopy(
            src.at[to], dst.at[pair], self.ss.at[s, o], self.rs.at[s, o], (2 * to + c, z)
        )

    def copy_wo(self, o):
        d, z, c, pair, g, y = self.here
        src, dst = self.wo
        n = len(self.arrays)
        per = self.np_ // 4
        to = lax.rem(pair + o, self.np_)
        if o == 0:
            return pltpu.make_async_copy(src.at[lax.rem(pair, per)], dst.at[pair], self.ls.at[n])
        return rcopy(
            src.at[lax.rem(to, per)], dst.at[pair], self.ss.at[n, o], self.rs.at[n, o],
            (2 * to + c, z),
        )

    def collects(self, pair2):
        d, z, c, pair, g, y = self.here
        return lax.div(pair2, self.np_ // 4) == 2 * y + c

    def start(self):
        d, z, c, pair, g, y = self.here
        for s in range(len(self.arrays)):
            for o in range(1, self.np_):
                self.copy(s, o).start()
            self.copy(s, 0).start()
        if self.wo is not None:
            for o in range(self.np_):
                @pl.when(self.collects(lax.rem(pair + o, self.np_)))
                def _():
                    self.copy_wo(o).start()

    def finish(self):
        d, z, c, pair, g, y = self.here
        for s in range(len(self.arrays)):
            for o in range(self.np_):
                self.copy(s, o).wait()
        if self.wo is not None:
            for o in range(self.np_):
                @pl.when(self.collects(lax.rem(pair + o, self.np_)))
                def _():
                    if o == 0:
                        self.copy_wo(o).wait()
                    else:
                        self.copy_wo(o).wait_send()

                if o > 0:
                    @pl.when(self.collects(pair))
                    def _():
                        self.copy_wo(o).wait_recv()


def group_peer(o):
    d, z, c, pair, g, y = place()
    c2 = 1 - c if o % 2 else c
    z2 = z + 1 - 2 * lax.rem(z, 2) if o // 2 else z
    return 2 * pair + c2, z2


class Group:
    def __init__(self, own, all_, ls, ss, rs):
        self.own, self.all_, self.ls, self.ss, self.rs = own, all_, ls, ss, rs
        d, z, c, pair, g, y = place()
        self.k = 2 * y + c

    def copy(self, o):
        if o == 0:
            return pltpu.make_async_copy(self.own, self.all_.at[self.k], self.ls)
        return rcopy(
            self.own, self.all_.at[self.k], self.ss.at[o - 1], self.rs.at[o - 1], group_peer(o)
        )

    def start(self):
        for o in range(4):
            self.copy(o).start()

    def finish(self):
        for o in range(4):
            self.copy(o).wait()


def norm_back(total, x, dy):
    xhat, inverse = norm_parts(x.astype(f32))
    back = inverse * (
        total
        - jnp.mean(total, axis=-1, keepdims=True)
        - xhat * jnp.mean(total * xhat, axis=-1, keepdims=True)
    )
    return dy.astype(f32) + back


def same_slice_peer(np_, e):
    d, z, c, pair, g, y = place()
    to = lax.rem(pair * 2 + g + e, 2 * np_)
    pair2, g2 = lax.div(to, 2), lax.rem(to, 2)
    return to, (2 * pair2 + c, jnp.where(g2 == g, z, 3 - z))


def one_hot_tables(np_, r_in, r_ff, part):
    f = np.arange(D)
    lane = np.arange(PAD)
    place_qkv = (f // part) * D + f % part
    tables_ = [f % r_in, f % r_ff] + [(place_qkv + k * part) % (3 * r_in) for k in range(4)]
    hot = np.stack([(t[:, None] == lane[None, :]) for t in tables_]).astype(np.float32)
    hot[2:, 3 * part :] = 0.0
    return jnp.asarray(hot, bf16), jnp.asarray(place_qkv[None], jnp.int32)


def pieces_of(np_, sums_all, sums, hot_ref, qkv_at, r_in, r_ff, part, msg):
    d, z, c, pair, g, y = place()
    n = 2 * np_
    e = lax.broadcasted_iota(jnp.int32, (n, D), 0)
    f = lax.broadcasted_iota(jnp.int32, (n, D), 1)
    group = lax.rem(e, 2)
    index = (lax.div(e, 2) * 2 + c) * 4 + jnp.where(group == 0, y, 3 - y)

    def select(rows_, inside, hot):
        picked = []
        for row in rows_:
            for v in split3(row):
                picked.append(jnp.where(inside, v, 0.0))
        got = dot(jnp.concatenate(picked, axis=0).astype(bf16), hot)
        return [
            got[3 * s * n : (3 * s + 1) * n] + got[(3 * s + 1) * n : (3 * s + 2) * n]
            + got[(3 * s + 2) * n : (3 * s + 3) * n]
            for s in range(len(rows_))
        ]

    d_vecs = sums_all[0, 0:4] + sums_all[1, 0:4] + sums_all[2, 0:4] + sums_all[3, 0:4]
    rows_ = [d_vecs[s : s + 1] for s in range(4)] + [sums[6:7]]
    inside = jnp.logical_and(f >= index * r_in, f < (index + 1) * r_in)
    got = select(rows_, inside, hot_ref[0])
    first = got[0]
    for s in range(1, 5):
        first = first + pltpu.roll(got[s], s * r_in, 1)
    second = jnp.zeros((n, PAD), f32)
    for k in range(4):
        at = qkv_at[...] + k * part
        inside = jnp.logical_and(at >= index * (3 * r_in), at < (index + 1) * (3 * r_in))
        second = second + select([sums_all[k, 5:6]], inside, hot_ref[2 + k])[0]
    inside = jnp.logical_and(f >= e * r_ff, f < (e + 1) * r_ff)
    third = select([sums[4:5]], inside, hot_ref[1])[0]
    squares = squares_of(d_vecs) + 2.0 * squares_of(sums[6:7])
    for k in range(4):
        squares = squares + squares_of(sums_all[k, 4:6]) + sums_all[k, 7:8, 0:1]
    for s in range(n):
        msg[s, 0:1] = first[s : s + 1]
        msg[s, 1:2] = second[s : s + 1]
        msg[s, 2:3] = third[s : s + 1]
        msg[s, 3:4] = jnp.broadcast_to(squares, (1, PAD))
        msg[s, 4:8] = jnp.zeros((4, PAD), f32)


def meet(np_):
    d, z, c, pair, g, y = place()
    bar = pltpu.get_barrier_semaphore()
    for o in range(1, 8):
        c2, z2 = column_peer(pair, c, z, o)
        pl.semaphore_signal(bar, inc=1, device_id=(2 * pair + c2, z2), device_id_type=MESH)
    for e in range(1, 2 * np_):
        unused, peer = same_slice_peer(np_, e)
        pl.semaphore_signal(bar, inc=1, device_id=peer, device_id_type=MESH)
    pl.semaphore_wait(bar, 7 + 2 * np_ - 1)


def finish_all(
    np_, r_in, r_ff, part_w, red_out, red, swap1, back,
    dw, sums, hot_ref, qkv_at, t1, tq, t2, to, pieces,
    ls_w, ss_w, rs_w, sums_all, ls_g, ss_g, rs_g,
    b1, bq, b2, bo, s1, sq, s2, so, msg, m_all, p_out, ls, ss_m, rs_m, ss, rs,
):
    d, z, c, pair, g, y = place()
    grp = Group(sums, sums_all, ls_g, ss_g, rs_g)
    swap = Swap(np_, [(dw, bq)], None, ls_w, ss_w, rs_w)
    grp.start()
    swap.start()
    red.ready(mirror(0, g))
    grp.finish()
    pieces_of(np_, sums_all, sums, hot_ref, qkv_at, r_in, r_ff, part_w, msg)
    me = pair * 2 + g

    def tell(e):
        to_, peer = same_slice_peer(np_, e)
        return rcopy(msg.at[to_], m_all.at[me], ss_m.at[e], rs_m.at[e], peer)

    own = pltpu.make_async_copy(msg.at[me], m_all.at[me], ls.at[0])
    own.start()
    for e in range(1, 2 * np_):
        tell(e).start()
    red.push(mirror(0, g))
    red.pull(mirror(1, g), back)
    own.wait()
    for e in range(1, 2 * np_):
        tell(e).wait()
    norms = [jnp.sqrt(m_all[e, 3:4, 0:1]) for e in range(2 * np_)]
    mean_norm = sum(norms) / (2 * np_)
    factors = [mean_norm / jnp.maximum(n, mean_norm) for n in norms]
    p_out[...] = sum(f * m_all[e] for e, f in enumerate(factors))
    p_out[4:5, 0:1] = sum(jnp.where(d == e, n, 0.0) for e, n in enumerate(norms))
    group_factors = [
        jnp.where(g == 0, factors[2 * n], factors[2 * n + 1]) for n in range(np_)
    ]
    final = pltpu.make_async_copy(p_out, pieces, ls.at[9])
    final.start()
    collects = swap1.collects(pair)
    swap1.finish()

    def rows_to(s, src, dst, o, slot):
        c2, z2 = column_peer(pair, c, z, o)
        if o == 0:
            return pltpu.make_async_copy(src.at[c2, z2], dst.at[slot], ls.at[5 + s])
        return rcopy(
            src.at[c2, z2], dst.at[slot], ss.at[s, o], rs.at[s, o], (2 * pair + c2, z2)
        )

    def scaled(n, buf, acc, dst):
        for c2 in range(2):
            for z2 in range(4):
                at = pl.ds((c2 * 4 + z2) * r_in, r_in)
                total = sum(f * buf[m, at].astype(f32) for m, f in enumerate(group_factors))
                acc[c2, z2] = total.astype(acc.dtype)
        for o in range(8):
            rows_to(n, acc, dst, o, c * 4 + z).start()

    for t in range(2):
        at = pl.ds(t * r_ff, r_ff)
        total = sum(f * b2[m, at].astype(f32) for m, f in enumerate(group_factors))
        s2[t] = total.astype(s2.dtype)
    mirror_copy = rcopy(s2.at[1 - g], t2.at[1], ss.at[2, 0], rs.at[2, 0], (d, 3 - z))
    mirror_copy.start()
    kept = pltpu.make_async_copy(s2.at[g], t2.at[0], ls.at[7])
    kept.start()
    scaled(1, b1, s1, t1)
    swap.finish()
    scaled(0, bq, sq, tq)

    def wo_to(o):
        c2, z2 = column_peer(pair, c, z, o)
        if o == 0:
            return pltpu.make_async_copy(so.at[c2, z2], to.at[g], ls.at[8])
        return rcopy(
            so.at[c2, z2], to.at[g], ss.at[3, o], rs.at[3, g], (2 * pair + c2, z2)
        )

    @pl.when(collects)
    def _():
        for c2 in range(2):
            for z2 in range(4):
                at = pl.ds((c2 * 4 + z2) * r_in, r_in)
                total = sum(f * bo[m, at].astype(f32) for m, f in enumerate(group_factors))
                so[c2, z2] = total.astype(so.dtype)
        for o in range(8):
            wo_to(o).start()

    red.pull(mirror(0, g), back)
    for n, (acc, dst) in enumerate(((sq, tq), (s1, t1))):
        for o in range(8):
            rows_to(n, acc, dst, o, c * 4 + z).wait()
    mirror_copy.wait()
    kept.wait()

    @pl.when(collects)
    def _():
        wo_to(0).wait()
        for o in range(1, 8):
            wo_to(o).wait_send()

    for t in range(2):
        @pl.when(jnp.logical_or(jnp.logical_not(collects), g != t))
        def _():
            rcopy(so.at[0, 0], to.at[t], ss.at[3, 0], rs.at[3, t], (d, 3 - z)).wait_recv()

    final.wait()
    red_out.finish()
    red.finish()


def local(
    block_in, out_grad, lengths, ln1_gain, ln1_bias, qkv_weight, qkv_bias, out_weight, out_bias,
    ln2_gain, ln2_bias, fc1_weight, fc1_bias, fc2_weight, fc2_bias,
):
    tp = lax.axis_size("ctx")
    dp = lax.axis_size("dp")
    np_ = dp // 2
    world = dp * tp
    nh = HEADS // tp
    local_rows = block_in.shape[1]
    t = local_rows * tp
    rows = min(512, local_rows)
    part = D // tp
    r_in = D // world
    r_ff = fc2_weight.shape[0]
    ff = r_ff * dp

    length_parts = jnp.stack([lengths[0] // 256, lengths[0] % 256]).astype(bf16)
    packed, at = jnp.zeros((16 * PAD,), bf16), 0
    for row_of in (
        (ln1_gain, ln1_bias, out_bias, ln2_gain, ln2_bias), (fc2_bias, qkv_bias),
        (fc1_bias, length_parts),
    ):
        start = at
        for one in row_of:
            packed = packed + jnp.pad(one, (start, 16 * PAD - start - one.shape[0]))
            start += one.shape[0]
        at += PAD
    xq, dy_own, w_qkv, w1, w2, wo, tab, b_pad, length = gather(
        np_, r_in, r_ff, nh, lengths, block_in[0], out_grad[0], qkv_weight, fc1_weight, fc2_weight,
        out_weight, packed.reshape(16, PAD),
    )
    x = xq.reshape(t, D)
    w_qkv, w1 = w_qkv.reshape(D, 3 * part), w1.reshape(D, ff)
    cosine, sine = tables(t)
    q, k, v, cf, ctx, dyq, w2, wo = attn_fwd(
        np_, length, x, tab, w_qkv, b_pad, cosine, sine, dy_own, w2, wo, nh, rows
    )
    w2, wo = w2.reshape(ff, D), wo.reshape(part, D)
    out_part, u_mlp, dc, dw1, dw2, dwo, vec = mlp(
        x, dyq.reshape(t, D), ctx, cf, tab, wo, w1, w2, rows
    )
    per = np_ // 4
    block_out, input_grad, t1, tq, t2, to, mine = attn_bwd(
        np_, r_in, r_ff, x, u_mlp, q, k, v, dc, tab, w_qkv, cosine, sine, vec,
        out_part.reshape(4, local_rows, D), xq, dyq, dw1.reshape(np_, D // np_, ff),
        dw2.reshape(np_, 2 * r_ff, D), dwo.reshape(per, part // per, D),
    )
    outs = assemble(np_, block_out, input_grad, t1, tq, t2, to, mine)
    return (outs[0][None], outs[1][None]) + tuple(outs[2:])


def solution(mesh):
    both = ("dp", "ctx")
    vec, mat, act = P(both), P(both, None), P("dp", "ctx", None)
    weights = (vec, vec, mat, vec, mat, vec, vec, vec, mat, vec, mat, vec)
    return jax.shard_map(
        local,
        mesh=mesh,
        in_specs=(act, act, P("dp")) + weights,
        out_specs=(act, act) + weights + (P("dp"),),
        check_vma=False,
    )
```

```python
import functools
import math

import jax
import jax.numpy as jnp
import numpy as np
from jax import lax
from jax.experimental import pallas as pl
from jax.experimental.pallas import tpu as pltpu
from jax.sharding import PartitionSpec as P

D = 768
HEADS = 12
HEAD_DIM = 64
ROT = 16
PAD = 128
eps_norm = 1e-05
neg_big = -1e30
root_half = math.sqrt(0.5)
inv_root_two_pi = 1.0 / math.sqrt(2.0 * math.pi)
f32 = jnp.float32
bf16 = jnp.bfloat16
VMEM_BYTES = 60 * 2**20


def dot(a, b, dims=((1,), (0,))):
    return lax.dot_general(a, b, (dims, ((), ())), preferred_element_type=f32)


def norm_parts(values):
    centered = values - jnp.mean(values, axis=-1, keepdims=True)
    row_var = jnp.mean(centered * centered, axis=-1, keepdims=True)
    inverse = lax.rsqrt(row_var + eps_norm)
    return centered * inverse, inverse


def turn(u, cosine, sine, first):
    partner = jnp.where(first, pltpu.roll(u, PAD - ROT // 2, 1), pltpu.roll(u, ROT // 2, 1))
    return u * cosine + partner * sine


def split3(v):
    hi = v.astype(bf16).astype(f32)
    mid = (v - hi).astype(bf16).astype(f32)
    low = (v - hi - mid).astype(bf16).astype(f32)
    return hi, mid, low


def fold(op, s):
    out = s[:, :PAD]
    for t in range(1, s.shape[1] // PAD):
        out = op(out, s[:, t * PAD : (t + 1) * PAD])
    return out


def attn_fwd_kernel(
    np_, len_ref, x_ref, tab_ref, w_ref, wb_ref, cos_ref, sin_ref, dy, w2, wo,
    q_ref, k_ref, v_ref, cf_ref, c_ref, dyg, w2g, wog,
    w_scr, s_scr, q_scr, m_scr, l_scr, acc_scr, ls_dy, ss_dy, rs_dy, ls_w, ss_w, rs_w,
):
    i = pl.program_id(0)
    nh = k_ref.shape[0]
    rows = x_ref.shape[0]
    spread = Spread(dy, dyg, ls_dy, ss_dy, rs_dy)
    weights = Rows(np_, (w2, w2g), (wo, wog), ls_w, ss_w, rs_w)

    @pl.when(i == 0)
    def _():
        d, z, c, pair, g, y = place()
        barrier_all(np_, d, z, c, pair)
        weights.start()
        spread.start()

    @pl.when(i == 2)
    def _():
        spread.forward(1)

    @pl.when(i == 3)
    def _():
        spread.forward(3)

    @pl.when(i == 0)
    def _():
        for h in range(3 * nh):
            w_scr[:, h * PAD : h * PAD + HEAD_DIM] = w_ref[:, h * HEAD_DIM : (h + 1) * HEAD_DIM]
            w_scr[:, h * PAD + HEAD_DIM : (h + 1) * PAD] = jnp.zeros((D, PAD - HEAD_DIM), bf16)

    xhat, unused = norm_parts(x_ref[...].astype(f32))
    a1 = (xhat * tab_ref[0:1] + tab_ref[1:2]).astype(bf16)
    cosine, sine = cos_ref[...], sin_ref[...]
    lane = lax.broadcasted_iota(jnp.int32, (rows, PAD), 1)
    first = lane < ROT // 2
    key_pos = i * rows + lax.broadcasted_iota(jnp.int32, (rows, PAD), 0)
    key_bias = jnp.where(key_pos.astype(f32) < len_ref[...], 0.0, neg_big)
    here = pl.ds(pl.multiple_of(i * rows, rows), rows)
    qkv = dot(a1, w_scr[...]) + wb_ref[...]
    for h in range(nh):
        q = turn(qkv[:, h * PAD : (h + 1) * PAD], cosine, sine, first) * HEAD_DIM**-0.5
        q_scr[h] = q.astype(bf16)
        k = turn(qkv[:, (nh + h) * PAD : (nh + h + 1) * PAD], cosine, sine, first)
        k_ref[h, here] = jnp.where(lane == HEAD_DIM, key_bias, k).astype(bf16)
        v_ref[h, here] = qkv[:, (2 * nh + h) * PAD : (2 * nh + h + 1) * PAD].astype(bf16)

    causal = lax.broadcasted_iota(jnp.int32, (rows, rows), 0) >= lax.broadcasted_iota(
        jnp.int32, (rows, rows), 1
    )
    for h in range(nh):
        s = dot(q_scr[h], k_ref[h, here], ((1,), (1,)))
        s = jnp.where(causal, s, neg_big)
        s_scr[h, i] = s
        m_scr[h] = fold(jnp.maximum, s)

    def scores(j, carry):
        there = pl.ds(pl.multiple_of(j * rows, rows), rows)
        for h in range(nh):
            s = dot(q_scr[h], k_ref[h, there], ((1,), (1,)))
            s_scr[h, j] = s
            m_scr[h] = jnp.maximum(m_scr[h], fold(jnp.maximum, s))
        return carry

    lax.fori_loop(0, i, scores, 0)

    @pl.when(i == 1)
    def _():
        spread.forward(0)

    @pl.when(i == 2)
    def _():
        spread.forward(2)

    for h in range(nh):
        m_scr[h] = jnp.broadcast_to(jnp.max(m_scr[h], axis=-1, keepdims=True), (rows, PAD))
        l_scr[h] = jnp.zeros((rows, PAD), f32)
        acc_scr[h] = jnp.zeros((rows, PAD), f32)

    def weigh(j, carry):
        there = pl.ds(pl.multiple_of(j * rows, rows), rows)
        for h in range(nh):
            p = jnp.exp(s_scr[h, j] - m_scr[h][:, :1])
            l_scr[h] += fold(jnp.add, p)
            acc_scr[h] += dot(p.astype(bf16), v_ref[h, there])
        return carry

    lax.fori_loop(0, i + 1, weigh, 0)
    for h in range(nh):
        total = jnp.sum(l_scr[h], axis=-1, keepdims=True)
        context = acc_scr[h] / total
        cf_ref[:, h * PAD : (h + 1) * PAD] = context
        c_ref[:, h * HEAD_DIM : (h + 1) * HEAD_DIM] = context[:, :HEAD_DIM].astype(bf16)
        hi, mid, low = split3(-(m_scr[h][:, :1] + jnp.log(total)))
        q = q_scr[h].astype(f32)
        q = jnp.where(lane == HEAD_DIM + 1, hi, q)
        q = jnp.where(lane == HEAD_DIM + 2, mid, q)
        q = jnp.where(lane == HEAD_DIM + 3, low, q)
        q_ref[h] = q.astype(bf16)

    @pl.when(i == pl.num_programs(0) - 1)
    def _():
        spread.finish()
        weights.finish()


def squares_of(m):
    return jnp.sum(jnp.sum(m * m, axis=0, keepdims=True), axis=1, keepdims=True)


def mlp_kernel(
    x_ref, dy_ref, c_ref, cf_ref, tab_ref, wo_ref, w1_ref, w2_ref,
    part_ref, u_ref, dc_ref, dw1_ref, dw2_ref, dwo_ref, vec_ref,
    dw1_scr, dw2_scr, dwo_scr, wo_scr,
):
    i = pl.program_id(0)
    nh = wo_ref.shape[0] // HEAD_DIM
    rows = x_ref.shape[0]

    @pl.when(i == 0)
    def _():
        dw1_scr[...] = jnp.zeros_like(dw1_scr)
        dw2_scr[...] = jnp.zeros_like(dw2_scr)
        dwo_scr[...] = jnp.zeros_like(dwo_scr)
        vec_ref[...] = jnp.zeros_like(vec_ref)
        for h in range(nh):
            wo_scr[h * PAD : h * PAD + HEAD_DIM] = wo_ref[h * HEAD_DIM : (h + 1) * HEAD_DIM]
            wo_scr[h * PAD + HEAD_DIM : (h + 1) * PAD] = jnp.zeros((PAD - HEAD_DIM, D), bf16)

    xhat, unused = norm_parts(x_ref[...].astype(f32))
    gain = tab_ref[3:4]
    a2 = (xhat * gain + tab_ref[4:5]).astype(bf16)
    z = dot(a2, w1_ref[...]) + tab_ref[5:6]
    cdf = 0.5 * (1.0 + lax.erf(z * root_half))
    hidden = (z * cdf).astype(bf16)
    context = c_ref[...]
    part = dot(hidden, w2_ref[...]) + dot(context, wo_ref[...])
    part_ref[...] = part.astype(part_ref.dtype)
    dy = dy_ref[...]
    slope = cdf + z * jnp.exp(-0.5 * z * z) * inv_root_two_pi
    dz = (dot(dy, w2_ref[...], ((1,), (1,))) * slope).astype(bf16)

    da2 = dot(dz, w1_ref[...], ((1,), (1,)))
    u_ref[...] = (da2 * gain).astype(u_ref.dtype)
    lane = lax.broadcasted_iota(jnp.int32, (rows, PAD), 1)
    dc_all = dot(dy, wo_scr[...], ((1,), (1,))).astype(bf16)
    for h in range(nh):
        dc = dc_all[:, h * PAD : (h + 1) * PAD].astype(f32)
        delta = jnp.sum(dc * cf_ref[:, h * PAD : (h + 1) * PAD], axis=-1, keepdims=True)
        hi, mid, low = split3(-delta)
        dc = jnp.where(lane == HEAD_DIM, hi, dc)
        dc = jnp.where(lane == HEAD_DIM + 1, mid, dc)
        dc = jnp.where(lane == HEAD_DIM + 2, low, dc)
        dc_ref[h] = dc.astype(bf16)
    dw1_scr[...] += dot(a2, dz, ((0,), (0,)))
    dw2_scr[...] += dot(hidden, dy, ((0,), (0,)))
    dwo_scr[...] += dot(context, dy, ((0,), (0,)))
    vec_ref[2:3] += jnp.sum(da2 * xhat, axis=0, keepdims=True)
    vec_ref[3:4] += jnp.sum(da2, axis=0, keepdims=True)
    vec_ref[4:5] += jnp.sum(dz.astype(f32), axis=0, keepdims=True)
    vec_ref[6:7] += jnp.sum(dy.astype(f32), axis=0, keepdims=True)

    @pl.when(i == pl.num_programs(0) - 1)
    def _():
        dw1_ref[...] = dw1_scr[...].astype(bf16)
        dw2_ref[...] = dw2_scr[...].astype(bf16)
        dwo_ref[...] = dwo_scr[...].astype(bf16)
        vec_ref[7:8, 0:1] = (
            squares_of(dw1_scr[...]) + squares_of(dw2_scr[...]) + squares_of(dwo_scr[...])
        )


def attn_bwd_kernel(
    np_, r_in, r_ff, x_ref, u_in_ref, q_ref, k_ref, v_ref, dc_ref, tab_ref, w_ref,
    cos_ref, sin_ref, vec_in_ref, hot_ref, qkv_at, part, xg, dyg, dw1, dw2, dwo,
    block_out, input_grad, t1, tq, t2, to, pieces,
    dk_scr, dv_scr, dq_scr, dqkv_scr, dw_scr, vec_ref, u_scr, dw,
    from_sib, from_far, to_far, mine, done, xq, ls_o, ss_o, rs_o,
    from_sib2, from_far2, to_far2, done2, dyq, ls_u, ss_u, rs_u,
    ls_s, ss_s, rs_s, ls_w, ss_w, rs_w, sums_all, ls_g, ss_g, rs_g,
    b1, bq, b2, bo, s1, sq, s2, so, msg, m_all, p_out, ls, ss_m, rs_m, ss, rs,
):
    step = pl.program_id(0)
    blocks = pl.num_programs(0)
    g, y = place()[4:6]
    b = far_first(step)
    nh = k_ref.shape[0]
    rows = x_ref.shape[0]
    wide = 3 * nh * HEAD_DIM
    lane = lax.broadcasted_iota(jnp.int32, (rows, PAD), 1)
    first = lane < ROT // 2

    def block_rows(n):
        return pl.ds(pl.multiple_of(n * rows, rows), rows)

    here = block_rows(b)
    red = Reduce(
        part, block_out, [(xg, xq)], (from_sib, from_far, to_far, mine, done), ls_o, ss_o, rs_o
    )
    red_u = ReduceQuarters(
        u_scr, input_grad, (from_sib2, from_far2, to_far2, done2), ls_u, ss_u, rs_u
    )
    swap = Swap(np_, [(dw1, b1), (dw2, b2)], (dwo, bo), ls_s, ss_s, rs_s)

    load_dy = pltpu.make_async_copy(dyg.at[red.q_here], dyq, ls.at[4])

    def back(total, r):
        return norm_back(total, xq[r], dyq[r])

    @pl.when(step == 0)
    def _():
        meet(np_)
        red.start()
        load_dy.start()
        swap.start()
        dk_scr[...] = jnp.zeros_like(dk_scr)
        dv_scr[...] = jnp.zeros_like(dv_scr)
        dq_scr[...] = jnp.zeros_like(dq_scr)
        dw_scr[...] = jnp.zeros_like(dw_scr)
        vec_ref[...] = vec_in_ref[...]

    @pl.when(step == 1)
    def _():
        red.add_far(lambda total, r: xq[r].astype(f32) + tab_ref[2:3] + total, (0, 1))

    causal = lax.broadcasted_iota(jnp.int32, (rows, rows), 0) <= lax.broadcasted_iota(
        jnp.int32, (rows, rows), 1
    )

    def block(n, m, diagonal):
        asks, keys = block_rows(n), block_rows(m)
        for h in range(nh):
            k = k_ref[h, keys]
            q = q_ref[h, asks]
            dc = dc_ref[h, asks]
            pt = jnp.exp(dot(k, q, ((1,), (1,))))
            if diagonal:
                pt = jnp.where(causal, pt, 0.0)
            dpt = dot(v_ref[h, keys], dc, ((1,), (1,)))
            dst = (pt * dpt).astype(bf16)
            dv_scr[h, keys] += dot(pt.astype(bf16), dc)
            dk_scr[h, keys] += dot(dst, q)
            dq_scr[h, asks] += dot(dst, k, ((0,), (0,)))

    @pl.when(step == 0)
    def _():
        red.add_near()

    block(b, b, True)

    def off(n, carry):
        block(jnp.where(g == 0, b, b + 1 + n), jnp.where(g == 0, n, b), False)
        return carry

    lax.fori_loop(0, blocks - 1 - step, off, 0)

    @pl.when(step == 1)
    def _():
        red.add_far(lambda total, r: xq[r].astype(f32) + tab_ref[2:3] + total, (2, 3))
        load_dy.wait()

    @pl.when(step == 2)
    def _():
        red_u.pull(mirror(3, g), back)

    @pl.when(step == 3)
    def _():
        red_u.pull(mirror(2, g), back)

    cosine, sine = cos_ref[...], -sin_ref[...]
    for h in range(nh):
        dq = turn(dq_scr[h, here], cosine, sine, first) * HEAD_DIM**-0.5
        dk = turn(dk_scr[h, here], cosine, sine, first)
        for at, piece in ((h, dq), (nh + h, dk), (2 * nh + h, dv_scr[h, here])):
            dqkv_scr[:, at * HEAD_DIM : (at + 1) * HEAD_DIM] = piece[:, :HEAD_DIM].astype(bf16)
    dqkv = dqkv_scr[...]
    xhat, unused = norm_parts(x_ref[...].astype(f32))
    gain = tab_ref[0:1]
    a1 = (xhat * gain + tab_ref[1:2]).astype(bf16)
    da1 = dot(dqkv, w_ref[...], ((1,), (1,)))
    u_scr[b] = (u_in_ref[...] + da1 * gain).astype(bf16)

    @pl.when(step < blocks - 1)
    def _():
        red_u.ready(b)

    dw_scr[...] += dot(a1, dqkv, ((0,), (0,)))
    vec_ref[0:1] += jnp.sum(da1 * xhat, axis=0, keepdims=True)
    vec_ref[1:2] += jnp.sum(da1, axis=0, keepdims=True)
    vec_ref[5:6, :wide] += jnp.sum(dqkv.astype(f32), axis=0, keepdims=True)

    @pl.when(step < blocks - 1)
    def _():
        red_u.push(b)

    @pl.when(step == blocks - 1)
    def _():
        vec_ref[7:8, 0:1] += squares_of(dw_scr[...])
        finish_all(
            np_, r_in, r_ff, wide // 3, red, red_u, swap, back,
            dw, dw_scr, vec_ref, hot_ref, qkv_at, t1, tq, t2, to, pieces,
            ls_w, ss_w, rs_w, sums_all, ls_g, ss_g, rs_g,
            b1, bq, b2, bo, s1, sq, s2, so, msg, m_all, p_out, ls, ss_m, rs_m, ss, rs,
        )


def whole(shape):
    return pl.BlockSpec(shape, lambda i: (0,) * len(shape), pipeline_mode=pl.Buffered(1))


def sds(shape, dtype):
    return jax.ShapeDtypeStruct(shape, dtype)


def params(collective_id=None):
    return pltpu.CompilerParams(
        dimension_semantics=("arbitrary",), vmem_limit_bytes=VMEM_BYTES,
        collective_id=collective_id, has_side_effects=collective_id is not None,
    )


def weight_sems(np_, n):
    return [
        pltpu.SemaphoreType.DMA((n,)),
        pltpu.SemaphoreType.DMA((n, 8 + np_)),
        pltpu.SemaphoreType.DMA((n, 8 + np_)),
    ]


def attn_fwd(np_, length, x, tab, w, wb, cosine, sine, dy, w2, wo, nh, rows):
    t = x.shape[0]
    lanes = pl.BlockSpec((rows, PAD), lambda i: (i, 0))
    any_ = pl.BlockSpec(memory_space=pl.ANY)
    return pl.pallas_call(
        functools.partial(attn_fwd_kernel, np_),
        grid=(t // rows,),
        out_shape=(
            sds((nh, t, PAD), bf16), sds((nh, t, PAD), bf16), sds((nh, t, PAD), bf16),
            sds((t, nh * PAD), f32), sds((t, nh * HEAD_DIM), bf16),
            sds((4,) + dy.shape, bf16),
            sds((np_,) + w2.shape, bf16), sds(wo.shape, bf16),
        ),
        in_specs=[
            whole((1, PAD)), pl.BlockSpec((rows, D), lambda i: (i, 0)),
            whole((8, D)), whole(w.shape), whole(wb.shape), lanes, lanes,
            pl.BlockSpec(memory_space=pltpu.VMEM), any_, any_,
        ],
        out_specs=(
            pl.BlockSpec((nh, rows, PAD), lambda i: (0, i, 0)),
            whole((nh, t, PAD)), whole((nh, t, PAD)),
            pl.BlockSpec((rows, nh * PAD), lambda i: (i, 0)),
            pl.BlockSpec((rows, nh * HEAD_DIM), lambda i: (i, 0)),
            any_, any_, any_,
        ),
        scratch_shapes=[
            pltpu.VMEM((D, 3 * nh * PAD), bf16),
            pltpu.VMEM((nh, t // rows, rows, rows), f32),
            pltpu.VMEM((nh, rows, PAD), bf16),
            pltpu.VMEM((nh, rows, PAD), f32),
            pltpu.VMEM((nh, rows, PAD), f32),
            pltpu.VMEM((nh, rows, PAD), f32),
        ] + spread_sems() + swap_sems(np_, 2),
        compiler_params=params(2),
        name="attn_fwd",
    )(length, x, tab, w, wb, cosine, sine, dy, w2, wo)


def far_first(i):
    return mirror(3 - i, place()[4])


def mlp(x, dy, c, cf, tab, wo, w1, w2, rows):
    t = x.shape[0]
    ff = w1.shape[1]
    nh = wo.shape[0] // HEAD_DIM
    at = lambda cols: pl.BlockSpec((rows, cols), lambda i: (i, 0))
    vm = pltpu.VMEM
    return pl.pallas_call(
        mlp_kernel,
        grid=(t // rows,),
        out_shape=(
            sds((t, D), bf16), sds((t, D), f32), sds((nh, t, PAD), bf16), sds((D, ff), bf16),
            sds((ff, D), bf16), sds(wo.shape, bf16), sds((8, D), f32),
        ),
        in_specs=[
            at(D), at(D), at(c.shape[1]), at(cf.shape[1]),
            whole((8, D)), whole(wo.shape), whole(w1.shape), whole(w2.shape),
        ],
        out_specs=(
            at(D), at(D), pl.BlockSpec((nh, rows, PAD), lambda i: (0, i, 0)),
            whole((D, ff)), whole((ff, D)), whole(wo.shape), whole((8, D)),
        ),
        scratch_shapes=[
            vm((D, ff), f32), vm((ff, D), f32), vm(wo.shape, f32), vm((nh * PAD, D), bf16),
        ],
        compiler_params=params(),
        name="mlp",
    )(x, dy, c, cf, tab, wo, w1, w2)


def attn_bwd(
    np_, r_in, r_ff, x, u_in, q, k, v, dc, tab, w, cosine, sine, vec,
    part, xg, dyg, dw1, dw2, dwo,
):
    t = x.shape[0]
    nh = q.shape[0]
    wide = w.shape[1]
    quarter = part.shape[1]
    ff = dw1.shape[2]
    at = lambda cols: pl.BlockSpec((quarter, cols), lambda i: (far_first(i), 0))
    any_ = pl.BlockSpec(memory_space=pl.ANY)
    dma = pltpu.SemaphoreType.DMA
    vm = pltpu.VMEM
    hot, qkv_at = one_hot_tables(np_, r_in, r_ff, wide // 3)
    per_owner = lambda cols: vm((2, 4, r_in, cols), bf16)
    block = vm((quarter, D), bf16)
    return pl.pallas_call(
        functools.partial(attn_bwd_kernel, np_, r_in, r_ff),
        grid=(4,),
        out_shape=(
            sds((quarter, D), bf16), sds((quarter, D), bf16), sds((8, r_in, ff), bf16),
            sds((8, r_in, wide), bf16), sds((2, r_ff, D), bf16), sds((2, r_in, D), bf16),
            sds((8, PAD), f32),
        ),
        in_specs=[
            at(D), at(D), whole(q.shape), whole(k.shape), whole(v.shape), whole(dc.shape),
            whole((8, D)), whole(w.shape), at(PAD), at(PAD), whole((8, D)), whole(hot.shape),
            whole(qkv_at.shape),
        ] + [any_] * 6,
        out_specs=(any_,) * 7,
        scratch_shapes=[
            vm((nh, t, PAD), f32), vm((nh, t, PAD), f32), vm((nh, t, PAD), f32),
            vm((quarter, wide), bf16), vm((D, wide), f32), vm((8, D), f32),
            vm((4, quarter, D), bf16), vm((np_, D // np_, wide), bf16),
        ] + reduce_scratch(quarter, 1) + [
            vm((2, quarter, D), bf16), block, block, block, block,
            dma((5,)), dma((4, PIECES)), dma((4, PIECES)),
        ] + swap_sems(np_, 3) + swap_sems(np_, 1) + [
            vm((4, 8, D), f32), dma, dma((3,)), dma((3,)),
            vm(dw1.shape, bf16), vm((np_, D // np_, wide), bf16), vm(dw2.shape, bf16),
            vm((np_,) + dwo.shape[1:], bf16),
            per_owner(ff), per_owner(wide), vm((2, r_ff, D), bf16), per_owner(D),
            vm((2 * np_, 8, PAD), f32), vm((2 * np_, 8, PAD), f32), vm((8, PAD), f32),
            dma((10,)), dma((2 * np_,)), dma((2 * np_,)), dma((4, 8)), dma((4, 8)),
        ],
        compiler_params=params(3),
        name="attn_bwd",
    )(
        x, u_in, q, k, v, dc, tab, w, cosine, sine, vec, hot, qkv_at,
        part, xg, dyg, dw1, dw2, dwo,
    )


def assemble_kernel(
    np_, out_in, grad_in, t1, tq, t2, to, pieces,
    out_o, grad_o, g1, b1, qkv, qkv_b, out, out_b, g2, b2, fc1, fc1_b, fc2, fc2_b, norm,
):
    r_ff, r_in = t2.shape[1], t1.shape[1]
    part_w = tq.shape[2] // 3
    out_o[...] = out_in[...]
    grad_o[...] = grad_in[...]
    for s, ref in enumerate((g1, b1, g2, b2, out_b)):
        ref[...] = pieces[0, s * r_in : (s + 1) * r_in]
    fc2_b[...] = pieces[0, 4 * r_in : 5 * r_in]
    qkv_b[...] = pieces[1, : 3 * r_in]
    fc1_b[...] = pieces[2, :r_ff]
    norm[...] = pieces[4, :1]
    for c in range(2):
        for y in range(2):
            a, b = (0, 3) if y == 0 else (1, 2)
            up = t1[4 * c + a].astype(f32) + t1[4 * c + b].astype(f32)
            for pair in range(np_):
                for e, z in enumerate((a, b)):
                    to_at = r_ff * (4 * (2 * pair + c) + z)
                    at = r_ff * (2 * pair + e)
                    fc1[:, to_at : to_at + r_ff] = up[:, at : at + r_ff]
            into = tq[4 * c + a].astype(f32) + tq[4 * c + b].astype(f32)
            for s in range(3):
                to_at = s * D + (2 * y + c) * part_w
                qkv[:, to_at : to_at + part_w] = into[:, s * part_w : (s + 1) * part_w]
    fc2[...] = t2[0].astype(f32) + t2[1].astype(f32)
    out[...] = to[0].astype(f32) + to[1].astype(f32)


def assemble(np_, out, grad, t1, tq, t2, to, pieces):
    r_in, r_ff = t1.shape[1], t2.shape[1]
    vmem = pl.BlockSpec(memory_space=pltpu.VMEM)
    vec = sds((r_in,), f32)
    outs = (
        sds(out.shape, bf16), sds(grad.shape, bf16), vec, vec,
        sds((r_in, tq.shape[2] * 4), f32), sds((3 * r_in,), f32), sds(to.shape[1:], f32), vec,
        vec, vec, sds((r_in, t1.shape[2] * 4), f32), sds((r_ff,), f32), sds(t2.shape[1:], f32),
        vec, sds((1,), f32),
    )
    return pl.pallas_call(
        functools.partial(assemble_kernel, np_),
        out_shape=outs,
        in_specs=[vmem] * 7,
        out_specs=(vmem,) * len(outs),
        name="assemble",
    )(out, grad, t1, tq, t2, to, pieces)


def swap_sems(np_, n):
    return [
        pltpu.SemaphoreType.DMA((n,)),
        pltpu.SemaphoreType.DMA((n, np_)),
        pltpu.SemaphoreType.DMA((n, np_)),
    ]


def tables(t):
    inv_freqs = np.exp(np.arange(ROT // 2, dtype=np.float32) * np.float32(-2.0 * math.log(10000.0) / ROT))
    angles = np.arange(t, dtype=np.float32)[:, None] * inv_freqs.astype(np.float32)[None, :]
    cosine = np.ones((t, PAD), np.float32)
    sine = np.zeros((t, PAD), np.float32)
    half = ROT // 2
    cosine[:, :half] = cosine[:, half:ROT] = np.cos(angles)
    sine[:, :half] = -np.sin(angles)
    sine[:, half:ROT] = np.sin(angles)
    return jnp.asarray(cosine), jnp.asarray(sine)


MESH = pl.DeviceIdType.MESH
AX = ("dp", "ctx")
CHUNKS = 4


def place():
    d, z = lax.axis_index("dp"), lax.axis_index("ctx")
    c, pair, g = lax.rem(d, 2), lax.div(d, 2), lax.div(z, 2)
    y = lax.rem(g + lax.rem(z, 2), 2)
    return d, z, c, pair, g, y


def mirror(m, g):
    return jnp.where(g == 0, m, 3 - m)


def rcopy(src, dst, ss, rs, device):
    return pltpu.make_async_remote_copy(
        src_ref=src, dst_ref=dst, send_sem=ss, recv_sem=rs, device_id=device, device_id_type=MESH
    )


def column_peer(pair, c, z, o):
    m = lax.rem(c * 4 + z + o, 8)
    return lax.div(m, 4), lax.rem(m, 4)


def barrier_all(np_, d, z, c, pair):
    bar = pltpu.get_barrier_semaphore()
    for o in range(1, 8):
        c2, z2 = column_peer(pair, c, z, o)
        pl.semaphore_signal(bar, inc=1, device_id=(2 * pair + c2, z2), device_id_type=MESH)
    for o in range(1, np_):
        pl.semaphore_signal(
            bar, inc=1, device_id=(2 * lax.rem(pair + o, np_) + c, z), device_id_type=MESH
        )
    pl.semaphore_wait(bar, 7 + np_ - 1)


class Spread:
    def __init__(self, own, out, ls, ss, rs):
        self.own, self.out, self.ls, self.ss, self.rs = own, out, ls, ss, rs
        self.rows = out.shape[1] // CHUNKS
        d, z, c, pair, g, y = place()
        self.d, self.z, self.c, self.g, self.y = d, z, c, g, y
        self.prim = c == g
        self.sib = (d + 1 - 2 * c, z)
        self.partner = (d, z + 1 - 2 * lax.rem(z, 2))
        self.far = (d, 1 + c)

    def cut(self, ref, j):
        return ref.at[pl.ds(j * self.rows, self.rows)]

    def send(self, q, j, way, device, src=None):
        src = self.cut(self.out.at[q], j) if src is None else src
        return rcopy(
            src, self.cut(self.out.at[q], j), self.ss.at[way, q, j], self.rs.at[q, j], device
        )

    def start(self):
        own = [self.cut(self.own, j) for j in range(CHUNKS)]

        @pl.when(self.prim)
        def _():
            pltpu.make_async_copy(self.own, self.out.at[self.z], self.ls).start()
            for j in range(CHUNKS):
                self.send(self.z, j, 0, self.partner, own[j]).start()
            for j in range(CHUNKS):
                self.send(self.z, j, 1, self.sib, own[j]).start()

        @pl.when(jnp.logical_not(self.prim))
        def _():
            for j in range(CHUNKS):
                self.send(self.z, j, 0, self.far, own[j]).start()

    def wait_recv(self, q, j):
        self.send(q, j, 0, self.sib).wait_recv()

    def forward(self, j):
        far = (mirror(2, self.g), mirror(3, self.g))
        end, mid = mirror(0, self.g), mirror(1, self.g)

        @pl.when(jnp.logical_and(self.prim, self.y == 1))
        def _():
            for q in far:
                self.wait_recv(q, j)
                self.send(q, j, 0, self.partner).start()
                self.send(q, j, 1, self.sib).start()
            self.wait_recv(end, j)
            self.send(end, j, 1, self.sib).start()

        @pl.when(jnp.logical_and(self.prim, self.y == 0))
        def _():
            self.wait_recv(mid, j)
            self.send(mid, j, 1, self.sib).start()
            if j > 0:
                for q in far:
                    self.wait_recv(q, j - 1)
                    self.send(q, j - 1, 1, self.sib).start()

    def finish(self):
        far = (mirror(2, self.g), mirror(3, self.g))
        end, mid = mirror(0, self.g), mirror(1, self.g)

        @pl.when(jnp.logical_and(self.prim, self.y == 0))
        def _():
            for q in far:
                self.wait_recv(q, CHUNKS - 1)
                self.send(q, CHUNKS - 1, 1, self.sib).start()
            for j in range(CHUNKS):
                self.send(end, j, 0, self.partner).wait_send()

        @pl.when(jnp.logical_and(self.prim, self.y == 1))
        def _():
            for j in range(CHUNKS):
                for q in far + (mid,):
                    self.send(q, j, 0, self.partner).wait_send()

        @pl.when(self.prim)
        def _():
            pltpu.make_async_copy(self.own, self.out.at[self.z], self.ls).wait()
            for q in range(4):
                for j in range(CHUNKS):
                    self.send(q, j, 1, self.sib).wait_send()

        @pl.when(jnp.logical_not(self.prim))
        def _():
            for q in range(4):
                for j in range(CHUNKS):
                    self.wait_recv(q, j)
            for j in range(CHUNKS):
                self.send(self.z, j, 0, self.far).wait_send()


class Weights:
    def __init__(self, np_, sliced, w2, wo, ls, ss, rs):
        self.np_, self.sliced, self.w2, self.wo = np_, sliced, w2, wo
        self.ls, self.ss, self.rs = ls, ss, rs
        self.here = place()

    def first(self, s, o):
        d, z, c, pair, g, y = self.here
        src, out, by_slice = self.sliced[s]
        if o == 0:
            return pltpu.make_async_copy(
                src.at[2 * y + c] if by_slice else src, out.at[pair, c, z], self.ls.at[s]
            )
        c2, z2 = column_peer(pair, c, z, o)
        y2 = lax.rem(lax.div(z2, 2) + lax.rem(z2, 2), 2)
        return rcopy(
            src.at[2 * y2 + c2] if by_slice else src, out.at[pair, c, z],
            self.ss.at[s, o - 1], self.rs.at[s, o - 1], (2 * pair + c2, z2),
        )

    def second(self, s, o):
        d, z, c, pair, g, y = self.here
        out = self.sliced[s][1]
        return rcopy(
            out.at[pair], out.at[pair], self.ss.at[s, 7 + o - 1], self.rs.at[s, 7 + o - 1],
            (2 * lax.rem(pair + o, self.np_) + c, z),
        )

    def start(self):
        d, z, c, pair, g, y = self.here
        n = len(self.sliced)
        for s in range(n):
            for o in range(8):
                self.first(s, o).start()

    def start_rows(self):
        for o in range(2):
            self.w2_first(o).start()
        self.wo_first(lambda cp: cp.start())

    def w2_first(self, o):
        d, z, c, pair, g, y = self.here
        src, out = self.w2
        n = len(self.sliced)
        if o == 0:
            return pltpu.make_async_copy(src, out.at[g], self.ls.at[n])
        return rcopy(src, out.at[g], self.ss.at[n, 0], self.rs.at[n, 0], (d, 3 - z))

    def wo_parts(self):
        d, z, c, pair, g, y = self.here
        per = self.np_ // 4
        owner = lax.div(pair, per)
        return per, owner, lax.rem(owner, 2), lax.div(owner, 2)

    def wo_first(self, do, sending=True):
        d, z, c, pair, g, y = self.here
        src, out = self.wo
        n = len(self.sliced) + 1
        per, owner, c_to, y_to = self.wo_parts()
        slot = out.at[lax.rem(pair, per), c, z]
        for t in range(2):
            z_to = jnp.where(t == 0, y_to, 3 - y_to)
            mine = jnp.logical_and(c == c_to, z == z_to)

            @pl.when(mine)
            def _():
                do(pltpu.make_async_copy(src, slot, self.ls.at[n]))

            @pl.when(jnp.logical_not(mine))
            def _():
                cp = rcopy(
                    src, slot, self.ss.at[n, t], self.rs.at[n, c * 4 + z], (2 * pair + c_to, z_to)
                )
                do(cp)

    def between(self, s):
        self.first(s, 0).wait()
        for o in range(1, 8):
            self.first(s, o).wait_recv()
        for o in range(1, self.np_):
            self.second(s, o).start()

    def finish_rows(self):
        d, z, c, pair, g, y = self.here
        n = len(self.sliced) + 1
        per, owner, c_to, y_to = self.wo_parts()
        for o in range(2):
            self.w2_first(o).wait()

        @pl.when(owner == 2 * y + c)
        def _():
            for c2 in range(2):
                for z2 in range(4):
                    own = jnp.logical_and(c == c2, z == z2)

                    @pl.when(jnp.logical_not(own))
                    def _():
                        slot = self.wo[1].at[0, c2, z2]
                        rcopy(
                            slot, slot, self.ss.at[n, 0], self.rs.at[n, c2 * 4 + z2],
                            (d + 1 - 2 * c, z),
                        ).wait_recv()
            pltpu.make_async_copy(
                self.wo[0], self.wo[1].at[0, c, z], self.ls.at[n]
            ).wait()

        for t in range(2):
            z_to = jnp.where(t == 0, y_to, 3 - y_to)

            @pl.when(jnp.logical_not(jnp.logical_and(c == c_to, z == z_to)))
            def _():
                rcopy(
                    self.wo[0], self.wo[1].at[0, c, z], self.ss.at[n, t], self.rs.at[n, 0],
                    (d + 1 - 2 * c, z),
                ).wait_send()

    def finish(self, s):
        for o in range(1, 8):
            self.first(s, o).wait_send()
        for o in range(1, self.np_):
            self.second(s, o).wait()


class Rows:
    def __init__(self, np_, w2, wo, ls, ss, rs):
        self.np_, self.w2, self.wo, self.ls, self.ss, self.rs = np_, w2, wo, ls, ss, rs
        self.here = place()

    def copy_w2(self, o):
        d, z, c, pair, g, y = self.here
        src, out = self.w2
        if o == 0:
            return pltpu.make_async_copy(src, out.at[pair], self.ls.at[0])
        to = (2 * lax.rem(pair + o, self.np_) + c, z)
        return rcopy(src, out.at[pair], self.ss.at[0, o], self.rs.at[0, o], to)

    def copy_wo(self, o):
        d, z, c, pair, g, y = self.here
        src, out = self.wo
        slot = lax.rem(pair, self.np_ // 4)
        if o == 0:
            return pltpu.make_async_copy(src.at[slot], out.at[slot], self.ls.at[1])
        to = (2 * lax.rem(pair + o, self.np_) + c, z)
        return rcopy(src.at[slot], out.at[slot], self.ss.at[1, o], self.rs.at[1, o], to)

    def holds(self, pair):
        d, z, c, unused, g, y = self.here
        return lax.div(pair, self.np_ // 4) == 2 * y + c

    def start(self):
        @pl.when(self.holds(self.here[3]))
        def _():
            for o in range(1, self.np_):
                self.copy_wo(o).start()
            self.copy_wo(0).start()

        for o in range(1, self.np_):
            self.copy_w2(o).start()
        self.copy_w2(0).start()

    def finish(self):
        pair = self.here[3]
        for o in range(self.np_):
            self.copy_w2(o).wait()

        @pl.when(self.holds(pair))
        def _():
            self.copy_wo(0).wait()
            for o in range(1, self.np_):
                self.copy_wo(o).wait_send()

        for o in range(1, self.np_):
            @pl.when(self.holds(lax.rem(pair + self.np_ - o, self.np_)))
            def _():
                self.copy_wo(o).wait_recv()


def decode_tables(np_, r_in, r_ff, part, nh):
    wide = 3 * nh * PAD
    f = np.arange(D)
    by_d = np.zeros((8, D), np.int32)
    by_d[0], by_d[1] = f // r_in, f % r_in
    by_d[2], by_d[3], by_d[4] = f // (2 * r_ff), (f // r_ff) % 2, f % r_ff
    p = np.arange(wide)
    head, lane = p // PAD, p % PAD
    by_q = np.full((8, wide), -1, np.int32)
    for k in range(4):
        at = (head // nh) * D + k * part + (head % nh) * HEAD_DIM + lane
        real = lane < HEAD_DIM
        by_q[k, real] = (at // (3 * r_in))[real]
        by_q[4 + k, real] = (r_in + at % (3 * r_in))[real]
    extra = np.zeros((1, wide), np.float32)
    extra[0, (head < nh) & (lane == HEAD_DIM)] = HEAD_DIM**0.5
    keys = (head >= nh) & (head < 2 * nh)
    extra[0, keys & (lane > HEAD_DIM) & (lane < HEAD_DIM + 4)] = 1.0
    extra[0, (head >= 2 * nh) & (lane >= HEAD_DIM) & (lane < HEAD_DIM + 3)] = 1.0
    return jnp.asarray(by_d), jnp.asarray(by_q), jnp.asarray(extra)


def decode(np_, r_in, r_ff, vec, by_d, by_q, extra, tab, b_pad, length):
    d, z, c, pair, g, y = place()
    world = 8 * np_
    packed = vec[...].reshape(world * 16, PAD)
    m = lax.broadcasted_iota(jnp.int32, (world, world * 16), 1)
    n = lax.broadcasted_iota(jnp.int32, (world, world * 16), 0)
    row = [
        dot(jnp.where(m == 16 * n + r, 1.0, 0.0).astype(bf16), packed).astype(bf16)
        for r in range(3)
    ]

    def pick(x, lanes, owner):
        w = lanes.shape[1]
        hot = lax.broadcasted_iota(jnp.int32, (PAD, w), 0) == lanes
        got = dot(x, jnp.where(hot, 1.0, 0.0).astype(bf16))
        mine = lax.broadcasted_iota(jnp.int32, (world, w), 0) == owner
        return jnp.sum(jnp.where(mine, got, 0.0), axis=0, keepdims=True)

    owner, lanes = by_d[0:1], by_d[1:2]
    tab[0:1] = pick(row[0], lanes, owner)
    tab[1:2] = pick(row[0], lanes + r_in, owner)
    tab[2:3] = pick(row[0], lanes + 2 * r_in, owner) + pick(row[1], lanes, owner)
    tab[3:4] = pick(row[0], lanes + 3 * r_in, owner)
    tab[4:5] = pick(row[0], lanes + 4 * r_in, owner)
    owner = by_d[2:3] * 8 + c * 4 + jnp.where(by_d[3:4] == 0, y, 3 - y)
    tab[5:6] = pick(row[2], by_d[4:5], owner)
    tab[6:8] = jnp.zeros((2, D), f32)
    k = 2 * y + c
    b_pad[...] = pick(row[1], by_q[pl.ds(4 + k, 1)], by_q[pl.ds(k, 1)]) + extra[...]
    mine = lax.broadcasted_iota(jnp.int32, (world, PAD), 0) == (2 * pair + g) * 4
    parts = jnp.sum(jnp.where(mine, row[2].astype(f32), 0.0), axis=0, keepdims=True)
    lane = lax.broadcasted_iota(jnp.int32, (1, PAD), 1)
    parts = jnp.where(lane == r_ff, parts * 256.0, jnp.where(lane == r_ff + 1, parts, 0.0))
    length[...] = jnp.broadcast_to(jnp.sum(parts, axis=1, keepdims=True), (1, PAD))


def gather_kernel(
    np_, r_in, r_ff, len_ref, x, grad, qkv_w, fc1_w, w2, wo, vec_own, by_d, by_q, extra,
    xg, dy_own, wqg, w1g, w2p, wop, tab, b_pad, length, wq, w1, dy, ls_m, vec, ls_x, ss_x, rs_x, ls_w, ss_w, rs_w,
):
    d, z, c, pair, g, y = place()
    load = pltpu.make_async_copy(grad, dy, ls_m.at[0])
    load.start()
    part_w = wq.shape[2] // 3
    for k in range(4):
        y2, c2 = k // 2, k % 2
        for s in range(3):
            at = s * D + k * part_w
            wq[k, :, s * part_w : (s + 1) * part_w] = qkv_w[:, at : at + part_w]
        for n in range(np_):
            for e, z2 in enumerate((0, 3) if y2 == 0 else (1, 2)):
                at = r_ff * (4 * (2 * n + c2) + z2)
                to = r_ff * (2 * n + e)
                w1[k, :, to : to + r_ff] = fc1_w[:, at : at + r_ff]
    barrier_all(np_, d, z, c, pair)
    spread = Spread(x, xg, ls_x, ss_x, rs_x)
    weights = Weights(
        np_, [(vec_own, vec, False), (wq, wqg, True), (w1, w1g, True)], (w2, w2p), (wo, wop),
        ls_w, ss_w, rs_w,
    )
    weights.start()
    spread.start()
    weights.start_rows()
    load.wait()
    pos = z * dy.shape[0] + lax.broadcasted_iota(jnp.int32, (dy.shape[0], 1), 0)
    dy[...] = jnp.where(pos < len_ref[0], dy[...].astype(f32), 0.0).astype(bf16)
    store = pltpu.make_async_copy(dy, dy_own, ls_m.at[1])
    store.start()
    for s in range(2):
        weights.between(s)
    spread.forward(0)
    weights.between(2)
    weights.finish(0)
    for j in range(1, CHUNKS):
        spread.forward(j)
    decode(np_, r_in, r_ff, vec, by_d, by_q, extra, tab, b_pad, length)
    spread.finish()
    for s in range(1, 3):
        weights.finish(s)
    weights.finish_rows()
    store.wait()


def spread_sems():
    return [
        pltpu.SemaphoreType.DMA,
        pltpu.SemaphoreType.DMA((2, 4, CHUNKS)),
        pltpu.SemaphoreType.DMA((4, CHUNKS)),
    ]


def gather(
    np_, r_in, r_ff, nh, length, x, grad, qkv_w, fc1_w, w2, wo, vec, collective_id=1
):
    any_ = pl.BlockSpec(memory_space=pl.ANY)
    vmem = pl.BlockSpec(memory_space=pltpu.VMEM)
    wide = 3 * nh * PAD
    thin, ff = qkv_w.shape[1] // 4, fc1_w.shape[1] // 4
    return pl.pallas_call(
        functools.partial(gather_kernel, np_, r_in, r_ff),
        out_shape=(
            sds((4,) + x.shape, bf16), sds(x.shape, bf16), sds((np_, 2, 4, r_in, thin), bf16),
            sds((np_, 2, 4, r_in, ff), bf16), sds((2,) + w2.shape, bf16),
            sds((np_ // 4, 2, 4) + wo.shape, bf16),
            sds((8, D), f32), sds((1, wide), f32), sds((1, PAD), f32),
        ),
        in_specs=[pl.BlockSpec(memory_space=pltpu.SMEM), any_, any_, vmem, vmem, any_, any_, any_]
        + [vmem] * 3,
        out_specs=(any_,) * 6 + (vmem,) * 3,
        scratch_shapes=[
            pltpu.VMEM((4, r_in, thin), bf16), pltpu.VMEM((4, r_in, ff), bf16),
            pltpu.VMEM(x.shape, bf16), pltpu.SemaphoreType.DMA((2,)),
            pltpu.VMEM((np_, 2, 4, 16, PAD), bf16),
        ] + spread_sems() + weight_sems(np_, 5),
        compiler_params=pltpu.CompilerParams(
            collective_id=collective_id, has_side_effects=True, vmem_limit_bytes=VMEM_BYTES
        ),
        name="gather",
    )(length, x, grad, qkv_w, fc1_w, w2, wo, vec, *decode_tables(np_, r_in, r_ff, thin // 3, nh))


PIECES = 4


class Reduce:
    def __init__(self, part, out, extra, bufs, ls, ss, rs):
        self.part, self.out, self.extra = part, out, extra
        self.from_sib, self.from_far, self.to_far, self.mine, self.done = bufs
        self.ls, self.ss, self.rs = ls, ss, rs
        d, z, c, pair, g, y = place()
        self.role = jnp.where(c == g, 0, 1)
        self.y = y
        self.sib = (d + 1 - 2 * c, z)
        self.partner = (d, z + 1 - 2 * lax.rem(z, 2))
        self.q_here = mirror(2 * y + self.role, g)
        self.q_there = mirror(2 * (1 - y) + self.role, g)
        self.sib_here = mirror(2 * y + 1 - self.role, g)
        self.sib_there = mirror(2 * (1 - y) + 1 - self.role, g)
        self.owner = (2 * pair + g, self.q_here)
        self.self_owner = jnp.logical_and(self.role == 0, y == 0)
        self.self_source = jnp.where(c == 0, z, 3 - z) == 0
        self.rows = self.out.shape[0] // PIECES

    def rows_of(self, j):
        return pl.ds(j * self.rows, self.rows)

    def to_sib(self, t, j):
        q = self.sib_there if t == 0 else self.sib_here
        r = self.rows_of(j)
        return rcopy(
            self.part.at[q, r], self.from_sib.at[t, r], self.ss.at[t, j], self.rs.at[t, j], self.sib
        )

    def load(self, t):
        q = self.q_there if t == 0 else self.q_here
        return pltpu.make_async_copy(self.part.at[q], self.mine.at[t], self.ls.at[t])

    def load_extra(self, e):
        src, dst = self.extra[e]
        return pltpu.make_async_copy(src.at[self.q_here], dst, self.ls.at[2 + e])

    def across(self, j):
        r = self.rows_of(j)
        return rcopy(
            self.to_far.at[r], self.from_far.at[r], self.ss.at[2, j], self.rs.at[2, j], self.partner
        )

    def home(self, j):
        r = self.rows_of(j)
        return rcopy(
            self.done.at[r], self.out.at[r], self.ss.at[3, j], self.rs.at[3, j], self.owner
        )

    def keep(self):
        return pltpu.make_async_copy(self.done, self.out, self.ls.at[4])

    def start(self):
        for t in range(2):
            for j in range(PIECES):
                self.to_sib(t, j).start()
        for t in range(2):
            self.load(t).start()
        for e in range(len(self.extra)):
            self.load_extra(e).start()

    def add_near(self):
        self.load(0).wait()
        for j in range(PIECES):
            r = self.rows_of(j)
            self.to_sib(0, j).wait_recv()
            total = self.mine[0, r].astype(f32) + self.from_sib[0, r].astype(f32)
            self.to_far[r] = total.astype(bf16)
            self.across(j).start()
        self.load(1).wait()
        for e in range(len(self.extra)):
            self.load_extra(e).wait()

    def add_far(self, finish, pieces=range(PIECES)):
        for j in pieces:
            r = self.rows_of(j)
            self.to_sib(1, j).wait_recv()
            self.across(j).wait_recv()
            total = self.mine[1, r].astype(f32) + self.from_sib[1, r].astype(f32)
            total = total + self.from_far[r].astype(f32)
            self.done[r] = finish(total, r).astype(bf16)

            @pl.when(jnp.logical_not(self.self_owner))
            def _():
                self.home(j).start()

    def finish(self):
        @pl.when(self.self_owner)
        def _():
            self.keep().start()
            self.keep().wait()

        for j in range(PIECES):
            @pl.when(jnp.logical_not(self.self_source))
            def _():
                self.home(j).wait_recv()

        for j in range(PIECES):
            self.to_sib(0, j).wait_send()
            self.to_sib(1, j).wait_send()
            self.across(j).wait_send()

            @pl.when(jnp.logical_not(self.self_owner))
            def _():
                self.home(j).wait_send()


def reduce_scratch(rows, extras):
    return [
        pltpu.VMEM((2, rows, D), bf16), pltpu.VMEM((rows, D), bf16), pltpu.VMEM((rows, D), bf16),
        pltpu.VMEM((2, rows, D), bf16), pltpu.VMEM((rows, D), bf16),
    ] + [pltpu.VMEM((rows, D), bf16)] * extras + [
        pltpu.SemaphoreType.DMA((5,)),
        pltpu.SemaphoreType.DMA((4, PIECES)),
        pltpu.SemaphoreType.DMA((4, PIECES)),
    ]


class ReduceQuarters(Reduce):
    def __init__(self, part, out, bufs, ls, ss, rs):
        from_sib, from_far, to_far, done = bufs
        super().__init__(part, out, [], (from_sib, from_far, to_far, None, done), ls, ss, rs)

    def ready(self, q):
        for t, mine in ((0, self.sib_there), (1, self.sib_here)):
            @pl.when(mine == q)
            def _():
                for j in range(PIECES):
                    self.to_sib(t, j).start()

    def push(self, q):
        @pl.when(self.q_there == q)
        def _():
            for j in range(PIECES):
                r = self.rows_of(j)
                self.to_sib(0, j).wait_recv()
                total = self.part[q, r].astype(f32) + self.from_sib[0, r].astype(f32)
                self.to_far[r] = total.astype(bf16)
                self.across(j).start()

    def pull(self, q, finish):
        @pl.when(self.q_here == q)
        def _():
            for j in range(PIECES):
                r = self.rows_of(j)
                self.to_sib(1, j).wait_recv()
                self.across(j).wait_recv()
                total = self.part[q, r].astype(f32) + self.from_sib[1, r].astype(f32)
                total = total + self.from_far[r].astype(f32)
                self.done[r] = finish(total, r).astype(bf16)

                @pl.when(jnp.logical_not(self.self_owner))
                def _():
                    self.home(j).start()


class Swap:
    def __init__(self, np_, arrays, wo, ls, ss, rs):
        self.np_, self.arrays, self.wo, self.ls, self.ss, self.rs = np_, arrays, wo, ls, ss, rs
        self.here = place()

    def copy(self, s, o):
        d, z, c, pair, g, y = self.here
        src, dst = self.arrays[s]
        to = lax.rem(pair + o, self.np_)
        if o == 0:
            return pltpu.make_async_copy(src.at[pair], dst.at[pair], self.ls.at[s])
        return rcopy(
            src.at[to], dst.at[pair], self.ss.at[s, o], self.rs.at[s, o], (2 * to + c, z)
        )

    def copy_wo(self, o):
        d, z, c, pair, g, y = self.here
        src, dst = self.wo
        n = len(self.arrays)
        per = self.np_ // 4
        to = lax.rem(pair + o, self.np_)
        if o == 0:
            return pltpu.make_async_copy(src.at[lax.rem(pair, per)], dst.at[pair], self.ls.at[n])
        return rcopy(
            src.at[lax.rem(to, per)], dst.at[pair], self.ss.at[n, o], self.rs.at[n, o],
            (2 * to + c, z),
        )

    def collects(self, pair2):
        d, z, c, pair, g, y = self.here
        return lax.div(pair2, self.np_ // 4) == 2 * y + c

    def start(self):
        d, z, c, pair, g, y = self.here
        for s in range(len(self.arrays)):
            for o in range(1, self.np_):
                self.copy(s, o).start()
            self.copy(s, 0).start()
        if self.wo is not None:
            for o in range(self.np_):
                @pl.when(self.collects(lax.rem(pair + o, self.np_)))
                def _():
                    self.copy_wo(o).start()

    def finish(self):
        d, z, c, pair, g, y = self.here
        for s in range(len(self.arrays)):
            for o in range(self.np_):
                self.copy(s, o).wait()
        if self.wo is not None:
            for o in range(self.np_):
                @pl.when(self.collects(lax.rem(pair + o, self.np_)))
                def _():
                    if o == 0:
                        self.copy_wo(o).wait()
                    else:
                        self.copy_wo(o).wait_send()

                if o > 0:
                    @pl.when(self.collects(pair))
                    def _():
                        self.copy_wo(o).wait_recv()


def group_peer(o):
    d, z, c, pair, g, y = place()
    c2 = 1 - c if o % 2 else c
    z2 = z + 1 - 2 * lax.rem(z, 2) if o // 2 else z
    return 2 * pair + c2, z2


class Group:
    def __init__(self, own, all_, ls, ss, rs):
        self.own, self.all_, self.ls, self.ss, self.rs = own, all_, ls, ss, rs
        d, z, c, pair, g, y = place()
        self.k = 2 * y + c

    def copy(self, o):
        if o == 0:
            return pltpu.make_async_copy(self.own, self.all_.at[self.k], self.ls)
        return rcopy(
            self.own, self.all_.at[self.k], self.ss.at[o - 1], self.rs.at[o - 1], group_peer(o)
        )

    def start(self):
        for o in range(4):
            self.copy(o).start()

    def finish(self):
        for o in range(4):
            self.copy(o).wait()


def norm_back(total, x, dy):
    xhat, inverse = norm_parts(x.astype(f32))
    back = inverse * (
        total
        - jnp.mean(total, axis=-1, keepdims=True)
        - xhat * jnp.mean(total * xhat, axis=-1, keepdims=True)
    )
    return dy.astype(f32) + back


def same_slice_peer(np_, e):
    d, z, c, pair, g, y = place()
    to = lax.rem(pair * 2 + g + e, 2 * np_)
    pair2, g2 = lax.div(to, 2), lax.rem(to, 2)
    return to, (2 * pair2 + c, jnp.where(g2 == g, z, 3 - z))


def one_hot_tables(np_, r_in, r_ff, part):
    f = np.arange(D)
    lane = np.arange(PAD)
    place_qkv = (f // part) * D + f % part
    tables_ = [f % r_in, f % r_ff] + [(place_qkv + k * part) % (3 * r_in) for k in range(4)]
    hot = np.stack([(t[:, None] == lane[None, :]) for t in tables_]).astype(np.float32)
    hot[2:, 3 * part :] = 0.0
    return jnp.asarray(hot, bf16), jnp.asarray(place_qkv[None], jnp.int32)


def pieces_of(np_, sums_all, sums, hot_ref, qkv_at, r_in, r_ff, part, msg):
    d, z, c, pair, g, y = place()
    n = 2 * np_
    e = lax.broadcasted_iota(jnp.int32, (n, D), 0)
    f = lax.broadcasted_iota(jnp.int32, (n, D), 1)
    group = lax.rem(e, 2)
    index = (lax.div(e, 2) * 2 + c) * 4 + jnp.where(group == 0, y, 3 - y)

    def select(rows_, inside, hot):
        picked = []
        for row in rows_:
            for v in split3(row):
                picked.append(jnp.where(inside, v, 0.0))
        got = dot(jnp.concatenate(picked, axis=0).astype(bf16), hot)
        return [
            got[3 * s * n : (3 * s + 1) * n] + got[(3 * s + 1) * n : (3 * s + 2) * n]
            + got[(3 * s + 2) * n : (3 * s + 3) * n]
            for s in range(len(rows_))
        ]

    d_vecs = sums_all[0, 0:4] + sums_all[1, 0:4] + sums_all[2, 0:4] + sums_all[3, 0:4]
    rows_ = [d_vecs[s : s + 1] for s in range(4)] + [sums[6:7]]
    inside = jnp.logical_and(f >= index * r_in, f < (index + 1) * r_in)
    got = select(rows_, inside, hot_ref[0])
    first = got[0]
    for s in range(1, 5):
        first = first + pltpu.roll(got[s], s * r_in, 1)
    second = jnp.zeros((n, PAD), f32)
    for k in range(4):
        at = qkv_at[...] + k * part
        inside = jnp.logical_and(at >= index * (3 * r_in), at < (index + 1) * (3 * r_in))
        second = second + select([sums_all[k, 5:6]], inside, hot_ref[2 + k])[0]
    inside = jnp.logical_and(f >= e * r_ff, f < (e + 1) * r_ff)
    third = select([sums[4:5]], inside, hot_ref[1])[0]
    squares = squares_of(d_vecs) + 2.0 * squares_of(sums[6:7])
    for k in range(4):
        squares = squares + squares_of(sums_all[k, 4:6]) + sums_all[k, 7:8, 0:1]
    for s in range(n):
        msg[s, 0:1] = first[s : s + 1]
        msg[s, 1:2] = second[s : s + 1]
        msg[s, 2:3] = third[s : s + 1]
        msg[s, 3:4] = jnp.broadcast_to(squares, (1, PAD))
        msg[s, 4:8] = jnp.zeros((4, PAD), f32)


def meet(np_):
    d, z, c, pair, g, y = place()
    bar = pltpu.get_barrier_semaphore()
    for o in range(1, 8):
        c2, z2 = column_peer(pair, c, z, o)
        pl.semaphore_signal(bar, inc=1, device_id=(2 * pair + c2, z2), device_id_type=MESH)
    for e in range(1, 2 * np_):
        unused, peer = same_slice_peer(np_, e)
        pl.semaphore_signal(bar, inc=1, device_id=peer, device_id_type=MESH)
    pl.semaphore_wait(bar, 7 + 2 * np_ - 1)


def finish_all(
    np_, r_in, r_ff, part_w, red_out, red, swap1, back,
    dw, dw_sum, sums, hot_ref, qkv_at, t1, tq, t2, to, pieces,
    ls_w, ss_w, rs_w, sums_all, ls_g, ss_g, rs_g,
    b1, bq, b2, bo, s1, sq, s2, so, msg, m_all, p_out, ls, ss_m, rs_m, ss, rs,
):
    d, z, c, pair, g, y = place()
    grp = Group(sums, sums_all, ls_g, ss_g, rs_g)
    swap = Swap(np_, [(dw, bq)], None, ls_w, ss_w, rs_w)
    grp.start()
    share = D // np_
    for n in range(np_):
        dw[n] = dw_sum[n * share : (n + 1) * share].astype(bf16)
    swap.start()
    red.ready(mirror(0, g))
    grp.finish()
    pieces_of(np_, sums_all, sums, hot_ref, qkv_at, r_in, r_ff, part_w, msg)
    me = pair * 2 + g

    def tell(e):
        to_, peer = same_slice_peer(np_, e)
        return rcopy(msg.at[to_], m_all.at[me], ss_m.at[e], rs_m.at[e], peer)

    own = pltpu.make_async_copy(msg.at[me], m_all.at[me], ls.at[0])
    own.start()
    for e in range(1, 2 * np_):
        tell(e).start()
    red.push(mirror(0, g))
    red.pull(mirror(1, g), back)
    own.wait()
    for e in range(1, 2 * np_):
        tell(e).wait()
    norms = [jnp.sqrt(m_all[e, 3:4, 0:1]) for e in range(2 * np_)]
    mean_norm = sum(norms) / (2 * np_)
    factors = [mean_norm / jnp.maximum(n, mean_norm) for n in norms]
    p_out[...] = sum(f * m_all[e] for e, f in enumerate(factors))
    p_out[4:5, 0:1] = sum(jnp.where(d == e, n, 0.0) for e, n in enumerate(norms))
    group_factors = [
        jnp.where(g == 0, factors[2 * n], factors[2 * n + 1]) for n in range(np_)
    ]
    final = pltpu.make_async_copy(p_out, pieces, ls.at[9])
    final.start()
    collects = swap1.collects(pair)
    swap1.finish()

    def rows_to(s, src, dst, o, slot):
        c2, z2 = column_peer(pair, c, z, o)
        if o == 0:
            return pltpu.make_async_copy(src.at[c2, z2], dst.at[slot], ls.at[5 + s])
        return rcopy(
            src.at[c2, z2], dst.at[slot], ss.at[s, o], rs.at[s, o], (2 * pair + c2, z2)
        )

    def scaled(n, buf, acc, dst):
        for c2 in range(2):
            for z2 in range(4):
                at = pl.ds((c2 * 4 + z2) * r_in, r_in)
                total = sum(f * buf[m, at].astype(f32) for m, f in enumerate(group_factors))
                acc[c2, z2] = total.astype(acc.dtype)
        for o in range(8):
            rows_to(n, acc, dst, o, c * 4 + z).start()

    for t in range(2):
        at = pl.ds(t * r_ff, r_ff)
        total = sum(f * b2[m, at].astype(f32) for m, f in enumerate(group_factors))
        s2[t] = total.astype(s2.dtype)
    mirror_copy = rcopy(s2.at[1 - g], t2.at[1], ss.at[2, 0], rs.at[2, 0], (d, 3 - z))
    mirror_copy.start()
    kept = pltpu.make_async_copy(s2.at[g], t2.at[0], ls.at[7])
    kept.start()
    scaled(1, b1, s1, t1)
    swap.finish()
    scaled(0, bq, sq, tq)

    def wo_to(o):
        c2, z2 = column_peer(pair, c, z, o)
        if o == 0:
            return pltpu.make_async_copy(so.at[c2, z2], to.at[g], ls.at[8])
        return rcopy(
            so.at[c2, z2], to.at[g], ss.at[3, o], rs.at[3, g], (2 * pair + c2, z2)
        )

    @pl.when(collects)
    def _():
        for c2 in range(2):
            for z2 in range(4):
                at = pl.ds((c2 * 4 + z2) * r_in, r_in)
                total = sum(f * bo[m, at].astype(f32) for m, f in enumerate(group_factors))
                so[c2, z2] = total.astype(so.dtype)
        for o in range(8):
            wo_to(o).start()

    red.pull(mirror(0, g), back)
    for n, (acc, dst) in enumerate(((sq, tq), (s1, t1))):
        for o in range(8):
            rows_to(n, acc, dst, o, c * 4 + z).wait()
    mirror_copy.wait()
    kept.wait()

    @pl.when(collects)
    def _():
        wo_to(0).wait()
        for o in range(1, 8):
            wo_to(o).wait_send()

    for t in range(2):
        @pl.when(jnp.logical_or(jnp.logical_not(collects), g != t))
        def _():
            rcopy(so.at[0, 0], to.at[t], ss.at[3, 0], rs.at[3, t], (d, 3 - z)).wait_recv()

    final.wait()
    red_out.finish()
    red.finish()


def local(
    block_in, out_grad, lengths, ln1_gain, ln1_bias, qkv_weight, qkv_bias, out_weight, out_bias,
    ln2_gain, ln2_bias, fc1_weight, fc1_bias, fc2_weight, fc2_bias,
):
    tp = lax.axis_size("ctx")
    dp = lax.axis_size("dp")
    np_ = dp // 2
    world = dp * tp
    nh = HEADS // tp
    local_rows = block_in.shape[1]
    t = local_rows * tp
    rows = min(512, local_rows)
    part = D // tp
    r_in = D // world
    r_ff = fc2_weight.shape[0]
    ff = r_ff * dp

    length_parts = jnp.stack([lengths[0] // 256, lengths[0] % 256]).astype(bf16)
    packed, at = jnp.zeros((16 * PAD,), bf16), 0
    for row_of in (
        (ln1_gain, ln1_bias, out_bias, ln2_gain, ln2_bias), (fc2_bias, qkv_bias),
        (fc1_bias, length_parts),
    ):
        start = at
        for one in row_of:
            packed = packed + jnp.pad(one, (start, 16 * PAD - start - one.shape[0]))
            start += one.shape[0]
        at += PAD
    xq, dy_own, w_qkv, w1, w2, wo, tab, b_pad, length = gather(
        np_, r_in, r_ff, nh, lengths, block_in[0], out_grad[0], qkv_weight, fc1_weight, fc2_weight,
        out_weight, packed.reshape(16, PAD),
    )
    x = xq.reshape(t, D)
    w_qkv, w1 = w_qkv.reshape(D, 3 * part), w1.reshape(D, ff)
    cosine, sine = tables(t)
    q, k, v, cf, ctx, dyq, w2, wo = attn_fwd(
        np_, length, x, tab, w_qkv, b_pad, cosine, sine, dy_own, w2, wo, nh, rows
    )
    w2, wo = w2.reshape(ff, D), wo.reshape(part, D)
    out_part, u_mlp, dc, dw1, dw2, dwo, vec = mlp(
        x, dyq.reshape(t, D), ctx, cf, tab, wo, w1, w2, rows
    )
    per = np_ // 4
    block_out, input_grad, t1, tq, t2, to, mine = attn_bwd(
        np_, r_in, r_ff, x, u_mlp, q, k, v, dc, tab, w_qkv, cosine, sine, vec,
        out_part.reshape(4, local_rows, D), xq, dyq, dw1.reshape(np_, D // np_, ff),
        dw2.reshape(np_, 2 * r_ff, D), dwo.reshape(per, part // per, D),
    )
    outs = assemble(np_, block_out, input_grad, t1, tq, t2, to, mine)
    return (outs[0][None], outs[1][None]) + tuple(outs[2:])


def solution(mesh):
    both = ("dp", "ctx")
    vec, mat, act = P(both), P(both, None), P("dp", "ctx", None)
    weights = (vec, vec, mat, vec, mat, vec, vec, vec, mat, vec, mat, vec)
    return jax.shard_map(
        local,
        mesh=mesh,
        in_specs=(act, act, P("dp")) + weights,
        out_specs=(act, act) + weights + (P("dp"),),
        check_vma=False,
    )
```

```python
import functools
import math

import jax
import jax.numpy as jnp
import numpy as np
from jax import lax
from jax.experimental import pallas as pl
from jax.experimental.pallas import tpu as pltpu
from jax.sharding import PartitionSpec as P

D = 768
HEADS = 12
HEAD_DIM = 64
ROT = 16
PAD = 128
eps_norm = 1e-05
neg_big = -1e30
root_half = math.sqrt(0.5)
inv_root_two_pi = 1.0 / math.sqrt(2.0 * math.pi)
f32 = jnp.float32
bf16 = jnp.bfloat16
VMEM_BYTES = 60 * 2**20


def dot(a, b, dims=((1,), (0,))):
    return lax.dot_general(a, b, (dims, ((), ())), preferred_element_type=f32)


def norm_parts(values):
    centered = values - jnp.mean(values, axis=-1, keepdims=True)
    row_var = jnp.mean(centered * centered, axis=-1, keepdims=True)
    inverse = lax.rsqrt(row_var + eps_norm)
    return centered * inverse, inverse


def turn(u, cosine, sine, first):
    partner = jnp.where(first, pltpu.roll(u, PAD - ROT // 2, 1), pltpu.roll(u, ROT // 2, 1))
    return u * cosine + partner * sine


def split3(v):
    hi = v.astype(bf16).astype(f32)
    mid = (v - hi).astype(bf16).astype(f32)
    low = (v - hi - mid).astype(bf16).astype(f32)
    return hi, mid, low


def fold(op, s):
    out = s[:, :PAD]
    for t in range(1, s.shape[1] // PAD):
        out = op(out, s[:, t * PAD : (t + 1) * PAD])
    return out


def attn_fwd_kernel(
    np_, len_ref, x_ref, tab_ref, w_ref, wb_ref, cos_ref, sin_ref, dy, w2, wo,
    q_ref, k_ref, v_ref, cf_ref, c_ref, dyg, w2g, wog,
    w_scr, s_scr, q_scr, m_scr, l_scr, acc_scr, ls_dy, ss_dy, rs_dy, ls_w, ss_w, rs_w,
):
    i = pl.program_id(0)
    nh = k_ref.shape[0]
    rows = x_ref.shape[0]
    spread = Spread(dy, dyg, ls_dy, ss_dy, rs_dy)
    weights = Rows(np_, (w2, w2g), (wo, wog), ls_w, ss_w, rs_w)

    @pl.when(i == 0)
    def _():
        d, z, c, pair, g, y = place()
        barrier_all(np_, d, z, c, pair)
        weights.start()
        spread.start()

    @pl.when(i == 2)
    def _():
        spread.forward(1)

    @pl.when(i == 3)
    def _():
        spread.forward(3)

    @pl.when(i == 0)
    def _():
        for h in range(3 * nh):
            w_scr[:, h * PAD : h * PAD + HEAD_DIM] = w_ref[:, h * HEAD_DIM : (h + 1) * HEAD_DIM]
            w_scr[:, h * PAD + HEAD_DIM : (h + 1) * PAD] = jnp.zeros((D, PAD - HEAD_DIM), bf16)

    xhat, unused = norm_parts(x_ref[...].astype(f32))
    a1 = (xhat * tab_ref[0:1] + tab_ref[1:2]).astype(bf16)
    cosine, sine = cos_ref[...], sin_ref[...]
    lane = lax.broadcasted_iota(jnp.int32, (rows, PAD), 1)
    first = lane < ROT // 2
    key_pos = i * rows + lax.broadcasted_iota(jnp.int32, (rows, PAD), 0)
    key_bias = jnp.where(key_pos.astype(f32) < len_ref[...], 0.0, neg_big)
    here = pl.ds(pl.multiple_of(i * rows, rows), rows)
    qkv = dot(a1, w_scr[...]) + wb_ref[...]
    for h in range(nh):
        q = turn(qkv[:, h * PAD : (h + 1) * PAD], cosine, sine, first) * HEAD_DIM**-0.5
        q_scr[h] = q.astype(bf16)
        k = turn(qkv[:, (nh + h) * PAD : (nh + h + 1) * PAD], cosine, sine, first)
        k_ref[h, here] = jnp.where(lane == HEAD_DIM, key_bias, k).astype(bf16)
        v_ref[h, here] = qkv[:, (2 * nh + h) * PAD : (2 * nh + h + 1) * PAD].astype(bf16)

    causal = lax.broadcasted_iota(jnp.int32, (rows, rows), 0) >= lax.broadcasted_iota(
        jnp.int32, (rows, rows), 1
    )
    for h in range(nh):
        s = dot(q_scr[h], k_ref[h, here], ((1,), (1,)))
        s = jnp.where(causal, s, neg_big)
        s_scr[h, i] = s
        m_scr[h] = fold(jnp.maximum, s)

    def scores(j, carry):
        there = pl.ds(pl.multiple_of(j * rows, rows), rows)
        for h in range(nh):
            s = dot(q_scr[h], k_ref[h, there], ((1,), (1,)))
            s_scr[h, j] = s
            m_scr[h] = jnp.maximum(m_scr[h], fold(jnp.maximum, s))
        return carry

    lax.fori_loop(0, i, scores, 0)

    @pl.when(i == 1)
    def _():
        spread.forward(0)

    @pl.when(i == 2)
    def _():
        spread.forward(2)

    for h in range(nh):
        m_scr[h] = jnp.broadcast_to(jnp.max(m_scr[h], axis=-1, keepdims=True), (rows, PAD))
        l_scr[h] = jnp.zeros((rows, PAD), f32)
        acc_scr[h] = jnp.zeros((rows, PAD), f32)

    def weigh(j, carry):
        there = pl.ds(pl.multiple_of(j * rows, rows), rows)
        for h in range(nh):
            p = jnp.exp(s_scr[h, j] - m_scr[h][:, :1])
            l_scr[h] += fold(jnp.add, p)
            acc_scr[h] += dot(p.astype(bf16), v_ref[h, there])
        return carry

    lax.fori_loop(0, i + 1, weigh, 0)
    for h in range(nh):
        total = jnp.sum(l_scr[h], axis=-1, keepdims=True)
        context = acc_scr[h] / total
        cf_ref[:, h * PAD : (h + 1) * PAD] = context
        c_ref[:, h * HEAD_DIM : (h + 1) * HEAD_DIM] = context[:, :HEAD_DIM].astype(bf16)
        hi, mid, low = split3(-(m_scr[h][:, :1] + jnp.log(total)))
        q = q_scr[h].astype(f32)
        q = jnp.where(lane == HEAD_DIM + 1, hi, q)
        q = jnp.where(lane == HEAD_DIM + 2, mid, q)
        q = jnp.where(lane == HEAD_DIM + 3, low, q)
        q_ref[h] = q.astype(bf16)

    @pl.when(i == pl.num_programs(0) - 1)
    def _():
        spread.finish()
        weights.finish()


def squares_of(m):
    return jnp.sum(jnp.sum(m * m, axis=0, keepdims=True), axis=1, keepdims=True)


def mlp_kernel(
    x_ref, dy_ref, c_ref, cf_ref, tab_ref, wo_ref, w1_ref, w2_ref,
    part_ref, u_ref, dc_ref, dw1_ref, dw2_ref, dwo_ref, vec_ref,
    dw1_scr, dw2_scr, dwo_scr, wo_scr,
):
    i = pl.program_id(0)
    nh = wo_ref.shape[0] // HEAD_DIM
    rows = x_ref.shape[0]

    @pl.when(i == 0)
    def _():
        dw1_scr[...] = jnp.zeros_like(dw1_scr)
        dw2_scr[...] = jnp.zeros_like(dw2_scr)
        dwo_scr[...] = jnp.zeros_like(dwo_scr)
        vec_ref[...] = jnp.zeros_like(vec_ref)
        for h in range(nh):
            wo_scr[h * PAD : h * PAD + HEAD_DIM] = wo_ref[h * HEAD_DIM : (h + 1) * HEAD_DIM]
            wo_scr[h * PAD + HEAD_DIM : (h + 1) * PAD] = jnp.zeros((PAD - HEAD_DIM, D), bf16)

    xhat, unused = norm_parts(x_ref[...].astype(f32))
    gain = tab_ref[3:4]
    a2 = (xhat * gain + tab_ref[4:5]).astype(bf16)
    z = dot(a2, w1_ref[...]) + tab_ref[5:6]
    cdf = 0.5 * (1.0 + lax.erf(z * root_half))
    hidden = (z * cdf).astype(bf16)
    context = c_ref[...]
    part = dot(hidden, w2_ref[...]) + dot(context, wo_ref[...])
    part_ref[...] = part.astype(part_ref.dtype)
    dy = dy_ref[...]
    slope = cdf + z * jnp.exp(-0.5 * z * z) * inv_root_two_pi
    dz = (dot(dy, w2_ref[...], ((1,), (1,))) * slope).astype(bf16)

    da2 = dot(dz, w1_ref[...], ((1,), (1,)))
    u_ref[...] = (da2 * gain).astype(u_ref.dtype)
    lane = lax.broadcasted_iota(jnp.int32, (rows, PAD), 1)
    dc_all = dot(dy, wo_scr[...], ((1,), (1,))).astype(bf16)
    for h in range(nh):
        dc = dc_all[:, h * PAD : (h + 1) * PAD].astype(f32)
        delta = jnp.sum(dc * cf_ref[:, h * PAD : (h + 1) * PAD], axis=-1, keepdims=True)
        hi, mid, low = split3(-delta)
        dc = jnp.where(lane == HEAD_DIM, hi, dc)
        dc = jnp.where(lane == HEAD_DIM + 1, mid, dc)
        dc = jnp.where(lane == HEAD_DIM + 2, low, dc)
        dc_ref[h] = dc.astype(bf16)
    dw1_scr[...] += dot(a2, dz, ((0,), (0,)))
    dw2_scr[...] += dot(hidden, dy, ((0,), (0,)))
    dwo_scr[...] += dot(context, dy, ((0,), (0,)))
    vec_ref[2:3] += jnp.sum(da2 * xhat, axis=0, keepdims=True)
    vec_ref[3:4] += jnp.sum(da2, axis=0, keepdims=True)
    vec_ref[4:5] += jnp.sum(dz.astype(f32), axis=0, keepdims=True)
    vec_ref[6:7] += jnp.sum(dy.astype(f32), axis=0, keepdims=True)

    @pl.when(i == pl.num_programs(0) - 1)
    def _():
        dw1_ref[...] = dw1_scr[...].astype(bf16)
        dw2_ref[...] = dw2_scr[...].astype(bf16)
        dwo_ref[...] = dwo_scr[...].astype(bf16)
        vec_ref[7:8, 0:1] = (
            squares_of(dw1_scr[...]) + squares_of(dw2_scr[...]) + squares_of(dwo_scr[...])
        )


def attn_bwd_kernel(
    np_, r_in, r_ff, x_ref, u_in_ref, q_ref, k_ref, v_ref, dc_ref, tab_ref, w_ref,
    cos_ref, sin_ref, vec_in_ref, hot_ref, qkv_at, part, xg, dyg, dw1, dw2, dwo,
    block_out, input_grad, t1, tq, t2, to, pieces,
    dk_scr, dv_scr, dq_scr, dqkv_scr, dw_scr, vec_ref, u_scr, dw,
    from_sib, from_far, to_far, mine, done, xq, ls_o, ss_o, rs_o,
    from_sib2, from_far2, to_far2, done2, dyq, ls_u, ss_u, rs_u,
    ls_s, ss_s, rs_s, ls_w, ss_w, rs_w, sums_all, ls_g, ss_g, rs_g,
    b1, bq, b2, bo, s1, sq, s2, so, msg, m_all, p_out, ls, ss_m, rs_m, ss, rs,
):
    step = pl.program_id(0)
    blocks = pl.num_programs(0)
    g, y = place()[4:6]
    b = far_first(step)
    nh = k_ref.shape[0]
    rows = x_ref.shape[0]
    wide = 3 * nh * HEAD_DIM
    lane = lax.broadcasted_iota(jnp.int32, (rows, PAD), 1)
    first = lane < ROT // 2

    def block_rows(n):
        return pl.ds(pl.multiple_of(n * rows, rows), rows)

    here = block_rows(b)
    red = Reduce(
        part, block_out, [(xg, xq)], (from_sib, from_far, to_far, mine, done), ls_o, ss_o, rs_o
    )
    red_u = ReduceQuarters(
        u_scr, input_grad, (from_sib2, from_far2, to_far2, done2), ls_u, ss_u, rs_u
    )
    swap = Swap(np_, [(dw1, b1), (dw2, b2)], (dwo, bo), ls_s, ss_s, rs_s)

    load_dy = pltpu.make_async_copy(dyg.at[red.q_here], dyq, ls.at[4])

    def back(total, r):
        return norm_back(total, xq[r], dyq[r])

    @pl.when(step == 0)
    def _():
        meet(np_)
        red.start()
        load_dy.start()
        swap.start()
        dk_scr[...] = jnp.zeros_like(dk_scr)
        dv_scr[...] = jnp.zeros_like(dv_scr)
        dq_scr[...] = jnp.zeros_like(dq_scr)
        dw_scr[...] = jnp.zeros_like(dw_scr)
        vec_ref[...] = vec_in_ref[...]

    @pl.when(step == 1)
    def _():
        red.add_far(lambda total, r: xq[r].astype(f32) + tab_ref[2:3] + total, (0, 1, 2, 3))

    causal = lax.broadcasted_iota(jnp.int32, (rows, rows), 0) <= lax.broadcasted_iota(
        jnp.int32, (rows, rows), 1
    )

    def block(n, m, diagonal):
        asks, keys = block_rows(n), block_rows(m)
        for h in range(nh):
            k = k_ref[h, keys]
            q = q_ref[h, asks]
            dc = dc_ref[h, asks]
            pt = jnp.exp(dot(k, q, ((1,), (1,))))
            if diagonal:
                pt = jnp.where(causal, pt, 0.0)
            dpt = dot(v_ref[h, keys], dc, ((1,), (1,)))
            dst = (pt * dpt).astype(bf16)
            dv_scr[h, keys] += dot(pt.astype(bf16), dc)
            dk_scr[h, keys] += dot(dst, q)
            dq_scr[h, asks] += dot(dst, k, ((0,), (0,)))

    @pl.when(step == 0)
    def _():
        red.add_near()

    block(b, b, True)

    def off(n, carry):
        block(jnp.where(g == 0, b, b + 1 + n), jnp.where(g == 0, n, b), False)
        return carry

    lax.fori_loop(0, blocks - 1 - step, off, 0)

    @pl.when(step == 1)
    def _():
        red.add_far(lambda total, r: xq[r].astype(f32) + tab_ref[2:3] + total, (4, 5, 6, 7))
        load_dy.wait()

    @pl.when(step == 2)
    def _():
        red_u.pull(mirror(3, g), back)

    @pl.when(step == 3)
    def _():
        red_u.pull(mirror(2, g), back)

    cosine, sine = cos_ref[...], -sin_ref[...]
    for h in range(nh):
        dq = turn(dq_scr[h, here], cosine, sine, first) * HEAD_DIM**-0.5
        dk = turn(dk_scr[h, here], cosine, sine, first)
        for at, piece in ((h, dq), (nh + h, dk), (2 * nh + h, dv_scr[h, here])):
            dqkv_scr[:, at * HEAD_DIM : (at + 1) * HEAD_DIM] = piece[:, :HEAD_DIM].astype(bf16)
    dqkv = dqkv_scr[...]
    xhat, unused = norm_parts(x_ref[...].astype(f32))
    gain = tab_ref[0:1]
    a1 = (xhat * gain + tab_ref[1:2]).astype(bf16)
    da1 = dot(dqkv, w_ref[...], ((1,), (1,)))
    u_scr[b] = (u_in_ref[...] + da1 * gain).astype(bf16)

    @pl.when(step < blocks - 1)
    def _():
        red_u.ready(b)

    dw_scr[...] += dot(a1, dqkv, ((0,), (0,)))
    vec_ref[0:1] += jnp.sum(da1 * xhat, axis=0, keepdims=True)
    vec_ref[1:2] += jnp.sum(da1, axis=0, keepdims=True)
    vec_ref[5:6, :wide] += jnp.sum(dqkv.astype(f32), axis=0, keepdims=True)

    @pl.when(step < blocks - 1)
    def _():
        red_u.push(b)

    @pl.when(step == blocks - 1)
    def _():
        vec_ref[7:8, 0:1] += squares_of(dw_scr[...])
        finish_all(
            np_, r_in, r_ff, wide // 3, red, red_u, swap, back,
            dw, dw_scr, vec_ref, hot_ref, qkv_at, t1, tq, t2, to, pieces,
            ls_w, ss_w, rs_w, sums_all, ls_g, ss_g, rs_g,
            b1, bq, b2, bo, s1, sq, s2, so, msg, m_all, p_out, ls, ss_m, rs_m, ss, rs,
        )


def whole(shape):
    return pl.BlockSpec(shape, lambda i: (0,) * len(shape), pipeline_mode=pl.Buffered(1))


def sds(shape, dtype):
    return jax.ShapeDtypeStruct(shape, dtype)


def params(collective_id=None):
    return pltpu.CompilerParams(
        dimension_semantics=("arbitrary",), vmem_limit_bytes=VMEM_BYTES,
        collective_id=collective_id, has_side_effects=collective_id is not None,
    )


def weight_sems(np_, n):
    return [
        pltpu.SemaphoreType.DMA((n,)),
        pltpu.SemaphoreType.DMA((n, 8 + np_)),
        pltpu.SemaphoreType.DMA((n, 8 + np_)),
    ]


def attn_fwd(np_, length, x, tab, w, wb, cosine, sine, dy, w2, wo, nh, rows):
    t = x.shape[0]
    lanes = pl.BlockSpec((rows, PAD), lambda i: (i, 0))
    any_ = pl.BlockSpec(memory_space=pl.ANY)
    return pl.pallas_call(
        functools.partial(attn_fwd_kernel, np_),
        grid=(t // rows,),
        out_shape=(
            sds((nh, t, PAD), bf16), sds((nh, t, PAD), bf16), sds((nh, t, PAD), bf16),
            sds((t, nh * PAD), f32), sds((t, nh * HEAD_DIM), bf16),
            sds((4,) + dy.shape, bf16),
            sds((np_,) + w2.shape, bf16), sds(wo.shape, bf16),
        ),
        in_specs=[
            whole((1, PAD)), pl.BlockSpec((rows, D), lambda i: (i, 0)),
            whole((8, D)), whole(w.shape), whole(wb.shape), lanes, lanes,
            pl.BlockSpec(memory_space=pltpu.VMEM), any_, any_,
        ],
        out_specs=(
            pl.BlockSpec((nh, rows, PAD), lambda i: (0, i, 0)),
            whole((nh, t, PAD)), whole((nh, t, PAD)),
            pl.BlockSpec((rows, nh * PAD), lambda i: (i, 0)),
            pl.BlockSpec((rows, nh * HEAD_DIM), lambda i: (i, 0)),
            any_, any_, any_,
        ),
        scratch_shapes=[
            pltpu.VMEM((D, 3 * nh * PAD), bf16),
            pltpu.VMEM((nh, t // rows, rows, rows), f32),
            pltpu.VMEM((nh, rows, PAD), bf16),
            pltpu.VMEM((nh, rows, PAD), f32),
            pltpu.VMEM((nh, rows, PAD), f32),
            pltpu.VMEM((nh, rows, PAD), f32),
        ] + spread_sems() + swap_sems(np_, 2),
        compiler_params=params(2),
        name="attn_fwd",
    )(length, x, tab, w, wb, cosine, sine, dy, w2, wo)


def far_first(i):
    return mirror(3 - i, place()[4])


def mlp(x, dy, c, cf, tab, wo, w1, w2, rows):
    t = x.shape[0]
    ff = w1.shape[1]
    nh = wo.shape[0] // HEAD_DIM
    at = lambda cols: pl.BlockSpec((rows, cols), lambda i: (i, 0))
    vm = pltpu.VMEM
    return pl.pallas_call(
        mlp_kernel,
        grid=(t // rows,),
        out_shape=(
            sds((t, D), bf16), sds((t, D), f32), sds((nh, t, PAD), bf16), sds((D, ff), bf16),
            sds((ff, D), bf16), sds(wo.shape, bf16), sds((8, D), f32),
        ),
        in_specs=[
            at(D), at(D), at(c.shape[1]), at(cf.shape[1]),
            whole((8, D)), whole(wo.shape), whole(w1.shape), whole(w2.shape),
        ],
        out_specs=(
            at(D), at(D), pl.BlockSpec((nh, rows, PAD), lambda i: (0, i, 0)),
            whole((D, ff)), whole((ff, D)), whole(wo.shape), whole((8, D)),
        ),
        scratch_shapes=[
            vm((D, ff), f32), vm((ff, D), f32), vm(wo.shape, f32), vm((nh * PAD, D), bf16),
        ],
        compiler_params=params(),
        name="mlp",
    )(x, dy, c, cf, tab, wo, w1, w2)


def attn_bwd(
    np_, r_in, r_ff, x, u_in, q, k, v, dc, tab, w, cosine, sine, vec,
    part, xg, dyg, dw1, dw2, dwo,
):
    t = x.shape[0]
    nh = q.shape[0]
    wide = w.shape[1]
    quarter = part.shape[1]
    ff = dw1.shape[2]
    at = lambda cols: pl.BlockSpec((quarter, cols), lambda i: (far_first(i), 0))
    any_ = pl.BlockSpec(memory_space=pl.ANY)
    dma = pltpu.SemaphoreType.DMA
    vm = pltpu.VMEM
    hot, qkv_at = one_hot_tables(np_, r_in, r_ff, wide // 3)
    per_owner = lambda cols: vm((2, 4, r_in, cols), bf16)
    block = vm((quarter, D), bf16)
    return pl.pallas_call(
        functools.partial(attn_bwd_kernel, np_, r_in, r_ff),
        grid=(4,),
        out_shape=(
            sds((quarter, D), bf16), sds((quarter, D), bf16), sds((8, r_in, ff), bf16),
            sds((8, r_in, wide), bf16), sds((2, r_ff, D), bf16), sds((2, r_in, D), bf16),
            sds((8, PAD), f32),
        ),
        in_specs=[
            at(D), at(D), whole(q.shape), whole(k.shape), whole(v.shape), whole(dc.shape),
            whole((8, D)), whole(w.shape), at(PAD), at(PAD), whole((8, D)), whole(hot.shape),
            whole(qkv_at.shape),
        ] + [any_] * 6,
        out_specs=(any_,) * 7,
        scratch_shapes=[
            vm((nh, t, PAD), f32), vm((nh, t, PAD), f32), vm((nh, t, PAD), f32),
            vm((quarter, wide), bf16), vm((D, wide), f32), vm((8, D), f32),
            vm((4, quarter, D), bf16), vm((np_, D // np_, wide), bf16),
        ] + reduce_scratch(quarter, 1) + [
            vm((2, quarter, D), bf16), block, block, block, block,
            dma((5,)), dma((4, PIECES)), dma((4, PIECES)),
        ] + swap_sems(np_, 3) + swap_sems(np_, 1) + [
            vm((4, 8, D), f32), dma, dma((3,)), dma((3,)),
            vm(dw1.shape, bf16), vm((np_, D // np_, wide), bf16), vm(dw2.shape, bf16),
            vm((np_,) + dwo.shape[1:], bf16),
            per_owner(ff), per_owner(wide), vm((2, r_ff, D), bf16), per_owner(D),
            vm((2 * np_, 8, PAD), f32), vm((2 * np_, 8, PAD), f32), vm((8, PAD), f32),
            dma((10,)), dma((2 * np_,)), dma((2 * np_,)), dma((4, 8)), dma((4, 8)),
        ],
        compiler_params=params(3),
        name="attn_bwd",
    )(
        x, u_in, q, k, v, dc, tab, w, cosine, sine, vec, hot, qkv_at,
        part, xg, dyg, dw1, dw2, dwo,
    )


def assemble_kernel(
    np_, out_in, grad_in, t1, tq, t2, to, pieces,
    out_o, grad_o, g1, b1, qkv, qkv_b, out, out_b, g2, b2, fc1, fc1_b, fc2, fc2_b, norm,
):
    r_ff, r_in = t2.shape[1], t1.shape[1]
    part_w = tq.shape[2] // 3
    out_o[...] = out_in[...]
    grad_o[...] = grad_in[...]
    for s, ref in enumerate((g1, b1, g2, b2, out_b)):
        ref[...] = pieces[0, s * r_in : (s + 1) * r_in]
    fc2_b[...] = pieces[0, 4 * r_in : 5 * r_in]
    qkv_b[...] = pieces[1, : 3 * r_in]
    fc1_b[...] = pieces[2, :r_ff]
    norm[...] = pieces[4, :1]
    for c in range(2):
        for y in range(2):
            a, b = (0, 3) if y == 0 else (1, 2)
            up = t1[4 * c + a].astype(f32) + t1[4 * c + b].astype(f32)
            for pair in range(np_):
                for e, z in enumerate((a, b)):
                    to_at = r_ff * (4 * (2 * pair + c) + z)
                    at = r_ff * (2 * pair + e)
                    fc1[:, to_at : to_at + r_ff] = up[:, at : at + r_ff]
            into = tq[4 * c + a].astype(f32) + tq[4 * c + b].astype(f32)
            for s in range(3):
                to_at = s * D + (2 * y + c) * part_w
                qkv[:, to_at : to_at + part_w] = into[:, s * part_w : (s + 1) * part_w]
    fc2[...] = t2[0].astype(f32) + t2[1].astype(f32)
    out[...] = to[0].astype(f32) + to[1].astype(f32)


def assemble(np_, out, grad, t1, tq, t2, to, pieces):
    r_in, r_ff = t1.shape[1], t2.shape[1]
    vmem = pl.BlockSpec(memory_space=pltpu.VMEM)
    vec = sds((r_in,), f32)
    outs = (
        sds(out.shape, bf16), sds(grad.shape, bf16), vec, vec,
        sds((r_in, tq.shape[2] * 4), f32), sds((3 * r_in,), f32), sds(to.shape[1:], f32), vec,
        vec, vec, sds((r_in, t1.shape[2] * 4), f32), sds((r_ff,), f32), sds(t2.shape[1:], f32),
        vec, sds((1,), f32),
    )
    return pl.pallas_call(
        functools.partial(assemble_kernel, np_),
        out_shape=outs,
        in_specs=[vmem] * 7,
        out_specs=(vmem,) * len(outs),
        name="assemble",
    )(out, grad, t1, tq, t2, to, pieces)


def swap_sems(np_, n):
    return [
        pltpu.SemaphoreType.DMA((n,)),
        pltpu.SemaphoreType.DMA((n, np_)),
        pltpu.SemaphoreType.DMA((n, np_)),
    ]


def tables(t):
    inv_freqs = np.exp(np.arange(ROT // 2, dtype=np.float32) * np.float32(-2.0 * math.log(10000.0) / ROT))
    angles = np.arange(t, dtype=np.float32)[:, None] * inv_freqs.astype(np.float32)[None, :]
    cosine = np.ones((t, PAD), np.float32)
    sine = np.zeros((t, PAD), np.float32)
    half = ROT // 2
    cosine[:, :half] = cosine[:, half:ROT] = np.cos(angles)
    sine[:, :half] = -np.sin(angles)
    sine[:, half:ROT] = np.sin(angles)
    return jnp.asarray(cosine), jnp.asarray(sine)


MESH = pl.DeviceIdType.MESH
AX = ("dp", "ctx")
CHUNKS = 4


def place():
    d, z = lax.axis_index("dp"), lax.axis_index("ctx")
    c, pair, g = lax.rem(d, 2), lax.div(d, 2), lax.div(z, 2)
    y = lax.rem(g + lax.rem(z, 2), 2)
    return d, z, c, pair, g, y


def mirror(m, g):
    return jnp.where(g == 0, m, 3 - m)


def rcopy(src, dst, ss, rs, device):
    return pltpu.make_async_remote_copy(
        src_ref=src, dst_ref=dst, send_sem=ss, recv_sem=rs, device_id=device, device_id_type=MESH
    )


def column_peer(pair, c, z, o):
    m = lax.rem(c * 4 + z + o, 8)
    return lax.div(m, 4), lax.rem(m, 4)


def barrier_all(np_, d, z, c, pair):
    bar = pltpu.get_barrier_semaphore()
    for o in range(1, 8):
        c2, z2 = column_peer(pair, c, z, o)
        pl.semaphore_signal(bar, inc=1, device_id=(2 * pair + c2, z2), device_id_type=MESH)
    for o in range(1, np_):
        pl.semaphore_signal(
            bar, inc=1, device_id=(2 * lax.rem(pair + o, np_) + c, z), device_id_type=MESH
        )
    pl.semaphore_wait(bar, 7 + np_ - 1)


class Spread:
    def __init__(self, own, out, ls, ss, rs):
        self.own, self.out, self.ls, self.ss, self.rs = own, out, ls, ss, rs
        self.rows = out.shape[1] // CHUNKS
        d, z, c, pair, g, y = place()
        self.d, self.z, self.c, self.g, self.y = d, z, c, g, y
        self.prim = c == g
        self.sib = (d + 1 - 2 * c, z)
        self.partner = (d, z + 1 - 2 * lax.rem(z, 2))
        self.far = (d, 1 + c)

    def cut(self, ref, j):
        return ref.at[pl.ds(j * self.rows, self.rows)]

    def send(self, q, j, way, device, src=None):
        src = self.cut(self.out.at[q], j) if src is None else src
        return rcopy(
            src, self.cut(self.out.at[q], j), self.ss.at[way, q, j], self.rs.at[q, j], device
        )

    def start(self):
        own = [self.cut(self.own, j) for j in range(CHUNKS)]

        @pl.when(self.prim)
        def _():
            pltpu.make_async_copy(self.own, self.out.at[self.z], self.ls).start()
            for j in range(CHUNKS):
                self.send(self.z, j, 0, self.partner, own[j]).start()
            for j in range(CHUNKS):
                self.send(self.z, j, 1, self.sib, own[j]).start()

        @pl.when(jnp.logical_not(self.prim))
        def _():
            for j in range(CHUNKS):
                self.send(self.z, j, 0, self.far, own[j]).start()

    def wait_recv(self, q, j):
        self.send(q, j, 0, self.sib).wait_recv()

    def forward(self, j):
        far = (mirror(2, self.g), mirror(3, self.g))
        end, mid = mirror(0, self.g), mirror(1, self.g)

        @pl.when(jnp.logical_and(self.prim, self.y == 1))
        def _():
            for q in far:
                self.wait_recv(q, j)
                self.send(q, j, 0, self.partner).start()
                self.send(q, j, 1, self.sib).start()
            self.wait_recv(end, j)
            self.send(end, j, 1, self.sib).start()

        @pl.when(jnp.logical_and(self.prim, self.y == 0))
        def _():
            self.wait_recv(mid, j)
            self.send(mid, j, 1, self.sib).start()
            if j > 0:
                for q in far:
                    self.wait_recv(q, j - 1)
                    self.send(q, j - 1, 1, self.sib).start()

    def finish(self):
        far = (mirror(2, self.g), mirror(3, self.g))
        end, mid = mirror(0, self.g), mirror(1, self.g)

        @pl.when(jnp.logical_and(self.prim, self.y == 0))
        def _():
            for q in far:
                self.wait_recv(q, CHUNKS - 1)
                self.send(q, CHUNKS - 1, 1, self.sib).start()
            for j in range(CHUNKS):
                self.send(end, j, 0, self.partner).wait_send()

        @pl.when(jnp.logical_and(self.prim, self.y == 1))
        def _():
            for j in range(CHUNKS):
                for q in far + (mid,):
                    self.send(q, j, 0, self.partner).wait_send()

        @pl.when(self.prim)
        def _():
            pltpu.make_async_copy(self.own, self.out.at[self.z], self.ls).wait()
            for q in range(4):
                for j in range(CHUNKS):
                    self.send(q, j, 1, self.sib).wait_send()

        @pl.when(jnp.logical_not(self.prim))
        def _():
            for q in range(4):
                for j in range(CHUNKS):
                    self.wait_recv(q, j)
            for j in range(CHUNKS):
                self.send(self.z, j, 0, self.far).wait_send()


class Weights:
    def __init__(self, np_, sliced, w2, wo, ls, ss, rs):
        self.np_, self.sliced, self.w2, self.wo = np_, sliced, w2, wo
        self.ls, self.ss, self.rs = ls, ss, rs
        self.here = place()

    def first(self, s, o):
        d, z, c, pair, g, y = self.here
        src, out, by_slice = self.sliced[s]
        if o == 0:
            return pltpu.make_async_copy(
                src.at[2 * y + c] if by_slice else src, out.at[pair, c, z], self.ls.at[s]
            )
        c2, z2 = column_peer(pair, c, z, o)
        y2 = lax.rem(lax.div(z2, 2) + lax.rem(z2, 2), 2)
        return rcopy(
            src.at[2 * y2 + c2] if by_slice else src, out.at[pair, c, z],
            self.ss.at[s, o - 1], self.rs.at[s, o - 1], (2 * pair + c2, z2),
        )

    def second(self, s, o):
        d, z, c, pair, g, y = self.here
        out = self.sliced[s][1]
        return rcopy(
            out.at[pair], out.at[pair], self.ss.at[s, 7 + o - 1], self.rs.at[s, 7 + o - 1],
            (2 * lax.rem(pair + o, self.np_) + c, z),
        )

    def start(self):
        d, z, c, pair, g, y = self.here
        n = len(self.sliced)
        for s in range(n):
            for o in range(8):
                self.first(s, o).start()

    def start_rows(self):
        for o in range(2):
            self.w2_first(o).start()
        self.wo_first(lambda cp: cp.start())

    def w2_first(self, o):
        d, z, c, pair, g, y = self.here
        src, out = self.w2
        n = len(self.sliced)
        if o == 0:
            return pltpu.make_async_copy(src, out.at[g], self.ls.at[n])
        return rcopy(src, out.at[g], self.ss.at[n, 0], self.rs.at[n, 0], (d, 3 - z))

    def wo_parts(self):
        d, z, c, pair, g, y = self.here
        per = self.np_ // 4
        owner = lax.div(pair, per)
        return per, owner, lax.rem(owner, 2), lax.div(owner, 2)

    def wo_first(self, do, sending=True):
        d, z, c, pair, g, y = self.here
        src, out = self.wo
        n = len(self.sliced) + 1
        per, owner, c_to, y_to = self.wo_parts()
        slot = out.at[lax.rem(pair, per), c, z]
        for t in range(2):
            z_to = jnp.where(t == 0, y_to, 3 - y_to)
            mine = jnp.logical_and(c == c_to, z == z_to)

            @pl.when(mine)
            def _():
                do(pltpu.make_async_copy(src, slot, self.ls.at[n]))

            @pl.when(jnp.logical_not(mine))
            def _():
                cp = rcopy(
                    src, slot, self.ss.at[n, t], self.rs.at[n, c * 4 + z], (2 * pair + c_to, z_to)
                )
                do(cp)

    def between(self, s):
        self.first(s, 0).wait()
        for o in range(1, 8):
            self.first(s, o).wait_recv()
        for o in range(1, self.np_):
            self.second(s, o).start()

    def finish_rows(self):
        d, z, c, pair, g, y = self.here
        n = len(self.sliced) + 1
        per, owner, c_to, y_to = self.wo_parts()
        for o in range(2):
            self.w2_first(o).wait()

        @pl.when(owner == 2 * y + c)
        def _():
            for c2 in range(2):
                for z2 in range(4):
                    own = jnp.logical_and(c == c2, z == z2)

                    @pl.when(jnp.logical_not(own))
                    def _():
                        slot = self.wo[1].at[0, c2, z2]
                        rcopy(
                            slot, slot, self.ss.at[n, 0], self.rs.at[n, c2 * 4 + z2],
                            (d + 1 - 2 * c, z),
                        ).wait_recv()
            pltpu.make_async_copy(
                self.wo[0], self.wo[1].at[0, c, z], self.ls.at[n]
            ).wait()

        for t in range(2):
            z_to = jnp.where(t == 0, y_to, 3 - y_to)

            @pl.when(jnp.logical_not(jnp.logical_and(c == c_to, z == z_to)))
            def _():
                rcopy(
                    self.wo[0], self.wo[1].at[0, c, z], self.ss.at[n, t], self.rs.at[n, 0],
                    (d + 1 - 2 * c, z),
                ).wait_send()

    def finish(self, s):
        for o in range(1, 8):
            self.first(s, o).wait_send()
        for o in range(1, self.np_):
            self.second(s, o).wait()


class Rows:
    def __init__(self, np_, w2, wo, ls, ss, rs):
        self.np_, self.w2, self.wo, self.ls, self.ss, self.rs = np_, w2, wo, ls, ss, rs
        self.here = place()

    def copy_w2(self, o):
        d, z, c, pair, g, y = self.here
        src, out = self.w2
        if o == 0:
            return pltpu.make_async_copy(src, out.at[pair], self.ls.at[0])
        to = (2 * lax.rem(pair + o, self.np_) + c, z)
        return rcopy(src, out.at[pair], self.ss.at[0, o], self.rs.at[0, o], to)

    def copy_wo(self, o):
        d, z, c, pair, g, y = self.here
        src, out = self.wo
        slot = lax.rem(pair, self.np_ // 4)
        if o == 0:
            return pltpu.make_async_copy(src.at[slot], out.at[slot], self.ls.at[1])
        to = (2 * lax.rem(pair + o, self.np_) + c, z)
        return rcopy(src.at[slot], out.at[slot], self.ss.at[1, o], self.rs.at[1, o], to)

    def holds(self, pair):
        d, z, c, unused, g, y = self.here
        return lax.div(pair, self.np_ // 4) == 2 * y + c

    def start(self):
        @pl.when(self.holds(self.here[3]))
        def _():
            for o in range(1, self.np_):
                self.copy_wo(o).start()
            self.copy_wo(0).start()

        for o in range(1, self.np_):
            self.copy_w2(o).start()
        self.copy_w2(0).start()

    def finish(self):
        pair = self.here[3]
        for o in range(self.np_):
            self.copy_w2(o).wait()

        @pl.when(self.holds(pair))
        def _():
            self.copy_wo(0).wait()
            for o in range(1, self.np_):
                self.copy_wo(o).wait_send()

        for o in range(1, self.np_):
            @pl.when(self.holds(lax.rem(pair + self.np_ - o, self.np_)))
            def _():
                self.copy_wo(o).wait_recv()


def decode_tables(np_, r_in, r_ff, part, nh):
    wide = 3 * nh * PAD
    f = np.arange(D)
    by_d = np.zeros((8, D), np.int32)
    by_d[0], by_d[1] = f // r_in, f % r_in
    by_d[2], by_d[3], by_d[4] = f // (2 * r_ff), (f // r_ff) % 2, f % r_ff
    p = np.arange(wide)
    head, lane = p // PAD, p % PAD
    by_q = np.full((8, wide), -1, np.int32)
    for k in range(4):
        at = (head // nh) * D + k * part + (head % nh) * HEAD_DIM + lane
        real = lane < HEAD_DIM
        by_q[k, real] = (at // (3 * r_in))[real]
        by_q[4 + k, real] = (r_in + at % (3 * r_in))[real]
    extra = np.zeros((1, wide), np.float32)
    extra[0, (head < nh) & (lane == HEAD_DIM)] = HEAD_DIM**0.5
    keys = (head >= nh) & (head < 2 * nh)
    extra[0, keys & (lane > HEAD_DIM) & (lane < HEAD_DIM + 4)] = 1.0
    extra[0, (head >= 2 * nh) & (lane >= HEAD_DIM) & (lane < HEAD_DIM + 3)] = 1.0
    return jnp.asarray(by_d), jnp.asarray(by_q), jnp.asarray(extra)


def decode(np_, r_in, r_ff, vec, by_d, by_q, extra, tab, b_pad, length):
    d, z, c, pair, g, y = place()
    world = 8 * np_
    packed = vec[...].reshape(world * 16, PAD)
    m = lax.broadcasted_iota(jnp.int32, (world, world * 16), 1)
    n = lax.broadcasted_iota(jnp.int32, (world, world * 16), 0)
    row = [
        dot(jnp.where(m == 16 * n + r, 1.0, 0.0).astype(bf16), packed).astype(bf16)
        for r in range(3)
    ]

    def pick(x, lanes, owner):
        w = lanes.shape[1]
        hot = lax.broadcasted_iota(jnp.int32, (PAD, w), 0) == lanes
        got = dot(x, jnp.where(hot, 1.0, 0.0).astype(bf16))
        mine = lax.broadcasted_iota(jnp.int32, (world, w), 0) == owner
        return jnp.sum(jnp.where(mine, got, 0.0), axis=0, keepdims=True)

    owner, lanes = by_d[0:1], by_d[1:2]
    tab[0:1] = pick(row[0], lanes, owner)
    tab[1:2] = pick(row[0], lanes + r_in, owner)
    tab[2:3] = pick(row[0], lanes + 2 * r_in, owner) + pick(row[1], lanes, owner)
    tab[3:4] = pick(row[0], lanes + 3 * r_in, owner)
    tab[4:5] = pick(row[0], lanes + 4 * r_in, owner)
    owner = by_d[2:3] * 8 + c * 4 + jnp.where(by_d[3:4] == 0, y, 3 - y)
    tab[5:6] = pick(row[2], by_d[4:5], owner)
    tab[6:8] = jnp.zeros((2, D), f32)
    k = 2 * y + c
    b_pad[...] = pick(row[1], by_q[pl.ds(4 + k, 1)], by_q[pl.ds(k, 1)]) + extra[...]
    mine = lax.broadcasted_iota(jnp.int32, (world, PAD), 0) == (2 * pair + g) * 4
    parts = jnp.sum(jnp.where(mine, row[2].astype(f32), 0.0), axis=0, keepdims=True)
    lane = lax.broadcasted_iota(jnp.int32, (1, PAD), 1)
    parts = jnp.where(lane == r_ff, parts * 256.0, jnp.where(lane == r_ff + 1, parts, 0.0))
    length[...] = jnp.broadcast_to(jnp.sum(parts, axis=1, keepdims=True), (1, PAD))


def gather_kernel(
    np_, r_in, r_ff, len_ref, x, grad, qkv_w, fc1_w, w2, wo, vec_own, by_d, by_q, extra,
    xg, dy_own, wqg, w1g, w2p, wop, tab, b_pad, length, wq, w1, dy, ls_m, vec, ls_x, ss_x, rs_x, ls_w, ss_w, rs_w,
):
    d, z, c, pair, g, y = place()
    load = pltpu.make_async_copy(grad, dy, ls_m.at[0])
    load.start()
    part_w = wq.shape[2] // 3
    for k in range(4):
        y2, c2 = k // 2, k % 2
        for s in range(3):
            at = s * D + k * part_w
            wq[k, :, s * part_w : (s + 1) * part_w] = qkv_w[:, at : at + part_w]
        for n in range(np_):
            for e, z2 in enumerate((0, 3) if y2 == 0 else (1, 2)):
                at = r_ff * (4 * (2 * n + c2) + z2)
                to = r_ff * (2 * n + e)
                w1[k, :, to : to + r_ff] = fc1_w[:, at : at + r_ff]
    barrier_all(np_, d, z, c, pair)
    spread = Spread(x, xg, ls_x, ss_x, rs_x)
    weights = Weights(
        np_, [(vec_own, vec, False), (wq, wqg, True), (w1, w1g, True)], (w2, w2p), (wo, wop),
        ls_w, ss_w, rs_w,
    )
    weights.start()
    spread.start()
    weights.start_rows()
    load.wait()
    pos = z * dy.shape[0] + lax.broadcasted_iota(jnp.int32, (dy.shape[0], 1), 0)
    dy[...] = jnp.where(pos < len_ref[0], dy[...].astype(f32), 0.0).astype(bf16)
    store = pltpu.make_async_copy(dy, dy_own, ls_m.at[1])
    store.start()
    for s in range(2):
        weights.between(s)
    spread.forward(0)
    weights.between(2)
    weights.finish(0)
    for j in range(1, CHUNKS):
        spread.forward(j)
    decode(np_, r_in, r_ff, vec, by_d, by_q, extra, tab, b_pad, length)
    spread.finish()
    for s in range(1, 3):
        weights.finish(s)
    weights.finish_rows()
    store.wait()


def spread_sems():
    return [
        pltpu.SemaphoreType.DMA,
        pltpu.SemaphoreType.DMA((2, 4, CHUNKS)),
        pltpu.SemaphoreType.DMA((4, CHUNKS)),
    ]


def gather(
    np_, r_in, r_ff, nh, length, x, grad, qkv_w, fc1_w, w2, wo, vec, collective_id=1
):
    any_ = pl.BlockSpec(memory_space=pl.ANY)
    vmem = pl.BlockSpec(memory_space=pltpu.VMEM)
    wide = 3 * nh * PAD
    thin, ff = qkv_w.shape[1] // 4, fc1_w.shape[1] // 4
    return pl.pallas_call(
        functools.partial(gather_kernel, np_, r_in, r_ff),
        out_shape=(
            sds((4,) + x.shape, bf16), sds(x.shape, bf16), sds((np_, 2, 4, r_in, thin), bf16),
            sds((np_, 2, 4, r_in, ff), bf16), sds((2,) + w2.shape, bf16),
            sds((np_ // 4, 2, 4) + wo.shape, bf16),
            sds((8, D), f32), sds((1, wide), f32), sds((1, PAD), f32),
        ),
        in_specs=[pl.BlockSpec(memory_space=pltpu.SMEM), any_, any_, vmem, vmem, any_, any_, any_]
        + [vmem] * 3,
        out_specs=(any_,) * 6 + (vmem,) * 3,
        scratch_shapes=[
            pltpu.VMEM((4, r_in, thin), bf16), pltpu.VMEM((4, r_in, ff), bf16),
            pltpu.VMEM(x.shape, bf16), pltpu.SemaphoreType.DMA((2,)),
            pltpu.VMEM((np_, 2, 4, 16, PAD), bf16),
        ] + spread_sems() + weight_sems(np_, 5),
        compiler_params=pltpu.CompilerParams(
            collective_id=collective_id, has_side_effects=True, vmem_limit_bytes=VMEM_BYTES
        ),
        name="gather",
    )(length, x, grad, qkv_w, fc1_w, w2, wo, vec, *decode_tables(np_, r_in, r_ff, thin // 3, nh))


PIECES = 8


class Reduce:
    def __init__(self, part, out, extra, bufs, ls, ss, rs):
        self.part, self.out, self.extra = part, out, extra
        self.from_sib, self.from_far, self.to_far, self.mine, self.done = bufs
        self.ls, self.ss, self.rs = ls, ss, rs
        d, z, c, pair, g, y = place()
        self.role = jnp.where(c == g, 0, 1)
        self.y = y
        self.sib = (d + 1 - 2 * c, z)
        self.partner = (d, z + 1 - 2 * lax.rem(z, 2))
        self.q_here = mirror(2 * y + self.role, g)
        self.q_there = mirror(2 * (1 - y) + self.role, g)
        self.sib_here = mirror(2 * y + 1 - self.role, g)
        self.sib_there = mirror(2 * (1 - y) + 1 - self.role, g)
        self.owner = (2 * pair + g, self.q_here)
        self.self_owner = jnp.logical_and(self.role == 0, y == 0)
        self.self_source = jnp.where(c == 0, z, 3 - z) == 0
        self.rows = self.out.shape[0] // PIECES

    def rows_of(self, j):
        return pl.ds(j * self.rows, self.rows)

    def to_sib(self, t, j):
        q = self.sib_there if t == 0 else self.sib_here
        r = self.rows_of(j)
        return rcopy(
            self.part.at[q, r], self.from_sib.at[t, r], self.ss.at[t, j], self.rs.at[t, j], self.sib
        )

    def load(self, t):
        q = self.q_there if t == 0 else self.q_here
        return pltpu.make_async_copy(self.part.at[q], self.mine.at[t], self.ls.at[t])

    def load_extra(self, e):
        src, dst = self.extra[e]
        return pltpu.make_async_copy(src.at[self.q_here], dst, self.ls.at[2 + e])

    def across(self, j):
        r = self.rows_of(j)
        return rcopy(
            self.to_far.at[r], self.from_far.at[r], self.ss.at[2, j], self.rs.at[2, j], self.partner
        )

    def home(self, j):
        r = self.rows_of(j)
        return rcopy(
            self.done.at[r], self.out.at[r], self.ss.at[3, j], self.rs.at[3, j], self.owner
        )

    def keep(self):
        return pltpu.make_async_copy(self.done, self.out, self.ls.at[4])

    def start(self):
        for t in range(2):
            for j in range(PIECES):
                self.to_sib(t, j).start()
        for t in range(2):
            self.load(t).start()
        for e in range(len(self.extra)):
            self.load_extra(e).start()

    def add_near(self):
        self.load(0).wait()
        for j in range(PIECES):
            r = self.rows_of(j)
            self.to_sib(0, j).wait_recv()
            total = self.mine[0, r].astype(f32) + self.from_sib[0, r].astype(f32)
            self.to_far[r] = total.astype(bf16)
            self.across(j).start()
        self.load(1).wait()
        for e in range(len(self.extra)):
            self.load_extra(e).wait()

    def add_far(self, finish, pieces=range(PIECES)):
        for j in pieces:
            r = self.rows_of(j)
            self.to_sib(1, j).wait_recv()
            self.across(j).wait_recv()
            total = self.mine[1, r].astype(f32) + self.from_sib[1, r].astype(f32)
            total = total + self.from_far[r].astype(f32)
            self.done[r] = finish(total, r).astype(bf16)

            @pl.when(jnp.logical_not(self.self_owner))
            def _():
                self.home(j).start()

    def finish(self):
        @pl.when(self.self_owner)
        def _():
            self.keep().start()
            self.keep().wait()

        for j in range(PIECES):
            @pl.when(jnp.logical_not(self.self_source))
            def _():
                self.home(j).wait_recv()

        for j in range(PIECES):
            self.to_sib(0, j).wait_send()
            self.to_sib(1, j).wait_send()
            self.across(j).wait_send()

            @pl.when(jnp.logical_not(self.self_owner))
            def _():
                self.home(j).wait_send()


def reduce_scratch(rows, extras):
    return [
        pltpu.VMEM((2, rows, D), bf16), pltpu.VMEM((rows, D), bf16), pltpu.VMEM((rows, D), bf16),
        pltpu.VMEM((2, rows, D), bf16), pltpu.VMEM((rows, D), bf16),
    ] + [pltpu.VMEM((rows, D), bf16)] * extras + [
        pltpu.SemaphoreType.DMA((5,)),
        pltpu.SemaphoreType.DMA((4, PIECES)),
        pltpu.SemaphoreType.DMA((4, PIECES)),
    ]


class ReduceQuarters(Reduce):
    def __init__(self, part, out, bufs, ls, ss, rs):
        from_sib, from_far, to_far, done = bufs
        super().__init__(part, out, [], (from_sib, from_far, to_far, None, done), ls, ss, rs)

    def ready(self, q):
        for t, mine in ((0, self.sib_there), (1, self.sib_here)):
            @pl.when(mine == q)
            def _():
                for j in range(PIECES):
                    self.to_sib(t, j).start()

    def push(self, q):
        @pl.when(self.q_there == q)
        def _():
            for j in range(PIECES):
                r = self.rows_of(j)
                self.to_sib(0, j).wait_recv()
                total = self.part[q, r].astype(f32) + self.from_sib[0, r].astype(f32)
                self.to_far[r] = total.astype(bf16)
                self.across(j).start()

    def pull(self, q, finish):
        @pl.when(self.q_here == q)
        def _():
            for j in range(PIECES):
                r = self.rows_of(j)
                self.to_sib(1, j).wait_recv()
                self.across(j).wait_recv()
                total = self.part[q, r].astype(f32) + self.from_sib[1, r].astype(f32)
                total = total + self.from_far[r].astype(f32)
                self.done[r] = finish(total, r).astype(bf16)

                @pl.when(jnp.logical_not(self.self_owner))
                def _():
                    self.home(j).start()


class Swap:
    def __init__(self, np_, arrays, wo, ls, ss, rs):
        self.np_, self.arrays, self.wo, self.ls, self.ss, self.rs = np_, arrays, wo, ls, ss, rs
        self.here = place()

    def copy(self, s, o):
        d, z, c, pair, g, y = self.here
        src, dst = self.arrays[s]
        to = lax.rem(pair + o, self.np_)
        if o == 0:
            return pltpu.make_async_copy(src.at[pair], dst.at[pair], self.ls.at[s])
        return rcopy(
            src.at[to], dst.at[pair], self.ss.at[s, o], self.rs.at[s, o], (2 * to + c, z)
        )

    def copy_wo(self, o):
        d, z, c, pair, g, y = self.here
        src, dst = self.wo
        n = len(self.arrays)
        per = self.np_ // 4
        to = lax.rem(pair + o, self.np_)
        if o == 0:
            return pltpu.make_async_copy(src.at[lax.rem(pair, per)], dst.at[pair], self.ls.at[n])
        return rcopy(
            src.at[lax.rem(to, per)], dst.at[pair], self.ss.at[n, o], self.rs.at[n, o],
            (2 * to + c, z),
        )

    def collects(self, pair2):
        d, z, c, pair, g, y = self.here
        return lax.div(pair2, self.np_ // 4) == 2 * y + c

    def start(self):
        d, z, c, pair, g, y = self.here
        for s in range(len(self.arrays)):
            for o in range(1, self.np_):
                self.copy(s, o).start()
            self.copy(s, 0).start()
        if self.wo is not None:
            for o in range(self.np_):
                @pl.when(self.collects(lax.rem(pair + o, self.np_)))
                def _():
                    self.copy_wo(o).start()

    def finish(self):
        d, z, c, pair, g, y = self.here
        for s in range(len(self.arrays)):
            for o in range(self.np_):
                self.copy(s, o).wait()
        if self.wo is not None:
            for o in range(self.np_):
                @pl.when(self.collects(lax.rem(pair + o, self.np_)))
                def _():
                    if o == 0:
                        self.copy_wo(o).wait()
                    else:
                        self.copy_wo(o).wait_send()

                if o > 0:
                    @pl.when(self.collects(pair))
                    def _():
                        self.copy_wo(o).wait_recv()


def group_peer(o):
    d, z, c, pair, g, y = place()
    c2 = 1 - c if o % 2 else c
    z2 = z + 1 - 2 * lax.rem(z, 2) if o // 2 else z
    return 2 * pair + c2, z2


class Group:
    def __init__(self, own, all_, ls, ss, rs):
        self.own, self.all_, self.ls, self.ss, self.rs = own, all_, ls, ss, rs
        d, z, c, pair, g, y = place()
        self.k = 2 * y + c

    def copy(self, o):
        if o == 0:
            return pltpu.make_async_copy(self.own, self.all_.at[self.k], self.ls)
        return rcopy(
            self.own, self.all_.at[self.k], self.ss.at[o - 1], self.rs.at[o - 1], group_peer(o)
        )

    def start(self):
        for o in range(4):
            self.copy(o).start()

    def finish(self):
        for o in range(4):
            self.copy(o).wait()


def norm_back(total, x, dy):
    xhat, inverse = norm_parts(x.astype(f32))
    back = inverse * (
        total
        - jnp.mean(total, axis=-1, keepdims=True)
        - xhat * jnp.mean(total * xhat, axis=-1, keepdims=True)
    )
    return dy.astype(f32) + back


def same_slice_peer(np_, e):
    d, z, c, pair, g, y = place()
    to = lax.rem(pair * 2 + g + e, 2 * np_)
    pair2, g2 = lax.div(to, 2), lax.rem(to, 2)
    return to, (2 * pair2 + c, jnp.where(g2 == g, z, 3 - z))


def one_hot_tables(np_, r_in, r_ff, part):
    f = np.arange(D)
    lane = np.arange(PAD)
    place_qkv = (f // part) * D + f % part
    tables_ = [f % r_in, f % r_ff] + [(place_qkv + k * part) % (3 * r_in) for k in range(4)]
    hot = np.stack([(t[:, None] == lane[None, :]) for t in tables_]).astype(np.float32)
    hot[2:, 3 * part :] = 0.0
    return jnp.asarray(hot, bf16), jnp.asarray(place_qkv[None], jnp.int32)


def pieces_of(np_, sums_all, sums, hot_ref, qkv_at, r_in, r_ff, part, msg):
    d, z, c, pair, g, y = place()
    n = 2 * np_
    e = lax.broadcasted_iota(jnp.int32, (n, D), 0)
    f = lax.broadcasted_iota(jnp.int32, (n, D), 1)
    group = lax.rem(e, 2)
    index = (lax.div(e, 2) * 2 + c) * 4 + jnp.where(group == 0, y, 3 - y)

    def select(rows_, inside, hot):
        picked = []
        for row in rows_:
            for v in split3(row):
                picked.append(jnp.where(inside, v, 0.0))
        got = dot(jnp.concatenate(picked, axis=0).astype(bf16), hot)
        return [
            got[3 * s * n : (3 * s + 1) * n] + got[(3 * s + 1) * n : (3 * s + 2) * n]
            + got[(3 * s + 2) * n : (3 * s + 3) * n]
            for s in range(len(rows_))
        ]

    d_vecs = sums_all[0, 0:4] + sums_all[1, 0:4] + sums_all[2, 0:4] + sums_all[3, 0:4]
    rows_ = [d_vecs[s : s + 1] for s in range(4)] + [sums[6:7]]
    inside = jnp.logical_and(f >= index * r_in, f < (index + 1) * r_in)
    got = select(rows_, inside, hot_ref[0])
    first = got[0]
    for s in range(1, 5):
        first = first + pltpu.roll(got[s], s * r_in, 1)
    second = jnp.zeros((n, PAD), f32)
    for k in range(4):
        at = qkv_at[...] + k * part
        inside = jnp.logical_and(at >= index * (3 * r_in), at < (index + 1) * (3 * r_in))
        second = second + select([sums_all[k, 5:6]], inside, hot_ref[2 + k])[0]
    inside = jnp.logical_and(f >= e * r_ff, f < (e + 1) * r_ff)
    third = select([sums[4:5]], inside, hot_ref[1])[0]
    squares = squares_of(d_vecs) + 2.0 * squares_of(sums[6:7])
    for k in range(4):
        squares = squares + squares_of(sums_all[k, 4:6]) + sums_all[k, 7:8, 0:1]
    for s in range(n):
        msg[s, 0:1] = first[s : s + 1]
        msg[s, 1:2] = second[s : s + 1]
        msg[s, 2:3] = third[s : s + 1]
        msg[s, 3:4] = jnp.broadcast_to(squares, (1, PAD))
        msg[s, 4:8] = jnp.zeros((4, PAD), f32)


def meet(np_):
    d, z, c, pair, g, y = place()
    bar = pltpu.get_barrier_semaphore()
    for o in range(1, 8):
        c2, z2 = column_peer(pair, c, z, o)
        pl.semaphore_signal(bar, inc=1, device_id=(2 * pair + c2, z2), device_id_type=MESH)
    for e in range(1, 2 * np_):
        unused, peer = same_slice_peer(np_, e)
        pl.semaphore_signal(bar, inc=1, device_id=peer, device_id_type=MESH)
    pl.semaphore_wait(bar, 7 + 2 * np_ - 1)


def finish_all(
    np_, r_in, r_ff, part_w, red_out, red, swap1, back,
    dw, dw_sum, sums, hot_ref, qkv_at, t1, tq, t2, to, pieces,
    ls_w, ss_w, rs_w, sums_all, ls_g, ss_g, rs_g,
    b1, bq, b2, bo, s1, sq, s2, so, msg, m_all, p_out, ls, ss_m, rs_m, ss, rs,
):
    d, z, c, pair, g, y = place()
    grp = Group(sums, sums_all, ls_g, ss_g, rs_g)
    swap = Swap(np_, [(dw, bq)], None, ls_w, ss_w, rs_w)
    grp.start()
    share = D // np_
    for n in range(np_):
        dw[n] = dw_sum[n * share : (n + 1) * share].astype(bf16)
    swap.start()
    red.ready(mirror(0, g))
    grp.finish()
    pieces_of(np_, sums_all, sums, hot_ref, qkv_at, r_in, r_ff, part_w, msg)
    me = pair * 2 + g

    def tell(e):
        to_, peer = same_slice_peer(np_, e)
        return rcopy(msg.at[to_], m_all.at[me], ss_m.at[e], rs_m.at[e], peer)

    own = pltpu.make_async_copy(msg.at[me], m_all.at[me], ls.at[0])
    own.start()
    for e in range(1, 2 * np_):
        tell(e).start()
    red.push(mirror(0, g))
    red.pull(mirror(1, g), back)
    own.wait()
    for e in range(1, 2 * np_):
        tell(e).wait()
    norms = [jnp.sqrt(m_all[e, 3:4, 0:1]) for e in range(2 * np_)]
    mean_norm = sum(norms) / (2 * np_)
    factors = [mean_norm / jnp.maximum(n, mean_norm) for n in norms]
    p_out[...] = sum(f * m_all[e] for e, f in enumerate(factors))
    p_out[4:5, 0:1] = sum(jnp.where(d == e, n, 0.0) for e, n in enumerate(norms))
    group_factors = [
        jnp.where(g == 0, factors[2 * n], factors[2 * n + 1]) for n in range(np_)
    ]
    final = pltpu.make_async_copy(p_out, pieces, ls.at[9])
    final.start()
    collects = swap1.collects(pair)
    swap1.finish()

    def rows_to(s, src, dst, o, slot):
        c2, z2 = column_peer(pair, c, z, o)
        if o == 0:
            return pltpu.make_async_copy(src.at[c2, z2], dst.at[slot], ls.at[5 + s])
        return rcopy(
            src.at[c2, z2], dst.at[slot], ss.at[s, o], rs.at[s, o], (2 * pair + c2, z2)
        )

    def scaled(n, buf, acc, dst):
        for c2 in range(2):
            for z2 in range(4):
                at = pl.ds((c2 * 4 + z2) * r_in, r_in)
                total = sum(f * buf[m, at].astype(f32) for m, f in enumerate(group_factors))
                acc[c2, z2] = total.astype(acc.dtype)
        for o in range(8):
            rows_to(n, acc, dst, o, c * 4 + z).start()

    for t in range(2):
        at = pl.ds(t * r_ff, r_ff)
        total = sum(f * b2[m, at].astype(f32) for m, f in enumerate(group_factors))
        s2[t] = total.astype(s2.dtype)
    mirror_copy = rcopy(s2.at[1 - g], t2.at[1], ss.at[2, 0], rs.at[2, 0], (d, 3 - z))
    mirror_copy.start()
    kept = pltpu.make_async_copy(s2.at[g], t2.at[0], ls.at[7])
    kept.start()
    scaled(1, b1, s1, t1)
    swap.finish()
    scaled(0, bq, sq, tq)

    def wo_to(o):
        c2, z2 = column_peer(pair, c, z, o)
        if o == 0:
            return pltpu.make_async_copy(so.at[c2, z2], to.at[g], ls.at[8])
        return rcopy(
            so.at[c2, z2], to.at[g], ss.at[3, o], rs.at[3, g], (2 * pair + c2, z2)
        )

    @pl.when(collects)
    def _():
        for c2 in range(2):
            for z2 in range(4):
                at = pl.ds((c2 * 4 + z2) * r_in, r_in)
                total = sum(f * bo[m, at].astype(f32) for m, f in enumerate(group_factors))
                so[c2, z2] = total.astype(so.dtype)
        for o in range(8):
            wo_to(o).start()

    red.pull(mirror(0, g), back)
    for n, (acc, dst) in enumerate(((sq, tq), (s1, t1))):
        for o in range(8):
            rows_to(n, acc, dst, o, c * 4 + z).wait()
    mirror_copy.wait()
    kept.wait()

    @pl.when(collects)
    def _():
        wo_to(0).wait()
        for o in range(1, 8):
            wo_to(o).wait_send()

    for t in range(2):
        @pl.when(jnp.logical_or(jnp.logical_not(collects), g != t))
        def _():
            rcopy(so.at[0, 0], to.at[t], ss.at[3, 0], rs.at[3, t], (d, 3 - z)).wait_recv()

    final.wait()
    red_out.finish()
    red.finish()


def local(
    block_in, out_grad, lengths, ln1_gain, ln1_bias, qkv_weight, qkv_bias, out_weight, out_bias,
    ln2_gain, ln2_bias, fc1_weight, fc1_bias, fc2_weight, fc2_bias,
):
    tp = lax.axis_size("ctx")
    dp = lax.axis_size("dp")
    np_ = dp // 2
    world = dp * tp
    nh = HEADS // tp
    local_rows = block_in.shape[1]
    t = local_rows * tp
    rows = min(512, local_rows)
    part = D // tp
    r_in = D // world
    r_ff = fc2_weight.shape[0]
    ff = r_ff * dp

    length_parts = jnp.stack([lengths[0] // 256, lengths[0] % 256]).astype(bf16)
    packed, at = jnp.zeros((16 * PAD,), bf16), 0
    for row_of in (
        (ln1_gain, ln1_bias, out_bias, ln2_gain, ln2_bias), (fc2_bias, qkv_bias),
        (fc1_bias, length_parts),
    ):
        start = at
        for one in row_of:
            packed = packed + jnp.pad(one, (start, 16 * PAD - start - one.shape[0]))
            start += one.shape[0]
        at += PAD
    xq, dy_own, w_qkv, w1, w2, wo, tab, b_pad, length = gather(
        np_, r_in, r_ff, nh, lengths, block_in[0], out_grad[0], qkv_weight, fc1_weight, fc2_weight,
        out_weight, packed.reshape(16, PAD),
    )
    x = xq.reshape(t, D)
    w_qkv, w1 = w_qkv.reshape(D, 3 * part), w1.reshape(D, ff)
    cosine, sine = tables(t)
    q, k, v, cf, ctx, dyq, w2, wo = attn_fwd(
        np_, length, x, tab, w_qkv, b_pad, cosine, sine, dy_own, w2, wo, nh, rows
    )
    w2, wo = w2.reshape(ff, D), wo.reshape(part, D)
    out_part, u_mlp, dc, dw1, dw2, dwo, vec = mlp(
        x, dyq.reshape(t, D), ctx, cf, tab, wo, w1, w2, rows
    )
    per = np_ // 4
    block_out, input_grad, t1, tq, t2, to, mine = attn_bwd(
        np_, r_in, r_ff, x, u_mlp, q, k, v, dc, tab, w_qkv, cosine, sine, vec,
        out_part.reshape(4, local_rows, D), xq, dyq, dw1.reshape(np_, D // np_, ff),
        dw2.reshape(np_, 2 * r_ff, D), dwo.reshape(per, part // per, D),
    )
    outs = assemble(np_, block_out, input_grad, t1, tq, t2, to, mine)
    return (outs[0][None], outs[1][None]) + tuple(outs[2:])


def solution(mesh):
    both = ("dp", "ctx")
    vec, mat, act = P(both), P(both, None), P("dp", "ctx", None)
    weights = (vec, vec, mat, vec, mat, vec, vec, vec, mat, vec, mat, vec)
    return jax.shard_map(
        local,
        mesh=mesh,
        in_specs=(act, act, P("dp")) + weights,
        out_specs=(act, act) + weights + (P("dp"),),
        check_vma=False,
    )
```
